32 devices in a mesh: grp: 4 (over x, core), sub: 8 (over z, y).
Axes of the slice: x: 2, y: 2, z: 4, core: 2. Of those that a mesh axis runs over, the one named last changes fastest.
Arguments:
- states: bfloat16 [131072, 128], P(('grp', 'sub')), may hold values from -6 to 6
- cotangent: bfloat16 [131072, 128], P(('grp', 'sub')), may hold values from -6 to 6
- fine_self: bfloat16 [128, 128], replicated, may hold values from -0.5 to 0.5
- fine_other: bfloat16 [128, 128], replicated, may hold values from -0.5 to 0.5
- fine_node: bfloat16 [128, 128], replicated, may hold values from -0.375 to 0.375
- coarse_self: bfloat16 [128, 128], replicated, may hold values from -0.5 to 0.5
- coarse_other: bfloat16 [128, 128], replicated, may hold values from -0.5 to 0.5
- coarse_node: bfloat16 [128, 128], replicated, may hold values from -0.375 to 0.375
- prolong: bfloat16 [128, 128], replicated, may hold values from -0.5 to 0.5
- fine_nbr: int32 [131072, 8], P(('grp', 'sub')), may hold values from 0 to 5119, as said below
- fine_mask: int32 [131072, 8], P(('grp', 'sub')), may hold values 0 or 1
- fine_send_lo: int32 [16384], P(('grp', 'sub')), may hold values from 0 to 4095
- fine_send_hi: int32 [16384], P(('grp', 'sub')), may hold values from 0 to 4095
- coarse_nbr: int32 [8192, 8], P('sub'), may hold values from 0 to 1151, as said below
- coarse_mask: int32 [8192, 8], P('sub'), may hold values 0 or 1
- coarse_send_lo: int32 [512], P('sub'), may hold values from 0 to 1023
- coarse_send_hi: int32 [512], P('sub'), may hold values from 0 to 1023
- coarse_owner: int32 [131072], P(('grp', 'sub')), may hold values from 0 to 1023, as said below
Outputs:
- result: bfloat16 [131072, 128], P(('grp', 'sub'))
- grad_states: bfloat16 [131072, 128], P(('grp', 'sub'))
- grad_weights: float32 [7, 128, 128], replicated
The draws below stay inside these ranges and needn't reach their ends.
Inputs may be any that keep to these rules, and one draw needn't show every extreme that they name: `coarse_owner`: on the devices of grp index 0 every mid-level cell is named by exactly 4096 // 1024 fine cells of that device; elsewhere names are drawn freely. `fine_nbr`: with B = 64, local row r of a device lies in block b = r // B; each of its slots names a row of block b of the local rows (b * B to b * B + B - 1), or row 4096 + (b % 8) * B + j, or row 4608 + (b % 8) * B + j, for some j below B. `coarse_nbr`: local row r of a partition lies in block b = r // 64; each of its slots names a row of block b of the local rows, or any of the 128 halo rows of the table.
All inputs are finite; a program needn't handle non-finite values. No bound on the sum of `fine_mask` or of `coarse_mask` on one device may be relied on, other than what follows from the above.
Results may differ from the reference program's by a relative error of at most 0.015.
Values may be sent and summed in bfloat16 or wider, within the bound.
No kernel may reach another device: no remote copies, remote signals or barrier semaphores. Data moves between devices by JAX's collectives and lax.ppermute only.
A program may use at most 128 MiB of HBM per device.

```python
import jax
import jax.numpy as jnp
from jax import lax

D = 128
K = 8
NF_DEV = 4096
NC_DEV = 1024
HALO = 512
HALO_C = 64
NF = 131072
NC = 8192
N_GRP = 4
N_SUB = 8


def local_slots(key, rows_dev, halo_rows, block_rows, devices):
    total_rows = rows_dev * devices
    positions = jnp.arange(total_rows, dtype=jnp.int32)
    local_row = positions % rows_dev
    block_index = local_row // block_rows
    halo_blocks = halo_rows // block_rows
    halo_index = block_index % halo_blocks
    picks = jax.random.randint(key, (total_rows, K), 0, 3 * block_rows).astype(jnp.int32)
    base_local = (block_index * block_rows)[:, None]
    base_low = (rows_dev + halo_index * block_rows)[:, None]
    base_high = (rows_dev + halo_rows + halo_index * block_rows)[:, None]
    chosen = jnp.where(picks < block_rows, base_local + picks, jnp.where(picks < 2 * block_rows, base_low + picks - block_rows, base_high + picks - 2 * block_rows))
    return chosen.astype(jnp.int32)


def draw_fine_nbr(key, part):
    key = jax.random.fold_in(key, 11)
    return local_slots(key, NF_DEV, HALO, NF_DEV // 64, N_GRP * N_SUB)


def draw_coarse_nbr(key, part):
    key = jax.random.fold_in(key, 13)
    return local_slots(key, NC_DEV, HALO_C, HALO_C, N_SUB)


def draw_coarse_owner(key, part):
    key = jax.random.fold_in(key, 5)
    total_rows = NF_DEV * N_GRP * N_SUB
    positions = jnp.arange(total_rows, dtype=jnp.int32)
    local_row = positions % NF_DEV
    device_part = positions // NF_DEV % N_SUB
    group_index = positions // (NF_DEV * N_SUB)
    part_keys = jax.random.split(key, N_SUB)
    orders = jax.vmap(lambda single: jax.random.permutation(single, NF_DEV))(part_keys)
    covered = orders[device_part, local_row] % NC_DEV
    drawn = jax.random.randint(jax.random.fold_in(key, 1), (total_rows,), 0, NC_DEV)
    return jnp.where(group_index == 0, covered, drawn).astype(jnp.int32)


def touch_ends(array, key, smallest, top_value):
    longest = array.shape.index(max(array.shape))
    spots = []
    for shift in (0, 1):
        where = [jax.random.randint(jax.random.fold_in(key, axis), (), 0, length) for axis, length in enumerate(array.shape)]
        where[longest] = (where[longest] + shift) % array.shape[longest]
        spots.append(tuple(where))
    return array.at[spots[0]].set(smallest).at[spots[1]].set(top_value)


def block_levels(stream_key, extent, cuts, smallest, largest):
    gain = 1.0
    for dim, blocks in cuts:
        draws = jax.random.uniform(jax.random.fold_in(jax.random.fold_in(stream_key, 6), dim), (blocks,), jnp.float32, smallest / len(cuts), largest / len(cuts))
        gain = gain * jnp.repeat(jnp.exp(draws), extent[dim] // blocks).reshape((-1,) + (1,) * (len(extent) - 1 - dim))
    return gain


def noise(own_key, extent, deviation, most, shards=(), held_as=jnp.bfloat16):
    values = jax.random.normal(own_key, extent, jnp.float32) * deviation
    if len(shards) > 0:
        values = block_levels(own_key, extent, shards, -0.22, 0.18) * values
    return jnp.clip(values, min=-most, max=most).astype(held_as)


def setup_inputs(seed: int = 0) -> dict:
    splits = jax.random.split(jax.random.key(seed), 19)
    return {
        "states": noise(splits[0], (NF, D), 1.0, 6.0, ((0, 32),)),
        "cotangent": noise(splits[1], (NF, D), 1.0, 6.0, ((0, 32),)),
        "fine_self": noise(splits[2], (D, D), D ** -0.5, 0.5),
        "fine_other": noise(splits[3], (D, D), D ** -0.5, 0.5),
        "fine_node": noise(splits[4], (D, D), (2 * D) ** -0.5, 0.375),
        "coarse_self": noise(splits[5], (D, D), D ** -0.5, 0.5),
        "coarse_other": noise(splits[6], (D, D), D ** -0.5, 0.5),
        "coarse_node": noise(splits[7], (D, D), (2 * D) ** -0.5, 0.375),
        "prolong": noise(splits[8], (D, D), D ** -0.5, 0.5),
        "fine_nbr": draw_fine_nbr(jax.random.fold_in(splits[18], 71), 0),
        "fine_mask": touch_ends((jax.random.randint(splits[10], (NF, K), 0, 4) < 3).astype(jnp.int32), jax.random.fold_in(splits[10], 1), 0, 1),
        "fine_send_lo": touch_ends(jax.random.randint(splits[11], (N_GRP * N_SUB * HALO,), 0, NF_DEV), jax.random.fold_in(splits[11], 1), 0, NF_DEV - 1).astype(jnp.int32),
        "fine_send_hi": touch_ends(jax.random.randint(splits[12], (N_GRP * N_SUB * HALO,), 0, NF_DEV), jax.random.fold_in(splits[12], 1), 0, NF_DEV - 1).astype(jnp.int32),
        "coarse_nbr": draw_coarse_nbr(jax.random.fold_in(splits[18], 71), 0),
        "coarse_mask": touch_ends((jax.random.randint(splits[14], (NC, K), 0, 4) < 3).astype(jnp.int32), jax.random.fold_in(splits[14], 1), 0, 1),
        "coarse_send_lo": touch_ends(jax.random.randint(splits[15], (N_SUB * HALO_C,), 0, NC_DEV), jax.random.fold_in(splits[15], 1), 0, NC_DEV - 1).astype(jnp.int32),
        "coarse_send_hi": touch_ends(jax.random.randint(splits[16], (N_SUB * HALO_C,), 0, NC_DEV), jax.random.fold_in(splits[16], 1), 0, NC_DEV - 1).astype(jnp.int32),
        "coarse_owner": draw_coarse_owner(jax.random.fold_in(splits[18], 71), 0),
    }


highest = lax.Precision.HIGHEST


def halo_table(far_term, send_lo, send_hi):
    groups, parts = far_term.shape[0], far_term.shape[1]
    group_index = jnp.arange(groups)[:, None, None]
    part_index = jnp.arange(parts)[None, :, None]
    going_up = far_term[group_index, part_index, send_hi]
    going_down = far_term[group_index, part_index, send_lo]
    zero_rows = jnp.zeros_like(going_up[:, :1])
    from_lower = jnp.concatenate([zero_rows, going_up[:, :-1]], axis=1)
    from_upper = jnp.concatenate([going_down[:, 1:], zero_rows], axis=1)
    return jnp.concatenate([far_term, from_lower, from_upper], axis=2)


def edge_sum(own_term, table, neighbours, in_use):
    preact = own_term[:, None, :] + table[neighbours].astype(jnp.float32)
    return (jax.nn.silu(preact) * in_use[..., None].astype(jnp.float32)).sum(1).astype(jnp.bfloat16)


def edge_back(own_term, table, neighbours, in_use, grad_sum):
    preact = own_term[:, None, :] + table[neighbours].astype(jnp.float32)
    gate_value = jax.nn.sigmoid(preact)
    slope = gate_value * (1.0 + preact * (1.0 - gate_value))
    grad_pre = grad_sum[:, None, :] * in_use[..., None].astype(jnp.float32) * slope
    features = own_term.shape[1]
    grad_table = jax.ops.segment_sum(grad_pre.reshape(-1, features), neighbours.reshape(-1), num_segments=table.shape[0])
    return grad_pre.sum(1), grad_table


def level_forward(latents, w_self, w_other, w_node, neighbours, in_use, send_lo, send_hi):
    groups, parts, rows, features = latents.shape
    flat = latents.reshape(-1, features)
    own_term = jnp.dot(flat, w_self, preferred_element_type=jnp.float32).reshape(groups, parts, rows, features)
    far_term = jnp.dot(flat, w_other, preferred_element_type=jnp.float32).astype(jnp.bfloat16).reshape(groups, parts, rows, features)
    table = halo_table(far_term, send_lo, send_hi)
    table_rows = table.shape[2]
    summed = lax.map(lambda piece: edge_sum(*piece), (own_term.reshape(-1, rows, features), table.reshape(-1, table_rows, features), neighbours.reshape(-1, rows, neighbours.shape[-1]), in_use.reshape(-1, rows, neighbours.shape[-1])))
    summed = summed.reshape(groups, parts, rows, features)
    updated = flat.astype(jnp.float32) + jnp.dot(summed.reshape(-1, features), w_node, preferred_element_type=jnp.float32)
    return updated.reshape(groups, parts, rows, features), own_term, table, summed


def level_backward(latents, w_self, w_other, w_node, own_term, table, summed, neighbours, in_use, send_lo, send_hi, grad_up):
    groups, parts, rows, features = latents.shape
    halo_rows = send_lo.shape[2]
    grad_flat = grad_up.reshape(-1, features)
    grad_sum = jnp.dot(grad_flat, w_node.astype(jnp.float32).T, precision=highest)
    grad_node = jnp.dot(summed.reshape(-1, features).astype(jnp.float32).T, grad_flat, precision=highest)
    table_rows = table.shape[2]
    grad_own, grad_table = lax.map(lambda piece: edge_back(*piece), (own_term.reshape(-1, rows, features), table.reshape(-1, table_rows, features), neighbours.reshape(-1, rows, neighbours.shape[-1]), in_use.reshape(-1, rows, neighbours.shape[-1]), grad_sum.reshape(-1, rows, features)))
    grad_own = grad_own.reshape(groups, parts, rows, features)
    grad_table = grad_table.reshape(groups, parts, table_rows, features)
    lower_part = grad_table[:, :, rows:rows + halo_rows]
    upper_part = grad_table[:, :, rows + halo_rows:]
    zero_rows = jnp.zeros_like(lower_part[:, :1])
    back_down = jnp.concatenate([lower_part[:, 1:], zero_rows], axis=1)
    back_up = jnp.concatenate([zero_rows, upper_part[:, :-1]], axis=1)
    group_index = jnp.arange(groups)[:, None, None]
    part_index = jnp.arange(parts)[None, :, None]
    grad_far = grad_table[:, :, :rows]
    grad_far = grad_far.at[group_index, part_index, send_hi].add(back_down)
    grad_far = grad_far.at[group_index, part_index, send_lo].add(back_up)
    own_flat = grad_own.reshape(-1, features)
    far_flat = grad_far.reshape(-1, features)
    latent_flat = latents.reshape(-1, features).astype(jnp.float32)
    grad_self = jnp.dot(latent_flat.T, own_flat, precision=highest)
    grad_other = jnp.dot(latent_flat.T, far_flat, precision=highest)
    grad_latent = grad_flat + jnp.dot(own_flat, w_self.astype(jnp.float32).T, precision=highest) + jnp.dot(far_flat, w_other.astype(jnp.float32).T, precision=highest)
    return grad_latent, grad_self, grad_other, grad_node


def reference(states, cotangent, fine_self, fine_other, fine_node, coarse_self, coarse_other, coarse_node, prolong, fine_nbr, fine_mask, fine_send_lo, fine_send_hi, coarse_nbr, coarse_mask, coarse_send_lo, coarse_send_hi, coarse_owner):
    groups, parts = N_GRP, N_SUB
    features = states.shape[1]
    slots = fine_nbr.shape[1]
    fine_rows = states.shape[0] // (groups * parts)
    coarse_rows = coarse_nbr.shape[0] // parts
    latents = states.reshape(groups, parts, fine_rows, features)
    fine_n = fine_nbr.reshape(groups, parts, fine_rows, slots)
    fine_m = fine_mask.reshape(groups, parts, fine_rows, slots)
    fine_lo = fine_send_lo.reshape(groups, parts, -1)
    fine_hi = fine_send_hi.reshape(groups, parts, -1)
    updated, own_term, table, summed = level_forward(latents, fine_self, fine_other, fine_node, fine_n, fine_m, fine_lo, fine_hi)
    segment_ids = (jnp.arange(parts, dtype=jnp.int32)[None, :, None] * coarse_rows + coarse_owner.reshape(groups, parts, fine_rows)).reshape(-1).astype(jnp.int32)
    totals = jax.ops.segment_sum(updated.reshape(-1, features), segment_ids, num_segments=parts * coarse_rows)
    counts = jax.ops.segment_sum(jnp.ones(segment_ids.shape[0], jnp.float32), segment_ids, num_segments=parts * coarse_rows)
    coarse_in = (totals / counts[:, None]).astype(jnp.bfloat16).reshape(1, parts, coarse_rows, features)
    coarse_n = coarse_nbr.reshape(1, parts, coarse_rows, slots)
    coarse_m = coarse_mask.reshape(1, parts, coarse_rows, slots)
    coarse_lo = coarse_send_lo.reshape(1, parts, -1)
    coarse_hi = coarse_send_hi.reshape(1, parts, -1)
    coarse_up, coarse_own, coarse_table, coarse_sum = level_forward(coarse_in, coarse_self, coarse_other, coarse_node, coarse_n, coarse_m, coarse_lo, coarse_hi)
    coarse_out = coarse_up.astype(jnp.bfloat16).reshape(-1, features)
    picked = coarse_out[segment_ids]
    result = (updated.reshape(-1, features) + jnp.dot(picked, prolong, preferred_element_type=jnp.float32)).astype(jnp.bfloat16)
    grad_out = cotangent.astype(jnp.float32)
    grad_prolong = jnp.dot(picked.astype(jnp.float32).T, grad_out, precision=highest)
    grad_picked = jnp.dot(grad_out, prolong.astype(jnp.float32).T, precision=highest)
    grad_coarse = jax.ops.segment_sum(grad_picked, segment_ids, num_segments=parts * coarse_rows)
    grad_cin, grad_cself, grad_cother, grad_cnode = level_backward(coarse_in, coarse_self, coarse_other, coarse_node, coarse_own, coarse_table, coarse_sum, coarse_n, coarse_m, coarse_lo, coarse_hi, grad_coarse.reshape(1, parts, coarse_rows, features))
    grad_mean = grad_cin.reshape(-1, features) / counts[:, None]
    grad_updated = grad_out + grad_mean[segment_ids]
    grad_latent, grad_fself, grad_fother, grad_fnode = level_backward(latents, fine_self, fine_other, fine_node, own_term, table, summed, fine_n, fine_m, fine_lo, fine_hi, grad_updated.reshape(groups, parts, fine_rows, features))
    grad_weights = jnp.stack([grad_fself, grad_fother, grad_fnode, grad_cself, grad_cother, grad_cnode, grad_prolong])
    return result, grad_latent.astype(jnp.bfloat16), grad_weights
```

```python
import functools

import jax
import jax.numpy as jnp
from jax import lax
from jax.experimental import pallas as pl
from jax.experimental.pallas import tpu as pltpu
from jax.sharding import PartitionSpec as P

f32 = jnp.float32
bf16 = jnp.bfloat16
BLOCK = 64
PAIR = 2 * BLOCK
NEVER = -1e30
DIGIT = 64.0
VMEM = pl.BlockSpec(memory_space=pltpu.VMEM)
SMEM = pl.BlockSpec(memory_space=pltpu.SMEM)
PARAMS = pltpu.CompilerParams(vmem_limit_bytes=48 * 1024 * 1024)


def dot(a, b):
    return jnp.dot(a, b, preferred_element_type=f32)


def dot_nt(a, b):
    return lax.dot_general(a, b, (((1,), (1,)), ((), ())), preferred_element_type=f32)


def dot_tn(a, b):
    return lax.dot_general(a, b, (((0,), (0,)), ((), ())), preferred_element_type=f32)


def pick(condition):
    return jnp.where(condition, 1.0, 0.0).astype(bf16)


def pick16(values, places):
    return jnp.where(values == places, jnp.ones((), bf16), jnp.zeros((), bf16))


def call(kernel, out_shape, args, in_specs=None, scratch=()):
    many = isinstance(out_shape, (list, tuple))
    return pl.pallas_call(
        kernel,
        out_shape=out_shape,
        in_specs=in_specs or [VMEM] * len(args),
        out_specs=[VMEM] * len(out_shape) if many else VMEM,
        scratch_shapes=list(scratch),
        compiler_params=PARAMS,
    )(*args)


def shape(rows, columns, dtype):
    return jax.ShapeDtypeStruct((rows, columns), dtype)


def slot_columns(pair, nbr, mask, rows, halo_rows):
    lane = lax.broadcasted_iota(jnp.int32, nbr.shape, 1)
    block = 2 * pair + lane // BLOCK
    halo = lax.rem(block, halo_rows // BLOCK) * BLOCK
    column = jnp.where(
        nbr < rows,
        nbr - block * BLOCK,
        jnp.where(
            nbr < rows + halo_rows,
            BLOCK + nbr - rows - halo,
            2 * BLOCK + nbr - rows - halo_rows - halo,
        ),
    )
    return jnp.where(mask > 0, column, 3 * BLOCK).astype(f32)


def selector(columns_t, half):
    first = lax.broadcasted_iota(jnp.int32, (BLOCK, 128), 1).astype(bf16)
    second = (lax.broadcasted_iota(jnp.int32, (BLOCK, 128), 1) + 128).astype(bf16)
    parts = []
    for k in range(8):
        own = columns_t[half * BLOCK : (half + 1) * BLOCK, k : k + 1]
        wide = jnp.broadcast_to(own, (BLOCK, 128)).astype(bf16)
        parts.append(jnp.concatenate([pick16(wide, first), pick16(wide, second)], 1))
    return jnp.concatenate(parts, 0)


def selector_t(columns, rolled, half):
    lane = lax.broadcasted_iota(jnp.int32, (1, 128), 1)
    place = lax.broadcasted_iota(jnp.int32, (3 * BLOCK, 128), 0).astype(bf16)
    parts = []
    for j in range(4):
        left, right = (columns, rolled) if half == 0 else (rolled, columns)
        row = jnp.where(lane < BLOCK, left[2 * j : 2 * j + 1], right[2 * j + 1 : 2 * j + 2])
        wide = jnp.broadcast_to(row, (3 * BLOCK, 128)).astype(bf16)
        parts.append(pick16(wide, place))
    return jnp.concatenate(parts, 1)


def window_of(far_half, halo_ref, block, halo_rows):
    start = pl.multiple_of(lax.rem(block, halo_rows // BLOCK) * BLOCK, BLOCK)
    return jnp.concatenate(
        [
            far_half,
            halo_ref[pl.ds(start, BLOCK), :],
            halo_ref[pl.ds(halo_rows + start, BLOCK), :],
            jnp.full((BLOCK, far_half.shape[1]), NEVER, bf16),
        ],
        0,
    )


def rows_of(pair):
    return pl.ds(pl.multiple_of(pair * PAIR, PAIR), PAIR)


def gather_kernel(lo_ref, hi_ref, x_ref, up_ref, down_ref, wide, up, down):
    wide[...] = x_ref[...].astype(f32)

    def step(r, carry):
        up[pl.ds(r, 1), :] = wide[pl.ds(hi_ref[r], 1), :]
        down[pl.ds(r, 1), :] = wide[pl.ds(lo_ref[r], 1), :]
        return carry

    lax.fori_loop(0, up.shape[0], step, None, unroll=16)
    up_ref[...] = up[...].astype(bf16)
    down_ref[...] = down[...].astype(bf16)


def gather_rows(x, send_lo, send_hi):
    rows, features = x.shape
    count = send_lo.shape[0]
    out = shape(count, features, bf16)
    return call(
        gather_kernel,
        [out, out],
        [send_lo, send_hi, x],
        [SMEM, SMEM, VMEM],
        [
            pltpu.VMEM((rows, features), f32),
            pltpu.VMEM((count, features), f32),
            pltpu.VMEM((count, features), f32),
        ],
    )


def owner_sums(owner_ref, tile, values):
    place = lax.broadcasted_iota(jnp.int32, (128, 128), 0) + tile * 128
    groups = owner_ref.shape[0]
    rows = jnp.concatenate(
        [pick(owner_ref[q : q + 1, :] == place) for q in range(groups)], 1
    )
    return dot(rows, values)


def cotangent_kernel(owner_ref, g_ref, out_ref, *, coarse_rows):
    tiles = coarse_rows // 128

    def step(tile, carry):
        out_ref[rows_of(tile), :] = owner_sums(owner_ref, tile, g_ref[...]).astype(bf16)
        return carry

    lax.fori_loop(0, tiles, step, None)
    owner = owner_ref[...]
    high, low = owner // 128, lax.rem(owner, 128)
    groups = owner.shape[0]
    place = lax.broadcasted_iota(jnp.int32, (128, 128), 0)
    high_rows = jnp.concatenate(
        [pick(high[q : q + 1, :] == place[:tiles]) for q in range(groups)], 1
    )
    low_rows = jnp.concatenate(
        [pick(low[q : q + 1, :] == place) for q in range(groups)], 1
    )
    counts = dot_nt(high_rows, low_rows)
    most = jnp.floor(counts * (1 / DIGIT))
    out_ref[coarse_rows:, :] = jnp.concatenate([most, counts - DIGIT * most], 0).astype(bf16)


def fine_forward_kernel(
    h_ref,
    lower_ref,
    upper_ref,
    self_ref,
    other_ref,
    node_ref,
    nbr_ref,
    mask_ref,
    owner_ref,
    summed_ref,
    totals_ref,
    halo,
    new,
):
    rows = h_ref.shape[0]
    halo_rows = lower_ref.shape[0]
    other = other_ref[...] * 0.5
    both = jnp.concatenate([self_ref[...] * 0.5, other], 1)
    halo[:halo_rows, :] = dot(lower_ref[...], other).astype(bf16)
    halo[halo_rows:, :] = dot(upper_ref[...], other).astype(bf16)

    def step(pair, carry):
        here = rows_of(pair)
        h = h_ref[here, :]
        terms = dot(h, both)
        own, far = terms[:, :128], terms[:, 128:].astype(bf16)
        columns = slot_columns(pair, nbr_ref[:, here], mask_ref[:, here], rows, halo_rows)
        columns_t = columns.T
        sums = []
        for half in range(2):
            part = slice(half * BLOCK, (half + 1) * BLOCK)
            window = window_of(far[part], halo, 2 * pair + half, halo_rows)
            picked = dot(selector(columns_t, half), window)
            total = None
            for k in range(8):
                y = picked[k * BLOCK : (k + 1) * BLOCK] + own[part]
                value = y + y * jnp.tanh(y)
                total = value if total is None else total + value
            sums.append(total)
        summed = jnp.concatenate(sums, 0).astype(bf16)
        summed_ref[here, :] = summed
        new[here, :] = (h.astype(f32) + dot(summed, node_ref[...])).astype(bf16)
        return carry

    lax.fori_loop(0, rows // PAIR, step, None)

    def tile_step(tile, carry):
        totals_ref[rows_of(tile), :] = owner_sums(owner_ref, tile, new[...]).astype(bf16)
        return carry

    lax.fori_loop(0, totals_ref.shape[0] // 128, tile_step, None)


def count_columns(counts_ref):
    return counts_ref[...].T


def coarse_input_kernel(totals_ref, counts_ref, lo_ref, hi_ref, cin_ref, up_ref, down_ref):
    per_row = count_columns(counts_ref)
    for tile in range(totals_ref.shape[0] // 128):
        here = slice(tile * 128, (tile + 1) * 128)
        cin_ref[here, :] = (totals_ref[here, :] / per_row[:, tile : tile + 1]).astype(bf16)
    cin = cin_ref[...]
    place = lax.broadcasted_iota(jnp.int32, (cin.shape[0], lo_ref.shape[1]), 0)
    up_ref[...] = dot_tn(pick(hi_ref[...] == place), cin).astype(bf16)
    down_ref[...] = dot_tn(pick(lo_ref[...] == place), cin).astype(bf16)


def pair_backward(pair, own, far, halo, halo_rows, columns, grad_sum, halo_grad):
    columns_t = columns.T
    rolled = pltpu.roll(columns, BLOCK, 1)
    sums, downs, locals_ = [], [], []
    for half in range(2):
        part = slice(half * BLOCK, (half + 1) * BLOCK)
        block = 2 * pair + half
        window = window_of(far[part], halo, block, halo_rows)
        picked = dot(selector(columns_t, half), window)
        total, down, pieces = None, None, []
        for k in range(8):
            y = picked[k * BLOCK : (k + 1) * BLOCK] + own[part]
            t = jnp.tanh(y)
            up = 1.0 + t
            value = y * up
            grad = grad_sum[part] * (up * (1.0 + (y - y * t)))
            total = value if total is None else total + value
            down = grad if down is None else down + grad
            pieces.append(grad.astype(bf16))
        grad_window = dot(selector_t(columns, rolled, half), jnp.concatenate(pieces, 0))
        start = pl.multiple_of(lax.rem(block, halo_rows // BLOCK) * BLOCK, BLOCK)
        for side in range(2):
            place = pl.ds(side * halo_rows + start, BLOCK)
            halo_grad[place, :] += grad_window[(side + 1) * BLOCK : (side + 2) * BLOCK]
        sums.append(total)
        downs.append(down)
        locals_.append(grad_window[:BLOCK])
    return (
        jnp.concatenate(sums, 0),
        jnp.concatenate(downs, 0),
        jnp.concatenate(locals_, 0),
    )


def coarse_kernel(
    cin_ref,
    lower_ref,
    upper_ref,
    sums_ref,
    self_ref,
    other_ref,
    node_ref,
    prolong_ref,
    nbr_ref,
    mask_ref,
    part_ref,
    lower_grad_ref,
    upper_grad_ref,
    fine_ref,
    weights_ref,
    halo,
    halo_grad,
    summed,
    ups,
    downs,
):
    rows = cin_ref.shape[0]
    halo_rows = lower_ref.shape[0]
    other = other_ref[...] * 0.5
    both = jnp.concatenate([self_ref[...] * 0.5, other], 1)
    plain = jnp.concatenate([self_ref[...], other_ref[...]], 1)
    halo[:halo_rows, :] = dot(lower_ref[...], other).astype(bf16)
    halo[halo_rows:, :] = dot(upper_ref[...], other).astype(bf16)
    halo_grad[...] = jnp.zeros_like(halo_grad)

    def step(pair, carry):
        here = rows_of(pair)
        cin = cin_ref[here, :]
        grad_up = dot_nt(sums_ref[here, :], prolong_ref[...])
        up16 = grad_up.astype(bf16)
        grad_sum = dot_nt(up16, node_ref[...]) * 0.5
        terms = dot(cin, both)
        columns = slot_columns(pair, nbr_ref[:, here], mask_ref[:, here], rows, halo_rows)
        total, down, local = pair_backward(
            pair, terms[:, :128], terms[:, 128:].astype(bf16), halo, halo_rows, columns,
            grad_sum, halo_grad,
        )
        both_down = jnp.concatenate([down, local], 1).astype(bf16)
        summed[here, :] = total.astype(bf16)
        ups[here, :] = up16
        downs[here, :] = both_down
        part_ref[here, :] = grad_up + dot_nt(both_down, plain)
        return carry

    lax.fori_loop(0, rows // PAIR, step, None)
    lower_grad = halo_grad[:halo_rows, :].astype(bf16)
    upper_grad = halo_grad[halo_rows:, :].astype(bf16)
    lower_grad_ref[...] = lower_grad
    upper_grad_ref[...] = upper_grad
    cin = cin_ref[...]
    out = (cin.astype(f32) + dot(summed[...], node_ref[...])).astype(bf16)
    fine_ref[...] = dot(out, prolong_ref[...]).astype(bf16)
    pair_grad = dot_tn(cin, downs[...])
    other_grad = (
        pair_grad[:, 128:] + dot_tn(lower_ref[...], lower_grad) + dot_tn(upper_ref[...], upper_grad)
    )
    weights_ref[0:128, :] = pair_grad[:, :128]
    weights_ref[128:256, :] = other_grad
    weights_ref[256:384, :] = dot_tn(summed[...], ups[...])
    weights_ref[384:512, :] = dot_tn(out, sums_ref[...])


def owner_column(owner_ref, pair):
    row = owner_ref[pl.ds(pair, 1), :].astype(f32)
    return jnp.broadcast_to(row, (8, 128)).T[:, 0:1]


def owner_rows(owner_ref, pair, values):
    wide = jnp.broadcast_to(owner_column(owner_ref, pair), (128, 128))
    lane = lax.broadcasted_iota(jnp.int32, (128, 128), 1).astype(f32)
    tiles = values.shape[0] // 128
    rows = jnp.concatenate([pick(wide == lane + 128.0 * tile) for tile in range(tiles)], 1)
    return dot(rows, values)


def result_kernel(h_ref, summed_ref, node_ref, owner_ref, fine_ref, out_ref):
    def step(pair, carry):
        here = rows_of(pair)
        updated = h_ref[here, :].astype(f32) + dot(summed_ref[here, :], node_ref[...])
        out_ref[here, :] = (updated + owner_rows(owner_ref, pair, fine_ref[...])).astype(bf16)
        return carry

    lax.fori_loop(0, h_ref.shape[0] // PAIR, step, None)


def fine_backward_kernel(
    h_ref,
    lower_ref,
    upper_ref,
    g_ref,
    summed_ref,
    self_ref,
    other_ref,
    node_ref,
    nbr_ref,
    mask_ref,
    owner_ref,
    part_ref,
    counts_ref,
    back_ref,
    sends_ref,
    coarse_other_ref,
    out_ref,
    lower_grad_ref,
    upper_grad_ref,
    weights_ref,
    halo,
    halo_grad,
    mean,
    ups,
    downs,
):
    rows = h_ref.shape[0]
    halo_rows = lower_ref.shape[0]
    coarse_rows = part_ref.shape[0]
    other = other_ref[...] * 0.5
    both = jnp.concatenate([self_ref[...] * 0.5, other], 1)
    plain = jnp.concatenate([self_ref[...], other_ref[...]], 1)
    halo[:halo_rows, :] = dot(lower_ref[...], other).astype(bf16)
    halo[halo_rows:, :] = dot(upper_ref[...], other).astype(bf16)
    halo_grad[...] = jnp.zeros_like(halo_grad)
    place = lax.broadcasted_iota(jnp.int32, (coarse_rows, sends_ref.shape[1]), 0)
    back = dot_nt(back_ref[...], coarse_other_ref[...]).astype(bf16)
    grad_in = part_ref[...] + dot(pick(sends_ref[...] == place), back)
    per_row = count_columns(counts_ref)
    for tile in range(coarse_rows // 128):
        here = slice(tile * 128, (tile + 1) * 128)
        mean[here, :] = (grad_in[here, :] / per_row[:, tile : tile + 1]).astype(bf16)

    def step(pair, carry):
        here = rows_of(pair)
        h = h_ref[here, :]
        grad_up = g_ref[here, :].astype(f32) + owner_rows(owner_ref, pair, mean[...])
        up16 = grad_up.astype(bf16)
        grad_sum = dot_nt(up16, node_ref[...]) * 0.5
        terms = dot(h, both)
        columns = slot_columns(pair, nbr_ref[:, here], mask_ref[:, here], rows, halo_rows)
        _, down, local = pair_backward(
            pair, terms[:, :128], terms[:, 128:].astype(bf16), halo, halo_rows, columns,
            grad_sum, halo_grad,
        )
        both_down = jnp.concatenate([down, local], 1).astype(bf16)
        ups[here, :] = up16
        downs[here, :] = both_down
        out_ref[here, :] = grad_up + dot_nt(both_down, plain)
        return carry

    lax.fori_loop(0, rows // PAIR, step, None)
    lower_grad = halo_grad[:halo_rows, :].astype(bf16)
    upper_grad = halo_grad[halo_rows:, :].astype(bf16)
    lower_grad_ref[...] = lower_grad
    upper_grad_ref[...] = upper_grad
    pair_grad = dot_tn(h_ref[...], downs[...])
    weights_ref[0:128, :] = pair_grad[:, :128]
    weights_ref[128:256, :] = (
        pair_grad[:, 128:] + dot_tn(lower_ref[...], lower_grad) + dot_tn(upper_ref[...], upper_grad)
    )
    weights_ref[256:384, :] = dot_tn(summed_ref[...], ups[...])


def finish_kernel(part_ref, up_ref, down_ref, lo_ref, hi_ref, other_ref, out_ref):
    other = other_ref[...]
    back = jnp.concatenate([dot_nt(up_ref[...], other), dot_nt(down_ref[...], other)], 0)
    back = back.astype(bf16)
    sends = jnp.concatenate([lo_ref[...], hi_ref[...]], 1)
    place = lax.broadcasted_iota(jnp.int32, (PAIR, sends.shape[1]), 0)

    def step(pair, carry):
        here = rows_of(pair)
        rows = pick(sends - pair * PAIR == place)
        out_ref[here, :] = (part_ref[here, :] + dot(rows, back)).astype(bf16)
        return carry

    lax.fori_loop(0, part_ref.shape[0] // PAIR, step, None)


def shifted(block, axis, distance):
    devices = range(lax.axis_size(axis))
    route = [(i - distance, i) for i in devices if i - distance in devices]
    return lax.ppermute(block, axis, route)


def swapped(block, axis, distance):
    return lax.ppermute(block, axis, [(i, i ^ distance) for i in range(lax.axis_size(axis))])


def total_over(block, axis):
    distance = 1
    total = block
    while distance < lax.axis_size(axis):
        other = swapped(total.astype(bf16), axis, distance)
        total = total.astype(f32) + other.astype(f32)
        distance *= 2
    return total


def total_over_all(block, axes):
    devices = lax.axis_size(axes)
    share = block.shape[0] // devices
    parts = lax.all_to_all(
        block.astype(bf16).reshape(devices, share, 128), axes, 0, 0, tiled=False
    )
    mine = parts.astype(f32).sum(0).astype(bf16)
    return lax.all_to_all(
        jnp.broadcast_to(mine[None], (devices, share, 128)), axes, 0, 0, tiled=False
    ).reshape(block.shape)


def per_device(
    states,
    cotangent,
    fine_self,
    fine_other,
    fine_node,
    coarse_self,
    coarse_other,
    coarse_node,
    prolong,
    fine_nbr,
    fine_mask,
    fine_send_lo,
    fine_send_hi,
    coarse_nbr,
    coarse_mask,
    coarse_send_lo,
    coarse_send_hi,
    coarse_owner,
):
    rows, features = states.shape
    coarse_rows = coarse_nbr.shape[0]
    halo_rows = fine_send_lo.shape[0]
    coarse_halo = coarse_send_lo.shape[0]
    count_rows = coarse_rows // 128
    owner = coarse_owner.reshape(rows // 128, 128)
    fine_nbr, fine_mask = fine_nbr.T, fine_mask.T
    coarse_nbr, coarse_mask = coarse_nbr.T, coarse_mask.T
    coarse_lo, coarse_hi = coarse_send_lo[None], coarse_send_hi[None]

    going_up, going_down = gather_rows(states, fine_send_lo, fine_send_hi)
    lower = shifted(going_up, "sub", 1)
    upper = shifted(going_down, "sub", -1)

    sums_counts = call(
        functools.partial(cotangent_kernel, coarse_rows=coarse_rows),
        shape(coarse_rows + 2 * count_rows, features, bf16),
        [owner, cotangent],
    )
    sums_counts = total_over(sums_counts, "grp")
    grad_sums = sums_counts[:coarse_rows].astype(bf16)
    counts = (
        DIGIT * sums_counts[coarse_rows : coarse_rows + count_rows]
        + sums_counts[coarse_rows + count_rows :]
    )

    summed, totals = call(
        fine_forward_kernel,
        [shape(rows, features, bf16), shape(coarse_rows, features, bf16)],
        [states, lower, upper, fine_self, fine_other, fine_node, fine_nbr, fine_mask, owner],
        scratch=[
            pltpu.VMEM((2 * halo_rows, features), bf16),
            pltpu.VMEM((rows, features), bf16),
        ],
    )
    totals = total_over(totals, "grp")

    coarse_in, coarse_up, coarse_down = call(
        coarse_input_kernel,
        [
            shape(coarse_rows, features, bf16),
            shape(coarse_halo, features, bf16),
            shape(coarse_halo, features, bf16),
        ],
        [totals, counts, coarse_lo, coarse_hi],
    )
    coarse_lower = shifted(coarse_up, "sub", 1)
    coarse_upper = shifted(coarse_down, "sub", -1)

    coarse_part, lower_grad, upper_grad, fine_term, coarse_weights = call(
        coarse_kernel,
        [
            shape(coarse_rows, features, f32),
            shape(coarse_halo, features, bf16),
            shape(coarse_halo, features, bf16),
            shape(coarse_rows, features, bf16),
            shape(4 * features, features, f32),
        ],
        [
            coarse_in, coarse_lower, coarse_upper, grad_sums,
            coarse_self, coarse_other, coarse_node, prolong, coarse_nbr, coarse_mask,
        ],
        scratch=[
            pltpu.VMEM((2 * coarse_halo, features), bf16),
            pltpu.VMEM((2 * coarse_halo, features), f32),
            pltpu.VMEM((coarse_rows, features), bf16),
            pltpu.VMEM((coarse_rows, features), bf16),
            pltpu.VMEM((coarse_rows, 2 * features), bf16),
        ],
    )
    back_up = shifted(upper_grad, "sub", 1)
    back_down = shifted(lower_grad, "sub", -1)
    coarse_back = jnp.concatenate([back_up, back_down], 0)
    coarse_sends = jnp.concatenate([coarse_lo, coarse_hi], 1)

    result = call(
        result_kernel,
        shape(rows, features, bf16),
        [states, summed, fine_node, owner, fine_term],
    )

    grad_part, lower_grad, upper_grad, fine_weights = call(
        fine_backward_kernel,
        [
            shape(rows, features, f32),
            shape(halo_rows, features, bf16),
            shape(halo_rows, features, bf16),
            shape(3 * features, features, f32),
        ],
        [
            states, lower, upper, cotangent, summed, fine_self, fine_other, fine_node,
            fine_nbr, fine_mask, owner, coarse_part, counts, coarse_back, coarse_sends,
            coarse_other,
        ],
        scratch=[
            pltpu.VMEM((2 * halo_rows, features), bf16),
            pltpu.VMEM((2 * halo_rows, features), f32),
            pltpu.VMEM((coarse_rows, features), bf16),
            pltpu.VMEM((rows, features), bf16),
            pltpu.VMEM((rows, 2 * features), bf16),
        ],
    )
    back_up = shifted(upper_grad, "sub", 1)
    back_down = shifted(lower_grad, "sub", -1)

    scale = 1.0 / lax.axis_size("grp")
    weights = jnp.concatenate(
        [fine_weights, coarse_weights * scale, jnp.zeros((features, features), f32)], 0
    )
    weights = total_over_all(weights, ("grp", "sub"))
    grad_weights = weights[: 7 * features].astype(f32).reshape(7, features, features)

    grad_states = call(
        finish_kernel,
        shape(rows, features, bf16),
        [grad_part, back_up, back_down, fine_send_lo[None], fine_send_hi[None], fine_other],
    )
    return (result, grad_states, grad_weights)


def solution(mesh):
    fine = P(("grp", "sub"), None)
    fine_row = P(("grp", "sub"))
    in_specs = (
        (fine, fine)
        + (P(),) * 7
        + (fine, fine, fine_row, fine_row)
        + (P("sub", None), P("sub", None), P("sub"), P("sub"), fine_row)
    )
    return jax.shard_map(
        per_device, mesh=mesh, in_specs=in_specs, out_specs=(fine, fine, P()), check_vma=False
    )
```

```python
import functools

import jax
import jax.numpy as jnp
from jax import lax
from jax.experimental import pallas as pl
from jax.experimental.pallas import tpu as pltpu
from jax.sharding import PartitionSpec as P

f32 = jnp.float32
bf16 = jnp.bfloat16
BLOCK = 64
PAIR = 2 * BLOCK
STEP = 8
CHUNK = 512
NEVER = -1e30
DIGIT = 64.0
VMEM = pl.BlockSpec(memory_space=pltpu.VMEM)
SMEM = pl.BlockSpec(memory_space=pltpu.SMEM)
ANY = pl.BlockSpec(memory_space=pl.ANY)
PARAMS = pltpu.CompilerParams(vmem_limit_bytes=48 * 1024 * 1024)


def dot(a, b):
    return jnp.dot(a, b, preferred_element_type=f32)


def dot_nt(a, b):
    return lax.dot_general(a, b, (((1,), (1,)), ((), ())), preferred_element_type=f32)


def dot_tn(a, b):
    return lax.dot_general(a, b, (((0,), (0,)), ((), ())), preferred_element_type=f32)


def pick(condition):
    return jnp.where(condition, 1.0, 0.0).astype(bf16)


def pick16(values, places):
    return jnp.where(values == places, jnp.ones((), bf16), jnp.zeros((), bf16))


def call(kernel, out_shape, args, in_specs=None, scratch=()):
    many = isinstance(out_shape, (list, tuple))
    return pl.pallas_call(
        kernel,
        out_shape=out_shape,
        in_specs=in_specs or [VMEM] * len(args),
        out_specs=[VMEM] * len(out_shape) if many else VMEM,
        scratch_shapes=list(scratch),
        compiler_params=PARAMS,
    )(*args)


def shape(rows, columns, dtype):
    return jax.ShapeDtypeStruct((rows, columns), dtype)


def slot_columns(nbr, mask, halo_rows):
    rows = nbr.shape[1]
    block = lax.broadcasted_iota(jnp.int32, nbr.shape, 1) // BLOCK
    halo = lax.rem(block, halo_rows // BLOCK) * BLOCK
    column = jnp.where(
        nbr < rows,
        nbr - block * BLOCK,
        jnp.where(
            nbr < rows + halo_rows,
            BLOCK + nbr - rows - halo,
            2 * BLOCK + nbr - rows - halo_rows - halo,
        ),
    )
    return jnp.where(mask > 0, column, 3 * BLOCK).astype(f32)


def selector(columns_t):
    first = lax.broadcasted_iota(jnp.int32, (BLOCK, 128), 1).astype(bf16)
    second = (lax.broadcasted_iota(jnp.int32, (BLOCK, 128), 1) + 128).astype(bf16)
    parts = []
    for k in range(8):
        wide = jnp.broadcast_to(columns_t[:, k : k + 1], (BLOCK, 128)).astype(bf16)
        parts.append(jnp.concatenate([pick16(wide, first), pick16(wide, second)], 1))
    return jnp.concatenate(parts, 0)


def selector_t(columns, rolled, half):
    lane = lax.broadcasted_iota(jnp.int32, (1, 128), 1)
    place = lax.broadcasted_iota(jnp.int32, (3 * BLOCK, 128), 0).astype(bf16)
    parts = []
    for j in range(4):
        left, right = (columns, rolled) if half == 0 else (rolled, columns)
        row = jnp.where(lane < BLOCK, left[2 * j : 2 * j + 1], right[2 * j + 1 : 2 * j + 2])
        wide = jnp.broadcast_to(row, (3 * BLOCK, 128)).astype(bf16)
        parts.append(pick16(wide, place))
    return jnp.concatenate(parts, 1)


def window_of(far, halo, place):
    halo_rows = halo.shape[0] // 2
    start = place * BLOCK
    return jnp.concatenate(
        [
            far,
            halo[start : start + BLOCK, :],
            halo[halo_rows + start : halo_rows + start + BLOCK, :],
            jnp.full((BLOCK, far.shape[1]), NEVER, bf16),
        ],
        0,
    )


def chunk_of(index, count):
    return pl.ds(pl.multiple_of(index * count, count), count)


def level_terms(h_ref, lower_ref, upper_ref, self_ref, other_ref, own, far, halo):
    halo_rows = lower_ref.shape[0]
    other = other_ref[...] * 0.5
    h = h_ref[...]
    own[...] = dot(h, self_ref[...] * 0.5)
    far[...] = dot(h, other).astype(bf16)
    halo[:halo_rows, :] = dot(lower_ref[...], other).astype(bf16)
    halo[halo_rows:, :] = dot(upper_ref[...], other).astype(bf16)


def edge_loop(own, far, halo, columns, columns_t, finish):
    places = halo.shape[0] // (2 * BLOCK)
    assert STEP % places == 0

    def step(index, carry):
        own_rows = own[chunk_of(index, STEP * BLOCK), :]
        far_rows = far[chunk_of(index, STEP * BLOCK), :]
        slots = columns_t[chunk_of(index, STEP * BLOCK), :]
        tables = []
        for n in range(STEP):
            part = slice(n * BLOCK, (n + 1) * BLOCK)
            window = window_of(far_rows[part], halo, n % places)
            tables.append((own_rows[part], dot(selector(slots[part]), window)))
        finish(index, tables)
        return carry

    lax.fori_loop(0, own.shape[0] // (STEP * BLOCK), step, None)


def forward_sums(tables):
    sums = []
    for own, picked in tables:
        total = None
        for k in range(8):
            y = picked[k * BLOCK : (k + 1) * BLOCK] + own
            value = y + y * jnp.tanh(y)
            total = value if total is None else total + value
        sums.append(total)
    return jnp.concatenate(sums, 0).astype(bf16)


def backward_edges(tables, grad_sum, columns, halo_grad, summed=None):
    places = halo_grad.shape[0] // (2 * BLOCK)
    halo_rows = halo_grad.shape[0] // 2
    sums, downs, grads = [], [], []
    for n, (own, picked) in enumerate(tables):
        part = grad_sum[n * BLOCK : (n + 1) * BLOCK]
        total, down, pieces = None, None, []
        for k in range(8):
            y = picked[k * BLOCK : (k + 1) * BLOCK] + own
            t = jnp.tanh(y)
            up = 1.0 + t
            if summed is not None:
                total = y * up if total is None else total + y * up
            grad = part * (up * (1.0 + (y - y * t)))
            down = grad if down is None else down + grad
            pieces.append(grad.astype(bf16))
        sums.append(total)
        downs.append(down)
        grads.append(jnp.concatenate(pieces, 0))
    windows = []
    for n, grad in enumerate(grads):
        mine = columns[:, n // 2 * PAIR : (n // 2 + 1) * PAIR]
        windows.append(dot(selector_t(mine, pltpu.roll(mine, BLOCK, 1), n % 2), grad))
    for place in range(places):
        for side in range(2):
            start = side * halo_rows + place * BLOCK
            total = halo_grad[start : start + BLOCK, :]
            for window in windows[place::places]:
                total = total + window[(side + 1) * BLOCK : (side + 2) * BLOCK]
            halo_grad[start : start + BLOCK, :] = total
    local = jnp.concatenate([window[:BLOCK] for window in windows], 0)
    down = jnp.concatenate(downs, 0)
    if summed is None:
        return None, down, local
    return jnp.concatenate(sums, 0).astype(bf16), down, local


def gather_kernel(lo_ref, hi_ref, x_ref, up_ref, down_ref, wide, up, down):
    wide[...] = x_ref[...].astype(f32)

    def step(r, carry):
        up[pl.ds(r, 1), :] = wide[pl.ds(hi_ref[r], 1), :]
        down[pl.ds(r, 1), :] = wide[pl.ds(lo_ref[r], 1), :]
        return carry

    lax.fori_loop(0, up.shape[0], step, None, unroll=16)
    up_ref[...] = up[...].astype(bf16)
    down_ref[...] = down[...].astype(bf16)


def gather_rows(x, send_lo, send_hi):
    rows, features = x.shape
    count = send_lo.shape[0]
    out = shape(count, features, bf16)
    return call(
        gather_kernel,
        [out, out],
        [send_lo, send_hi, x],
        [SMEM, SMEM, VMEM],
        [
            pltpu.VMEM((rows, features), f32),
            pltpu.VMEM((count, features), f32),
            pltpu.VMEM((count, features), f32),
        ],
    )


def owner_sums(owner_ref, tile, values):
    place = lax.broadcasted_iota(jnp.int32, (128, 128), 0) + tile * 128
    groups = owner_ref.shape[0]
    rows = jnp.concatenate(
        [pick(owner_ref[q : q + 1, :] == place) for q in range(groups)], 1
    )
    return dot(rows, values)


def cotangent_kernel(owner_ref, g_ref, after_ref, out_ref, *, coarse_rows):
    tiles = coarse_rows // 128

    def step(tile, carry):
        out_ref[chunk_of(tile, 128), :] = owner_sums(owner_ref, tile, g_ref[...]).astype(bf16)
        return carry

    lax.fori_loop(0, tiles, step, None)
    owner = owner_ref[...]
    high, low = owner // 128, lax.rem(owner, 128)
    groups = owner.shape[0]
    place = lax.broadcasted_iota(jnp.int32, (128, 128), 0)
    high_rows = jnp.concatenate(
        [pick(high[q : q + 1, :] == place[:tiles]) for q in range(groups)], 1
    )
    low_rows = jnp.concatenate(
        [pick(low[q : q + 1, :] == place) for q in range(groups)], 1
    )
    counts = dot_nt(high_rows, low_rows)
    most = jnp.floor(counts * (1 / DIGIT))
    out_ref[coarse_rows:, :] = jnp.concatenate([most, counts - DIGIT * most], 0).astype(bf16)


def fine_forward_kernel(
    h_ref,
    lower_ref,
    upper_ref,
    self_ref,
    other_ref,
    node_ref,
    nbr_ref,
    mask_ref,
    owner_ref,
    after_ref,
    summed_ref,
    totals_ref,
    own,
    far,
    halo,
    columns_t,
    new,
):
    level_terms(h_ref, lower_ref, upper_ref, self_ref, other_ref, own, far, halo)
    columns_t[...] = slot_columns(nbr_ref[...], mask_ref[...], lower_ref.shape[0]).T

    def finish(index, tables):
        summed_ref[chunk_of(index, STEP * BLOCK), :] = forward_sums(tables)

    edge_loop(own, far, halo, None, columns_t, finish)
    new[...] = (h_ref[...].astype(f32) + dot(summed_ref[...], node_ref[...])).astype(bf16)

    def tile_step(tile, carry):
        totals_ref[chunk_of(tile, 128), :] = owner_sums(owner_ref, tile, new[...]).astype(bf16)
        return carry

    lax.fori_loop(0, totals_ref.shape[0] // 128, tile_step, None)


def count_columns(counts_ref):
    return counts_ref[...].T


def coarse_input_kernel(totals_ref, counts_ref, lo_ref, hi_ref, cin_ref, up_ref, down_ref):
    per_row = count_columns(counts_ref)
    for tile in range(totals_ref.shape[0] // 128):
        here = slice(tile * 128, (tile + 1) * 128)
        cin_ref[here, :] = (totals_ref[here, :] / per_row[:, tile : tile + 1]).astype(bf16)
    cin = cin_ref[...]
    place = lax.broadcasted_iota(jnp.int32, (cin.shape[0], lo_ref.shape[1]), 0)
    up_ref[...] = dot_tn(pick(hi_ref[...] == place), cin).astype(bf16)
    down_ref[...] = dot_tn(pick(lo_ref[...] == place), cin).astype(bf16)


def coarse_kernel(
    cin_ref,
    lower_ref,
    upper_ref,
    sums_ref,
    self_ref,
    other_ref,
    node_ref,
    prolong_ref,
    nbr_ref,
    mask_ref,
    part_ref,
    lower_grad_ref,
    upper_grad_ref,
    summed_ref,
    ups_ref,
    downs_ref,
    own,
    far,
    halo,
    columns,
    columns_t,
    grad_sum,
    halo_grad,
):
    halo_rows = lower_ref.shape[0]
    level_terms(cin_ref, lower_ref, upper_ref, self_ref, other_ref, own, far, halo)
    columns[...] = slot_columns(nbr_ref[...], mask_ref[...], halo_rows)
    columns_t[...] = columns[...].T
    halo_grad[...] = jnp.zeros_like(halo_grad)
    part_ref[...] = dot_nt(sums_ref[...], prolong_ref[...])
    ups_ref[...] = part_ref[...].astype(bf16)
    grad_sum[...] = dot_nt(ups_ref[...], node_ref[...]) * 0.5

    def finish(index, tables):
        here = chunk_of(index, STEP * BLOCK)
        total, down, local = backward_edges(
            tables, grad_sum[here, :], columns[:, here], halo_grad, summed_ref
        )
        summed_ref[here, :] = total
        downs_ref[here, :] = jnp.concatenate([down, local], 1).astype(bf16)

    edge_loop(own, far, halo, columns, columns_t, finish)
    lower_grad_ref[...] = halo_grad[:halo_rows, :].astype(bf16)
    upper_grad_ref[...] = halo_grad[halo_rows:, :].astype(bf16)


def coarse_tail_kernel(
    cin_ref,
    lower_ref,
    upper_ref,
    sums_ref,
    node_ref,
    prolong_ref,
    lower_grad_ref,
    upper_grad_ref,
    summed_ref,
    ups_ref,
    downs_ref,
    fine_ref,
    weights_ref,
):
    cin = cin_ref[...]
    out = (cin.astype(f32) + dot(summed_ref[...], node_ref[...])).astype(bf16)
    fine_ref[...] = dot(out, prolong_ref[...]).astype(bf16)
    pair_grad = dot_tn(cin, downs_ref[...])
    weights_ref[0:128, :] = pair_grad[:, :128]
    weights_ref[128:256, :] = (
        pair_grad[:, 128:]
        + dot_tn(lower_ref[...], lower_grad_ref[...])
        + dot_tn(upper_ref[...], upper_grad_ref[...])
    )
    weights_ref[256:384, :] = dot_tn(summed_ref[...], ups_ref[...])
    weights_ref[384:512, :] = dot_tn(out, sums_ref[...])


def owner_columns(owner_ref):
    owner = owner_ref[...].astype(f32)
    row = jnp.concatenate([owner[q : q + 1, :] for q in range(owner.shape[0])], 1)
    return jnp.broadcast_to(row, (8, row.shape[1])).T


def owner_rows(owners, values):
    count = owners.shape[0]
    wide = jnp.broadcast_to(owners[:, 0:1], (count, 128))
    lane = lax.broadcasted_iota(jnp.int32, (count, 128), 1).astype(f32)
    tiles = values.shape[0] // 128
    rows = jnp.concatenate([pick(wide == lane + 128.0 * tile) for tile in range(tiles)], 1)
    return dot(rows, values)


def result_kernel(h_ref, summed_ref, node_ref, owner_ref, fine_ref, out_ref, owners):
    owners[...] = owner_columns(owner_ref)

    def step(index, carry):
        here = chunk_of(index, CHUNK)
        updated = h_ref[here, :].astype(f32) + dot(summed_ref[here, :], node_ref[...])
        out_ref[here, :] = (updated + owner_rows(owners[here, :], fine_ref[...])).astype(bf16)
        return carry

    lax.fori_loop(0, h_ref.shape[0] // CHUNK, step, None)


def fine_backward_kernel(
    h_ref,
    lower_ref,
    upper_ref,
    g_ref,
    summed_ref,
    self_ref,
    other_ref,
    node_ref,
    nbr_ref,
    mask_ref,
    owner_ref,
    part_ref,
    counts_ref,
    coarse_downs_ref,
    back_ref,
    sends_ref,
    coarse_self_ref,
    coarse_other_ref,
    ups_ref,
    downs_ref,
    lower_grad_ref,
    upper_grad_ref,
    weights_ref,
    own,
    far,
    halo,
    columns,
    columns_t,
    grad_sum,
    halo_grad,
    mean,
):
    halo_rows = lower_ref.shape[0]
    coarse_rows = part_ref.shape[0]
    level_terms(h_ref, lower_ref, upper_ref, self_ref, other_ref, own, far, halo)
    columns[...] = slot_columns(nbr_ref[...], mask_ref[...], halo_rows)
    halo_grad[...] = jnp.zeros_like(halo_grad)

    place = lax.broadcasted_iota(jnp.int32, (coarse_rows, sends_ref.shape[1]), 0)
    back = dot_nt(back_ref[...], coarse_other_ref[...]).astype(bf16)
    plain = jnp.concatenate([coarse_self_ref[...], coarse_other_ref[...]], 1)
    grad_in = (
        part_ref[...]
        + dot_nt(coarse_downs_ref[...], plain)
        + dot(pick(sends_ref[...] == place), back)
    )
    per_row = count_columns(counts_ref)
    for tile in range(coarse_rows // 128):
        here = slice(tile * 128, (tile + 1) * 128)
        mean[here, :] = (grad_in[here, :] / per_row[:, tile : tile + 1]).astype(bf16)

    columns_t[...] = owner_columns(owner_ref)

    def owner_step(index, carry):
        here = chunk_of(index, CHUNK)
        grad_up = g_ref[here, :].astype(f32) + owner_rows(columns_t[here, :], mean[...])
        ups_ref[here, :] = grad_up.astype(bf16)
        return carry

    lax.fori_loop(0, h_ref.shape[0] // CHUNK, owner_step, None)
    grad_sum[...] = dot_nt(ups_ref[...], node_ref[...]) * 0.5
    columns_t[...] = columns[...].T

    def finish(index, tables):
        here = chunk_of(index, STEP * BLOCK)
        _, down, local = backward_edges(
            tables, grad_sum[here, :], columns[:, here], halo_grad
        )
        downs_ref[here, :] = jnp.concatenate([down, local], 1).astype(bf16)

    edge_loop(own, far, halo, columns, columns_t, finish)
    lower_grad = halo_grad[:halo_rows, :].astype(bf16)
    upper_grad = halo_grad[halo_rows:, :].astype(bf16)
    lower_grad_ref[...] = lower_grad
    upper_grad_ref[...] = upper_grad
    pair_grad = dot_tn(h_ref[...], downs_ref[...])
    weights_ref[0:128, :] = pair_grad[:, :128]
    weights_ref[128:256, :] = (
        pair_grad[:, 128:] + dot_tn(lower_ref[...], lower_grad) + dot_tn(upper_ref[...], upper_grad)
    )
    weights_ref[256:384, :] = dot_tn(summed_ref[...], ups_ref[...])


def finish_kernel(
    ups_ref, downs_ref, up_ref, down_ref, lo_ref, hi_ref, self_ref, other_ref, out_ref
):
    other = other_ref[...]
    plain = jnp.concatenate([self_ref[...], other], 1)
    back = jnp.concatenate([dot_nt(up_ref[...], other), dot_nt(down_ref[...], other)], 0)
    back = back.astype(bf16)
    sends = jnp.concatenate([lo_ref[...], hi_ref[...]], 1)
    place = lax.broadcasted_iota(jnp.int32, (CHUNK, sends.shape[1]), 0)

    def step(index, carry):
        here = chunk_of(index, CHUNK)
        rows = pick(sends - index * CHUNK == place)
        grad = ups_ref[here, :].astype(f32) + dot_nt(downs_ref[here, :], plain)
        out_ref[here, :] = (grad + dot(rows, back)).astype(bf16)
        return carry

    lax.fori_loop(0, ups_ref.shape[0] // CHUNK, step, None)


def shifted(block, axis, distance):
    devices = range(lax.axis_size(axis))
    route = [(i - distance, i) for i in devices if i - distance in devices]
    return lax.ppermute(block, axis, route)


def swapped(block, axis, distance):
    return lax.ppermute(block, axis, [(i, i ^ distance) for i in range(lax.axis_size(axis))])


def total_over(block, axis):
    distance = 1
    total = block
    while distance < lax.axis_size(axis):
        sent = total.astype(bf16)
        total = total.astype(f32) + swapped(sent, axis, distance).astype(f32)
        distance *= 2
    return sent, total


def total_over_all(block, axes):
    devices = lax.axis_size(axes)
    share = block.shape[0] // devices
    parts = lax.all_to_all(
        block.astype(bf16).reshape(devices, share, 128), axes, 0, 0, tiled=False
    )
    mine = parts.astype(f32).sum(0).astype(bf16)
    return lax.all_to_all(
        jnp.broadcast_to(mine[None], (devices, share, 128)), axes, 0, 0, tiled=False
    ).reshape(block.shape)


def per_device(
    states,
    cotangent,
    fine_self,
    fine_other,
    fine_node,
    coarse_self,
    coarse_other,
    coarse_node,
    prolong,
    fine_nbr,
    fine_mask,
    fine_send_lo,
    fine_send_hi,
    coarse_nbr,
    coarse_mask,
    coarse_send_lo,
    coarse_send_hi,
    coarse_owner,
):
    rows, features = states.shape
    coarse_rows = coarse_nbr.shape[0]
    halo_rows = fine_send_lo.shape[0]
    coarse_halo = coarse_send_lo.shape[0]
    count_rows = coarse_rows // 128
    owner = coarse_owner.reshape(rows // 128, 128)
    fine_nbr, fine_mask = fine_nbr.T, fine_mask.T
    coarse_nbr, coarse_mask = coarse_nbr.T, coarse_mask.T
    coarse_lo, coarse_hi = coarse_send_lo[None], coarse_send_hi[None]

    def buffer(count, columns, dtype):
        return pltpu.VMEM((count, columns), dtype)

    going_up, going_down = gather_rows(states, fine_send_lo, fine_send_hi)
    lower = shifted(going_up, "sub", 1)
    upper = shifted(going_down, "sub", -1)

    sums_counts = call(
        functools.partial(cotangent_kernel, coarse_rows=coarse_rows),
        shape(coarse_rows + 2 * count_rows, features, bf16),
        [owner, cotangent, going_up],
        [VMEM, VMEM, ANY],
    )
    chip_sums, sums_counts = total_over(sums_counts, "grp")
    grad_sums = sums_counts[:coarse_rows].astype(bf16)
    counts = (
        DIGIT * sums_counts[coarse_rows : coarse_rows + count_rows]
        + sums_counts[coarse_rows + count_rows :]
    )

    summed, totals = call(
        fine_forward_kernel,
        [shape(rows, features, bf16), shape(coarse_rows, features, bf16)],
        [
            states, lower, upper, fine_self, fine_other, fine_node, fine_nbr, fine_mask, owner,
            chip_sums,
        ],
        [VMEM] * 9 + [ANY],
        [
            buffer(rows, features, f32),
            buffer(rows, features, bf16),
            buffer(2 * halo_rows, features, bf16),
            buffer(rows, 8, f32),
            buffer(rows, features, bf16),
        ],
    )
    _, totals = total_over(totals, "grp")

    coarse_in, coarse_up, coarse_down = call(
        coarse_input_kernel,
        [
            shape(coarse_rows, features, bf16),
            shape(coarse_halo, features, bf16),
            shape(coarse_halo, features, bf16),
        ],
        [totals, counts, coarse_lo, coarse_hi],
    )
    coarse_lower = shifted(coarse_up, "sub", 1)
    coarse_upper = shifted(coarse_down, "sub", -1)

    coarse_part, lower_grad, upper_grad, coarse_sum, coarse_ups, coarse_downs = call(
        coarse_kernel,
        [
            shape(coarse_rows, features, f32),
            shape(coarse_halo, features, bf16),
            shape(coarse_halo, features, bf16),
            shape(coarse_rows, features, bf16),
            shape(coarse_rows, features, bf16),
            shape(coarse_rows, 2 * features, bf16),
        ],
        [
            coarse_in, coarse_lower, coarse_upper, grad_sums,
            coarse_self, coarse_other, coarse_node, prolong, coarse_nbr, coarse_mask,
        ],
        scratch=[
            buffer(coarse_rows, features, f32),
            buffer(coarse_rows, features, bf16),
            buffer(2 * coarse_halo, features, bf16),
            buffer(8, coarse_rows, f32),
            buffer(coarse_rows, 8, f32),
            buffer(coarse_rows, features, f32),
            buffer(2 * coarse_halo, features, f32),
        ],
    )
    back_up = shifted(upper_grad, "sub", 1)
    back_down = shifted(lower_grad, "sub", -1)
    coarse_back = jnp.concatenate([back_up, back_down], 0)
    coarse_sends = jnp.concatenate([coarse_lo, coarse_hi], 1)

    fine_term, coarse_weights = call(
        coarse_tail_kernel,
        [shape(coarse_rows, features, bf16), shape(4 * features, features, f32)],
        [
            coarse_in, coarse_lower, coarse_upper, grad_sums, coarse_node, prolong,
            lower_grad, upper_grad, coarse_sum, coarse_ups, coarse_downs,
        ],
    )
    result = call(
        result_kernel,
        shape(rows, features, bf16),
        [states, summed, fine_node, owner, fine_term],
        scratch=[buffer(rows, 8, f32)],
    )

    ups, downs, lower_grad, upper_grad, fine_weights = call(
        fine_backward_kernel,
        [
            shape(rows, features, bf16),
            shape(rows, 2 * features, bf16),
            shape(halo_rows, features, bf16),
            shape(halo_rows, features, bf16),
            shape(3 * features, features, f32),
        ],
        [
            states, lower, upper, cotangent, summed, fine_self, fine_other, fine_node,
            fine_nbr, fine_mask, owner, coarse_part, counts, coarse_downs, coarse_back,
            coarse_sends, coarse_self, coarse_other,
        ],
        scratch=[
            buffer(rows, features, f32),
            buffer(rows, features, bf16),
            buffer(2 * halo_rows, features, bf16),
            buffer(8, rows, f32),
            buffer(rows, 8, f32),
            buffer(rows, features, f32),
            buffer(2 * halo_rows, features, f32),
            buffer(coarse_rows, features, bf16),
        ],
    )
    back_up = shifted(upper_grad, "sub", 1)
    back_down = shifted(lower_grad, "sub", -1)

    scale = 1.0 / lax.axis_size("grp")
    weights = jnp.concatenate(
        [fine_weights, coarse_weights * scale, jnp.zeros((features, features), f32)], 0
    )
    weights = total_over_all(weights, ("grp", "sub"))
    grad_weights = weights[: 7 * features].astype(f32).reshape(7, features, features)

    grad_states = call(
        finish_kernel,
        shape(rows, features, bf16),
        [
            ups, downs, back_up, back_down, fine_send_lo[None], fine_send_hi[None],
            fine_self, fine_other,
        ],
    )
    return (result, grad_states, grad_weights)


def solution(mesh):
    fine = P(("grp", "sub"), None)
    fine_row = P(("grp", "sub"))
    in_specs = (
        (fine, fine)
        + (P(),) * 7
        + (fine, fine, fine_row, fine_row)
        + (P("sub", None), P("sub", None), P("sub"), P("sub"), fine_row)
    )
    return jax.shard_map(
        per_device, mesh=mesh, in_specs=in_specs, out_specs=(fine, fine, P()), check_vma=False
    )
```

```python
import functools

import jax
import jax.numpy as jnp
from jax import lax
from jax.experimental import pallas as pl
from jax.experimental.pallas import tpu as pltpu
from jax.sharding import PartitionSpec as P

f32 = jnp.float32
bf16 = jnp.bfloat16
BLOCK = 64
PAIR = 2 * BLOCK
STEP = 8
CHUNK = 512
NEVER = -1e30
DIGIT = 64.0
VMEM = pl.BlockSpec(memory_space=pltpu.VMEM)
SMEM = pl.BlockSpec(memory_space=pltpu.SMEM)
ANY = pl.BlockSpec(memory_space=pl.ANY)
PARAMS = pltpu.CompilerParams(vmem_limit_bytes=32 * 1024 * 1024)


def dot(a, b):
    return jnp.dot(a, b, preferred_element_type=f32)


def dot_nt(a, b):
    return lax.dot_general(a, b, (((1,), (1,)), ((), ())), preferred_element_type=f32)


def dot_tn(a, b):
    return lax.dot_general(a, b, (((0,), (0,)), ((), ())), preferred_element_type=f32)


def pick(condition):
    return jnp.where(condition, 1.0, 0.0).astype(bf16)


def pick16(values, places):
    return jnp.where(values == places, jnp.ones((), bf16), jnp.zeros((), bf16))


def call(kernel, out_shape, args, in_specs=None, scratch=()):
    many = isinstance(out_shape, (list, tuple))
    return pl.pallas_call(
        kernel,
        out_shape=out_shape,
        in_specs=in_specs or [VMEM] * len(args),
        out_specs=[VMEM] * len(out_shape) if many else VMEM,
        scratch_shapes=list(scratch),
        compiler_params=PARAMS,
    )(*args)


def shape(rows, columns, dtype):
    return jax.ShapeDtypeStruct((rows, columns), dtype)


def slot_columns(nbr, mask, halo_rows, even):
    rows = nbr.shape[1]
    block = lax.broadcasted_iota(jnp.int32, nbr.shape, 1) // BLOCK
    halo = lax.rem(block, halo_rows // BLOCK) * BLOCK
    lower = jnp.where(even, 2 * BLOCK, BLOCK)
    column = jnp.where(
        nbr < rows,
        nbr - block * BLOCK,
        jnp.where(
            nbr < rows + halo_rows,
            lower + nbr - rows - halo,
            3 * BLOCK - lower + nbr - rows - halo_rows - halo,
        ),
    )
    return jnp.where(mask > 0, column, 3 * BLOCK).astype(f32)


def selector(columns_t):
    first = lax.broadcasted_iota(jnp.int32, (BLOCK, 128), 1).astype(bf16)
    second = (lax.broadcasted_iota(jnp.int32, (BLOCK, 128), 1) + 128).astype(bf16)
    parts = []
    for k in range(8):
        wide = jnp.broadcast_to(columns_t[:, k : k + 1], (BLOCK, 128)).astype(bf16)
        parts.append(jnp.concatenate([pick16(wide, first), pick16(wide, second)], 1))
    return jnp.concatenate(parts, 0)


def selector_t(columns, rolled, half):
    lane = lax.broadcasted_iota(jnp.int32, (1, 128), 1)
    place = lax.broadcasted_iota(jnp.int32, (3 * BLOCK, 128), 0).astype(bf16)
    parts = []
    for j in range(4):
        left, right = (columns, rolled) if half == 0 else (rolled, columns)
        row = jnp.where(lane < BLOCK, left[2 * j : 2 * j + 1], right[2 * j + 1 : 2 * j + 2])
        wide = jnp.broadcast_to(row, (3 * BLOCK, 128)).astype(bf16)
        parts.append(pick16(wide, place))
    own_row = lax.broadcasted_iota(jnp.int32, (BLOCK, 128), 0)
    own_lane = lax.broadcasted_iota(jnp.int32, (BLOCK, 128), 1)
    own = pick(lax.rem(own_lane, BLOCK) == own_row)
    return jnp.concatenate([jnp.concatenate(parts, 1), jnp.concatenate([own] * 4, 1)], 0)


def window_of(far, halo, place):
    halo_rows = halo.shape[0] // 2
    start = place * BLOCK
    return jnp.concatenate(
        [
            far,
            halo[start : start + BLOCK, :],
            halo[halo_rows + start : halo_rows + start + BLOCK, :],
            jnp.full((BLOCK, far.shape[1]), NEVER, bf16),
        ],
        0,
    )


def chunk_of(index, count):
    return pl.ds(pl.multiple_of(index * count, count), count)


def level_terms(h_ref, halo_refs, self_ref, other_ref, own, far, halo):
    halo_rows = halo_refs[0].shape[0]
    other = other_ref[...] * 0.5
    h = h_ref[...]
    own[...] = dot(h, self_ref[...] * 0.5)
    far[...] = dot(h, other).astype(bf16)
    halo[:halo_rows, :] = dot(halo_refs[0][...], other).astype(bf16)
    halo[halo_rows:, :] = dot(halo_refs[1][...], other).astype(bf16)


def edges(own_rows, far_rows, slots, halo):
    places = halo.shape[0] // (2 * BLOCK)
    assert STEP % places == 0
    tables = []
    for n in range(STEP):
        part = slice(n * BLOCK, (n + 1) * BLOCK)
        window = window_of(far_rows[part], halo, n % places)
        tables.append(dot(selector(slots[part]), window))
    sums, slopes = [], []
    for n, picked in enumerate(tables):
        own = own_rows[n * BLOCK : (n + 1) * BLOCK]
        total, pieces = None, []
        for k in range(8):
            y = picked[k * BLOCK : (k + 1) * BLOCK] + own
            t = jnp.tanh(y)
            bent = y * t
            total = y + bent if total is None else total + (y + bent)
            pieces.append(((1.0 + t) * (1.0 + (y - bent))).astype(bf16))
        sums.append(total)
        slopes.append(jnp.concatenate(pieces, 0))
    return jnp.concatenate(sums, 0).astype(bf16), slopes


def edges_back(slopes, grad_sum, columns, halo_grad):
    places = halo_grad.shape[0] // (2 * BLOCK)
    halo_rows = halo_grad.shape[0] // 2
    windows = []
    for n, slope in enumerate(slopes):
        part = grad_sum[n * BLOCK : (n + 1) * BLOCK]
        grad = jnp.concatenate(
            [slope[k * BLOCK : (k + 1) * BLOCK] * part for k in range(8)], 0
        )
        mine = columns[:, n // 2 * PAIR : (n // 2 + 1) * PAIR]
        windows.append(dot(selector_t(mine, pltpu.roll(mine, BLOCK, 1), n % 2), grad))
    for place in range(places):
        for side in range(2):
            start = side * halo_rows + place * BLOCK
            total = halo_grad[start : start + BLOCK, :]
            for window in windows[place::places]:
                total = total + window[(side + 1) * BLOCK : (side + 2) * BLOCK]
            halo_grad[start : start + BLOCK, :] = total
    local = jnp.concatenate([window[:BLOCK] for window in windows], 0)
    down = jnp.concatenate([window[3 * BLOCK :] for window in windows], 0)
    return jnp.concatenate([down, local], 1).astype(bf16)


def gather_kernel(
    even_ref, lo_hbm, hi_hbm, x_hbm, first_ref, second_ref, x, wide, up, down, lo, hi, sems
):
    copies = [
        pltpu.make_async_copy(src, dst, sems.at[n])
        for n, (src, dst) in enumerate([(x_hbm, x), (lo_hbm, lo), (hi_hbm, hi)])
    ]
    for copy in copies:
        copy.start()
    for copy in copies:
        copy.wait()
    wide[...] = x[...].astype(f32)

    def step(r, carry):
        up[pl.ds(r, 1), :] = wide[pl.ds(hi[r], 1), :]
        down[pl.ds(r, 1), :] = wide[pl.ds(lo[r], 1), :]
        return carry

    lax.fori_loop(0, up.shape[0], step, None, unroll=16)
    even = even_ref[0] > 0
    first_ref[...] = jnp.where(even, up[...], down[...]).astype(bf16)
    second_ref[...] = jnp.where(even, down[...], up[...]).astype(bf16)


def gather_rows(even, x, send_lo, send_hi):
    rows, features = x.shape
    count = send_lo.shape[0]
    out = shape(count, features, bf16)
    return call(
        gather_kernel,
        [out, out],
        [even, send_lo, send_hi, x],
        [SMEM, ANY, ANY, ANY],
        [
            pltpu.VMEM((rows, features), bf16),
            pltpu.VMEM((rows, features), f32),
            pltpu.VMEM((count, features), f32),
            pltpu.VMEM((count, features), f32),
            pltpu.SMEM((count,), jnp.int32),
            pltpu.SMEM((count,), jnp.int32),
            pltpu.SemaphoreType.DMA((3,)),
        ],
    )


def owner_sums(owner_ref, tile, values):
    place = lax.broadcasted_iota(jnp.int32, (128, 128), 0) + tile * 128
    groups = owner_ref.shape[0]
    rows = jnp.concatenate(
        [pick(owner_ref[q : q + 1, :] == place) for q in range(groups)], 1
    )
    return dot(rows, values)


def prepare_kernel(
    even_ref,
    owner_ref,
    g_ref,
    nbr_ref,
    mask_ref,
    coarse_nbr_ref,
    coarse_mask_ref,
    after_ref,
    sums_ref,
    counts_ref,
    columns_ref,
    columns_t_ref,
    coarse_columns_ref,
    coarse_columns_t_ref,
    *,
    halo_rows,
    coarse_halo,
):
    even = even_ref[0] > 0
    columns_ref[...] = slot_columns(nbr_ref[...], mask_ref[...], halo_rows, even)
    columns_t_ref[...] = columns_ref[...].T
    coarse_columns_ref[...] = slot_columns(
        coarse_nbr_ref[...], coarse_mask_ref[...], coarse_halo, even
    )
    coarse_columns_t_ref[...] = coarse_columns_ref[...].T
    tiles = sums_ref.shape[0] // 128

    def step(tile, carry):
        sums_ref[chunk_of(tile, 128), :] = owner_sums(owner_ref, tile, g_ref[...]).astype(bf16)
        return carry

    lax.fori_loop(0, tiles, step, None)
    owner = owner_ref[...]
    high, low = owner // 128, lax.rem(owner, 128)
    groups = owner.shape[0]
    place = lax.broadcasted_iota(jnp.int32, (128, 128), 0)
    high_rows = jnp.concatenate(
        [pick(high[q : q + 1, :] == place[:tiles]) for q in range(groups)], 1
    )
    low_rows = jnp.concatenate(
        [pick(low[q : q + 1, :] == place) for q in range(groups)], 1
    )
    counts = dot_nt(high_rows, low_rows)
    most = jnp.floor(counts * (1 / DIGIT))
    counts_ref[...] = jnp.concatenate([most, counts - DIGIT * most], 0).astype(bf16)


def fine_forward_kernel(
    h_ref,
    first_ref,
    second_ref,
    self_ref,
    other_ref,
    node_ref,
    columns_t_ref,
    owner_ref,
    counts_ref,
    summed_ref,
    slope_ref,
    totals_ref,
    own,
    far,
    halo,
    new,
):
    level_terms(h_ref, (first_ref, second_ref), self_ref, other_ref, own, far, halo)

    def step(index, carry):
        here = chunk_of(index, STEP * BLOCK)
        total, slopes = edges(own[here, :], far[here, :], columns_t_ref[here, :], halo)
        summed_ref[here, :] = total
        slope_ref[chunk_of(index, 8 * STEP * BLOCK), :] = jnp.concatenate(slopes, 0)
        return carry

    lax.fori_loop(0, h_ref.shape[0] // (STEP * BLOCK), step, None)
    new[...] = (h_ref[...].astype(f32) + dot(summed_ref[...], node_ref[...])).astype(bf16)
    coarse_rows = totals_ref.shape[0] - counts_ref.shape[0]

    def tile_step(tile, carry):
        totals_ref[chunk_of(tile, 128), :] = owner_sums(owner_ref, tile, new[...]).astype(bf16)
        return carry

    lax.fori_loop(0, coarse_rows // 128, tile_step, None)
    totals_ref[coarse_rows:, :] = counts_ref[...]


def coarse_input_kernel(
    even_ref,
    totals_ref,
    more_totals_ref,
    sums_ref,
    more_sums_ref,
    lo_ref,
    hi_ref,
    cin_ref,
    first_ref,
    second_ref,
    chip_sums_ref,
    counts_ref,
):
    coarse_rows = cin_ref.shape[0]
    tiles = coarse_rows // 128
    chip_sums_ref[...] = (sums_ref[...].astype(f32) + more_sums_ref[...].astype(f32)).astype(bf16)
    totals = totals_ref[...].astype(f32) + more_totals_ref[...].astype(f32)
    digits = totals[coarse_rows:]
    counts_ref[...] = DIGIT * digits[:tiles] + digits[tiles:]
    per_row = counts_ref[...].T
    for tile in range(tiles):
        here = slice(tile * 128, (tile + 1) * 128)
        cin_ref[here, :] = (totals[here] / per_row[:, tile : tile + 1]).astype(bf16)
    cin = cin_ref[...]
    place = lax.broadcasted_iota(jnp.int32, (coarse_rows, lo_ref.shape[1]), 0)
    even = even_ref[0] > 0
    first = jnp.where(even, hi_ref[...], lo_ref[...])
    second = jnp.where(even, lo_ref[...], hi_ref[...])
    first_ref[...] = dot_tn(pick(first == place), cin).astype(bf16)
    second_ref[...] = dot_tn(pick(second == place), cin).astype(bf16)


def coarse_kernel(
    cin_ref,
    first_ref,
    second_ref,
    chip_sums_ref,
    more_sums_ref,
    self_ref,
    other_ref,
    node_ref,
    prolong_ref,
    columns_ref,
    columns_t_ref,
    part_ref,
    first_grad_ref,
    second_grad_ref,
    sums_ref,
    summed_ref,
    ups_ref,
    downs_ref,
    own,
    far,
    halo,
    grad_sum,
    halo_grad,
):
    halo_rows = first_ref.shape[0]
    level_terms(cin_ref, (first_ref, second_ref), self_ref, other_ref, own, far, halo)
    halo_grad[...] = jnp.zeros_like(halo_grad)
    sums_ref[...] = (chip_sums_ref[...].astype(f32) + more_sums_ref[...].astype(f32)).astype(bf16)
    part_ref[...] = dot_nt(sums_ref[...], prolong_ref[...])
    ups_ref[...] = part_ref[...].astype(bf16)
    grad_sum[...] = (dot_nt(ups_ref[...], node_ref[...]) * 0.5).astype(bf16)

    def step(index, carry):
        here = chunk_of(index, STEP * BLOCK)
        total, slopes = edges(own[here, :], far[here, :], columns_t_ref[here, :], halo)
        summed_ref[here, :] = total
        downs_ref[here, :] = edges_back(
            slopes, grad_sum[here, :], columns_ref[:, here], halo_grad
        )
        return carry

    lax.fori_loop(0, cin_ref.shape[0] // (STEP * BLOCK), step, None)
    first_grad_ref[...] = halo_grad[:halo_rows, :].astype(bf16)
    second_grad_ref[...] = halo_grad[halo_rows:, :].astype(bf16)


def coarse_tail_kernel(
    cin_ref,
    first_ref,
    second_ref,
    sums_ref,
    node_ref,
    prolong_ref,
    first_grad_ref,
    second_grad_ref,
    summed_ref,
    ups_ref,
    downs_ref,
    fine_ref,
    weights_ref,
    *,
    scale,
):
    cin = cin_ref[...]
    out = (cin.astype(f32) + dot(summed_ref[...], node_ref[...])).astype(bf16)
    fine_ref[...] = dot(out, prolong_ref[...]).astype(bf16)
    pair_grad = dot_tn(cin, downs_ref[...])
    other_grad = (
        pair_grad[:, 128:]
        + dot_tn(first_ref[...], first_grad_ref[...])
        + dot_tn(second_ref[...], second_grad_ref[...])
    )
    weights_ref[0:128, :] = (pair_grad[:, :128] * scale).astype(bf16)
    weights_ref[128:256, :] = (other_grad * scale).astype(bf16)
    weights_ref[256:384, :] = (dot_tn(summed_ref[...], ups_ref[...]) * scale).astype(bf16)
    weights_ref[384:512, :] = (dot_tn(out, sums_ref[...]) * scale).astype(bf16)


def owner_columns(owner_ref):
    owner = owner_ref[...].astype(f32)
    row = jnp.concatenate([owner[q : q + 1, :] for q in range(owner.shape[0])], 1)
    return jnp.broadcast_to(row, (8, row.shape[1])).T


def owner_rows(owners, values):
    count = owners.shape[0]
    wide = jnp.broadcast_to(owners[:, 0:1], (count, 128))
    lane = lax.broadcasted_iota(jnp.int32, (count, 128), 1).astype(f32)
    tiles = values.shape[0] // 128
    rows = jnp.concatenate([pick(wide == lane + 128.0 * tile) for tile in range(tiles)], 1)
    return dot(rows, values)


def result_kernel(h_ref, summed_ref, node_ref, owner_ref, fine_ref, out_ref, owners):
    owners[...] = owner_columns(owner_ref)

    def step(index, carry):
        here = chunk_of(index, CHUNK)
        updated = h_ref[here, :].astype(f32) + dot(summed_ref[here, :], node_ref[...])
        out_ref[here, :] = (updated + owner_rows(owners[here, :], fine_ref[...])).astype(bf16)
        return carry

    lax.fori_loop(0, h_ref.shape[0] // CHUNK, step, None)


def fine_backward_kernel(
    even_ref,
    h_ref,
    first_ref,
    second_ref,
    g_ref,
    summed_ref,
    slope_ref,
    node_ref,
    columns_ref,
    owner_ref,
    part_ref,
    counts_ref,
    coarse_downs_ref,
    first_back_ref,
    second_back_ref,
    lo_ref,
    hi_ref,
    coarse_self_ref,
    coarse_other_ref,
    coarse_weights_ref,
    ups_ref,
    downs_ref,
    first_grad_ref,
    second_grad_ref,
    weights_ref,
    owners,
    grad_sum,
    halo_grad,
    mean,
):
    halo_rows = first_ref.shape[0]
    coarse_rows = part_ref.shape[0]
    halo_grad[...] = jnp.zeros_like(halo_grad)
    owners[...] = owner_columns(owner_ref)

    even = even_ref[0] > 0
    first = jnp.where(even, hi_ref[...], lo_ref[...])
    second = jnp.where(even, lo_ref[...], hi_ref[...])
    place = lax.broadcasted_iota(jnp.int32, (coarse_rows, lo_ref.shape[1]), 0)
    sends = jnp.concatenate([pick(first == place), pick(second == place)], 1)
    back = jnp.concatenate([first_back_ref[...], second_back_ref[...]], 0)
    back = dot_nt(back, coarse_other_ref[...]).astype(bf16)
    plain = jnp.concatenate([coarse_self_ref[...], coarse_other_ref[...]], 1)
    grad_in = part_ref[...] + dot_nt(coarse_downs_ref[...], plain) + dot(sends, back)
    per_row = counts_ref[...].T
    for tile in range(coarse_rows // 128):
        here = slice(tile * 128, (tile + 1) * 128)
        mean[here, :] = (grad_in[here, :] / per_row[:, tile : tile + 1]).astype(bf16)

    count = STEP * BLOCK
    steps = h_ref.shape[0] // count

    def owner_step(index):
        here = chunk_of(index, count)
        grad_up = g_ref[here, :].astype(f32) + owner_rows(owners[here, :], mean[...])
        ups = grad_up.astype(bf16)
        ups_ref[here, :] = ups
        grad_sum[here, :] = (dot_nt(ups, node_ref[...]) * 0.5).astype(bf16)

    owner_step(0)

    def step(index, carry):
        here = chunk_of(index, count)
        slope = slope_ref[chunk_of(index, 8 * count), :]
        slopes = [slope[n * 8 * BLOCK : (n + 1) * 8 * BLOCK] for n in range(STEP)]
        downs_ref[here, :] = edges_back(
            slopes, grad_sum[here, :], columns_ref[:, here], halo_grad
        )
        owner_step(jnp.minimum(index + 1, steps - 1))
        return carry

    lax.fori_loop(0, steps, step, None)
    first_grad = halo_grad[:halo_rows, :].astype(bf16)
    second_grad = halo_grad[halo_rows:, :].astype(bf16)
    first_grad_ref[...] = first_grad
    second_grad_ref[...] = second_grad
    pair_grad = dot_tn(h_ref[...], downs_ref[...])
    weights_ref[0:128, :] = pair_grad[:, :128].astype(bf16)
    weights_ref[128:256, :] = (
        pair_grad[:, 128:]
        + dot_tn(first_ref[...], first_grad)
        + dot_tn(second_ref[...], second_grad)
    ).astype(bf16)
    weights_ref[256:384, :] = dot_tn(summed_ref[...], ups_ref[...]).astype(bf16)
    weights_ref[384:896, :] = coarse_weights_ref[...]
    weights_ref[896:1024, :] = jnp.zeros((128, 128), bf16)


def finish_kernel(
    even_ref,
    ups_ref,
    downs_ref,
    first_back_ref,
    second_back_ref,
    lo_ref,
    hi_ref,
    self_ref,
    other_ref,
    out_ref,
):
    other = other_ref[...]
    plain = jnp.concatenate([self_ref[...], other], 1)
    back = jnp.concatenate([first_back_ref[...], second_back_ref[...]], 0)
    back = dot_nt(back, other).astype(bf16)
    even = even_ref[0] > 0
    first = jnp.where(even, hi_ref[...], lo_ref[...])
    second = jnp.where(even, lo_ref[...], hi_ref[...])
    sends = jnp.concatenate([first, second], 1)
    place = lax.broadcasted_iota(jnp.int32, (CHUNK, sends.shape[1]), 0)

    def step(index, carry):
        here = chunk_of(index, CHUNK)
        rows = pick(sends - index * CHUNK == place)
        grad = ups_ref[here, :].astype(f32) + dot_nt(downs_ref[here, :], plain)
        out_ref[here, :] = (grad + dot(rows, back)).astype(bf16)
        return carry

    lax.fori_loop(0, ups_ref.shape[0] // CHUNK, step, None)


def share_kernel(parts_ref, after_ref, out_ref):
    total = parts_ref[0].astype(f32)
    for n in range(1, parts_ref.shape[0]):
        total = total + parts_ref[n].astype(f32)
    out_ref[...] = jnp.broadcast_to(total.astype(bf16)[None], out_ref.shape)


def widen_kernel(x_ref, out_ref):
    out_ref[...] = x_ref[: out_ref.shape[0], :].astype(f32)


def exchange(first, second):
    count = lax.axis_size("sub")
    routes = []
    for start in range(2):
        pairs = [(i, i + 1) for i in range(start, count - 1, 2)]
        routes.append(pairs + [(j, i) for i, j in pairs])
    return lax.ppermute(first, "sub", routes[0]), lax.ppermute(second, "sub", routes[1])


def swapped(block, axis, distance):
    return lax.ppermute(block, axis, [(i, i ^ distance) for i in range(lax.axis_size(axis))])


def total_over_all(block, axes, after):
    devices = lax.axis_size(axes)
    share = block.shape[0] // devices
    parts = lax.all_to_all(block.reshape(devices, share, 128), axes, 0, 0, tiled=False)
    mine = call(
        share_kernel,
        jax.ShapeDtypeStruct((devices, share, 128), bf16),
        [parts, after],
        [VMEM, ANY],
    )
    return lax.all_to_all(mine, axes, 0, 0, tiled=False).reshape(block.shape)


def per_device(
    states,
    cotangent,
    fine_self,
    fine_other,
    fine_node,
    coarse_self,
    coarse_other,
    coarse_node,
    prolong,
    fine_nbr,
    fine_mask,
    fine_send_lo,
    fine_send_hi,
    coarse_nbr,
    coarse_mask,
    coarse_send_lo,
    coarse_send_hi,
    coarse_owner,
):
    rows, features = states.shape
    coarse_rows = coarse_nbr.shape[0]
    halo_rows = fine_send_lo.shape[0]
    coarse_halo = coarse_send_lo.shape[0]
    count_rows = coarse_rows // 128
    owner = coarse_owner.reshape(rows // 128, 128)
    fine_nbr, fine_mask = fine_nbr.T, fine_mask.T
    coarse_nbr, coarse_mask = coarse_nbr.T, coarse_mask.T
    coarse_lo, coarse_hi = coarse_send_lo[None], coarse_send_hi[None]
    even = (1 - lax.rem(lax.axis_index("sub"), 2)).astype(jnp.int32).reshape(1)

    def buffer(count, columns, dtype):
        return pltpu.VMEM((count, columns), dtype)

    to_first, to_second = gather_rows(even, states, fine_send_lo, fine_send_hi)
    first, second = exchange(to_first, to_second)

    sums, counts, columns, columns_t, coarse_columns, coarse_columns_t = call(
        functools.partial(prepare_kernel, halo_rows=halo_rows, coarse_halo=coarse_halo),
        [
            shape(coarse_rows, features, bf16),
            shape(2 * count_rows, features, bf16),
            shape(8, rows, f32),
            shape(rows, 8, f32),
            shape(8, coarse_rows, f32),
            shape(coarse_rows, 8, f32),
        ],
        [even, owner, cotangent, fine_nbr, fine_mask, coarse_nbr, coarse_mask, to_first],
        [SMEM] + [VMEM] * 6 + [ANY],
    )
    more_sums = swapped(sums, "grp", 1)

    summed, slope, totals = call(
        fine_forward_kernel,
        [
            shape(rows, features, bf16),
            shape(8 * rows, features, bf16),
            shape(coarse_rows + 2 * count_rows, features, bf16),
        ],
        [states, first, second, fine_self, fine_other, fine_node, columns_t, owner, counts],
        scratch=[
            buffer(rows, features, f32),
            buffer(rows, features, bf16),
            buffer(2 * halo_rows, features, bf16),
            buffer(rows, features, bf16),
        ],
    )
    chip_totals = (totals.astype(f32) + swapped(totals, "grp", 1).astype(f32)).astype(bf16)
    more_totals = swapped(chip_totals, "grp", 2)

    coarse_in, to_first, to_second, chip_sums, counts = call(
        coarse_input_kernel,
        [
            shape(coarse_rows, features, bf16),
            shape(coarse_halo, features, bf16),
            shape(coarse_halo, features, bf16),
            shape(coarse_rows, features, bf16),
            shape(count_rows, features, f32),
        ],
        [even, chip_totals, more_totals, sums, more_sums, coarse_lo, coarse_hi],
        [SMEM] + [VMEM] * 6,
    )
    coarse_first, coarse_second = exchange(to_first, to_second)
    more_sums = swapped(chip_sums, "grp", 2)

    coarse_part, first_grad, second_grad, sums, coarse_sum, coarse_ups, coarse_downs = call(
        coarse_kernel,
        [
            shape(coarse_rows, features, f32),
            shape(coarse_halo, features, bf16),
            shape(coarse_halo, features, bf16),
            shape(coarse_rows, features, bf16),
            shape(coarse_rows, features, bf16),
            shape(coarse_rows, features, bf16),
            shape(coarse_rows, 2 * features, bf16),
        ],
        [
            coarse_in, coarse_first, coarse_second, chip_sums, more_sums,
            coarse_self, coarse_other, coarse_node, prolong, coarse_columns, coarse_columns_t,
        ],
        scratch=[
            buffer(coarse_rows, features, f32),
            buffer(coarse_rows, features, bf16),
            buffer(2 * coarse_halo, features, bf16),
            buffer(coarse_rows, features, bf16),
            buffer(2 * coarse_halo, features, f32),
        ],
    )
    first_back, second_back = exchange(first_grad, second_grad)

    fine_term, coarse_weights = call(
        functools.partial(coarse_tail_kernel, scale=1.0 / lax.axis_size("grp")),
        [shape(coarse_rows, features, bf16), shape(4 * features, features, bf16)],
        [
            coarse_in, coarse_first, coarse_second, sums, coarse_node, prolong,
            first_grad, second_grad, coarse_sum, coarse_ups, coarse_downs,
        ],
    )
    result = call(
        result_kernel,
        shape(rows, features, bf16),
        [states, summed, fine_node, owner, fine_term],
        scratch=[buffer(rows, 8, f32)],
    )

    ups, downs, first_grad, second_grad, weights = call(
        fine_backward_kernel,
        [
            shape(rows, features, bf16),
            shape(rows, 2 * features, bf16),
            shape(halo_rows, features, bf16),
            shape(halo_rows, features, bf16),
            shape(8 * features, features, bf16),
        ],
        [
            even, states, first, second, cotangent, summed, slope, fine_node, columns, owner,
            coarse_part, counts, coarse_downs, first_back, second_back, coarse_lo, coarse_hi,
            coarse_self, coarse_other, coarse_weights,
        ],
        [SMEM] + [VMEM] * 19,
        [
            buffer(rows, 8, f32),
            buffer(rows, features, bf16),
            buffer(2 * halo_rows, features, f32),
            buffer(coarse_rows, features, bf16),
        ],
    )
    weights = total_over_all(weights, ("grp", "sub"), result)
    first_back, second_back = exchange(first_grad, second_grad)

    grad_states = call(
        finish_kernel,
        shape(rows, features, bf16),
        [
            even, ups, downs, first_back, second_back, fine_send_lo[None], fine_send_hi[None],
            fine_self, fine_other,
        ],
        [SMEM] + [VMEM] * 8,
    )
    grad_weights = call(widen_kernel, shape(7 * features, features, f32), [weights])
    return (result, grad_states, grad_weights.reshape(7, features, features))


def solution(mesh):
    fine = P(("grp", "sub"), None)
    fine_row = P(("grp", "sub"))
    in_specs = (
        (fine, fine)
        + (P(),) * 7
        + (fine, fine, fine_row, fine_row)
        + (P("sub", None), P("sub", None), P("sub"), P("sub"), fine_row)
    )
    return jax.shard_map(
        per_device, mesh=mesh, in_specs=in_specs, out_specs=(fine, fine, P()), check_vma=False
    )
```

```python
import functools

import jax
import jax.numpy as jnp
from jax import lax
from jax.experimental import pallas as pl
from jax.experimental.pallas import tpu as pltpu
from jax.sharding import PartitionSpec as P

f32 = jnp.float32
bf16 = jnp.bfloat16
BLOCK = 64
PAIR = 2 * BLOCK
STEP = 8
CHUNK = 512
NEVER = -1e30
DIGIT = 64.0
VMEM = pl.BlockSpec(memory_space=pltpu.VMEM)
SMEM = pl.BlockSpec(memory_space=pltpu.SMEM)
ANY = pl.BlockSpec(memory_space=pl.ANY)
HBM = pl.BlockSpec(memory_space=pltpu.HBM)
PARAMS = pltpu.CompilerParams(vmem_limit_bytes=32 * 1024 * 1024)


def dot(a, b):
    return jnp.dot(a, b, preferred_element_type=f32)


def dot_nt(a, b):
    return lax.dot_general(a, b, (((1,), (1,)), ((), ())), preferred_element_type=f32)


def dot_tn(a, b):
    return lax.dot_general(a, b, (((0,), (0,)), ((), ())), preferred_element_type=f32)


def pick(condition):
    return jnp.where(condition, 1.0, 0.0).astype(bf16)


def pick16(values, places):
    return jnp.where(values == places, jnp.ones((), bf16), jnp.zeros((), bf16))


def call(kernel, out_shape, args, in_specs=None, scratch=(), out_specs=None):
    many = isinstance(out_shape, (list, tuple))
    in_specs = in_specs or [VMEM] * len(args)
    args = [
        pltpu.with_memory_space_constraint(arg, pltpu.HBM) if spec is HBM else arg
        for arg, spec in zip(args, in_specs)
    ]
    return pl.pallas_call(
        kernel,
        out_shape=out_shape,
        in_specs=in_specs,
        out_specs=out_specs or ([VMEM] * len(out_shape) if many else VMEM),
        scratch_shapes=list(scratch),
        compiler_params=PARAMS,
    )(*args)


def shape(rows, columns, dtype):
    return jax.ShapeDtypeStruct((rows, columns), dtype)


def slot_columns(nbr, mask, halo_rows, even):
    rows = nbr.shape[1]
    block = lax.broadcasted_iota(jnp.int32, nbr.shape, 1) // BLOCK
    halo = lax.rem(block, halo_rows // BLOCK) * BLOCK
    lower = jnp.where(even, 2 * BLOCK, BLOCK)
    column = jnp.where(
        nbr < rows,
        nbr - block * BLOCK,
        jnp.where(
            nbr < rows + halo_rows,
            lower + nbr - rows - halo,
            3 * BLOCK - lower + nbr - rows - halo_rows - halo,
        ),
    )
    return jnp.where(mask > 0, column, 3 * BLOCK).astype(f32)


def selector(columns_t):
    first = lax.broadcasted_iota(jnp.int32, (BLOCK, 128), 1).astype(bf16)
    second = (lax.broadcasted_iota(jnp.int32, (BLOCK, 128), 1) + 128).astype(bf16)
    parts = []
    for k in range(8):
        wide = jnp.broadcast_to(columns_t[:, k : k + 1], (BLOCK, 128)).astype(bf16)
        parts.append(jnp.concatenate([pick16(wide, first), pick16(wide, second)], 1))
    return jnp.concatenate(parts, 0)


def selector_t(columns, rolled, half):
    lane = lax.broadcasted_iota(jnp.int32, (1, 128), 1)
    place = lax.broadcasted_iota(jnp.int32, (3 * BLOCK, 128), 0).astype(bf16)
    parts = []
    for j in range(4):
        left, right = (columns, rolled) if half == 0 else (rolled, columns)
        row = jnp.where(lane < BLOCK, left[2 * j : 2 * j + 1], right[2 * j + 1 : 2 * j + 2])
        wide = jnp.broadcast_to(row, (3 * BLOCK, 128)).astype(bf16)
        parts.append(pick16(wide, place))
    own_row = lax.broadcasted_iota(jnp.int32, (BLOCK, 128), 0)
    own_lane = lax.broadcasted_iota(jnp.int32, (BLOCK, 128), 1)
    own = pick(lax.rem(own_lane, BLOCK) == own_row)
    return jnp.concatenate([jnp.concatenate(parts, 1), jnp.concatenate([own] * 4, 1)], 0)


def window_of(far, halo, place):
    halo_rows = halo.shape[0] // 2
    start = place * BLOCK
    return jnp.concatenate(
        [
            far,
            halo[start : start + BLOCK, :],
            halo[halo_rows + start : halo_rows + start + BLOCK, :],
            jnp.full((BLOCK, far.shape[1]), NEVER, bf16),
        ],
        0,
    )


def chunk_of(index, count):
    return pl.ds(pl.multiple_of(index * count, count), count)


def matrix(weights_ref, n):
    return weights_ref[128 * n : 128 * (n + 1), :]


def level_terms(h_ref, halo_refs, self_weight, other_weight, own, far, halo):
    halo_rows = halo_refs[0].shape[0]
    other = other_weight * 0.5
    h = h_ref[...]
    own[...] = dot(h, self_weight * 0.5)
    far[...] = dot(h, other).astype(bf16)
    halo[:halo_rows, :] = dot(halo_refs[0][...], other).astype(bf16)
    halo[halo_rows:, :] = dot(halo_refs[1][...], other).astype(bf16)


def edges(own_rows, far_rows, slots, halo):
    places = halo.shape[0] // (2 * BLOCK)
    assert STEP % places == 0
    tables = []
    for n in range(STEP):
        part = slice(n * BLOCK, (n + 1) * BLOCK)
        window = window_of(far_rows[part], halo, n % places)
        tables.append(dot(selector(slots[part]), window))
    sums, slopes = [], []
    for n, picked in enumerate(tables):
        own = own_rows[n * BLOCK : (n + 1) * BLOCK]
        total, pieces = None, []
        for k in range(8):
            y = picked[k * BLOCK : (k + 1) * BLOCK] + own
            t = jnp.tanh(y)
            bent = y * t
            total = y + bent if total is None else total + (y + bent)
            pieces.append(((1.0 + t) * (1.0 + (y - bent))).astype(bf16))
        sums.append(total)
        slopes.append(jnp.concatenate(pieces, 0))
    return jnp.concatenate(sums, 0).astype(bf16), slopes


def edges_back(slopes, grad_sum, columns, halo_grad):
    places = halo_grad.shape[0] // (2 * BLOCK)
    halo_rows = halo_grad.shape[0] // 2
    windows = []
    for n, slope in enumerate(slopes):
        part = grad_sum[n * BLOCK : (n + 1) * BLOCK]
        grad = jnp.concatenate(
            [slope[k * BLOCK : (k + 1) * BLOCK] * part for k in range(8)], 0
        )
        mine = columns[:, n // 2 * PAIR : (n // 2 + 1) * PAIR]
        windows.append(dot(selector_t(mine, pltpu.roll(mine, BLOCK, 1), n % 2), grad))
    for place in range(places):
        for side in range(2):
            start = side * halo_rows + place * BLOCK
            total = halo_grad[start : start + BLOCK, :]
            for window in windows[place::places]:
                total = total + window[(side + 1) * BLOCK : (side + 2) * BLOCK]
            halo_grad[start : start + BLOCK, :] = total
    local = jnp.concatenate([window[:BLOCK] for window in windows], 0)
    down = jnp.concatenate([window[3 * BLOCK :] for window in windows], 0)
    return jnp.concatenate([down, local], 1).astype(bf16)


def fetch(pairs, sems):
    copies = [pltpu.make_async_copy(src, dst, sems.at[n]) for n, (src, dst) in enumerate(pairs)]
    for copy in copies:
        copy.start()
    for copy in copies:
        copy.wait()


def gather_kernel(
    even_ref, lo_hbm, hi_hbm, x_hbm, first_ref, second_ref, x_ref, wide, up, down, lo, hi, sems
):
    fetch([(x_hbm, x_ref), (lo_hbm, lo), (hi_hbm, hi)], sems)
    wide[...] = x_ref[...].astype(f32)

    def step(r, carry):
        up[pl.ds(r, 1), :] = wide[pl.ds(hi[r], 1), :]
        down[pl.ds(r, 1), :] = wide[pl.ds(lo[r], 1), :]
        return carry

    lax.fori_loop(0, up.shape[0], step, None, unroll=16)
    even = even_ref[0] > 0
    first_ref[...] = jnp.where(even, up[...], down[...]).astype(bf16)
    second_ref[...] = jnp.where(even, down[...], up[...]).astype(bf16)


def gather_rows(even, x, send_lo, send_hi):
    rows, features = x.shape
    count = send_lo.shape[0]
    out = shape(count, features, bf16)
    return call(
        gather_kernel,
        [out, out, shape(rows, features, bf16)],
        [even, send_lo, send_hi, x],
        [SMEM, HBM, HBM, HBM],
        [
            pltpu.VMEM((rows, features), f32),
            pltpu.VMEM((count, features), f32),
            pltpu.VMEM((count, features), f32),
            pltpu.SMEM((count,), jnp.int32),
            pltpu.SMEM((count,), jnp.int32),
            pltpu.SemaphoreType.DMA((3,)),
        ],
    )


def owner_sums(owner_ref, tile, values):
    place = lax.broadcasted_iota(jnp.int32, (128, 128), 0) + tile * 128
    groups = owner_ref.shape[0]
    rows = jnp.concatenate(
        [pick(owner_ref[q : q + 1, :] == place) for q in range(groups)], 1
    )
    return dot(rows, values)


def prepare_kernel(
    even_ref,
    g_hbm,
    owner_hbm,
    nbr_hbm,
    mask_hbm,
    coarse_nbr_hbm,
    coarse_mask_hbm,
    lo_hbm,
    hi_hbm,
    coarse_lo_hbm,
    coarse_hi_hbm,
    *rest,
    halo_rows,
    coarse_halo,
):
    weight_hbms, rest = rest[:7], rest[7:]
    (
        after_ref,
        sums_ref,
        counts_ref,
        columns_ref,
        columns_t_ref,
        coarse_columns_ref,
        coarse_columns_t_ref,
        owners_t_ref,
        g_ref,
        weights_ref,
        sends_ref,
        coarse_sends_ref,
        owner_ref,
        nbr_ref,
        mask_ref,
        coarse_nbr_ref,
        coarse_mask_ref,
        lo_ref,
        hi_ref,
        coarse_lo_ref,
        coarse_hi_ref,
        sems,
    ) = rest
    fetch(
        [
            (g_hbm, g_ref),
            (owner_hbm, owner_ref),
            (nbr_hbm, nbr_ref),
            (mask_hbm, mask_ref),
            (coarse_nbr_hbm, coarse_nbr_ref),
            (coarse_mask_hbm, coarse_mask_ref),
            (lo_hbm, lo_ref),
            (hi_hbm, hi_ref),
            (coarse_lo_hbm, coarse_lo_ref),
            (coarse_hi_hbm, coarse_hi_ref),
        ]
        + [(w, weights_ref.at[pl.ds(128 * n, 128), :]) for n, w in enumerate(weight_hbms)],
        sems,
    )
    even = even_ref[0] > 0
    for low, high, out in (
        (lo_ref, hi_ref, sends_ref),
        (coarse_lo_ref, coarse_hi_ref, coarse_sends_ref),
    ):
        first = jnp.where(even, high[...], low[...])
        second = jnp.where(even, low[...], high[...])
        out[...] = jnp.concatenate([first, second], 1)
    owners_t_ref[...] = owner_columns(owner_ref)
    columns_ref[...] = slot_columns(nbr_ref[...], mask_ref[...], halo_rows, even)
    columns_t_ref[...] = columns_ref[...].T
    coarse_columns_ref[...] = slot_columns(
        coarse_nbr_ref[...], coarse_mask_ref[...], coarse_halo, even
    )
    coarse_columns_t_ref[...] = coarse_columns_ref[...].T
    tiles = sums_ref.shape[0] // 128

    def step(tile, carry):
        sums_ref[chunk_of(tile, 128), :] = owner_sums(owner_ref, tile, g_ref[...]).astype(bf16)
        return carry

    lax.fori_loop(0, tiles, step, None)
    owner = owner_ref[...]
    high, low = owner // 128, lax.rem(owner, 128)
    groups = owner.shape[0]
    place = lax.broadcasted_iota(jnp.int32, (128, 128), 0)
    high_rows = jnp.concatenate(
        [pick(high[q : q + 1, :] == place[:tiles]) for q in range(groups)], 1
    )
    low_rows = jnp.concatenate(
        [pick(low[q : q + 1, :] == place) for q in range(groups)], 1
    )
    counts = dot_nt(high_rows, low_rows)
    most = jnp.floor(counts * (1 / DIGIT))
    counts_ref[...] = jnp.concatenate([most, counts - DIGIT * most], 0).astype(bf16)


def fine_forward_kernel(
    h_ref,
    first_ref,
    second_ref,
    weights_ref,
    columns_t_ref,
    owner_ref,
    counts_ref,
    summed_ref,
    slope_ref,
    totals_ref,
    own,
    far,
    halo,
    new,
):
    self_weight, other_weight = matrix(weights_ref, 0), matrix(weights_ref, 1)
    level_terms(h_ref, (first_ref, second_ref), self_weight, other_weight, own, far, halo)

    def step(index, carry):
        here = chunk_of(index, STEP * BLOCK)
        total, slopes = edges(own[here, :], far[here, :], columns_t_ref[here, :], halo)
        summed_ref[here, :] = total
        slope_ref[chunk_of(index, 8 * STEP * BLOCK), :] = jnp.concatenate(slopes, 0)
        return carry

    lax.fori_loop(0, h_ref.shape[0] // (STEP * BLOCK), step, None)
    new[...] = (
        h_ref[...].astype(f32) + dot(summed_ref[...], matrix(weights_ref, 2))
    ).astype(bf16)
    coarse_rows = totals_ref.shape[0] - counts_ref.shape[0]

    def tile_step(tile, carry):
        totals_ref[chunk_of(tile, 128), :] = owner_sums(owner_ref, tile, new[...]).astype(bf16)
        return carry

    lax.fori_loop(0, coarse_rows // 128, tile_step, None)
    totals_ref[coarse_rows:, :] = counts_ref[...]


def coarse_input_kernel(
    totals_ref,
    more_totals_ref,
    sums_ref,
    more_sums_ref,
    sends_ref,
    cin_ref,
    first_ref,
    second_ref,
    chip_sums_ref,
    counts_ref,
):
    coarse_rows = cin_ref.shape[0]
    tiles = coarse_rows // 128
    chip_sums_ref[...] = (sums_ref[...].astype(f32) + more_sums_ref[...].astype(f32)).astype(bf16)
    totals = totals_ref[...].astype(f32) + more_totals_ref[...].astype(f32)
    digits = totals[coarse_rows:]
    counts_ref[...] = DIGIT * digits[:tiles] + digits[tiles:]
    per_row = counts_ref[...].T
    for tile in range(tiles):
        here = slice(tile * 128, (tile + 1) * 128)
        cin_ref[here, :] = (totals[here] / per_row[:, tile : tile + 1]).astype(bf16)
    cin = cin_ref[...]
    place = lax.broadcasted_iota(jnp.int32, (coarse_rows, sends_ref.shape[1]), 0)
    sent = dot_tn(pick(sends_ref[...] == place), cin).astype(bf16)
    halo_rows = first_ref.shape[0]
    first_ref[...] = sent[:halo_rows]
    second_ref[...] = sent[halo_rows:]


def coarse_kernel(
    cin_ref,
    first_ref,
    second_ref,
    chip_sums_ref,
    more_sums_ref,
    weights_ref,
    columns_ref,
    columns_t_ref,
    part_ref,
    first_grad_ref,
    second_grad_ref,
    sums_ref,
    summed_ref,
    ups_ref,
    downs_ref,
    own,
    far,
    halo,
    grad_sum,
    halo_grad,
):
    halo_rows = first_ref.shape[0]
    self_weight, other_weight = matrix(weights_ref, 3), matrix(weights_ref, 4)
    level_terms(cin_ref, (first_ref, second_ref), self_weight, other_weight, own, far, halo)
    halo_grad[...] = jnp.zeros_like(halo_grad)
    sums_ref[...] = (chip_sums_ref[...].astype(f32) + more_sums_ref[...].astype(f32)).astype(bf16)
    part_ref[...] = dot_nt(sums_ref[...], matrix(weights_ref, 6))
    ups_ref[...] = part_ref[...].astype(bf16)
    grad_sum[...] = (dot_nt(ups_ref[...], matrix(weights_ref, 5)) * 0.5).astype(bf16)

    def step(index, carry):
        here = chunk_of(index, STEP * BLOCK)
        total, slopes = edges(own[here, :], far[here, :], columns_t_ref[here, :], halo)
        summed_ref[here, :] = total
        downs_ref[here, :] = edges_back(
            slopes, grad_sum[here, :], columns_ref[:, here], halo_grad
        )
        return carry

    lax.fori_loop(0, cin_ref.shape[0] // (STEP * BLOCK), step, None)
    first_grad_ref[...] = halo_grad[:halo_rows, :].astype(bf16)
    second_grad_ref[...] = halo_grad[halo_rows:, :].astype(bf16)


def coarse_tail_kernel(
    cin_ref,
    first_ref,
    second_ref,
    sums_ref,
    matrices_ref,
    first_grad_ref,
    second_grad_ref,
    summed_ref,
    ups_ref,
    downs_ref,
    fine_ref,
    weights_ref,
    *,
    scale,
):
    cin = cin_ref[...]
    out = (cin.astype(f32) + dot(summed_ref[...], matrix(matrices_ref, 5))).astype(bf16)
    fine_ref[...] = dot(out, matrix(matrices_ref, 6)).astype(bf16)
    pair_grad = dot_tn(cin, downs_ref[...])
    other_grad = (
        pair_grad[:, 128:]
        + dot_tn(first_ref[...], first_grad_ref[...])
        + dot_tn(second_ref[...], second_grad_ref[...])
    )
    weights_ref[0:128, :] = (pair_grad[:, :128] * scale).astype(bf16)
    weights_ref[128:256, :] = (other_grad * scale).astype(bf16)
    weights_ref[256:384, :] = (dot_tn(summed_ref[...], ups_ref[...]) * scale).astype(bf16)
    weights_ref[384:512, :] = (dot_tn(out, sums_ref[...]) * scale).astype(bf16)


def owner_columns(owner_ref):
    owner = owner_ref[...].astype(f32)
    row = jnp.concatenate([owner[q : q + 1, :] for q in range(owner.shape[0])], 1)
    return jnp.broadcast_to(row, (8, row.shape[1])).T


def owner_rows(owners, values):
    count = owners.shape[0]
    wide = jnp.broadcast_to(owners[:, 0:1], (count, 128))
    lane = lax.broadcasted_iota(jnp.int32, (count, 128), 1).astype(f32)
    tiles = values.shape[0] // 128
    rows = jnp.concatenate([pick(wide == lane + 128.0 * tile) for tile in range(tiles)], 1)
    return dot(rows, values)


def result_kernel(h_ref, summed_ref, weights_ref, owners_ref, fine_ref, out_ref):
    def step(index, carry):
        here = chunk_of(index, CHUNK)
        updated = h_ref[here, :].astype(f32) + dot(summed_ref[here, :], matrix(weights_ref, 2))
        out_ref[here, :] = (updated + owner_rows(owners_ref[here, :], fine_ref[...])).astype(bf16)
        return carry

    lax.fori_loop(0, h_ref.shape[0] // CHUNK, step, None)


def fine_backward_kernel(
    h_ref,
    first_ref,
    second_ref,
    g_ref,
    summed_ref,
    slope_ref,
    matrices_ref,
    columns_ref,
    owners_ref,
    part_ref,
    counts_ref,
    coarse_downs_ref,
    first_back_ref,
    second_back_ref,
    sends_ref,
    coarse_weights_ref,
    ups_hbm,
    downs_hbm,
    first_grad_ref,
    second_grad_ref,
    weights_ref,
    ups_ref,
    downs_ref,
    grad_sum,
    halo_grad,
    mean,
    sems,
):
    halo_rows = first_ref.shape[0]
    coarse_rows = part_ref.shape[0]
    halo_grad[...] = jnp.zeros_like(halo_grad)

    place = lax.broadcasted_iota(jnp.int32, (coarse_rows, sends_ref.shape[1]), 0)
    sends = pick(sends_ref[...] == place)
    back = jnp.concatenate([first_back_ref[...], second_back_ref[...]], 0)
    back = dot_nt(back, matrix(matrices_ref, 4)).astype(bf16)
    plain = jnp.concatenate([matrix(matrices_ref, 3), matrix(matrices_ref, 4)], 1)
    grad_in = part_ref[...] + dot_nt(coarse_downs_ref[...], plain) + dot(sends, back)
    per_row = counts_ref[...].T
    for tile in range(coarse_rows // 128):
        here = slice(tile * 128, (tile + 1) * 128)
        mean[here, :] = (grad_in[here, :] / per_row[:, tile : tile + 1]).astype(bf16)

    count = STEP * BLOCK
    steps = h_ref.shape[0] // count

    def owner_step(index):
        here = chunk_of(index, count)
        grad_up = g_ref[here, :].astype(f32) + owner_rows(owners_ref[here, :], mean[...])
        ups = grad_up.astype(bf16)
        ups_ref[here, :] = ups
        grad_sum[here, :] = (dot_nt(ups, matrix(matrices_ref, 2)) * 0.5).astype(bf16)

    def edge_step(index):
        here = chunk_of(index, count)
        slope = slope_ref[chunk_of(index, 8 * count), :]
        slopes = [slope[n * 8 * BLOCK : (n + 1) * 8 * BLOCK] for n in range(STEP)]
        downs_ref[here, :] = edges_back(
            slopes, grad_sum[here, :], columns_ref[:, here], halo_grad
        )

    owner_step(0)

    def step(index, carry):
        edge_step(index)
        owner_step(index + 1)
        return carry

    lax.fori_loop(0, steps - 1, step, None)
    edge_step(steps - 1)
    copies = [
        pltpu.make_async_copy(ups_ref, ups_hbm, sems.at[0]),
        pltpu.make_async_copy(downs_ref, downs_hbm, sems.at[1]),
    ]
    for copy in copies:
        copy.start()
    first_grad = halo_grad[:halo_rows, :].astype(bf16)
    second_grad = halo_grad[halo_rows:, :].astype(bf16)
    first_grad_ref[...] = first_grad
    second_grad_ref[...] = second_grad
    pair_grad = dot_tn(h_ref[...], downs_ref[...])
    weights_ref[0:128, :] = pair_grad[:, :128].astype(bf16)
    weights_ref[128:256, :] = (
        pair_grad[:, 128:]
        + dot_tn(first_ref[...], first_grad)
        + dot_tn(second_ref[...], second_grad)
    ).astype(bf16)
    weights_ref[256:384, :] = dot_tn(summed_ref[...], ups_ref[...]).astype(bf16)
    weights_ref[384:896, :] = coarse_weights_ref[...]
    weights_ref[896:1024, :] = jnp.zeros((128, 128), bf16)
    for copy in copies:
        copy.wait()


def finish_kernel(
    ups_hbm,
    downs_hbm,
    first_back_ref,
    second_back_ref,
    sends_ref,
    matrices_ref,
    out_ref,
    ups_ref,
    downs_ref,
    sems,
):
    copies = [
        pltpu.make_async_copy(ups_hbm, ups_ref, sems.at[0]),
        pltpu.make_async_copy(downs_hbm, downs_ref, sems.at[1]),
    ]
    for copy in copies:
        copy.start()
    other = matrix(matrices_ref, 1)
    plain = jnp.concatenate([matrix(matrices_ref, 0), other], 1)
    back = jnp.concatenate([first_back_ref[...], second_back_ref[...]], 0)
    back = dot_nt(back, other).astype(bf16)
    sends = sends_ref[...]
    place = lax.broadcasted_iota(jnp.int32, (CHUNK, sends.shape[1]), 0)
    for copy in copies:
        copy.wait()

    def step(index, carry):
        here = chunk_of(index, CHUNK)
        rows = pick(sends - index * CHUNK == place)
        grad = ups_ref[here, :].astype(f32) + dot_nt(downs_ref[here, :], plain)
        out_ref[here, :] = (grad + dot(rows, back)).astype(bf16)
        return carry

    lax.fori_loop(0, ups_ref.shape[0] // CHUNK, step, None)


def share_kernel(parts_ref, after_ref, out_ref):
    total = parts_ref[0].astype(f32)
    for n in range(1, parts_ref.shape[0]):
        total = total + parts_ref[n].astype(f32)
    out_ref[...] = jnp.broadcast_to(total.astype(bf16)[None], out_ref.shape)


def widen_kernel(x_ref, out_ref):
    out_ref[...] = x_ref[: out_ref.shape[0], :].astype(f32)


def exchange(first, second):
    count = lax.axis_size("sub")
    routes = []
    for start in range(2):
        pairs = [(i, i + 1) for i in range(start, count - 1, 2)]
        routes.append(pairs + [(j, i) for i, j in pairs])
    return lax.ppermute(first, "sub", routes[0]), lax.ppermute(second, "sub", routes[1])


def swapped(block, axis, distance):
    return lax.ppermute(block, axis, [(i, i ^ distance) for i in range(lax.axis_size(axis))])


def total_over_all(block, axes, after):
    devices = lax.axis_size(axes)
    share = block.shape[0] // devices
    parts = lax.all_to_all(block.reshape(devices, share, 128), axes, 0, 0, tiled=False)
    mine = call(
        share_kernel,
        jax.ShapeDtypeStruct((devices, share, 128), bf16),
        [parts, after],
        [VMEM, HBM],
    )
    return lax.all_to_all(mine, axes, 0, 0, tiled=False).reshape(block.shape)


def per_device(
    states,
    cotangent,
    fine_self,
    fine_other,
    fine_node,
    coarse_self,
    coarse_other,
    coarse_node,
    prolong,
    fine_nbr,
    fine_mask,
    fine_send_lo,
    fine_send_hi,
    coarse_nbr,
    coarse_mask,
    coarse_send_lo,
    coarse_send_hi,
    coarse_owner,
):
    rows, features = states.shape
    coarse_rows = coarse_nbr.shape[0]
    halo_rows = fine_send_lo.shape[0]
    coarse_halo = coarse_send_lo.shape[0]
    count_rows = coarse_rows // 128
    owner = coarse_owner.reshape(rows // 128, 128)
    even = (1 - lax.rem(lax.axis_index("sub"), 2)).astype(jnp.int32).reshape(1)

    def buffer(count, columns, dtype):
        return pltpu.VMEM((count, columns), dtype)

    to_first, to_second, states = gather_rows(even, states, fine_send_lo, fine_send_hi)
    first, second = exchange(to_first, to_second)

    (
        sums, counts, columns, columns_t, coarse_columns, coarse_columns_t, owners_t, cotangent,
        matrices, sends, coarse_sends, owner,
    ) = call(
        functools.partial(prepare_kernel, halo_rows=halo_rows, coarse_halo=coarse_halo),
        [
            shape(coarse_rows, features, bf16),
            shape(2 * count_rows, features, bf16),
            shape(8, rows, f32),
            shape(rows, 8, f32),
            shape(8, coarse_rows, f32),
            shape(coarse_rows, 8, f32),
            shape(rows, 8, f32),
            shape(rows, features, bf16),
            shape(7 * features, features, bf16),
            shape(1, 2 * halo_rows, jnp.int32),
            shape(1, 2 * coarse_halo, jnp.int32),
            shape(rows // 128, 128, jnp.int32),
        ],
        [
            even, cotangent, owner, fine_nbr.T, fine_mask.T, coarse_nbr.T, coarse_mask.T,
            fine_send_lo[None], fine_send_hi[None], coarse_send_lo[None], coarse_send_hi[None],
            fine_self, fine_other, fine_node, coarse_self, coarse_other, coarse_node, prolong,
            to_first,
        ],
        [SMEM] + [HBM] * 17 + [ANY],
        [buffer(8, rows, jnp.int32)] * 2
        + [buffer(8, coarse_rows, jnp.int32)] * 2
        + [buffer(1, halo_rows, jnp.int32)] * 2
        + [buffer(1, coarse_halo, jnp.int32)] * 2
        + [pltpu.SemaphoreType.DMA((17,))],
    )
    more_sums = swapped(sums, "grp", 1)

    summed, slope, totals = call(
        fine_forward_kernel,
        [
            shape(rows, features, bf16),
            shape(8 * rows, features, bf16),
            shape(coarse_rows + 2 * count_rows, features, bf16),
        ],
        [states, first, second, matrices, columns_t, owner, counts],
        scratch=[
            buffer(rows, features, f32),
            buffer(rows, features, bf16),
            buffer(2 * halo_rows, features, bf16),
            buffer(rows, features, bf16),
        ],
    )
    chip_totals = (totals.astype(f32) + swapped(totals, "grp", 1).astype(f32)).astype(bf16)
    more_totals = swapped(chip_totals, "grp", 2)

    coarse_in, to_first, to_second, chip_sums, counts = call(
        coarse_input_kernel,
        [
            shape(coarse_rows, features, bf16),
            shape(coarse_halo, features, bf16),
            shape(coarse_halo, features, bf16),
            shape(coarse_rows, features, bf16),
            shape(count_rows, features, f32),
        ],
        [chip_totals, more_totals, sums, more_sums, coarse_sends],
    )
    coarse_first, coarse_second = exchange(to_first, to_second)
    more_sums = swapped(chip_sums, "grp", 2)

    coarse_part, first_grad, second_grad, sums, coarse_sum, coarse_ups, coarse_downs = call(
        coarse_kernel,
        [
            shape(coarse_rows, features, f32),
            shape(coarse_halo, features, bf16),
            shape(coarse_halo, features, bf16),
            shape(coarse_rows, features, bf16),
            shape(coarse_rows, features, bf16),
            shape(coarse_rows, features, bf16),
            shape(coarse_rows, 2 * features, bf16),
        ],
        [
            coarse_in, coarse_first, coarse_second, chip_sums, more_sums, matrices,
            coarse_columns, coarse_columns_t,
        ],
        scratch=[
            buffer(coarse_rows, features, f32),
            buffer(coarse_rows, features, bf16),
            buffer(2 * coarse_halo, features, bf16),
            buffer(coarse_rows, features, bf16),
            buffer(2 * coarse_halo, features, f32),
        ],
    )
    first_back, second_back = exchange(first_grad, second_grad)

    fine_term, coarse_weights = call(
        functools.partial(coarse_tail_kernel, scale=1.0 / lax.axis_size("grp")),
        [shape(coarse_rows, features, bf16), shape(4 * features, features, bf16)],
        [
            coarse_in, coarse_first, coarse_second, sums, matrices,
            first_grad, second_grad, coarse_sum, coarse_ups, coarse_downs,
        ],
    )
    result = call(
        result_kernel,
        shape(rows, features, bf16),
        [states, summed, matrices, owners_t, fine_term],
    )

    ups, downs, first_grad, second_grad, weights = call(
        fine_backward_kernel,
        [
            pltpu.HBM((rows, features), bf16),
            pltpu.HBM((rows, 2 * features), bf16),
            shape(halo_rows, features, bf16),
            shape(halo_rows, features, bf16),
            shape(8 * features, features, bf16),
        ],
        [
            states, first, second, cotangent, summed, slope, matrices, columns, owners_t,
            coarse_part, counts, coarse_downs, first_back, second_back, coarse_sends,
            coarse_weights,
        ],
        scratch=[
            buffer(rows, features, bf16),
            buffer(rows, 2 * features, bf16),
            buffer(rows, features, bf16),
            buffer(2 * halo_rows, features, f32),
            buffer(coarse_rows, features, bf16),
            pltpu.SemaphoreType.DMA((2,)),
        ],
        out_specs=[HBM, HBM, VMEM, VMEM, VMEM],
    )
    first_back, second_back = exchange(first_grad, second_grad)

    grad_states = call(
        finish_kernel,
        shape(rows, features, bf16),
        [ups, downs, first_back, second_back, sends, matrices],
        [HBM, HBM] + [VMEM] * 4,
        [
            buffer(rows, features, bf16),
            buffer(rows, 2 * features, bf16),
            pltpu.SemaphoreType.DMA((2,)),
        ],
    )
    weights = total_over_all(weights, ("grp", "sub"), grad_states)
    grad_weights = call(widen_kernel, shape(7 * features, features, f32), [weights])
    return (result, grad_states, grad_weights.reshape(7, features, features))


def solution(mesh):
    fine = P(("grp", "sub"), None)
    fine_row = P(("grp", "sub"))
    in_specs = (
        (fine, fine)
        + (P(),) * 7
        + (fine, fine, fine_row, fine_row)
        + (P("sub", None), P("sub", None), P("sub"), P("sub"), fine_row)
    )
    return jax.shard_map(
        per_device, mesh=mesh, in_specs=in_specs, out_specs=(fine, fine, P()), check_vma=False
    )
```

```python
import functools

import jax
import jax.numpy as jnp
from jax import lax
from jax.experimental import pallas as pl
from jax.experimental.pallas import tpu as pltpu
from jax.sharding import PartitionSpec as P

f32 = jnp.float32
bf16 = jnp.bfloat16
BLOCK = 64
PAIR = 2 * BLOCK
STEP = 8
CHUNK = 512
NEVER = -1e30
DIGIT = 64.0
VMEM = pl.BlockSpec(memory_space=pltpu.VMEM)
SMEM = pl.BlockSpec(memory_space=pltpu.SMEM)
ANY = pl.BlockSpec(memory_space=pl.ANY)
HBM = pl.BlockSpec(memory_space=pltpu.HBM)
PARAMS = pltpu.CompilerParams(vmem_limit_bytes=32 * 1024 * 1024)


def dot(a, b):
    return jnp.dot(a, b, preferred_element_type=f32)


def dot_nt(a, b):
    return lax.dot_general(a, b, (((1,), (1,)), ((), ())), preferred_element_type=f32)


def dot_tn(a, b):
    return lax.dot_general(a, b, (((0,), (0,)), ((), ())), preferred_element_type=f32)


def pick(condition):
    return jnp.where(condition, 1.0, 0.0).astype(bf16)


def pick16(values, places):
    return jnp.where(values == places, jnp.ones((), bf16), jnp.zeros((), bf16))


def call(kernel, out_shape, args, in_specs=None, scratch=(), out_specs=None):
    many = isinstance(out_shape, (list, tuple))
    in_specs = in_specs or [VMEM] * len(args)
    args = [
        pltpu.with_memory_space_constraint(arg, pltpu.HBM) if spec is HBM else arg
        for arg, spec in zip(args, in_specs)
    ]
    return pl.pallas_call(
        kernel,
        out_shape=out_shape,
        in_specs=in_specs,
        out_specs=out_specs or ([VMEM] * len(out_shape) if many else VMEM),
        scratch_shapes=list(scratch),
        compiler_params=PARAMS,
    )(*args)


def shape(rows, columns, dtype):
    return jax.ShapeDtypeStruct((rows, columns), dtype)


def slot_columns(nbr, mask, halo_rows, even):
    rows = nbr.shape[1]
    block = lax.broadcasted_iota(jnp.int32, nbr.shape, 1) // BLOCK
    halo = lax.rem(block, halo_rows // BLOCK) * BLOCK
    lower = jnp.where(even, 2 * BLOCK, BLOCK)
    column = jnp.where(
        nbr < rows,
        nbr - block * BLOCK,
        jnp.where(
            nbr < rows + halo_rows,
            lower + nbr - rows - halo,
            3 * BLOCK - lower + nbr - rows - halo_rows - halo,
        ),
    )
    return jnp.where(mask > 0, column, 3 * BLOCK).astype(f32)


def selector(columns_t):
    first = lax.broadcasted_iota(jnp.int32, (BLOCK, 128), 1).astype(bf16)
    second = (lax.broadcasted_iota(jnp.int32, (BLOCK, 128), 1) + 128).astype(bf16)
    parts = []
    for k in range(8):
        wide = jnp.broadcast_to(columns_t[:, k : k + 1], (BLOCK, 128)).astype(bf16)
        parts.append(jnp.concatenate([pick16(wide, first), pick16(wide, second)], 1))
    return jnp.concatenate(parts, 0)


def selector_t(columns, rolled, half):
    lane = lax.broadcasted_iota(jnp.int32, (1, 128), 1)
    place = lax.broadcasted_iota(jnp.int32, (3 * BLOCK, 128), 0).astype(bf16)
    parts = []
    for j in range(4):
        left, right = (columns, rolled) if half == 0 else (rolled, columns)
        row = jnp.where(lane < BLOCK, left[2 * j : 2 * j + 1], right[2 * j + 1 : 2 * j + 2])
        wide = jnp.broadcast_to(row, (3 * BLOCK, 128)).astype(bf16)
        parts.append(pick16(wide, place))
    return jnp.concatenate(parts, 1)


def window_of(far, halo, place):
    halo_rows = halo.shape[0] // 2
    start = place * BLOCK
    return jnp.concatenate(
        [
            far,
            halo[start : start + BLOCK, :],
            halo[halo_rows + start : halo_rows + start + BLOCK, :],
            jnp.full((BLOCK, far.shape[1]), NEVER, bf16),
        ],
        0,
    )


def chunk_of(index, count):
    return pl.ds(pl.multiple_of(index * count, count), count)


def matrix(weights_ref, n):
    return weights_ref[128 * n : 128 * (n + 1), :]


def level_terms(h_ref, halo_refs, self_weight, other_weight, own, far, halo):
    halo_rows = halo_refs[0].shape[0]
    other = other_weight * 0.5
    h = h_ref[...]
    own[...] = dot(h, self_weight * 0.5)
    far[...] = dot(h, other).astype(bf16)
    halo[:halo_rows, :] = dot(halo_refs[0][...], other).astype(bf16)
    halo[halo_rows:, :] = dot(halo_refs[1][...], other).astype(bf16)


def edges(own_rows, far_rows, slots, halo):
    places = halo.shape[0] // (2 * BLOCK)
    assert STEP % places == 0
    tables = []
    for n in range(STEP):
        part = slice(n * BLOCK, (n + 1) * BLOCK)
        window = window_of(far_rows[part], halo, n % places)
        tables.append(dot(selector(slots[part]), window))
    sums, slopes = [], []
    for n, picked in enumerate(tables):
        own = own_rows[n * BLOCK : (n + 1) * BLOCK]
        values, pieces = [], []
        for k in range(8):
            y = (picked[k * BLOCK : (k + 1) * BLOCK] + own).astype(bf16)
            t = jnp.tanh(y)
            bent = y * t
            values.append(y + bent)
            pieces.append((1 + t) * (1 + (y - bent)))
        while len(values) > 1:
            values = [left + right for left, right in zip(values[::2], values[1::2])]
        sums.append(values[0])
        slopes.append(jnp.concatenate(pieces, 0))
    return jnp.concatenate(sums, 0), slopes


def edges_back(slopes, grad_sum, columns, halo_grad):
    places = halo_grad.shape[0] // (2 * BLOCK)
    halo_rows = halo_grad.shape[0] // 2
    windows, downs = [], []
    for n, slope in enumerate(slopes):
        part = grad_sum[n * BLOCK : (n + 1) * BLOCK]
        grads = [slope[k * BLOCK : (k + 1) * BLOCK] * part for k in range(8)]
        downs.append(sum(grad.astype(f32) for grad in grads))
        mine = columns[:, n // 2 * PAIR : (n // 2 + 1) * PAIR]
        selected = selector_t(mine, pltpu.roll(mine, BLOCK, 1), n % 2)
        windows.append(dot(selected, jnp.concatenate(grads, 0)))
    for place in range(places):
        for side in range(2):
            start = side * halo_rows + place * BLOCK
            total = halo_grad[start : start + BLOCK, :]
            for window in windows[place::places]:
                total = total + window[(side + 1) * BLOCK : (side + 2) * BLOCK]
            halo_grad[start : start + BLOCK, :] = total
    local = jnp.concatenate([window[:BLOCK] for window in windows], 0)
    down = jnp.concatenate(downs, 0)
    return jnp.concatenate([down, local], 1).astype(bf16)


def fetch(pairs, sems):
    copies = [pltpu.make_async_copy(src, dst, sems.at[n]) for n, (src, dst) in enumerate(pairs)]
    for copy in copies:
        copy.start()
    for copy in copies:
        copy.wait()


def gather_kernel(
    even_ref, lo_hbm, hi_hbm, x_hbm, first_ref, second_ref, x_ref, wide, up, down, lo, hi, sems
):
    fetch([(x_hbm, x_ref), (lo_hbm, lo), (hi_hbm, hi)], sems)
    wide[...] = x_ref[...].astype(f32)

    def step(r, carry):
        up[pl.ds(r, 1), :] = wide[pl.ds(hi[r], 1), :]
        down[pl.ds(r, 1), :] = wide[pl.ds(lo[r], 1), :]
        return carry

    lax.fori_loop(0, up.shape[0], step, None, unroll=16)
    even = even_ref[0] > 0
    first_ref[...] = jnp.where(even, up[...], down[...]).astype(bf16)
    second_ref[...] = jnp.where(even, down[...], up[...]).astype(bf16)


def gather_rows(even, x, send_lo, send_hi):
    rows, features = x.shape
    count = send_lo.shape[0]
    out = shape(count, features, bf16)
    return call(
        gather_kernel,
        [out, out, shape(rows, features, bf16)],
        [even, send_lo, send_hi, x],
        [SMEM, HBM, HBM, HBM],
        [
            pltpu.VMEM((rows, features), f32),
            pltpu.VMEM((count, features), f32),
            pltpu.VMEM((count, features), f32),
            pltpu.SMEM((count,), jnp.int32),
            pltpu.SMEM((count,), jnp.int32),
            pltpu.SemaphoreType.DMA((3,)),
        ],
    )


def owner_sums(owner_ref, tile, values):
    place = lax.broadcasted_iota(jnp.int32, (256, 128), 0).astype(bf16)
    owner = (owner_ref[...] - tile * 256).astype(f32)
    rows = jnp.concatenate(
        [
            pick16(jnp.broadcast_to(owner[q : q + 1], (256, 128)).astype(bf16), place)
            for q in range(owner.shape[0])
        ],
        1,
    )
    return dot(rows, values)


def prepare_kernel(
    even_ref,
    g_hbm,
    owner_hbm,
    nbr_hbm,
    mask_hbm,
    coarse_nbr_hbm,
    coarse_mask_hbm,
    lo_hbm,
    hi_hbm,
    coarse_lo_hbm,
    coarse_hi_hbm,
    *rest,
    halo_rows,
    coarse_halo,
):
    weight_hbms, rest = rest[:7], rest[7:]
    (
        after_ref,
        counts_ref,
        columns_ref,
        columns_t_ref,
        coarse_columns_ref,
        coarse_columns_t_ref,
        g_ref,
        weights_ref,
        sends_ref,
        coarse_sends_ref,
        owner_ref,
        nbr_ref,
        mask_ref,
        coarse_nbr_ref,
        coarse_mask_ref,
        lo_ref,
        hi_ref,
        coarse_lo_ref,
        coarse_hi_ref,
        sems,
    ) = rest
    fetch(
        [
            (g_hbm, g_ref),
            (owner_hbm, owner_ref),
            (nbr_hbm, nbr_ref),
            (mask_hbm, mask_ref),
            (coarse_nbr_hbm, coarse_nbr_ref),
            (coarse_mask_hbm, coarse_mask_ref),
            (lo_hbm, lo_ref),
            (hi_hbm, hi_ref),
            (coarse_lo_hbm, coarse_lo_ref),
            (coarse_hi_hbm, coarse_hi_ref),
        ]
        + [(w, weights_ref.at[pl.ds(128 * n, 128), :]) for n, w in enumerate(weight_hbms)],
        sems,
    )
    even = even_ref[0] > 0
    for low, high, out in (
        (lo_ref, hi_ref, sends_ref),
        (coarse_lo_ref, coarse_hi_ref, coarse_sends_ref),
    ):
        first = jnp.where(even, high[...], low[...])
        second = jnp.where(even, low[...], high[...])
        out[...] = jnp.concatenate([first, second], 1)
    columns_ref[...] = slot_columns(nbr_ref[...], mask_ref[...], halo_rows, even)
    columns_t_ref[...] = columns_ref[...].T
    coarse_columns_ref[...] = slot_columns(
        coarse_nbr_ref[...], coarse_mask_ref[...], coarse_halo, even
    )
    coarse_columns_t_ref[...] = coarse_columns_ref[...].T
    tiles = counts_ref.shape[0] // 2
    owner = owner_ref[...]
    high, low = owner // 128, lax.rem(owner, 128)
    groups = owner.shape[0]
    place = lax.broadcasted_iota(jnp.int32, (128, 128), 0)
    high_rows = jnp.concatenate(
        [pick(high[q : q + 1, :] == place[:tiles]) for q in range(groups)], 1
    )
    low_rows = jnp.concatenate(
        [pick(low[q : q + 1, :] == place) for q in range(groups)], 1
    )
    counts = dot_nt(high_rows, low_rows)
    most = jnp.floor(counts * (1 / DIGIT))
    counts_ref[...] = jnp.concatenate([most, counts - DIGIT * most], 0).astype(bf16)


def sums_kernel(owner_ref, g_ref, after_ref, sums_ref):
    def step(tile, carry):
        sums_ref[chunk_of(tile, 256), :] = owner_sums(owner_ref, tile, g_ref[...]).astype(bf16)
        return carry

    lax.fori_loop(0, sums_ref.shape[0] // 256, step, None)


def owners_kernel(owner_ref, after_ref, owners_ref):
    owners_ref[...] = owner_columns(owner_ref)


def fine_forward_kernel(
    h_ref,
    first_ref,
    second_ref,
    weights_ref,
    columns_t_ref,
    owner_ref,
    counts_ref,
    summed_ref,
    slope_ref,
    totals_ref,
    own,
    far,
    halo,
    new,
):
    self_weight, other_weight = matrix(weights_ref, 0), matrix(weights_ref, 1)
    level_terms(h_ref, (first_ref, second_ref), self_weight, other_weight, own, far, halo)

    def step(index, carry):
        here = chunk_of(index, STEP * BLOCK)
        total, slopes = edges(own[here, :], far[here, :], columns_t_ref[here, :], halo)
        summed_ref[here, :] = total
        slope_ref[chunk_of(index, 8 * STEP * BLOCK), :] = jnp.concatenate(slopes, 0)
        return carry

    lax.fori_loop(0, h_ref.shape[0] // (STEP * BLOCK), step, None)
    new[...] = (
        h_ref[...].astype(f32) + dot(summed_ref[...], matrix(weights_ref, 2))
    ).astype(bf16)
    coarse_rows = totals_ref.shape[0] - counts_ref.shape[0]

    def tile_step(tile, carry):
        totals_ref[chunk_of(tile, 256), :] = owner_sums(owner_ref, tile, new[...]).astype(bf16)
        return carry

    lax.fori_loop(0, coarse_rows // 256, tile_step, None)
    totals_ref[coarse_rows:, :] = counts_ref[...]


def coarse_input_kernel(
    totals_ref,
    more_totals_ref,
    sums_ref,
    more_sums_ref,
    sends_ref,
    after_ref,
    cin_ref,
    first_ref,
    second_ref,
    chip_sums_ref,
    counts_ref,
):
    coarse_rows = cin_ref.shape[0]
    tiles = coarse_rows // 128
    chip_sums_ref[...] = (sums_ref[...].astype(f32) + more_sums_ref[...].astype(f32)).astype(bf16)
    totals = totals_ref[...].astype(f32) + more_totals_ref[...].astype(f32)
    digits = totals[coarse_rows:]
    counts_ref[...] = DIGIT * digits[:tiles] + digits[tiles:]
    per_row = counts_ref[...].T
    for tile in range(tiles):
        here = slice(tile * 128, (tile + 1) * 128)
        cin_ref[here, :] = (totals[here] / per_row[:, tile : tile + 1]).astype(bf16)
    cin = cin_ref[...]
    place = lax.broadcasted_iota(jnp.int32, (coarse_rows, sends_ref.shape[1]), 0)
    sent = dot_tn(pick(sends_ref[...] == place), cin).astype(bf16)
    halo_rows = first_ref.shape[0]
    first_ref[...] = sent[:halo_rows]
    second_ref[...] = sent[halo_rows:]


def coarse_kernel(
    cin_ref,
    first_ref,
    second_ref,
    chip_sums_ref,
    more_sums_ref,
    weights_ref,
    columns_ref,
    columns_t_ref,
    part_ref,
    first_grad_ref,
    second_grad_ref,
    sums_ref,
    summed_ref,
    ups_ref,
    downs_ref,
    own,
    far,
    halo,
    grad_sum,
    halo_grad,
):
    halo_rows = first_ref.shape[0]
    self_weight, other_weight = matrix(weights_ref, 3), matrix(weights_ref, 4)
    level_terms(cin_ref, (first_ref, second_ref), self_weight, other_weight, own, far, halo)
    halo_grad[...] = jnp.zeros_like(halo_grad)
    sums_ref[...] = (chip_sums_ref[...].astype(f32) + more_sums_ref[...].astype(f32)).astype(bf16)
    part_ref[...] = dot_nt(sums_ref[...], matrix(weights_ref, 6))
    ups_ref[...] = part_ref[...].astype(bf16)
    grad_sum[...] = (dot_nt(ups_ref[...], matrix(weights_ref, 5)) * 0.5).astype(bf16)

    def step(index, carry):
        here = chunk_of(index, STEP * BLOCK)
        total, slopes = edges(own[here, :], far[here, :], columns_t_ref[here, :], halo)
        summed_ref[here, :] = total
        downs_ref[here, :] = edges_back(
            slopes, grad_sum[here, :], columns_ref[:, here], halo_grad
        )
        return carry

    lax.fori_loop(0, cin_ref.shape[0] // (STEP * BLOCK), step, None)
    first_grad_ref[...] = halo_grad[:halo_rows, :].astype(bf16)
    second_grad_ref[...] = halo_grad[halo_rows:, :].astype(bf16)


def coarse_tail_kernel(
    cin_ref,
    first_ref,
    second_ref,
    sums_ref,
    matrices_ref,
    first_grad_ref,
    second_grad_ref,
    summed_ref,
    ups_ref,
    downs_ref,
    fine_ref,
    weights_ref,
    *,
    scale,
):
    cin = cin_ref[...]
    out = (cin.astype(f32) + dot(summed_ref[...], matrix(matrices_ref, 5))).astype(bf16)
    fine_ref[...] = dot(out, matrix(matrices_ref, 6)).astype(bf16)
    pair_grad = dot_tn(cin, downs_ref[...])
    other_grad = (
        pair_grad[:, 128:]
        + dot_tn(first_ref[...], first_grad_ref[...])
        + dot_tn(second_ref[...], second_grad_ref[...])
    )
    weights_ref[0:128, :] = (pair_grad[:, :128] * scale).astype(bf16)
    weights_ref[128:256, :] = (other_grad * scale).astype(bf16)
    weights_ref[256:384, :] = (dot_tn(summed_ref[...], ups_ref[...]) * scale).astype(bf16)
    weights_ref[384:512, :] = (dot_tn(out, sums_ref[...]) * scale).astype(bf16)


def owner_columns(owner_ref):
    owner = owner_ref[...].astype(f32)
    row = jnp.concatenate([owner[q : q + 1, :] for q in range(owner.shape[0])], 1)
    return jnp.broadcast_to(row, (8, row.shape[1])).T


def owner_rows(owners, values):
    count = owners.shape[0]
    wide = jnp.broadcast_to(owners[:, 0:1], (count, 128))
    lane = lax.broadcasted_iota(jnp.int32, (count, 128), 1)
    first, second = lane.astype(bf16), (lane + 128).astype(bf16)
    rows = []
    for tile in range(values.shape[0] // 256):
        here = (wide - 256.0 * tile).astype(bf16)
        rows += [pick16(here, first), pick16(here, second)]
    return dot(jnp.concatenate(rows, 1), values)


def result_kernel(h_ref, summed_ref, weights_ref, owners_ref, fine_ref, out_hbm, out_ref, sem):
    def step(index, carry):
        here = chunk_of(index, CHUNK)
        updated = h_ref[here, :].astype(f32) + dot(summed_ref[here, :], matrix(weights_ref, 2))
        out_ref[here, :] = (updated + owner_rows(owners_ref[here, :], fine_ref[...])).astype(bf16)
        pltpu.make_async_copy(out_ref.at[here, :], out_hbm.at[here, :], sem).start()
        return carry

    lax.fori_loop(0, h_ref.shape[0] // CHUNK, step, None)
    pltpu.make_async_copy(out_ref, out_hbm, sem).wait()


def fine_backward_kernel(
    h_ref,
    first_ref,
    second_ref,
    g_ref,
    summed_ref,
    slope_ref,
    matrices_ref,
    columns_ref,
    owners_ref,
    part_ref,
    counts_ref,
    coarse_downs_ref,
    first_back_ref,
    second_back_ref,
    sends_ref,
    coarse_weights_ref,
    ups_hbm,
    downs_hbm,
    first_grad_ref,
    second_grad_ref,
    weights_ref,
    ups_ref,
    downs_ref,
    grad_sum,
    halo_grad,
    mean,
    sems,
):
    halo_rows = first_ref.shape[0]
    coarse_rows = part_ref.shape[0]
    halo_grad[...] = jnp.zeros_like(halo_grad)

    place = lax.broadcasted_iota(jnp.int32, (coarse_rows, sends_ref.shape[1]), 0)
    sends = pick(sends_ref[...] == place)
    back = jnp.concatenate([first_back_ref[...], second_back_ref[...]], 0)
    back = dot_nt(back, matrix(matrices_ref, 4)).astype(bf16)
    plain = jnp.concatenate([matrix(matrices_ref, 3), matrix(matrices_ref, 4)], 1)
    grad_in = part_ref[...] + dot_nt(coarse_downs_ref[...], plain) + dot(sends, back)
    per_row = counts_ref[...].T
    for tile in range(coarse_rows // 128):
        here = slice(tile * 128, (tile + 1) * 128)
        mean[here, :] = (grad_in[here, :] / per_row[:, tile : tile + 1]).astype(bf16)

    count = STEP * BLOCK
    steps = h_ref.shape[0] // count

    def owner_step(index):
        here = chunk_of(index, count)
        grad_up = g_ref[here, :].astype(f32) + owner_rows(owners_ref[here, :], mean[...])
        ups = grad_up.astype(bf16)
        ups_ref[here, :] = ups
        grad_sum[here, :] = (dot_nt(ups, matrix(matrices_ref, 2)) * 0.5).astype(bf16)

    def edge_step(index):
        here = chunk_of(index, count)
        slope = slope_ref[chunk_of(index, 8 * count), :]
        slopes = [slope[n * 8 * BLOCK : (n + 1) * 8 * BLOCK] for n in range(STEP)]
        downs_ref[here, :] = edges_back(
            slopes, grad_sum[here, :], columns_ref[:, here], halo_grad
        )

    owner_step(0)

    def step(index, carry):
        edge_step(index)
        owner_step(index + 1)
        return carry

    lax.fori_loop(0, steps - 1, step, None)
    edge_step(steps - 1)
    copies = [
        pltpu.make_async_copy(ups_ref, ups_hbm, sems.at[0]),
        pltpu.make_async_copy(downs_ref, downs_hbm, sems.at[1]),
    ]
    for copy in copies:
        copy.start()
    first_grad = halo_grad[:halo_rows, :].astype(bf16)
    second_grad = halo_grad[halo_rows:, :].astype(bf16)
    first_grad_ref[...] = first_grad
    second_grad_ref[...] = second_grad
    pair_grad = dot_tn(h_ref[...], downs_ref[...])
    weights_ref[0:128, :] = pair_grad[:, :128].astype(bf16)
    weights_ref[128:256, :] = (
        pair_grad[:, 128:]
        + dot_tn(first_ref[...], first_grad)
        + dot_tn(second_ref[...], second_grad)
    ).astype(bf16)
    weights_ref[256:384, :] = dot_tn(summed_ref[...], ups_ref[...]).astype(bf16)
    weights_ref[384:896, :] = coarse_weights_ref[...]
    weights_ref[896:1024, :] = jnp.zeros((128, 128), bf16)
    for copy in copies:
        copy.wait()


def finish_kernel(
    ups_hbm,
    downs_hbm,
    first_back_ref,
    second_back_ref,
    sends_ref,
    matrices_ref,
    out_hbm,
    ups_ref,
    downs_ref,
    out_ref,
    ups_sems,
    downs_sems,
    out_sem,
):
    chunks = ups_ref.shape[0] // CHUNK

    def copies(index):
        here = chunk_of(index, CHUNK)
        return (
            pltpu.make_async_copy(ups_hbm.at[here, :], ups_ref.at[here, :], ups_sems.at[index]),
            pltpu.make_async_copy(
                downs_hbm.at[here, :], downs_ref.at[here, :], downs_sems.at[index]
            ),
        )

    for index in range(chunks):
        for copy in copies(index):
            copy.start()
    other = matrix(matrices_ref, 1)
    plain = jnp.concatenate([matrix(matrices_ref, 0), other], 1)
    back = jnp.concatenate([first_back_ref[...], second_back_ref[...]], 0)
    back = dot_nt(back, other).astype(bf16)
    sends = sends_ref[...]
    place = lax.broadcasted_iota(jnp.int32, (256, sends.shape[1]), 0).astype(bf16)

    def step(index, carry):
        here = chunk_of(index, CHUNK)
        rows = []
        for part in range(CHUNK // 256):
            local = (sends - (index * CHUNK + 256 * part)).astype(f32)
            rows.append(pick16(jnp.broadcast_to(local, place.shape).astype(bf16), place))
        spread = dot(jnp.concatenate(rows, 0), back)
        for copy in copies(index):
            copy.wait()
        grad = ups_ref[here, :].astype(f32) + dot_nt(downs_ref[here, :], plain)
        out_ref[here, :] = (grad + spread).astype(bf16)
        pltpu.make_async_copy(out_ref.at[here, :], out_hbm.at[here, :], out_sem).start()
        return carry

    lax.fori_loop(0, chunks, step, None)
    pltpu.make_async_copy(out_ref, out_hbm, out_sem).wait()


def share_kernel(parts_ref, result_ref, first_ref, second_ref, out_ref):
    total = parts_ref[0].astype(f32)
    for n in range(1, parts_ref.shape[0]):
        total = total + parts_ref[n].astype(f32)
    out_ref[...] = jnp.broadcast_to(total.astype(bf16)[None], out_ref.shape)


def widen_kernel(x_ref, out_ref):
    out_ref[...] = x_ref[: out_ref.shape[0], :].astype(f32)


def exchange(first, second):
    count = lax.axis_size("sub")
    routes = []
    for start in range(2):
        pairs = [(i, i + 1) for i in range(start, count - 1, 2)]
        routes.append(pairs + [(j, i) for i, j in pairs])
    return lax.ppermute(first, "sub", routes[0]), lax.ppermute(second, "sub", routes[1])


def swapped(block, axis, distance):
    return lax.ppermute(block, axis, [(i, i ^ distance) for i in range(lax.axis_size(axis))])


def total_over_all(block, axes, after):
    devices = lax.axis_size(axes)
    share = block.shape[0] // devices
    parts = lax.all_to_all(block.reshape(devices, share, 128), axes, 0, 0, tiled=False)
    mine = call(
        share_kernel,
        jax.ShapeDtypeStruct((devices, share, 128), bf16),
        [parts, *after],
        [VMEM, HBM, ANY, ANY],
    )
    return lax.all_to_all(mine, axes, 0, 0, tiled=False).reshape(block.shape)


def per_device(
    states,
    cotangent,
    fine_self,
    fine_other,
    fine_node,
    coarse_self,
    coarse_other,
    coarse_node,
    prolong,
    fine_nbr,
    fine_mask,
    fine_send_lo,
    fine_send_hi,
    coarse_nbr,
    coarse_mask,
    coarse_send_lo,
    coarse_send_hi,
    coarse_owner,
):
    rows, features = states.shape
    coarse_rows = coarse_nbr.shape[0]
    halo_rows = fine_send_lo.shape[0]
    coarse_halo = coarse_send_lo.shape[0]
    count_rows = coarse_rows // 128
    owner = coarse_owner.reshape(rows // 128, 128)
    even = (1 - lax.rem(lax.axis_index("sub"), 2)).astype(jnp.int32).reshape(1)

    def buffer(count, columns, dtype):
        return pltpu.VMEM((count, columns), dtype)

    to_first, to_second, states = gather_rows(even, states, fine_send_lo, fine_send_hi)
    first, second = exchange(to_first, to_second)

    (
        counts, columns, columns_t, coarse_columns, coarse_columns_t, cotangent, matrices, sends,
        coarse_sends, owner,
    ) = call(
        functools.partial(prepare_kernel, halo_rows=halo_rows, coarse_halo=coarse_halo),
        [
            shape(2 * count_rows, features, bf16),
            shape(8, rows, f32),
            shape(rows, 8, f32),
            shape(8, coarse_rows, f32),
            shape(coarse_rows, 8, f32),
            shape(rows, features, bf16),
            shape(7 * features, features, bf16),
            shape(1, 2 * halo_rows, jnp.int32),
            shape(1, 2 * coarse_halo, jnp.int32),
            shape(rows // 128, 128, jnp.int32),
        ],
        [
            even, cotangent, owner, fine_nbr.T, fine_mask.T, coarse_nbr.T, coarse_mask.T,
            fine_send_lo[None], fine_send_hi[None], coarse_send_lo[None], coarse_send_hi[None],
            fine_self, fine_other, fine_node, coarse_self, coarse_other, coarse_node, prolong,
            to_first,
        ],
        [SMEM] + [HBM] * 17 + [ANY],
        [buffer(8, rows, jnp.int32)] * 2
        + [buffer(8, coarse_rows, jnp.int32)] * 2
        + [buffer(1, halo_rows, jnp.int32)] * 2
        + [buffer(1, coarse_halo, jnp.int32)] * 2
        + [pltpu.SemaphoreType.DMA((17,))],
    )

    summed, slope, totals = call(
        fine_forward_kernel,
        [
            shape(rows, features, bf16),
            shape(8 * rows, features, bf16),
            shape(coarse_rows + 2 * count_rows, features, bf16),
        ],
        [states, first, second, matrices, columns_t, owner, counts],
        scratch=[
            buffer(rows, features, f32),
            buffer(rows, features, bf16),
            buffer(2 * halo_rows, features, bf16),
            buffer(rows, features, bf16),
        ],
    )
    chip_totals = (totals.astype(f32) + swapped(totals, "grp", 1).astype(f32)).astype(bf16)
    more_totals = swapped(chip_totals, "grp", 2)
    sums = call(
        sums_kernel,
        shape(coarse_rows, features, bf16),
        [owner, cotangent, totals],
        [VMEM, VMEM, ANY],
    )
    more_sums = swapped(sums, "grp", 1)
    owners_t = call(owners_kernel, shape(rows, 8, f32), [owner, chip_totals], [VMEM, ANY])

    coarse_in, to_first, to_second, chip_sums, counts = call(
        coarse_input_kernel,
        [
            shape(coarse_rows, features, bf16),
            shape(coarse_halo, features, bf16),
            shape(coarse_halo, features, bf16),
            shape(coarse_rows, features, bf16),
            shape(count_rows, features, f32),
        ],
        [chip_totals, more_totals, sums, more_sums, coarse_sends, owners_t],
        [VMEM] * 5 + [ANY],
    )
    coarse_first, coarse_second = exchange(to_first, to_second)
    more_sums = swapped(chip_sums, "grp", 2)

    coarse_part, first_grad, second_grad, sums, coarse_sum, coarse_ups, coarse_downs = call(
        coarse_kernel,
        [
            shape(coarse_rows, features, f32),
            shape(coarse_halo, features, bf16),
            shape(coarse_halo, features, bf16),
            shape(coarse_rows, features, bf16),
            shape(coarse_rows, features, bf16),
            shape(coarse_rows, features, bf16),
            shape(coarse_rows, 2 * features, bf16),
        ],
        [
            coarse_in, coarse_first, coarse_second, chip_sums, more_sums, matrices,
            coarse_columns, coarse_columns_t,
        ],
        scratch=[
            buffer(coarse_rows, features, f32),
            buffer(coarse_rows, features, bf16),
            buffer(2 * coarse_halo, features, bf16),
            buffer(coarse_rows, features, bf16),
            buffer(2 * coarse_halo, features, f32),
        ],
    )
    first_back, second_back = exchange(first_grad, second_grad)

    fine_term, coarse_weights = call(
        functools.partial(coarse_tail_kernel, scale=1.0 / lax.axis_size("grp")),
        [shape(coarse_rows, features, bf16), shape(4 * features, features, bf16)],
        [
            coarse_in, coarse_first, coarse_second, sums, matrices,
            first_grad, second_grad, coarse_sum, coarse_ups, coarse_downs,
        ],
    )
    result = call(
        result_kernel,
        pltpu.HBM((rows, features), bf16),
        [states, summed, matrices, owners_t, fine_term],
        scratch=[buffer(rows, features, bf16), pltpu.SemaphoreType.DMA],
        out_specs=HBM,
    )

    ups, downs, first_grad, second_grad, weights = call(
        fine_backward_kernel,
        [
            pltpu.HBM((rows, features), bf16),
            pltpu.HBM((rows, 2 * features), bf16),
            shape(halo_rows, features, bf16),
            shape(halo_rows, features, bf16),
            shape(8 * features, features, bf16),
        ],
        [
            states, first, second, cotangent, summed, slope, matrices, columns, owners_t,
            coarse_part, counts, coarse_downs, first_back, second_back, coarse_sends,
            coarse_weights,
        ],
        scratch=[
            buffer(rows, features, bf16),
            buffer(rows, 2 * features, bf16),
            buffer(rows, features, bf16),
            buffer(2 * halo_rows, features, f32),
            buffer(coarse_rows, features, bf16),
            pltpu.SemaphoreType.DMA((2,)),
        ],
        out_specs=[HBM, HBM, VMEM, VMEM, VMEM],
    )
    first_back, second_back = exchange(first_grad, second_grad)

    grad_states = call(
        finish_kernel,
        pltpu.HBM((rows, features), bf16),
        [ups, downs, first_back, second_back, sends, matrices],
        [HBM, HBM] + [VMEM] * 4,
        [
            buffer(rows, features, bf16),
            buffer(rows, 2 * features, bf16),
            buffer(rows, features, bf16),
            pltpu.SemaphoreType.DMA((rows // CHUNK,)),
            pltpu.SemaphoreType.DMA((rows // CHUNK,)),
            pltpu.SemaphoreType.DMA,
        ],
        out_specs=HBM,
    )
    weights = total_over_all(weights, ("grp", "sub"), (result, first_back, second_back))
    grad_weights = call(widen_kernel, shape(7 * features, features, f32), [weights])
    return (result, grad_states, grad_weights.reshape(7, features, features))


def solution(mesh):
    fine = P(("grp", "sub"), None)
    fine_row = P(("grp", "sub"))
    in_specs = (
        (fine, fine)
        + (P(),) * 7
        + (fine, fine, fine_row, fine_row)
        + (P("sub", None), P("sub", None), P("sub"), P("sub"), fine_row)
    )
    return jax.shard_map(
        per_device, mesh=mesh, in_specs=in_specs, out_specs=(fine, fine, P()), check_vma=False
    )
```

```python
import functools

import jax
import jax.numpy as jnp
from jax import lax
from jax.experimental import pallas as pl
from jax.experimental.pallas import tpu as pltpu
from jax.sharding import PartitionSpec as P

f32 = jnp.float32
bf16 = jnp.bfloat16
BLOCK = 64
PAIR = 2 * BLOCK
STEP = 8
CHUNK = 512
NEVER = -1e30
DIGIT = 64.0
VMEM = pl.BlockSpec(memory_space=pltpu.VMEM)
SMEM = pl.BlockSpec(memory_space=pltpu.SMEM)
ANY = pl.BlockSpec(memory_space=pl.ANY)
HBM = pl.BlockSpec(memory_space=pltpu.HBM)
PARAMS = pltpu.CompilerParams(vmem_limit_bytes=32 * 1024 * 1024)


def dot(a, b):
    return jnp.dot(a, b, preferred_element_type=f32)


def dot_nt(a, b):
    return lax.dot_general(a, b, (((1,), (1,)), ((), ())), preferred_element_type=f32)


def dot_tn(a, b):
    return lax.dot_general(a, b, (((0,), (0,)), ((), ())), preferred_element_type=f32)


def pick(condition):
    return jnp.where(condition, 1.0, 0.0).astype(bf16)


def pick16(values, places):
    return jnp.where(values == places, jnp.ones((), bf16), jnp.zeros((), bf16))


def call(kernel, out_shape, args, in_specs=None, scratch=(), out_specs=None):
    many = isinstance(out_shape, (list, tuple))
    in_specs = in_specs or [VMEM] * len(args)
    args = [
        pltpu.with_memory_space_constraint(arg, pltpu.HBM) if spec is HBM else arg
        for arg, spec in zip(args, in_specs)
    ]
    return pl.pallas_call(
        kernel,
        out_shape=out_shape,
        in_specs=in_specs,
        out_specs=out_specs or ([VMEM] * len(out_shape) if many else VMEM),
        scratch_shapes=list(scratch),
        compiler_params=PARAMS,
    )(*args)


def shape(rows, columns, dtype):
    return jax.ShapeDtypeStruct((rows, columns), dtype)


def slot_columns(nbr, mask, halo_rows, even):
    rows = nbr.shape[1]
    block = lax.broadcasted_iota(jnp.int32, nbr.shape, 1) // BLOCK
    halo = lax.rem(block, halo_rows // BLOCK) * BLOCK
    lower = jnp.where(even, 2 * BLOCK, BLOCK)
    column = jnp.where(
        nbr < rows,
        nbr - block * BLOCK,
        jnp.where(
            nbr < rows + halo_rows,
            lower + nbr - rows - halo,
            3 * BLOCK - lower + nbr - rows - halo_rows - halo,
        ),
    )
    return jnp.where(mask > 0, column, 3 * BLOCK).astype(f32)


def selector(columns_t):
    first = lax.broadcasted_iota(jnp.int32, (BLOCK, 128), 1).astype(bf16)
    second = (lax.broadcasted_iota(jnp.int32, (BLOCK, 128), 1) + 128).astype(bf16)
    parts = []
    for k in range(8):
        wide = jnp.broadcast_to(columns_t[:, k : k + 1], (BLOCK, 128)).astype(bf16)
        parts.append(jnp.concatenate([pick16(wide, first), pick16(wide, second)], 1))
    return jnp.concatenate(parts, 0)


def selector_t(columns, rolled, half):
    lane = lax.broadcasted_iota(jnp.int32, (1, 128), 1)
    place = lax.broadcasted_iota(jnp.int32, (3 * BLOCK, 128), 0).astype(bf16)
    parts = []
    for j in range(4):
        left, right = (columns, rolled) if half == 0 else (rolled, columns)
        row = jnp.where(lane < BLOCK, left[2 * j : 2 * j + 1], right[2 * j + 1 : 2 * j + 2])
        wide = jnp.broadcast_to(row, (3 * BLOCK, 128)).astype(bf16)
        parts.append(pick16(wide, place))
    return jnp.concatenate(parts, 1)


def window_of(far, halo, place):
    halo_rows = halo.shape[0] // 2
    start = place * BLOCK
    return jnp.concatenate(
        [
            far,
            halo[start : start + BLOCK, :],
            halo[halo_rows + start : halo_rows + start + BLOCK, :],
            jnp.full((BLOCK, far.shape[1]), NEVER, bf16),
        ],
        0,
    )


def chunk_of(index, count):
    return pl.ds(pl.multiple_of(index * count, count), count)


def matrix(weights_ref, n):
    return weights_ref[128 * n : 128 * (n + 1), :]


def level_terms(h_ref, halo_refs, self_weight, other_weight, own, far, halo):
    halo_rows = halo_refs[0].shape[0]
    other = other_weight * 0.5
    h = h_ref[...]
    own[...] = dot(h, self_weight * 0.5)
    far[...] = dot(h, other).astype(bf16)
    halo[:halo_rows, :] = dot(halo_refs[0][...], other).astype(bf16)
    halo[halo_rows:, :] = dot(halo_refs[1][...], other).astype(bf16)


def edges(own_rows, far_rows, slots, halo):
    places = halo.shape[0] // (2 * BLOCK)
    assert STEP % places == 0
    tables = []
    for n in range(STEP):
        part = slice(n * BLOCK, (n + 1) * BLOCK)
        window = window_of(far_rows[part], halo, n % places)
        tables.append(dot(selector(slots[part]), window))
    sums, slopes = [], []
    for n, picked in enumerate(tables):
        own = own_rows[n * BLOCK : (n + 1) * BLOCK]
        values, pieces = [], []
        for k in range(8):
            y = (picked[k * BLOCK : (k + 1) * BLOCK] + own).astype(bf16)
            t = jnp.tanh(y)
            bent = y * t
            values.append(y + bent)
            pieces.append((1 + t) * (1 + (y - bent)))
        while len(values) > 1:
            values = [left + right for left, right in zip(values[::2], values[1::2])]
        sums.append(values[0])
        slopes.append(jnp.concatenate(pieces, 0))
    return jnp.concatenate(sums, 0), slopes


def edges_back(slopes, grad_sum, columns, halo_grad):
    places = halo_grad.shape[0] // (2 * BLOCK)
    halo_rows = halo_grad.shape[0] // 2
    windows, downs = [], []
    for n, slope in enumerate(slopes):
        part = grad_sum[n * BLOCK : (n + 1) * BLOCK]
        grads = [slope[k * BLOCK : (k + 1) * BLOCK] * part for k in range(8)]
        downs.append(sum(grad.astype(f32) for grad in grads))
        mine = columns[:, n // 2 * PAIR : (n // 2 + 1) * PAIR]
        selected = selector_t(mine, pltpu.roll(mine, BLOCK, 1), n % 2)
        windows.append(dot(selected, jnp.concatenate(grads, 0)))
    for place in range(places):
        for side in range(2):
            start = side * halo_rows + place * BLOCK
            total = halo_grad[start : start + BLOCK, :]
            for window in windows[place::places]:
                total = total + window[(side + 1) * BLOCK : (side + 2) * BLOCK]
            halo_grad[start : start + BLOCK, :] = total
    local = jnp.concatenate([window[:BLOCK] for window in windows], 0)
    down = jnp.concatenate(downs, 0)
    return jnp.concatenate([down, local], 1).astype(bf16)


def fetch(pairs, sems):
    copies = [pltpu.make_async_copy(src, dst, sems.at[n]) for n, (src, dst) in enumerate(pairs)]
    for copy in copies:
        copy.start()
    for copy in copies:
        copy.wait()


def gather_kernel(
    even_ref, lo_hbm, hi_hbm, x_hbm, first_ref, second_ref, x_ref, wide, up, down, lo, hi, sems
):
    fetch([(x_hbm, x_ref), (lo_hbm, lo), (hi_hbm, hi)], sems)
    wide[...] = x_ref[...].astype(f32)

    def step(r, carry):
        up[pl.ds(r, 1), :] = wide[pl.ds(hi[r], 1), :]
        down[pl.ds(r, 1), :] = wide[pl.ds(lo[r], 1), :]
        return carry

    lax.fori_loop(0, up.shape[0], step, None, unroll=16)
    even = even_ref[0] > 0
    first_ref[...] = jnp.where(even, up[...], down[...]).astype(bf16)
    second_ref[...] = jnp.where(even, down[...], up[...]).astype(bf16)


def gather_rows(even, x, send_lo, send_hi):
    rows, features = x.shape
    count = send_lo.shape[0]
    out = shape(count, features, bf16)
    return call(
        gather_kernel,
        [out, out, shape(rows, features, bf16)],
        [even, send_lo, send_hi, x],
        [SMEM, HBM, HBM, HBM],
        [
            pltpu.VMEM((rows, features), f32),
            pltpu.VMEM((count, features), f32),
            pltpu.VMEM((count, features), f32),
            pltpu.SMEM((count,), jnp.int32),
            pltpu.SMEM((count,), jnp.int32),
            pltpu.SemaphoreType.DMA((3,)),
        ],
    )


def owner_sums(owner_ref, tile, values):
    place = lax.broadcasted_iota(jnp.int32, (256, 128), 0).astype(bf16)
    owner = (owner_ref[...] - tile * 256).astype(f32)
    rows = jnp.concatenate(
        [
            pick16(jnp.broadcast_to(owner[q : q + 1], (256, 128)).astype(bf16), place)
            for q in range(owner.shape[0])
        ],
        1,
    )
    return dot(rows, values)


def prepare_kernel(
    even_ref,
    g_hbm,
    owner_hbm,
    nbr_hbm,
    mask_hbm,
    coarse_nbr_hbm,
    coarse_mask_hbm,
    lo_hbm,
    hi_hbm,
    coarse_lo_hbm,
    coarse_hi_hbm,
    *rest,
    halo_rows,
    coarse_halo,
):
    weight_hbms, rest = rest[:7], rest[7:]
    (
        after_ref,
        counts_ref,
        columns_ref,
        columns_t_ref,
        coarse_columns_ref,
        coarse_columns_t_ref,
        g_ref,
        weights_ref,
        sends_ref,
        coarse_sends_ref,
        owner_ref,
        nbr_ref,
        mask_ref,
        coarse_nbr_ref,
        coarse_mask_ref,
        lo_ref,
        hi_ref,
        coarse_lo_ref,
        coarse_hi_ref,
        sems,
    ) = rest
    fetch(
        [
            (g_hbm, g_ref),
            (owner_hbm, owner_ref),
            (nbr_hbm, nbr_ref),
            (mask_hbm, mask_ref),
            (coarse_nbr_hbm, coarse_nbr_ref),
            (coarse_mask_hbm, coarse_mask_ref),
            (lo_hbm, lo_ref),
            (hi_hbm, hi_ref),
            (coarse_lo_hbm, coarse_lo_ref),
            (coarse_hi_hbm, coarse_hi_ref),
        ]
        + [(w, weights_ref.at[pl.ds(128 * n, 128), :]) for n, w in enumerate(weight_hbms)],
        sems,
    )
    even = even_ref[0] > 0
    for low, high, out in (
        (lo_ref, hi_ref, sends_ref),
        (coarse_lo_ref, coarse_hi_ref, coarse_sends_ref),
    ):
        first = jnp.where(even, high[...], low[...])
        second = jnp.where(even, low[...], high[...])
        out[...] = jnp.concatenate([first, second], 1)
    columns_ref[...] = slot_columns(nbr_ref[...], mask_ref[...], halo_rows, even)
    columns_t_ref[...] = columns_ref[...].T
    coarse_columns_ref[...] = slot_columns(
        coarse_nbr_ref[...], coarse_mask_ref[...], coarse_halo, even
    )
    coarse_columns_t_ref[...] = coarse_columns_ref[...].T
    tiles = counts_ref.shape[0] // 2
    owner = owner_ref[...]
    high, low = owner // 128, lax.rem(owner, 128)
    groups = owner.shape[0]
    place = lax.broadcasted_iota(jnp.int32, (128, 128), 0)
    high_rows = jnp.concatenate(
        [pick(high[q : q + 1, :] == place[:tiles]) for q in range(groups)], 1
    )
    low_rows = jnp.concatenate(
        [pick(low[q : q + 1, :] == place) for q in range(groups)], 1
    )
    counts = dot_nt(high_rows, low_rows)
    most = jnp.floor(counts * (1 / DIGIT))
    counts_ref[...] = jnp.concatenate([most, counts - DIGIT * most], 0).astype(bf16)


def sums_kernel(owner_ref, g_ref, after_ref, sums_ref):
    def step(tile, carry):
        sums_ref[chunk_of(tile, 256), :] = owner_sums(owner_ref, tile, g_ref[...]).astype(bf16)
        return carry

    lax.fori_loop(0, sums_ref.shape[0] // 256, step, None)


def owners_kernel(owner_ref, after_ref, owners_ref):
    owners_ref[...] = owner_columns(owner_ref)


def fine_forward_kernel(
    h_ref,
    first_ref,
    second_ref,
    weights_ref,
    columns_t_ref,
    owner_ref,
    counts_ref,
    summed_ref,
    slope_ref,
    totals_ref,
    own,
    far,
    halo,
    new,
):
    self_weight, other_weight = matrix(weights_ref, 0), matrix(weights_ref, 1)
    level_terms(h_ref, (first_ref, second_ref), self_weight, other_weight, own, far, halo)

    def step(index, carry):
        here = chunk_of(index, STEP * BLOCK)
        total, slopes = edges(own[here, :], far[here, :], columns_t_ref[here, :], halo)
        summed_ref[here, :] = total
        slope_ref[chunk_of(index, 8 * STEP * BLOCK), :] = jnp.concatenate(slopes, 0)
        return carry

    lax.fori_loop(0, h_ref.shape[0] // (STEP * BLOCK), step, None)
    new[...] = (
        h_ref[...].astype(f32) + dot(summed_ref[...], matrix(weights_ref, 2))
    ).astype(bf16)
    coarse_rows = totals_ref.shape[0] - counts_ref.shape[0]

    def tile_step(tile, carry):
        totals_ref[chunk_of(tile, 256), :] = owner_sums(owner_ref, tile, new[...]).astype(bf16)
        return carry

    lax.fori_loop(0, coarse_rows // 256, tile_step, None)
    totals_ref[coarse_rows:, :] = counts_ref[...]


def coarse_input_kernel(
    totals_ref,
    more_totals_ref,
    sums_ref,
    more_sums_ref,
    sends_ref,
    after_ref,
    cin_ref,
    first_ref,
    second_ref,
    chip_sums_ref,
    counts_ref,
):
    coarse_rows = cin_ref.shape[0]
    tiles = coarse_rows // 128
    chip_sums_ref[...] = (sums_ref[...].astype(f32) + more_sums_ref[...].astype(f32)).astype(bf16)
    totals = totals_ref[...].astype(f32) + more_totals_ref[...].astype(f32)
    digits = totals[coarse_rows:]
    counts_ref[...] = DIGIT * digits[:tiles] + digits[tiles:]
    per_row = counts_ref[...].T
    for tile in range(tiles):
        here = slice(tile * 128, (tile + 1) * 128)
        cin_ref[here, :] = (totals[here] / per_row[:, tile : tile + 1]).astype(bf16)
    cin = cin_ref[...]
    place = lax.broadcasted_iota(jnp.int32, (coarse_rows, sends_ref.shape[1]), 0)
    sent = dot_tn(pick(sends_ref[...] == place), cin).astype(bf16)
    halo_rows = first_ref.shape[0]
    first_ref[...] = sent[:halo_rows]
    second_ref[...] = sent[halo_rows:]


def coarse_kernel(
    cin_ref,
    first_ref,
    second_ref,
    chip_sums_ref,
    more_sums_ref,
    weights_ref,
    columns_ref,
    columns_t_ref,
    part_ref,
    first_grad_ref,
    second_grad_ref,
    sums_ref,
    summed_ref,
    ups_ref,
    downs_ref,
    own,
    far,
    halo,
    grad_sum,
    halo_grad,
):
    halo_rows = first_ref.shape[0]
    self_weight, other_weight = matrix(weights_ref, 3), matrix(weights_ref, 4)
    level_terms(cin_ref, (first_ref, second_ref), self_weight, other_weight, own, far, halo)
    halo_grad[...] = jnp.zeros_like(halo_grad)
    sums_ref[...] = (chip_sums_ref[...].astype(f32) + more_sums_ref[...].astype(f32)).astype(bf16)
    part_ref[...] = dot_nt(sums_ref[...], matrix(weights_ref, 6))
    ups_ref[...] = part_ref[...].astype(bf16)
    grad_sum[...] = (dot_nt(ups_ref[...], matrix(weights_ref, 5)) * 0.5).astype(bf16)

    def step(index, carry):
        here = chunk_of(index, STEP * BLOCK)
        total, slopes = edges(own[here, :], far[here, :], columns_t_ref[here, :], halo)
        summed_ref[here, :] = total
        downs_ref[here, :] = edges_back(
            slopes, grad_sum[here, :], columns_ref[:, here], halo_grad
        )
        return carry

    lax.fori_loop(0, cin_ref.shape[0] // (STEP * BLOCK), step, None)
    first_grad_ref[...] = halo_grad[:halo_rows, :].astype(bf16)
    second_grad_ref[...] = halo_grad[halo_rows:, :].astype(bf16)


def coarse_tail_kernel(
    group_ref,
    cin_ref,
    first_ref,
    second_ref,
    sums_ref,
    matrices_ref,
    first_grad_ref,
    second_grad_ref,
    summed_ref,
    ups_ref,
    downs_ref,
    fine_ref,
    weights_ref,
):
    cin = cin_ref[...]
    out = (cin.astype(f32) + dot(summed_ref[...], matrix(matrices_ref, 5))).astype(bf16)
    fine_ref[...] = dot(out, matrix(matrices_ref, 6)).astype(bf16)
    pair_grad = dot_tn(cin, downs_ref[...])
    other_grad = (
        pair_grad[:, 128:]
        + dot_tn(first_ref[...], first_grad_ref[...])
        + dot_tn(second_ref[...], second_grad_ref[...])
    )
    grads = [
        pair_grad[:, :128],
        other_grad,
        dot_tn(summed_ref[...], ups_ref[...]),
        dot_tn(out, sums_ref[...]),
    ]
    weights_ref[...] = choose(group_ref[0], grads).astype(bf16)


def choose(place, values):
    picked = values[-1]
    for n, value in enumerate(values[:-1]):
        picked = jnp.where(place == n, value, picked)
    return picked


def owner_columns(owner_ref):
    owner = owner_ref[...].astype(f32)
    row = jnp.concatenate([owner[q : q + 1, :] for q in range(owner.shape[0])], 1)
    return jnp.broadcast_to(row, (8, row.shape[1])).T


def owner_rows(owners, values):
    count = owners.shape[0]
    wide = jnp.broadcast_to(owners[:, 0:1], (count, 128))
    lane = lax.broadcasted_iota(jnp.int32, (count, 128), 1)
    first, second = lane.astype(bf16), (lane + 128).astype(bf16)
    rows = []
    for tile in range(values.shape[0] // 256):
        here = (wide - 256.0 * tile).astype(bf16)
        rows += [pick16(here, first), pick16(here, second)]
    return dot(jnp.concatenate(rows, 1), values)


def result_kernel(h_ref, summed_ref, weights_ref, owners_ref, fine_ref, out_hbm, out_ref, sem):
    def step(index, carry):
        here = chunk_of(index, CHUNK)
        updated = h_ref[here, :].astype(f32) + dot(summed_ref[here, :], matrix(weights_ref, 2))
        out_ref[here, :] = (updated + owner_rows(owners_ref[here, :], fine_ref[...])).astype(bf16)
        pltpu.make_async_copy(out_ref.at[here, :], out_hbm.at[here, :], sem).start()
        return carry

    lax.fori_loop(0, h_ref.shape[0] // CHUNK, step, None)
    pltpu.make_async_copy(out_ref, out_hbm, sem).wait()


def fine_backward_kernel(
    h_ref,
    first_ref,
    second_ref,
    g_ref,
    summed_ref,
    slope_ref,
    matrices_ref,
    columns_ref,
    owners_ref,
    part_ref,
    counts_ref,
    coarse_downs_ref,
    first_back_ref,
    second_back_ref,
    sends_ref,
    coarse_weights_ref,
    ups_hbm,
    downs_hbm,
    first_grad_ref,
    second_grad_ref,
    weights_ref,
    ups_ref,
    downs_ref,
    grad_sum,
    halo_grad,
    mean,
    sems,
):
    halo_rows = first_ref.shape[0]
    coarse_rows = part_ref.shape[0]
    halo_grad[...] = jnp.zeros_like(halo_grad)

    place = lax.broadcasted_iota(jnp.int32, (coarse_rows, sends_ref.shape[1]), 0)
    sends = pick(sends_ref[...] == place)
    back = jnp.concatenate([first_back_ref[...], second_back_ref[...]], 0)
    back = dot_nt(back, matrix(matrices_ref, 4)).astype(bf16)
    plain = jnp.concatenate([matrix(matrices_ref, 3), matrix(matrices_ref, 4)], 1)
    grad_in = part_ref[...] + dot_nt(coarse_downs_ref[...], plain) + dot(sends, back)
    per_row = counts_ref[...].T
    for tile in range(coarse_rows // 128):
        here = slice(tile * 128, (tile + 1) * 128)
        mean[here, :] = (grad_in[here, :] / per_row[:, tile : tile + 1]).astype(bf16)

    count = STEP * BLOCK
    steps = h_ref.shape[0] // count

    def owner_step(index):
        here = chunk_of(index, count)
        grad_up = g_ref[here, :].astype(f32) + owner_rows(owners_ref[here, :], mean[...])
        ups = grad_up.astype(bf16)
        ups_ref[here, :] = ups
        grad_sum[here, :] = (dot_nt(ups, matrix(matrices_ref, 2)) * 0.5).astype(bf16)

    def edge_step(index):
        here = chunk_of(index, count)
        slope = slope_ref[chunk_of(index, 8 * count), :]
        slopes = [slope[n * 8 * BLOCK : (n + 1) * 8 * BLOCK] for n in range(STEP)]
        downs_ref[here, :] = edges_back(
            slopes, grad_sum[here, :], columns_ref[:, here], halo_grad
        )

    owner_step(0)

    def step(index, carry):
        edge_step(index)
        owner_step(index + 1)
        return carry

    lax.fori_loop(0, steps - 1, step, None)
    edge_step(steps - 1)
    copies = [
        pltpu.make_async_copy(ups_ref, ups_hbm, sems.at[0]),
        pltpu.make_async_copy(downs_ref, downs_hbm, sems.at[1]),
    ]
    for copy in copies:
        copy.start()
    first_grad = halo_grad[:halo_rows, :].astype(bf16)
    second_grad = halo_grad[halo_rows:, :].astype(bf16)
    first_grad_ref[...] = first_grad
    second_grad_ref[...] = second_grad
    pair_grad = dot_tn(h_ref[...], downs_ref[...])
    weights_ref[0:128, :] = pair_grad[:, :128].astype(bf16)
    weights_ref[128:256, :] = (
        pair_grad[:, 128:]
        + dot_tn(first_ref[...], first_grad)
        + dot_tn(second_ref[...], second_grad)
    ).astype(bf16)
    weights_ref[256:384, :] = dot_tn(summed_ref[...], ups_ref[...]).astype(bf16)
    weights_ref[384:512, :] = coarse_weights_ref[...]
    for copy in copies:
        copy.wait()


def finish_kernel(
    ups_hbm,
    downs_hbm,
    first_back_ref,
    second_back_ref,
    sends_ref,
    matrices_ref,
    out_hbm,
    ups_ref,
    downs_ref,
    out_ref,
    ups_sems,
    downs_sems,
    out_sem,
):
    chunks = ups_ref.shape[0] // CHUNK

    def copies(index):
        here = chunk_of(index, CHUNK)
        return (
            pltpu.make_async_copy(ups_hbm.at[here, :], ups_ref.at[here, :], ups_sems.at[index]),
            pltpu.make_async_copy(
                downs_hbm.at[here, :], downs_ref.at[here, :], downs_sems.at[index]
            ),
        )

    for index in range(chunks):
        for copy in copies(index):
            copy.start()
    other = matrix(matrices_ref, 1)
    plain = jnp.concatenate([matrix(matrices_ref, 0), other], 1)
    back = jnp.concatenate([first_back_ref[...], second_back_ref[...]], 0)
    back = dot_nt(back, other).astype(bf16)
    sends = sends_ref[...]
    place = lax.broadcasted_iota(jnp.int32, (256, sends.shape[1]), 0).astype(bf16)

    def step(index, carry):
        here = chunk_of(index, CHUNK)
        rows = []
        for part in range(CHUNK // 256):
            local = (sends - (index * CHUNK + 256 * part)).astype(f32)
            rows.append(pick16(jnp.broadcast_to(local, place.shape).astype(bf16), place))
        spread = dot(jnp.concatenate(rows, 0), back)
        for copy in copies(index):
            copy.wait()
        grad = ups_ref[here, :].astype(f32) + dot_nt(downs_ref[here, :], plain)
        out_ref[here, :] = (grad + spread).astype(bf16)
        pltpu.make_async_copy(out_ref.at[here, :], out_hbm.at[here, :], out_sem).start()
        return carry

    lax.fori_loop(0, chunks, step, None)
    pltpu.make_async_copy(out_ref, out_hbm, out_sem).wait()


def add_kernel(mine_ref, theirs_ref, *rest):
    out_ref = rest[-1]
    out_ref[...] = (mine_ref[...].astype(f32) + theirs_ref[...].astype(f32)).astype(bf16)


def add_gather_kernel(mine_ref, theirs_ref, out_ref):
    mine, theirs = mine_ref[...].astype(f32), theirs_ref[...].astype(f32)
    out_ref[:384, :] = mine[:384] + theirs[:384]
    out_ref[384:512, :] = mine[384:]
    out_ref[512:, :] = theirs[384:]


def weights_kernel(group_ref, mine_ref, theirs_ref, out_ref):
    out_ref[:384, :] = mine_ref[:384, :] + theirs_ref[:384, :]
    group = group_ref[0]
    low, high = lax.rem(group, 2), group // 2
    for n in range(4):
        row = jnp.where(high == n // 2, 384, 512)
        here = pl.ds(pl.multiple_of(row, 128), 128)
        value = jnp.where(low == n % 2, mine_ref[here, :], theirs_ref[here, :])
        out_ref[384 + 128 * n : 512 + 128 * n, :] = value


def exchange(first, second):
    count = lax.axis_size("sub")
    routes = []
    for start in range(2):
        pairs = [(i, i + 1) for i in range(start, count - 1, 2)]
        routes.append(pairs + [(j, i) for i, j in pairs])
    return lax.ppermute(first, "sub", routes[0]), lax.ppermute(second, "sub", routes[1])


def swapped(block, axis, distance):
    return lax.ppermute(block, axis, [(i, i ^ distance) for i in range(lax.axis_size(axis))])


def total_weights(weights, group, after):
    distance, number = 1, 0
    while distance < lax.axis_size("sub"):
        theirs = swapped(weights, "sub", distance)
        waits = after[number] if number < len(after) else ()
        weights = call(
            add_kernel,
            shape(*weights.shape, bf16),
            [weights, theirs, *waits],
            [VMEM, VMEM] + [HBM] * len(waits),
        )
        distance, number = 2 * distance, number + 1
    weights = call(
        add_gather_kernel,
        shape(640, 128, f32),
        [weights, swapped(weights, "grp", 2)],
    )
    return call(
        weights_kernel,
        shape(896, 128, f32),
        [group, weights, swapped(weights, "grp", 1)],
        [SMEM, VMEM, VMEM],
    )


def per_device(
    states,
    cotangent,
    fine_self,
    fine_other,
    fine_node,
    coarse_self,
    coarse_other,
    coarse_node,
    prolong,
    fine_nbr,
    fine_mask,
    fine_send_lo,
    fine_send_hi,
    coarse_nbr,
    coarse_mask,
    coarse_send_lo,
    coarse_send_hi,
    coarse_owner,
):
    rows, features = states.shape
    coarse_rows = coarse_nbr.shape[0]
    halo_rows = fine_send_lo.shape[0]
    coarse_halo = coarse_send_lo.shape[0]
    count_rows = coarse_rows // 128
    owner = coarse_owner.reshape(rows // 128, 128)
    even = (1 - lax.rem(lax.axis_index("sub"), 2)).astype(jnp.int32).reshape(1)
    group = lax.axis_index("grp").astype(jnp.int32).reshape(1)

    def buffer(count, columns, dtype):
        return pltpu.VMEM((count, columns), dtype)

    to_first, to_second, states = gather_rows(even, states, fine_send_lo, fine_send_hi)
    first, second = exchange(to_first, to_second)

    (
        counts, columns, columns_t, coarse_columns, coarse_columns_t, cotangent, matrices, sends,
        coarse_sends, owner,
    ) = call(
        functools.partial(prepare_kernel, halo_rows=halo_rows, coarse_halo=coarse_halo),
        [
            shape(2 * count_rows, features, bf16),
            shape(8, rows, f32),
            shape(rows, 8, f32),
            shape(8, coarse_rows, f32),
            shape(coarse_rows, 8, f32),
            shape(rows, features, bf16),
            shape(7 * features, features, bf16),
            shape(1, 2 * halo_rows, jnp.int32),
            shape(1, 2 * coarse_halo, jnp.int32),
            shape(rows // 128, 128, jnp.int32),
        ],
        [
            even, cotangent, owner, fine_nbr.T, fine_mask.T, coarse_nbr.T, coarse_mask.T,
            fine_send_lo[None], fine_send_hi[None], coarse_send_lo[None], coarse_send_hi[None],
            fine_self, fine_other, fine_node, coarse_self, coarse_other, coarse_node, prolong,
            to_first,
        ],
        [SMEM] + [HBM] * 17 + [ANY],
        [buffer(8, rows, jnp.int32)] * 2
        + [buffer(8, coarse_rows, jnp.int32)] * 2
        + [buffer(1, halo_rows, jnp.int32)] * 2
        + [buffer(1, coarse_halo, jnp.int32)] * 2
        + [pltpu.SemaphoreType.DMA((17,))],
    )

    summed, slope, totals = call(
        fine_forward_kernel,
        [
            shape(rows, features, bf16),
            shape(8 * rows, features, bf16),
            shape(coarse_rows + 2 * count_rows, features, bf16),
        ],
        [states, first, second, matrices, columns_t, owner, counts],
        scratch=[
            buffer(rows, features, f32),
            buffer(rows, features, bf16),
            buffer(2 * halo_rows, features, bf16),
            buffer(rows, features, bf16),
        ],
    )
    chip_totals = (totals.astype(f32) + swapped(totals, "grp", 1).astype(f32)).astype(bf16)
    more_totals = swapped(chip_totals, "grp", 2)
    sums = call(
        sums_kernel,
        shape(coarse_rows, features, bf16),
        [owner, cotangent, totals],
        [VMEM, VMEM, ANY],
    )
    more_sums = swapped(sums, "grp", 1)
    owners_t = call(owners_kernel, shape(rows, 8, f32), [owner, chip_totals], [VMEM, ANY])

    coarse_in, to_first, to_second, chip_sums, counts = call(
        coarse_input_kernel,
        [
            shape(coarse_rows, features, bf16),
            shape(coarse_halo, features, bf16),
            shape(coarse_halo, features, bf16),
            shape(coarse_rows, features, bf16),
            shape(count_rows, features, f32),
        ],
        [chip_totals, more_totals, sums, more_sums, coarse_sends, owners_t],
        [VMEM] * 5 + [ANY],
    )
    coarse_first, coarse_second = exchange(to_first, to_second)
    more_sums = swapped(chip_sums, "grp", 2)

    coarse_part, first_grad, second_grad, sums, coarse_sum, coarse_ups, coarse_downs = call(
        coarse_kernel,
        [
            shape(coarse_rows, features, f32),
            shape(coarse_halo, features, bf16),
            shape(coarse_halo, features, bf16),
            shape(coarse_rows, features, bf16),
            shape(coarse_rows, features, bf16),
            shape(coarse_rows, features, bf16),
            shape(coarse_rows, 2 * features, bf16),
        ],
        [
            coarse_in, coarse_first, coarse_second, chip_sums, more_sums, matrices,
            coarse_columns, coarse_columns_t,
        ],
        scratch=[
            buffer(coarse_rows, features, f32),
            buffer(coarse_rows, features, bf16),
            buffer(2 * coarse_halo, features, bf16),
            buffer(coarse_rows, features, bf16),
            buffer(2 * coarse_halo, features, f32),
        ],
    )
    first_back, second_back = exchange(first_grad, second_grad)

    fine_term, coarse_weights = call(
        coarse_tail_kernel,
        [shape(coarse_rows, features, bf16), shape(features, features, bf16)],
        [
            group, coarse_in, coarse_first, coarse_second, sums, matrices,
            first_grad, second_grad, coarse_sum, coarse_ups, coarse_downs,
        ],
        [SMEM] + [VMEM] * 10,
    )
    result = call(
        result_kernel,
        pltpu.HBM((rows, features), bf16),
        [states, summed, matrices, owners_t, fine_term],
        scratch=[buffer(rows, features, bf16), pltpu.SemaphoreType.DMA],
        out_specs=HBM,
    )

    ups, downs, first_grad, second_grad, weights = call(
        fine_backward_kernel,
        [
            pltpu.HBM((rows, features), bf16),
            pltpu.HBM((rows, 2 * features), bf16),
            shape(halo_rows, features, bf16),
            shape(halo_rows, features, bf16),
            shape(4 * features, features, bf16),
        ],
        [
            states, first, second, cotangent, summed, slope, matrices, columns, owners_t,
            coarse_part, counts, coarse_downs, first_back, second_back, coarse_sends,
            coarse_weights,
        ],
        scratch=[
            buffer(rows, features, bf16),
            buffer(rows, 2 * features, bf16),
            buffer(rows, features, bf16),
            buffer(2 * halo_rows, features, f32),
            buffer(coarse_rows, features, bf16),
            pltpu.SemaphoreType.DMA((2,)),
        ],
        out_specs=[HBM, HBM, VMEM, VMEM, VMEM],
    )
    first_back, second_back = exchange(first_grad, second_grad)

    grad_states = call(
        finish_kernel,
        pltpu.HBM((rows, features), bf16),
        [ups, downs, first_back, second_back, sends, matrices],
        [HBM, HBM] + [VMEM] * 4,
        [
            buffer(rows, features, bf16),
            buffer(rows, 2 * features, bf16),
            buffer(rows, features, bf16),
            pltpu.SemaphoreType.DMA((rows // CHUNK,)),
            pltpu.SemaphoreType.DMA((rows // CHUNK,)),
            pltpu.SemaphoreType.DMA,
        ],
        out_specs=HBM,
    )
    grad_weights = total_weights(weights, group, ((), (result,), (grad_states,)))
    return (result, grad_states, grad_weights.reshape(7, features, features))


def solution(mesh):
    fine = P(("grp", "sub"), None)
    fine_row = P(("grp", "sub"))
    in_specs = (
        (fine, fine)
        + (P(),) * 7
        + (fine, fine, fine_row, fine_row)
        + (P("sub", None), P("sub", None), P("sub"), P("sub"), fine_row)
    )
    return jax.shard_map(
        per_device, mesh=mesh, in_specs=in_specs, out_specs=(fine, fine, P()), check_vma=False
    )
```

```python
import functools

import jax
import jax.numpy as jnp
from jax import lax
from jax.experimental import pallas as pl
from jax.experimental.pallas import tpu as pltpu
from jax.sharding import PartitionSpec as P

f32 = jnp.float32
bf16 = jnp.bfloat16
BLOCK = 64
PAIR = 2 * BLOCK
STEP = 16
CHUNK = 1024
NEVER = -1e30
DIGIT = 64.0
VMEM = pl.BlockSpec(memory_space=pltpu.VMEM)
SMEM = pl.BlockSpec(memory_space=pltpu.SMEM)
ANY = pl.BlockSpec(memory_space=pl.ANY)
HBM = pl.BlockSpec(memory_space=pltpu.HBM)
MIB = 1024 * 1024


def dot(a, b):
    return jnp.dot(a, b, preferred_element_type=f32)


def dot_nt(a, b):
    return lax.dot_general(a, b, (((1,), (1,)), ((), ())), preferred_element_type=f32)


def dot_tn(a, b):
    return lax.dot_general(a, b, (((0,), (0,)), ((), ())), preferred_element_type=f32)


def pick(condition):
    return jnp.where(condition, 1.0, 0.0).astype(bf16)


def pick16(values, places):
    return jnp.where(values == places, jnp.ones((), bf16), jnp.zeros((), bf16))


def call(kernel, out_shape, args, in_specs=None, scratch=(), out_specs=None, mib=16):
    many = isinstance(out_shape, (list, tuple))
    in_specs = in_specs or [VMEM] * len(args)
    args = [
        pltpu.with_memory_space_constraint(arg, pltpu.HBM) if spec is HBM else arg
        for arg, spec in zip(args, in_specs)
    ]
    return pl.pallas_call(
        kernel,
        out_shape=out_shape,
        in_specs=in_specs,
        out_specs=out_specs or ([VMEM] * len(out_shape) if many else VMEM),
        scratch_shapes=list(scratch),
        compiler_params=pltpu.CompilerParams(vmem_limit_bytes=mib * MIB),
    )(*args)


def shape(rows, columns, dtype):
    return jax.ShapeDtypeStruct((rows, columns), dtype)


def slot_columns(nbr, mask, halo_rows, even):
    rows = nbr.shape[1]
    block = lax.broadcasted_iota(jnp.int32, nbr.shape, 1) // BLOCK
    halo = lax.rem(block, halo_rows // BLOCK) * BLOCK
    lower = jnp.where(even, 2 * BLOCK, BLOCK)
    column = jnp.where(
        nbr < rows,
        nbr - block * BLOCK,
        jnp.where(
            nbr < rows + halo_rows,
            lower + nbr - rows - halo,
            3 * BLOCK - lower + nbr - rows - halo_rows - halo,
        ),
    )
    return jnp.where(mask > 0, column, 3 * BLOCK).astype(f32)


def selector(columns_t):
    first = lax.broadcasted_iota(jnp.int32, (BLOCK, 128), 1).astype(bf16)
    second = (lax.broadcasted_iota(jnp.int32, (BLOCK, 128), 1) + 128).astype(bf16)
    parts = []
    for k in range(8):
        wide = jnp.broadcast_to(columns_t[:, k : k + 1], (BLOCK, 128)).astype(bf16)
        parts.append(jnp.concatenate([pick16(wide, first), pick16(wide, second)], 1))
    return jnp.concatenate(parts, 0)


def selector_t(columns, rolled, half):
    lane = lax.broadcasted_iota(jnp.int32, (1, 128), 1)
    place = lax.broadcasted_iota(jnp.int32, (3 * BLOCK, 128), 0).astype(bf16)
    parts = []
    for j in range(4):
        left, right = (columns, rolled) if half == 0 else (rolled, columns)
        row = jnp.where(lane < BLOCK, left[2 * j : 2 * j + 1], right[2 * j + 1 : 2 * j + 2])
        wide = jnp.broadcast_to(row, (3 * BLOCK, 128)).astype(bf16)
        parts.append(pick16(wide, place))
    return jnp.concatenate(parts, 1)


def window_of(far, halo, place):
    halo_rows = halo.shape[0] // 2
    start = place * BLOCK
    return jnp.concatenate(
        [
            far,
            halo[start : start + BLOCK, :],
            halo[halo_rows + start : halo_rows + start + BLOCK, :],
            jnp.full((BLOCK, far.shape[1]), NEVER, bf16),
        ],
        0,
    )


def chunk_of(index, count):
    return pl.ds(pl.multiple_of(index * count, count), count)


def matrix(weights_ref, n):
    return weights_ref[128 * n : 128 * (n + 1), :]


def level_terms(h_ref, halo_refs, self_weight, other_weight, own, far, halo):
    halo_rows = halo_refs[0].shape[0]
    other = other_weight * 0.5
    h = h_ref[...]
    own[...] = dot(h, self_weight * 0.5)
    far[...] = dot(h, other).astype(bf16)
    halo[:halo_rows, :] = dot(halo_refs[0][...], other).astype(bf16)
    halo[halo_rows:, :] = dot(halo_refs[1][...], other).astype(bf16)


def edges(own_rows, far_rows, slots, halo):
    places = halo.shape[0] // (2 * BLOCK)
    assert STEP % places == 0
    tables = []
    for n in range(STEP):
        part = slice(n * BLOCK, (n + 1) * BLOCK)
        window = window_of(far_rows[part], halo, n % places)
        tables.append(dot(selector(slots[part]), window))
    sums, slopes = [], []
    for n, picked in enumerate(tables):
        own = own_rows[n * BLOCK : (n + 1) * BLOCK]
        values, pieces = [], []
        for k in range(8):
            y = (picked[k * BLOCK : (k + 1) * BLOCK] + own).astype(bf16)
            t = jnp.tanh(y)
            bent = y * t
            values.append(y + bent)
            pieces.append((1 + t) * (1 + (y - bent)))
        while len(values) > 1:
            values = [left + right for left, right in zip(values[::2], values[1::2])]
        sums.append(values[0])
        slopes.append(jnp.concatenate(pieces, 0))
    return jnp.concatenate(sums, 0), slopes


def edges_back(slopes, grad_sum, columns, halo_grad):
    places = halo_grad.shape[0] // (2 * BLOCK)
    halo_rows = halo_grad.shape[0] // 2
    windows, downs = [], []
    for n, slope in enumerate(slopes):
        part = grad_sum[n * BLOCK : (n + 1) * BLOCK]
        grads = [slope[k * BLOCK : (k + 1) * BLOCK] * part for k in range(8)]
        downs.append(sum(grad.astype(f32) for grad in grads))
        mine = columns[:, n // 2 * PAIR : (n // 2 + 1) * PAIR]
        selected = selector_t(mine, pltpu.roll(mine, BLOCK, 1), n % 2)
        windows.append(dot(selected, jnp.concatenate(grads, 0)))
    for place in range(places):
        for side in range(2):
            start = side * halo_rows + place * BLOCK
            total = halo_grad[start : start + BLOCK, :]
            for window in windows[place::places]:
                total = total + window[(side + 1) * BLOCK : (side + 2) * BLOCK]
            halo_grad[start : start + BLOCK, :] = total
    local = jnp.concatenate([window[:BLOCK] for window in windows], 0)
    down = jnp.concatenate(downs, 0)
    return jnp.concatenate([down, local], 1).astype(bf16)


def fetch(pairs, sems):
    copies = [pltpu.make_async_copy(src, dst, sems.at[n]) for n, (src, dst) in enumerate(pairs)]
    for copy in copies:
        copy.start()
    for copy in copies:
        copy.wait()


def gather_kernel(
    even_ref, lo_hbm, hi_hbm, x_hbm, first_ref, second_ref, x_ref, wide, up, down, lo, hi, sems
):
    fetch([(x_hbm, x_ref), (lo_hbm, lo), (hi_hbm, hi)], sems)
    wide[...] = x_ref[...].astype(f32)

    def step(r, carry):
        up[pl.ds(r, 1), :] = wide[pl.ds(hi[r], 1), :]
        down[pl.ds(r, 1), :] = wide[pl.ds(lo[r], 1), :]
        return carry

    lax.fori_loop(0, up.shape[0], step, None, unroll=16)
    even = even_ref[0] > 0
    first_ref[...] = jnp.where(even, up[...], down[...]).astype(bf16)
    second_ref[...] = jnp.where(even, down[...], up[...]).astype(bf16)


def gather_rows(even, x, send_lo, send_hi):
    rows, features = x.shape
    count = send_lo.shape[0]
    out = shape(count, features, bf16)
    return call(
        gather_kernel,
        [out, out, shape(rows, features, bf16)],
        [even, send_lo, send_hi, x],
        [SMEM, HBM, HBM, HBM],
        [
            pltpu.VMEM((rows, features), f32),
            pltpu.VMEM((count, features), f32),
            pltpu.VMEM((count, features), f32),
            pltpu.SMEM((count,), jnp.int32),
            pltpu.SMEM((count,), jnp.int32),
            pltpu.SemaphoreType.DMA((3,)),
        ],
    )


def owner_sums(owner_ref, tile, values):
    place = lax.broadcasted_iota(jnp.int32, (256, 128), 0).astype(bf16)
    owner = (owner_ref[...] - tile * 256).astype(f32)
    rows = jnp.concatenate(
        [
            pick16(jnp.broadcast_to(owner[q : q + 1], (256, 128)).astype(bf16), place)
            for q in range(owner.shape[0])
        ],
        1,
    )
    return dot(rows, values)


def prepare_kernel(
    even_ref,
    g_hbm,
    owner_hbm,
    nbr_hbm,
    mask_hbm,
    coarse_nbr_hbm,
    coarse_mask_hbm,
    lo_hbm,
    hi_hbm,
    coarse_lo_hbm,
    coarse_hi_hbm,
    *rest,
    halo_rows,
    coarse_halo,
):
    weight_hbms, rest = rest[:7], rest[7:]
    (
        after_ref,
        counts_ref,
        columns_ref,
        columns_t_ref,
        coarse_columns_ref,
        coarse_columns_t_ref,
        g_ref,
        weights_ref,
        sends_ref,
        coarse_sends_ref,
        owner_ref,
        nbr_ref,
        mask_ref,
        coarse_nbr_ref,
        coarse_mask_ref,
        lo_ref,
        hi_ref,
        coarse_lo_ref,
        coarse_hi_ref,
        sems,
    ) = rest
    fetch(
        [
            (g_hbm, g_ref),
            (owner_hbm, owner_ref),
            (nbr_hbm, nbr_ref),
            (mask_hbm, mask_ref),
            (coarse_nbr_hbm, coarse_nbr_ref),
            (coarse_mask_hbm, coarse_mask_ref),
            (lo_hbm, lo_ref),
            (hi_hbm, hi_ref),
            (coarse_lo_hbm, coarse_lo_ref),
            (coarse_hi_hbm, coarse_hi_ref),
        ]
        + [(w, weights_ref.at[pl.ds(128 * n, 128), :]) for n, w in enumerate(weight_hbms)],
        sems,
    )
    even = even_ref[0] > 0
    for low, high, out in (
        (lo_ref, hi_ref, sends_ref),
        (coarse_lo_ref, coarse_hi_ref, coarse_sends_ref),
    ):
        first = jnp.where(even, high[...], low[...])
        second = jnp.where(even, low[...], high[...])
        out[...] = jnp.concatenate([first, second], 1)
    columns_ref[...] = slot_columns(nbr_ref[...], mask_ref[...], halo_rows, even)
    columns_t_ref[...] = columns_ref[...].T
    coarse_columns_ref[...] = slot_columns(
        coarse_nbr_ref[...], coarse_mask_ref[...], coarse_halo, even
    )
    coarse_columns_t_ref[...] = coarse_columns_ref[...].T
    tiles = counts_ref.shape[0] // 2
    owner = owner_ref[...]
    high, low = owner // 128, lax.rem(owner, 128)
    groups = owner.shape[0]
    place = lax.broadcasted_iota(jnp.int32, (128, 128), 0)
    high_rows = jnp.concatenate(
        [pick(high[q : q + 1, :] == place[:tiles]) for q in range(groups)], 1
    )
    low_rows = jnp.concatenate(
        [pick(low[q : q + 1, :] == place) for q in range(groups)], 1
    )
    counts = dot_nt(high_rows, low_rows)
    most = jnp.floor(counts * (1 / DIGIT))
    counts_ref[...] = jnp.concatenate([most, counts - DIGIT * most], 0).astype(bf16)


def sums_kernel(owner_ref, g_ref, after_ref, sums_ref):
    def step(tile, carry):
        sums_ref[chunk_of(tile, 256), :] = owner_sums(owner_ref, tile, g_ref[...]).astype(bf16)
        return carry

    lax.fori_loop(0, sums_ref.shape[0] // 256, step, None)


def owners_kernel(owner_ref, after_ref, owners_ref):
    owners_ref[...] = owner_columns(owner_ref)


def fine_forward_kernel(
    h_ref,
    first_ref,
    second_ref,
    weights_ref,
    columns_t_ref,
    owner_ref,
    counts_ref,
    summed_ref,
    slope_hbm,
    totals_ref,
    own,
    far,
    halo,
    new,
    slope_ref,
    sem,
):
    self_weight, other_weight = matrix(weights_ref, 0), matrix(weights_ref, 1)
    level_terms(h_ref, (first_ref, second_ref), self_weight, other_weight, own, far, halo)

    def step(index, carry):
        here = chunk_of(index, STEP * BLOCK)
        total, slopes = edges(own[here, :], far[here, :], columns_t_ref[here, :], halo)
        summed_ref[here, :] = total
        edge = chunk_of(index, 8 * STEP * BLOCK)
        slope_ref[edge, :] = jnp.concatenate(slopes, 0)
        pltpu.make_async_copy(slope_ref.at[edge, :], slope_hbm.at[edge, :], sem).start()
        return carry

    lax.fori_loop(0, h_ref.shape[0] // (STEP * BLOCK), step, None)
    new[...] = (
        h_ref[...].astype(f32) + dot(summed_ref[...], matrix(weights_ref, 2))
    ).astype(bf16)
    coarse_rows = totals_ref.shape[0] - counts_ref.shape[0]

    def tile_step(tile, carry):
        totals_ref[chunk_of(tile, 256), :] = owner_sums(owner_ref, tile, new[...]).astype(bf16)
        return carry

    lax.fori_loop(0, coarse_rows // 256, tile_step, None)
    totals_ref[coarse_rows:, :] = counts_ref[...]
    pltpu.make_async_copy(slope_ref, slope_hbm, sem).wait()


def coarse_input_kernel(
    totals_ref,
    more_totals_ref,
    sums_ref,
    more_sums_ref,
    sends_ref,
    after_ref,
    cin_ref,
    first_ref,
    second_ref,
    chip_sums_ref,
    counts_ref,
):
    coarse_rows = cin_ref.shape[0]
    tiles = coarse_rows // 128
    chip_sums_ref[...] = (sums_ref[...].astype(f32) + more_sums_ref[...].astype(f32)).astype(bf16)
    totals = totals_ref[...].astype(f32) + more_totals_ref[...].astype(f32)
    digits = totals[coarse_rows:]
    counts_ref[...] = DIGIT * digits[:tiles] + digits[tiles:]
    per_row = counts_ref[...].T
    for tile in range(tiles):
        here = slice(tile * 128, (tile + 1) * 128)
        cin_ref[here, :] = (totals[here] / per_row[:, tile : tile + 1]).astype(bf16)
    cin = cin_ref[...]
    place = lax.broadcasted_iota(jnp.int32, (coarse_rows, sends_ref.shape[1]), 0)
    sent = dot_tn(pick(sends_ref[...] == place), cin).astype(bf16)
    halo_rows = first_ref.shape[0]
    first_ref[...] = sent[:halo_rows]
    second_ref[...] = sent[halo_rows:]


def coarse_kernel(
    cin_ref,
    first_ref,
    second_ref,
    chip_sums_ref,
    more_sums_ref,
    weights_ref,
    columns_ref,
    columns_t_ref,
    part_ref,
    first_grad_ref,
    second_grad_ref,
    sums_ref,
    summed_ref,
    ups_ref,
    downs_ref,
    own,
    far,
    halo,
    grad_sum,
    halo_grad,
):
    halo_rows = first_ref.shape[0]
    self_weight, other_weight = matrix(weights_ref, 3), matrix(weights_ref, 4)
    level_terms(cin_ref, (first_ref, second_ref), self_weight, other_weight, own, far, halo)
    halo_grad[...] = jnp.zeros_like(halo_grad)
    sums_ref[...] = (chip_sums_ref[...].astype(f32) + more_sums_ref[...].astype(f32)).astype(bf16)
    part_ref[...] = dot_nt(sums_ref[...], matrix(weights_ref, 6))
    ups_ref[...] = part_ref[...].astype(bf16)
    grad_sum[...] = (dot_nt(ups_ref[...], matrix(weights_ref, 5)) * 0.5).astype(bf16)

    def step(index, carry):
        here = chunk_of(index, STEP * BLOCK)
        total, slopes = edges(own[here, :], far[here, :], columns_t_ref[here, :], halo)
        summed_ref[here, :] = total
        downs_ref[here, :] = edges_back(
            slopes, grad_sum[here, :], columns_ref[:, here], halo_grad
        )
        return carry

    lax.fori_loop(0, cin_ref.shape[0] // (STEP * BLOCK), step, None)
    first_grad_ref[...] = halo_grad[:halo_rows, :].astype(bf16)
    second_grad_ref[...] = halo_grad[halo_rows:, :].astype(bf16)


def coarse_tail_kernel(
    group_ref,
    cin_ref,
    first_ref,
    second_ref,
    sums_ref,
    matrices_ref,
    first_grad_ref,
    second_grad_ref,
    summed_ref,
    ups_ref,
    downs_ref,
    fine_ref,
    weights_ref,
):
    cin = cin_ref[...]
    out = (cin.astype(f32) + dot(summed_ref[...], matrix(matrices_ref, 5))).astype(bf16)
    fine_ref[...] = dot(out, matrix(matrices_ref, 6)).astype(bf16)
    pair_grad = dot_tn(cin, downs_ref[...])
    other_grad = (
        pair_grad[:, 128:]
        + dot_tn(first_ref[...], first_grad_ref[...])
        + dot_tn(second_ref[...], second_grad_ref[...])
    )
    grads = [
        pair_grad[:, :128],
        other_grad,
        dot_tn(summed_ref[...], ups_ref[...]),
        dot_tn(out, sums_ref[...]),
    ]
    weights_ref[...] = choose(group_ref[0], grads).astype(bf16)


def choose(place, values):
    picked = values[-1]
    for n, value in enumerate(values[:-1]):
        picked = jnp.where(place == n, value, picked)
    return picked


def owner_columns(owner_ref):
    owner = owner_ref[...].astype(f32)
    row = jnp.concatenate([owner[q : q + 1, :] for q in range(owner.shape[0])], 1)
    return jnp.broadcast_to(row, (8, row.shape[1])).T


def owner_rows(owners, values):
    count = owners.shape[0]
    wide = jnp.broadcast_to(owners[:, 0:1], (count, 128))
    lane = lax.broadcasted_iota(jnp.int32, (count, 128), 1)
    first, second = lane.astype(bf16), (lane + 128).astype(bf16)
    rows = []
    for tile in range(values.shape[0] // 256):
        here = (wide - 256.0 * tile).astype(bf16)
        rows += [pick16(here, first), pick16(here, second)]
    return dot(jnp.concatenate(rows, 1), values)


def result_kernel(h_ref, summed_ref, weights_ref, owners_ref, fine_ref, out_hbm, out_ref, sem):
    def step(index, carry):
        here = chunk_of(index, CHUNK)
        updated = h_ref[here, :].astype(f32) + dot(summed_ref[here, :], matrix(weights_ref, 2))
        out_ref[here, :] = (updated + owner_rows(owners_ref[here, :], fine_ref[...])).astype(bf16)
        pltpu.make_async_copy(out_ref.at[here, :], out_hbm.at[here, :], sem).start()
        return carry

    lax.fori_loop(0, h_ref.shape[0] // CHUNK, step, None)
    pltpu.make_async_copy(out_ref, out_hbm, sem).wait()


def fine_backward_kernel(
    h_ref,
    first_ref,
    second_ref,
    g_ref,
    summed_ref,
    slope_hbm,
    matrices_ref,
    columns_ref,
    owners_ref,
    part_ref,
    counts_ref,
    coarse_downs_ref,
    first_back_ref,
    second_back_ref,
    sends_ref,
    coarse_weights_ref,
    ups_hbm,
    downs_hbm,
    first_grad_ref,
    second_grad_ref,
    weights_ref,
    ups_ref,
    downs_ref,
    grad_sum,
    halo_grad,
    mean,
    slope_ref,
    slope_sems,
    sems,
):
    count = STEP * BLOCK
    steps = h_ref.shape[0] // count

    def slope_copy(index):
        edge = chunk_of(index, 8 * count)
        return pltpu.make_async_copy(
            slope_hbm.at[edge, :], slope_ref.at[edge, :], slope_sems.at[index]
        )

    for index in range(steps):
        slope_copy(index).start()
    halo_rows = first_ref.shape[0]
    coarse_rows = part_ref.shape[0]
    halo_grad[...] = jnp.zeros_like(halo_grad)

    place = lax.broadcasted_iota(jnp.int32, (coarse_rows, sends_ref.shape[1]), 0)
    sends = pick(sends_ref[...] == place)
    back = jnp.concatenate([first_back_ref[...], second_back_ref[...]], 0)
    back = dot_nt(back, matrix(matrices_ref, 4)).astype(bf16)
    plain = jnp.concatenate([matrix(matrices_ref, 3), matrix(matrices_ref, 4)], 1)
    grad_in = part_ref[...] + dot_nt(coarse_downs_ref[...], plain) + dot(sends, back)
    per_row = counts_ref[...].T
    for tile in range(coarse_rows // 128):
        here = slice(tile * 128, (tile + 1) * 128)
        mean[here, :] = (grad_in[here, :] / per_row[:, tile : tile + 1]).astype(bf16)

    def owner_step(index):
        here = chunk_of(index, count)
        grad_up = g_ref[here, :].astype(f32) + owner_rows(owners_ref[here, :], mean[...])
        ups = grad_up.astype(bf16)
        ups_ref[here, :] = ups
        grad_sum[here, :] = (dot_nt(ups, matrix(matrices_ref, 2)) * 0.5).astype(bf16)

    def edge_step(index):
        here = chunk_of(index, count)
        slope_copy(index).wait()
        slope = slope_ref[chunk_of(index, 8 * count), :]
        slopes = [slope[n * 8 * BLOCK : (n + 1) * 8 * BLOCK] for n in range(STEP)]
        downs_ref[here, :] = edges_back(
            slopes, grad_sum[here, :], columns_ref[:, here], halo_grad
        )

    owner_step(0)

    def step(index, carry):
        edge_step(index)
        owner_step(index + 1)
        return carry

    lax.fori_loop(0, steps - 1, step, None)
    edge_step(steps - 1)
    copies = [
        pltpu.make_async_copy(ups_ref, ups_hbm, sems.at[0]),
        pltpu.make_async_copy(downs_ref, downs_hbm, sems.at[1]),
    ]
    for copy in copies:
        copy.start()
    first_grad = halo_grad[:halo_rows, :].astype(bf16)
    second_grad = halo_grad[halo_rows:, :].astype(bf16)
    first_grad_ref[...] = first_grad
    second_grad_ref[...] = second_grad
    pair_grad = dot_tn(h_ref[...], downs_ref[...])
    weights_ref[0:128, :] = pair_grad[:, :128].astype(bf16)
    weights_ref[128:256, :] = (
        pair_grad[:, 128:]
        + dot_tn(first_ref[...], first_grad)
        + dot_tn(second_ref[...], second_grad)
    ).astype(bf16)
    weights_ref[256:384, :] = dot_tn(summed_ref[...], ups_ref[...]).astype(bf16)
    weights_ref[384:512, :] = coarse_weights_ref[...]
    for copy in copies:
        copy.wait()


def finish_kernel(
    ups_hbm,
    downs_hbm,
    first_back_ref,
    second_back_ref,
    sends_ref,
    matrices_ref,
    out_hbm,
    ups_ref,
    downs_ref,
    out_ref,
    ups_sems,
    downs_sems,
    out_sem,
):
    chunks = ups_ref.shape[0] // CHUNK

    def copies(index):
        here = chunk_of(index, CHUNK)
        return (
            pltpu.make_async_copy(ups_hbm.at[here, :], ups_ref.at[here, :], ups_sems.at[index]),
            pltpu.make_async_copy(
                downs_hbm.at[here, :], downs_ref.at[here, :], downs_sems.at[index]
            ),
        )

    for index in range(chunks):
        for copy in copies(index):
            copy.start()
    other = matrix(matrices_ref, 1)
    plain = jnp.concatenate([matrix(matrices_ref, 0), other], 1)
    back = jnp.concatenate([first_back_ref[...], second_back_ref[...]], 0)
    back = dot_nt(back, other).astype(bf16)
    sends = sends_ref[...]
    place = lax.broadcasted_iota(jnp.int32, (256, sends.shape[1]), 0).astype(bf16)

    def step(index, carry):
        here = chunk_of(index, CHUNK)
        rows = []
        for part in range(CHUNK // 256):
            local = (sends - (index * CHUNK + 256 * part)).astype(f32)
            rows.append(pick16(jnp.broadcast_to(local, place.shape).astype(bf16), place))
        spread = dot(jnp.concatenate(rows, 0), back)
        for copy in copies(index):
            copy.wait()
        grad = ups_ref[here, :].astype(f32) + dot_nt(downs_ref[here, :], plain)
        out_ref[here, :] = (grad + spread).astype(bf16)
        pltpu.make_async_copy(out_ref.at[here, :], out_hbm.at[here, :], out_sem).start()
        return carry

    lax.fori_loop(0, chunks, step, None)
    pltpu.make_async_copy(out_ref, out_hbm, out_sem).wait()


def add_kernel(mine_ref, theirs_ref, *rest):
    out_ref = rest[-1]
    out_ref[...] = (mine_ref[...].astype(f32) + theirs_ref[...].astype(f32)).astype(bf16)


def add_gather_kernel(mine_ref, theirs_ref, out_ref):
    mine, theirs = mine_ref[...].astype(f32), theirs_ref[...].astype(f32)
    out_ref[:384, :] = mine[:384] + theirs[:384]
    out_ref[384:512, :] = mine[384:]
    out_ref[512:, :] = theirs[384:]


def weights_kernel(group_ref, mine_ref, theirs_ref, out_ref):
    out_ref[:384, :] = mine_ref[:384, :] + theirs_ref[:384, :]
    group = group_ref[0]
    low, high = lax.rem(group, 2), group // 2
    for n in range(4):
        row = jnp.where(high == n // 2, 384, 512)
        here = pl.ds(pl.multiple_of(row, 128), 128)
        value = jnp.where(low == n % 2, mine_ref[here, :], theirs_ref[here, :])
        out_ref[384 + 128 * n : 512 + 128 * n, :] = value


def exchange(first, second):
    count = lax.axis_size("sub")
    routes = []
    for start in range(2):
        pairs = [(i, i + 1) for i in range(start, count - 1, 2)]
        routes.append(pairs + [(j, i) for i, j in pairs])
    return lax.ppermute(first, "sub", routes[0]), lax.ppermute(second, "sub", routes[1])


def swapped(block, axis, distance):
    return lax.ppermute(block, axis, [(i, i ^ distance) for i in range(lax.axis_size(axis))])


def total_weights(weights, group, after):
    distance, number = 1, 0
    while distance < lax.axis_size("sub"):
        theirs = swapped(weights, "sub", distance)
        waits = after[number] if number < len(after) else ()
        weights = call(
            add_kernel,
            shape(*weights.shape, bf16),
            [weights, theirs, *waits],
            [VMEM, VMEM] + [HBM] * len(waits),
        )
        distance, number = 2 * distance, number + 1
    weights = call(
        add_gather_kernel,
        shape(640, 128, f32),
        [weights, swapped(weights, "grp", 2)],
    )
    return call(
        weights_kernel,
        shape(896, 128, f32),
        [group, weights, swapped(weights, "grp", 1)],
        [SMEM, VMEM, VMEM],
    )


def per_device(
    states,
    cotangent,
    fine_self,
    fine_other,
    fine_node,
    coarse_self,
    coarse_other,
    coarse_node,
    prolong,
    fine_nbr,
    fine_mask,
    fine_send_lo,
    fine_send_hi,
    coarse_nbr,
    coarse_mask,
    coarse_send_lo,
    coarse_send_hi,
    coarse_owner,
):
    rows, features = states.shape
    coarse_rows = coarse_nbr.shape[0]
    halo_rows = fine_send_lo.shape[0]
    coarse_halo = coarse_send_lo.shape[0]
    count_rows = coarse_rows // 128
    owner = coarse_owner.reshape(rows // 128, 128)
    even = (1 - lax.rem(lax.axis_index("sub"), 2)).astype(jnp.int32).reshape(1)
    group = lax.axis_index("grp").astype(jnp.int32).reshape(1)

    def buffer(count, columns, dtype):
        return pltpu.VMEM((count, columns), dtype)

    to_first, to_second, states = gather_rows(even, states, fine_send_lo, fine_send_hi)
    first, second = exchange(to_first, to_second)

    (
        counts, columns, columns_t, coarse_columns, coarse_columns_t, cotangent, matrices, sends,
        coarse_sends, owner,
    ) = call(
        functools.partial(prepare_kernel, halo_rows=halo_rows, coarse_halo=coarse_halo),
        [
            shape(2 * count_rows, features, bf16),
            shape(8, rows, f32),
            shape(rows, 8, f32),
            shape(8, coarse_rows, f32),
            shape(coarse_rows, 8, f32),
            shape(rows, features, bf16),
            shape(7 * features, features, bf16),
            shape(1, 2 * halo_rows, jnp.int32),
            shape(1, 2 * coarse_halo, jnp.int32),
            shape(rows // 128, 128, jnp.int32),
        ],
        [
            even, cotangent, owner, fine_nbr.T, fine_mask.T, coarse_nbr.T, coarse_mask.T,
            fine_send_lo[None], fine_send_hi[None], coarse_send_lo[None], coarse_send_hi[None],
            fine_self, fine_other, fine_node, coarse_self, coarse_other, coarse_node, prolong,
            to_first,
        ],
        [SMEM] + [HBM] * 17 + [ANY],
        [buffer(8, rows, jnp.int32)] * 2
        + [buffer(8, coarse_rows, jnp.int32)] * 2
        + [buffer(1, halo_rows, jnp.int32)] * 2
        + [buffer(1, coarse_halo, jnp.int32)] * 2
        + [pltpu.SemaphoreType.DMA((17,))],
    )

    summed, slope, totals = call(
        fine_forward_kernel,
        [
            shape(rows, features, bf16),
            pltpu.HBM((8 * rows, features), bf16),
            shape(coarse_rows + 2 * count_rows, features, bf16),
        ],
        [states, first, second, matrices, columns_t, owner, counts],
        scratch=[
            buffer(rows, features, f32),
            buffer(rows, features, bf16),
            buffer(2 * halo_rows, features, bf16),
            buffer(rows, features, bf16),
            buffer(8 * rows, features, bf16),
            pltpu.SemaphoreType.DMA,
        ],
        out_specs=[VMEM, HBM, VMEM],
        mib=32,
    )
    chip_totals = (totals.astype(f32) + swapped(totals, "grp", 1).astype(f32)).astype(bf16)
    more_totals = swapped(chip_totals, "grp", 2)
    sums = call(
        sums_kernel,
        shape(coarse_rows, features, bf16),
        [owner, cotangent, totals],
        [VMEM, VMEM, ANY],
    )
    more_sums = swapped(sums, "grp", 1)
    owners_t = call(owners_kernel, shape(rows, 8, f32), [owner, chip_totals], [VMEM, ANY])

    coarse_in, to_first, to_second, chip_sums, counts = call(
        coarse_input_kernel,
        [
            shape(coarse_rows, features, bf16),
            shape(coarse_halo, features, bf16),
            shape(coarse_halo, features, bf16),
            shape(coarse_rows, features, bf16),
            shape(count_rows, features, f32),
        ],
        [chip_totals, more_totals, sums, more_sums, coarse_sends, owners_t],
        [VMEM] * 5 + [ANY],
    )
    coarse_first, coarse_second = exchange(to_first, to_second)
    more_sums = swapped(chip_sums, "grp", 2)

    coarse_part, first_grad, second_grad, sums, coarse_sum, coarse_ups, coarse_downs = call(
        coarse_kernel,
        [
            shape(coarse_rows, features, f32),
            shape(coarse_halo, features, bf16),
            shape(coarse_halo, features, bf16),
            shape(coarse_rows, features, bf16),
            shape(coarse_rows, features, bf16),
            shape(coarse_rows, features, bf16),
            shape(coarse_rows, 2 * features, bf16),
        ],
        [
            coarse_in, coarse_first, coarse_second, chip_sums, more_sums, matrices,
            coarse_columns, coarse_columns_t,
        ],
        scratch=[
            buffer(coarse_rows, features, f32),
            buffer(coarse_rows, features, bf16),
            buffer(2 * coarse_halo, features, bf16),
            buffer(coarse_rows, features, bf16),
            buffer(2 * coarse_halo, features, f32),
        ],
    )
    first_back, second_back = exchange(first_grad, second_grad)

    fine_term, coarse_weights = call(
        coarse_tail_kernel,
        [shape(coarse_rows, features, bf16), shape(features, features, bf16)],
        [
            group, coarse_in, coarse_first, coarse_second, sums, matrices,
            first_grad, second_grad, coarse_sum, coarse_ups, coarse_downs,
        ],
        [SMEM] + [VMEM] * 10,
    )
    result = call(
        result_kernel,
        pltpu.HBM((rows, features), bf16),
        [states, summed, matrices, owners_t, fine_term],
        scratch=[buffer(rows, features, bf16), pltpu.SemaphoreType.DMA],
        out_specs=HBM,
    )

    ups, downs, first_grad, second_grad, weights = call(
        fine_backward_kernel,
        [
            pltpu.HBM((rows, features), bf16),
            pltpu.HBM((rows, 2 * features), bf16),
            shape(halo_rows, features, bf16),
            shape(halo_rows, features, bf16),
            shape(4 * features, features, bf16),
        ],
        [
            states, first, second, cotangent, summed, slope, matrices, columns, owners_t,
            coarse_part, counts, coarse_downs, first_back, second_back, coarse_sends,
            coarse_weights,
        ],
        [VMEM] * 5 + [HBM] + [VMEM] * 10,
        [
            buffer(rows, features, bf16),
            buffer(rows, 2 * features, bf16),
            buffer(rows, features, bf16),
            buffer(2 * halo_rows, features, f32),
            buffer(coarse_rows, features, bf16),
            buffer(8 * rows, features, bf16),
            pltpu.SemaphoreType.DMA((rows // (STEP * BLOCK),)),
            pltpu.SemaphoreType.DMA((2,)),
        ],
        out_specs=[HBM, HBM, VMEM, VMEM, VMEM],
        mib=32,
    )
    first_back, second_back = exchange(first_grad, second_grad)

    grad_states = call(
        finish_kernel,
        pltpu.HBM((rows, features), bf16),
        [ups, downs, first_back, second_back, sends, matrices],
        [HBM, HBM] + [VMEM] * 4,
        [
            buffer(rows, features, bf16),
            buffer(rows, 2 * features, bf16),
            buffer(rows, features, bf16),
            pltpu.SemaphoreType.DMA((rows // CHUNK,)),
            pltpu.SemaphoreType.DMA((rows // CHUNK,)),
            pltpu.SemaphoreType.DMA,
        ],
        out_specs=HBM,
    )
    grad_weights = total_weights(weights, group, ((), (result,), (grad_states,)))
    return (result, grad_states, grad_weights.reshape(7, features, features))


def solution(mesh):
    fine = P(("grp", "sub"), None)
    fine_row = P(("grp", "sub"))
    in_specs = (
        (fine, fine)
        + (P(),) * 7
        + (fine, fine, fine_row, fine_row)
        + (P("sub", None), P("sub", None), P("sub"), P("sub"), fine_row)
    )
    return jax.shard_map(
        per_device, mesh=mesh, in_specs=in_specs, out_specs=(fine, fine, P()), check_vma=False
    )
```

```python
import functools

import jax
import jax.numpy as jnp
from jax import lax
from jax.experimental import pallas as pl
from jax.experimental.pallas import tpu as pltpu
from jax.sharding import PartitionSpec as P

f32 = jnp.float32
bf16 = jnp.bfloat16
BLOCK = 64
PAIR = 2 * BLOCK
STEP = 16
CHUNK = 1024
NEVER = -1e30
DIGIT = 64.0
VMEM = pl.BlockSpec(memory_space=pltpu.VMEM)
SMEM = pl.BlockSpec(memory_space=pltpu.SMEM)
ANY = pl.BlockSpec(memory_space=pl.ANY)
HBM = pl.BlockSpec(memory_space=pltpu.HBM)
MIB = 1024 * 1024


def dot(a, b):
    return jnp.dot(a, b, preferred_element_type=f32)


def dot_nt(a, b):
    return lax.dot_general(a, b, (((1,), (1,)), ((), ())), preferred_element_type=f32)


def dot_tn(a, b):
    return lax.dot_general(a, b, (((0,), (0,)), ((), ())), preferred_element_type=f32)


def pick(condition):
    return jnp.where(condition, 1.0, 0.0).astype(bf16)


def pick16(values, places):
    return jnp.where(values == places, jnp.ones((), bf16), jnp.zeros((), bf16))


def call(kernel, out_shape, args, in_specs=None, scratch=(), out_specs=None, mib=16):
    many = isinstance(out_shape, (list, tuple))
    in_specs = in_specs or [VMEM] * len(args)
    args = [
        pltpu.with_memory_space_constraint(arg, pltpu.HBM) if spec is HBM else arg
        for arg, spec in zip(args, in_specs)
    ]
    return pl.pallas_call(
        kernel,
        out_shape=out_shape,
        in_specs=in_specs,
        out_specs=out_specs or ([VMEM] * len(out_shape) if many else VMEM),
        scratch_shapes=list(scratch),
        compiler_params=pltpu.CompilerParams(vmem_limit_bytes=mib * MIB),
    )(*args)


def shape(rows, columns, dtype):
    return jax.ShapeDtypeStruct((rows, columns), dtype)


def slot_columns(nbr, mask, halo_rows, even):
    rows = nbr.shape[1]
    block = lax.broadcasted_iota(jnp.int32, nbr.shape, 1) // BLOCK
    halo = lax.rem(block, halo_rows // BLOCK) * BLOCK
    lower = jnp.where(even, 2 * BLOCK, BLOCK)
    column = jnp.where(
        nbr < rows,
        nbr - block * BLOCK,
        jnp.where(
            nbr < rows + halo_rows,
            lower + nbr - rows - halo,
            3 * BLOCK - lower + nbr - rows - halo_rows - halo,
        ),
    )
    return jnp.where(mask > 0, column, 3 * BLOCK).astype(f32)


def selector(columns_t):
    first = lax.broadcasted_iota(jnp.int32, (BLOCK, 128), 1).astype(bf16)
    second = (lax.broadcasted_iota(jnp.int32, (BLOCK, 128), 1) + 128).astype(bf16)
    parts = []
    for k in range(8):
        wide = jnp.broadcast_to(columns_t[:, k : k + 1], (BLOCK, 128)).astype(bf16)
        parts.append(jnp.concatenate([pick16(wide, first), pick16(wide, second)], 1))
    return jnp.concatenate(parts, 0)


def selector_t(columns, rolled, half):
    lane = lax.broadcasted_iota(jnp.int32, (1, 128), 1)
    place = lax.broadcasted_iota(jnp.int32, (3 * BLOCK, 128), 0).astype(bf16)
    parts = []
    for j in range(4):
        left, right = (columns, rolled) if half == 0 else (rolled, columns)
        row = jnp.where(lane < BLOCK, left[2 * j : 2 * j + 1], right[2 * j + 1 : 2 * j + 2])
        wide = jnp.broadcast_to(row, (3 * BLOCK, 128)).astype(bf16)
        parts.append(pick16(wide, place))
    return jnp.concatenate(parts, 1)


def window_of(far, halo, place):
    halo_rows = halo.shape[0] // 2
    start = place * BLOCK
    return jnp.concatenate(
        [
            far,
            halo[start : start + BLOCK, :],
            halo[halo_rows + start : halo_rows + start + BLOCK, :],
            jnp.full((BLOCK, far.shape[1]), NEVER, bf16),
        ],
        0,
    )


def chunk_of(index, count):
    return pl.ds(pl.multiple_of(index * count, count), count)


def matrix(weights_ref, n):
    return weights_ref[128 * n : 128 * (n + 1), :]


def level_terms(h_ref, halo_refs, self_weight, other_weight, own, far, halo):
    halo_rows = halo_refs[0].shape[0]
    other = other_weight * 0.5
    h = h_ref[...]
    own[...] = dot(h, self_weight * 0.5)
    far[...] = dot(h, other).astype(bf16)
    halo[:halo_rows, :] = dot(halo_refs[0][...], other).astype(bf16)
    halo[halo_rows:, :] = dot(halo_refs[1][...], other).astype(bf16)


def edges(own_rows, far_rows, slots, halo):
    places = halo.shape[0] // (2 * BLOCK)
    assert STEP % places == 0
    tables = []
    for n in range(STEP):
        part = slice(n * BLOCK, (n + 1) * BLOCK)
        window = window_of(far_rows[part], halo, n % places)
        tables.append(dot(selector(slots[part]), window))
    sums, slopes = [], []
    for n, picked in enumerate(tables):
        own = own_rows[n * BLOCK : (n + 1) * BLOCK]
        values, pieces = [], []
        for k in range(8):
            y = (picked[k * BLOCK : (k + 1) * BLOCK] + own).astype(bf16)
            t = jnp.tanh(y)
            bent = y * t
            values.append(y + bent)
            pieces.append((1 + t) * (1 + (y - bent)))
        while len(values) > 1:
            values = [left + right for left, right in zip(values[::2], values[1::2])]
        sums.append(values[0])
        slopes.append(jnp.concatenate(pieces, 0))
    return jnp.concatenate(sums, 0), slopes


def edges_back(slopes, grad_sum, columns, halo_grad):
    places = halo_grad.shape[0] // (2 * BLOCK)
    halo_rows = halo_grad.shape[0] // 2
    windows, downs = [], []
    for n, slope in enumerate(slopes):
        part = grad_sum[n * BLOCK : (n + 1) * BLOCK]
        grads = [slope[k * BLOCK : (k + 1) * BLOCK] * part for k in range(8)]
        downs.append(sum(grad.astype(f32) for grad in grads))
        mine = columns[:, n // 2 * PAIR : (n // 2 + 1) * PAIR]
        selected = selector_t(mine, pltpu.roll(mine, BLOCK, 1), n % 2)
        windows.append(dot(selected, jnp.concatenate(grads, 0)))
    for place in range(places):
        for side in range(2):
            start = side * halo_rows + place * BLOCK
            total = halo_grad[start : start + BLOCK, :]
            for window in windows[place::places]:
                total = total + window[(side + 1) * BLOCK : (side + 2) * BLOCK]
            halo_grad[start : start + BLOCK, :] = total
    local = jnp.concatenate([window[:BLOCK] for window in windows], 0)
    down = jnp.concatenate(downs, 0)
    return jnp.concatenate([down, local], 1).astype(bf16)


def fetch(pairs, sems):
    copies = [pltpu.make_async_copy(src, dst, sems.at[n]) for n, (src, dst) in enumerate(pairs)]
    for copy in copies:
        copy.start()
    for copy in copies:
        copy.wait()


def gather_kernel(
    place_ref, lo_hbm, hi_hbm, x_hbm, first_ref, second_ref, x_ref, wide, up, down, lo, hi, sems
):
    fetch([(x_hbm, x_ref), (lo_hbm, lo), (hi_hbm, hi)], sems)
    wide[...] = x_ref[...].astype(f32)

    def step(r, carry):
        up[pl.ds(r, 1), :] = wide[pl.ds(hi[r], 1), :]
        down[pl.ds(r, 1), :] = wide[pl.ds(lo[r], 1), :]
        return carry

    lax.fori_loop(0, up.shape[0], step, None, unroll=16)
    even = place_ref[0] > 0
    first_ref[...] = jnp.where(even, up[...], down[...]).astype(bf16)
    second_ref[...] = jnp.where(even, down[...], up[...]).astype(bf16)


def gather_rows(place, x, send_lo, send_hi):
    rows, features = x.shape
    count = send_lo.shape[0]
    out = shape(count, features, bf16)
    return call(
        gather_kernel,
        [out, out, shape(rows, features, bf16)],
        [place, send_lo, send_hi, x],
        [SMEM, HBM, HBM, HBM],
        [
            pltpu.VMEM((rows, features), f32),
            pltpu.VMEM((count, features), f32),
            pltpu.VMEM((count, features), f32),
            pltpu.SMEM((count,), jnp.int32),
            pltpu.SMEM((count,), jnp.int32),
            pltpu.SemaphoreType.DMA((3,)),
        ],
    )


def owner_sums(owner_ref, tile, values):
    place = lax.broadcasted_iota(jnp.int32, (256, 128), 0).astype(bf16)
    owner = (owner_ref[...] - tile * 256).astype(f32)
    rows = jnp.concatenate(
        [
            pick16(jnp.broadcast_to(owner[q : q + 1], (256, 128)).astype(bf16), place)
            for q in range(owner.shape[0])
        ],
        1,
    )
    return dot(rows, values)


def prepare_kernel(
    place_ref,
    g_hbm,
    owner_hbm,
    nbr_hbm,
    mask_hbm,
    coarse_nbr_hbm,
    coarse_mask_hbm,
    lo_hbm,
    hi_hbm,
    coarse_lo_hbm,
    coarse_hi_hbm,
    *rest,
    halo_rows,
    coarse_halo,
):
    weight_hbms, rest = rest[:7], rest[7:]
    (
        after_ref,
        counts_ref,
        columns_ref,
        columns_t_ref,
        coarse_columns_ref,
        coarse_columns_t_ref,
        g_ref,
        weights_ref,
        sends_ref,
        coarse_sends_ref,
        owner_ref,
        nbr_ref,
        mask_ref,
        coarse_nbr_ref,
        coarse_mask_ref,
        lo_ref,
        hi_ref,
        coarse_lo_ref,
        coarse_hi_ref,
        sems,
    ) = rest
    fetch(
        [
            (g_hbm, g_ref),
            (owner_hbm, owner_ref),
            (nbr_hbm, nbr_ref),
            (mask_hbm, mask_ref),
            (coarse_nbr_hbm, coarse_nbr_ref),
            (coarse_mask_hbm, coarse_mask_ref),
            (lo_hbm, lo_ref),
            (hi_hbm, hi_ref),
            (coarse_lo_hbm, coarse_lo_ref),
            (coarse_hi_hbm, coarse_hi_ref),
        ]
        + [(w, weights_ref.at[pl.ds(128 * n, 128), :]) for n, w in enumerate(weight_hbms)],
        sems,
    )
    even = place_ref[0] > 0
    for low, high, out in (
        (lo_ref, hi_ref, sends_ref),
        (coarse_lo_ref, coarse_hi_ref, coarse_sends_ref),
    ):
        first = jnp.where(even, high[...], low[...])
        second = jnp.where(even, low[...], high[...])
        out[...] = jnp.concatenate([first, second], 1)
    columns_ref[...] = slot_columns(nbr_ref[...], mask_ref[...], halo_rows, even)
    columns_t_ref[...] = columns_ref[...].T
    coarse_columns_ref[...] = slot_columns(
        coarse_nbr_ref[...], coarse_mask_ref[...], coarse_halo, even
    )
    coarse_columns_t_ref[...] = coarse_columns_ref[...].T
    tiles = counts_ref.shape[0] // 2
    owner = owner_ref[...]
    high, low = owner // 128, lax.rem(owner, 128)
    groups = owner.shape[0]
    place = lax.broadcasted_iota(jnp.int32, (128, 128), 0)
    high_rows = jnp.concatenate(
        [pick(high[q : q + 1, :] == place[:tiles]) for q in range(groups)], 1
    )
    low_rows = jnp.concatenate(
        [pick(low[q : q + 1, :] == place) for q in range(groups)], 1
    )
    counts = dot_nt(high_rows, low_rows)
    most = jnp.floor(counts * (1 / DIGIT))
    counts_ref[...] = jnp.concatenate([most, counts - DIGIT * most], 0).astype(bf16)


def sums_kernel(owner_ref, g_ref, after_ref, sums_ref):
    def step(tile, carry):
        sums_ref[chunk_of(tile, 256), :] = owner_sums(owner_ref, tile, g_ref[...]).astype(bf16)
        return carry

    lax.fori_loop(0, sums_ref.shape[0] // 256, step, None)


def owners_kernel(owner_ref, after_ref, owners_ref):
    owners_ref[...] = owner_columns(owner_ref)


def fine_forward_kernel(
    h_ref,
    first_ref,
    second_ref,
    weights_ref,
    columns_t_ref,
    owner_ref,
    counts_ref,
    summed_ref,
    slope_hbm,
    totals_ref,
    own,
    far,
    halo,
    new,
    slope_ref,
    sem,
):
    self_weight, other_weight = matrix(weights_ref, 0), matrix(weights_ref, 1)
    level_terms(h_ref, (first_ref, second_ref), self_weight, other_weight, own, far, halo)

    def step(index, carry):
        here = chunk_of(index, STEP * BLOCK)
        total, slopes = edges(own[here, :], far[here, :], columns_t_ref[here, :], halo)
        summed_ref[here, :] = total
        edge = chunk_of(index, 8 * STEP * BLOCK)
        slope_ref[edge, :] = jnp.concatenate(slopes, 0)
        pltpu.make_async_copy(slope_ref.at[edge, :], slope_hbm.at[edge, :], sem).start()
        return carry

    lax.fori_loop(0, h_ref.shape[0] // (STEP * BLOCK), step, None)
    new[...] = (
        h_ref[...].astype(f32) + dot(summed_ref[...], matrix(weights_ref, 2))
    ).astype(bf16)
    coarse_rows = totals_ref.shape[0] - counts_ref.shape[0]

    def tile_step(tile, carry):
        totals_ref[chunk_of(tile, 256), :] = owner_sums(owner_ref, tile, new[...]).astype(bf16)
        return carry

    lax.fori_loop(0, coarse_rows // 256, tile_step, None)
    totals_ref[coarse_rows:, :] = counts_ref[...]
    pltpu.make_async_copy(slope_ref, slope_hbm, sem).wait()


def coarse_input_kernel(
    totals_ref,
    more_totals_ref,
    sums_ref,
    more_sums_ref,
    sends_ref,
    after_ref,
    cin_ref,
    first_ref,
    second_ref,
    chip_sums_ref,
    counts_ref,
):
    coarse_rows = cin_ref.shape[0]
    tiles = coarse_rows // 128
    chip_sums_ref[...] = (sums_ref[...].astype(f32) + more_sums_ref[...].astype(f32)).astype(bf16)
    totals = totals_ref[...].astype(f32) + more_totals_ref[...].astype(f32)
    digits = totals[coarse_rows:]
    counts_ref[...] = DIGIT * digits[:tiles] + digits[tiles:]
    per_row = counts_ref[...].T
    for tile in range(tiles):
        here = slice(tile * 128, (tile + 1) * 128)
        cin_ref[here, :] = (totals[here] / per_row[:, tile : tile + 1]).astype(bf16)
    cin = cin_ref[...]
    place = lax.broadcasted_iota(jnp.int32, (coarse_rows, sends_ref.shape[1]), 0)
    sent = dot_tn(pick(sends_ref[...] == place), cin).astype(bf16)
    halo_rows = first_ref.shape[0]
    first_ref[...] = sent[:halo_rows]
    second_ref[...] = sent[halo_rows:]


def coarse_kernel(
    cin_ref,
    first_ref,
    second_ref,
    chip_sums_ref,
    more_sums_ref,
    weights_ref,
    columns_ref,
    columns_t_ref,
    part_ref,
    first_grad_ref,
    second_grad_ref,
    sums_ref,
    summed_ref,
    ups_ref,
    downs_ref,
    own,
    far,
    halo,
    grad_sum,
    halo_grad,
):
    halo_rows = first_ref.shape[0]
    self_weight, other_weight = matrix(weights_ref, 3), matrix(weights_ref, 4)
    level_terms(cin_ref, (first_ref, second_ref), self_weight, other_weight, own, far, halo)
    halo_grad[...] = jnp.zeros_like(halo_grad)
    sums_ref[...] = (chip_sums_ref[...].astype(f32) + more_sums_ref[...].astype(f32)).astype(bf16)
    part_ref[...] = dot_nt(sums_ref[...], matrix(weights_ref, 6))
    ups_ref[...] = part_ref[...].astype(bf16)
    grad_sum[...] = (dot_nt(ups_ref[...], matrix(weights_ref, 5)) * 0.5).astype(bf16)

    def step(index, carry):
        here = chunk_of(index, STEP * BLOCK)
        total, slopes = edges(own[here, :], far[here, :], columns_t_ref[here, :], halo)
        summed_ref[here, :] = total
        downs_ref[here, :] = edges_back(
            slopes, grad_sum[here, :], columns_ref[:, here], halo_grad
        )
        return carry

    lax.fori_loop(0, cin_ref.shape[0] // (STEP * BLOCK), step, None)
    first_grad_ref[...] = halo_grad[:halo_rows, :].astype(bf16)
    second_grad_ref[...] = halo_grad[halo_rows:, :].astype(bf16)


def coarse_tail_kernel(
    place_ref,
    cin_ref,
    first_ref,
    second_ref,
    sums_ref,
    matrices_ref,
    first_grad_ref,
    second_grad_ref,
    summed_ref,
    ups_ref,
    downs_ref,
    fine_ref,
    weights_ref,
):
    cin = cin_ref[...]
    out = (cin.astype(f32) + dot(summed_ref[...], matrix(matrices_ref, 5))).astype(bf16)
    fine_ref[...] = dot(out, matrix(matrices_ref, 6)).astype(bf16)
    pair_grad = dot_tn(cin, downs_ref[...])
    other_grad = (
        pair_grad[:, 128:]
        + dot_tn(first_ref[...], first_grad_ref[...])
        + dot_tn(second_ref[...], second_grad_ref[...])
    )
    grads = [
        pair_grad[:, :128],
        other_grad,
        dot_tn(summed_ref[...], ups_ref[...]),
        dot_tn(out, sums_ref[...]),
    ]
    weights_ref[...] = choose(place_ref[1], grads).astype(bf16)


def choose(place, values):
    picked = values[-1]
    for n, value in enumerate(values[:-1]):
        picked = jnp.where(place == n, value, picked)
    return picked


def owner_columns(owner_ref):
    owner = owner_ref[...].astype(f32)
    row = jnp.concatenate([owner[q : q + 1, :] for q in range(owner.shape[0])], 1)
    return jnp.broadcast_to(row, (8, row.shape[1])).T


def owner_rows(owners, values):
    count = owners.shape[0]
    wide = jnp.broadcast_to(owners[:, 0:1], (count, 128))
    lane = lax.broadcasted_iota(jnp.int32, (count, 128), 1)
    first, second = lane.astype(bf16), (lane + 128).astype(bf16)
    rows = []
    for tile in range(values.shape[0] // 256):
        here = (wide - 256.0 * tile).astype(bf16)
        rows += [pick16(here, first), pick16(here, second)]
    return dot(jnp.concatenate(rows, 1), values)


def result_kernel(h_ref, summed_ref, weights_ref, owners_ref, fine_ref, out_hbm, out_ref, sem):
    def step(index, carry):
        here = chunk_of(index, CHUNK)
        updated = h_ref[here, :].astype(f32) + dot(summed_ref[here, :], matrix(weights_ref, 2))
        out_ref[here, :] = (updated + owner_rows(owners_ref[here, :], fine_ref[...])).astype(bf16)
        pltpu.make_async_copy(out_ref.at[here, :], out_hbm.at[here, :], sem).start()
        return carry

    lax.fori_loop(0, h_ref.shape[0] // CHUNK, step, None)
    pltpu.make_async_copy(out_ref, out_hbm, sem).wait()


def fine_backward_kernel(
    h_ref,
    first_ref,
    second_ref,
    g_ref,
    summed_ref,
    slope_hbm,
    matrices_ref,
    columns_ref,
    owners_ref,
    part_ref,
    counts_ref,
    coarse_downs_ref,
    first_back_ref,
    second_back_ref,
    sends_ref,
    coarse_weights_ref,
    ups_hbm,
    downs_hbm,
    first_grad_ref,
    second_grad_ref,
    weights_ref,
    ups_ref,
    downs_ref,
    grad_sum,
    halo_grad,
    mean,
    slope_ref,
    slope_sems,
    sems,
):
    count = STEP * BLOCK
    steps = h_ref.shape[0] // count

    def slope_copy(index):
        edge = chunk_of(index, 8 * count)
        return pltpu.make_async_copy(
            slope_hbm.at[edge, :], slope_ref.at[edge, :], slope_sems.at[index]
        )

    for index in range(steps):
        slope_copy(index).start()
    halo_rows = first_ref.shape[0]
    coarse_rows = part_ref.shape[0]
    halo_grad[...] = jnp.zeros_like(halo_grad)

    place = lax.broadcasted_iota(jnp.int32, (coarse_rows, sends_ref.shape[1]), 0)
    sends = pick(sends_ref[...] == place)
    back = jnp.concatenate([first_back_ref[...], second_back_ref[...]], 0)
    back = dot_nt(back, matrix(matrices_ref, 4)).astype(bf16)
    plain = jnp.concatenate([matrix(matrices_ref, 3), matrix(matrices_ref, 4)], 1)
    grad_in = part_ref[...] + dot_nt(coarse_downs_ref[...], plain) + dot(sends, back)
    per_row = counts_ref[...].T
    for tile in range(coarse_rows // 128):
        here = slice(tile * 128, (tile + 1) * 128)
        mean[here, :] = (grad_in[here, :] / per_row[:, tile : tile + 1]).astype(bf16)

    def owner_step(index):
        here = chunk_of(index, count)
        grad_up = g_ref[here, :].astype(f32) + owner_rows(owners_ref[here, :], mean[...])
        ups = grad_up.astype(bf16)
        ups_ref[here, :] = ups
        grad_sum[here, :] = (dot_nt(ups, matrix(matrices_ref, 2)) * 0.5).astype(bf16)

    def edge_step(index):
        here = chunk_of(index, count)
        slope_copy(index).wait()
        slope = slope_ref[chunk_of(index, 8 * count), :]
        slopes = [slope[n * 8 * BLOCK : (n + 1) * 8 * BLOCK] for n in range(STEP)]
        downs_ref[here, :] = edges_back(
            slopes, grad_sum[here, :], columns_ref[:, here], halo_grad
        )

    owner_step(0)

    def step(index, carry):
        edge_step(index)
        owner_step(index + 1)
        return carry

    lax.fori_loop(0, steps - 1, step, None)
    edge_step(steps - 1)
    copies = [
        pltpu.make_async_copy(ups_ref, ups_hbm, sems.at[0]),
        pltpu.make_async_copy(downs_ref, downs_hbm, sems.at[1]),
    ]
    for copy in copies:
        copy.start()
    first_grad = halo_grad[:halo_rows, :].astype(bf16)
    second_grad = halo_grad[halo_rows:, :].astype(bf16)
    first_grad_ref[...] = first_grad
    second_grad_ref[...] = second_grad
    pair_grad = dot_tn(h_ref[...], downs_ref[...])
    weights_ref[0:128, :] = pair_grad[:, :128].astype(bf16)
    weights_ref[128:256, :] = (
        pair_grad[:, 128:]
        + dot_tn(first_ref[...], first_grad)
        + dot_tn(second_ref[...], second_grad)
    ).astype(bf16)
    weights_ref[256:384, :] = dot_tn(summed_ref[...], ups_ref[...]).astype(bf16)
    weights_ref[384:512, :] = coarse_weights_ref[...]
    for copy in copies:
        copy.wait()


def finish_kernel(
    ups_hbm,
    downs_hbm,
    first_back_ref,
    second_back_ref,
    sends_ref,
    matrices_ref,
    out_hbm,
    ups_ref,
    downs_ref,
    out_ref,
    ups_sems,
    downs_sems,
    out_sem,
):
    chunks = ups_ref.shape[0] // CHUNK

    def copies(index):
        here = chunk_of(index, CHUNK)
        return (
            pltpu.make_async_copy(ups_hbm.at[here, :], ups_ref.at[here, :], ups_sems.at[index]),
            pltpu.make_async_copy(
                downs_hbm.at[here, :], downs_ref.at[here, :], downs_sems.at[index]
            ),
        )

    for index in range(chunks):
        for copy in copies(index):
            copy.start()
    other = matrix(matrices_ref, 1)
    plain = jnp.concatenate([matrix(matrices_ref, 0), other], 1)
    back = jnp.concatenate([first_back_ref[...], second_back_ref[...]], 0)
    back = dot_nt(back, other).astype(bf16)
    sends = sends_ref[...]
    place = lax.broadcasted_iota(jnp.int32, (256, sends.shape[1]), 0).astype(bf16)

    def step(index, carry):
        here = chunk_of(index, CHUNK)
        rows = []
        for part in range(CHUNK // 256):
            local = (sends - (index * CHUNK + 256 * part)).astype(f32)
            rows.append(pick16(jnp.broadcast_to(local, place.shape).astype(bf16), place))
        spread = dot(jnp.concatenate(rows, 0), back)
        for copy in copies(index):
            copy.wait()
        grad = ups_ref[here, :].astype(f32) + dot_nt(downs_ref[here, :], plain)
        out_ref[here, :] = (grad + spread).astype(bf16)
        pltpu.make_async_copy(out_ref.at[here, :], out_hbm.at[here, :], out_sem).start()
        return carry

    lax.fori_loop(0, chunks, step, None)
    pltpu.make_async_copy(out_ref, out_hbm, out_sem).wait()


def add_kernel(mine_ref, theirs_ref, *rest):
    out_ref = rest[-1]
    out_ref[...] = (mine_ref[...].astype(f32) + theirs_ref[...].astype(f32)).astype(bf16)


def add_gather_kernel(mine_ref, theirs_ref, out_ref):
    mine, theirs = mine_ref[...].astype(f32), theirs_ref[...].astype(f32)
    out_ref[:384, :] = mine[:384] + theirs[:384]
    out_ref[384:512, :] = mine[384:]
    out_ref[512:, :] = theirs[384:]


def weights_kernel(place_ref, mine_ref, theirs_ref, out_ref):
    out_ref[:384, :] = mine_ref[:384, :] + theirs_ref[:384, :]
    group = place_ref[1]
    low, high = lax.rem(group, 2), group // 2
    for n in range(4):
        row = jnp.where(high == n // 2, 384, 512)
        here = pl.ds(pl.multiple_of(row, 128), 128)
        value = jnp.where(low == n % 2, mine_ref[here, :], theirs_ref[here, :])
        out_ref[384 + 128 * n : 512 + 128 * n, :] = value


def exchange(first, second):
    count = lax.axis_size("sub")
    routes = []
    for start in range(2):
        pairs = [(i, i + 1) for i in range(start, count - 1, 2)]
        routes.append(pairs + [(j, i) for i, j in pairs])
    return lax.ppermute(first, "sub", routes[0]), lax.ppermute(second, "sub", routes[1])


def swapped(block, axis, distance):
    return lax.ppermute(block, axis, [(i, i ^ distance) for i in range(lax.axis_size(axis))])


def total_weights(weights, place, after):
    distance, number = 1, 0
    while distance < lax.axis_size("sub"):
        theirs = swapped(weights, "sub", distance)
        waits = after[number] if number < len(after) else ()
        weights = call(
            add_kernel,
            shape(*weights.shape, bf16),
            [weights, theirs, *waits],
            [VMEM, VMEM] + [HBM] * len(waits),
        )
        distance, number = 2 * distance, number + 1
    weights = call(
        add_gather_kernel,
        shape(640, 128, f32),
        [weights, swapped(weights, "grp", 2)],
    )
    return call(
        weights_kernel,
        shape(896, 128, f32),
        [place, weights, swapped(weights, "grp", 1)],
        [SMEM, VMEM, VMEM],
    )


def per_device(
    states,
    cotangent,
    fine_self,
    fine_other,
    fine_node,
    coarse_self,
    coarse_other,
    coarse_node,
    prolong,
    fine_nbr,
    fine_mask,
    fine_send_lo,
    fine_send_hi,
    coarse_nbr,
    coarse_mask,
    coarse_send_lo,
    coarse_send_hi,
    coarse_owner,
):
    rows, features = states.shape
    coarse_rows = coarse_nbr.shape[0]
    halo_rows = fine_send_lo.shape[0]
    coarse_halo = coarse_send_lo.shape[0]
    count_rows = coarse_rows // 128
    owner = coarse_owner.reshape(rows // 128, 128)
    place = jnp.stack([1 - lax.rem(lax.axis_index("sub"), 2), lax.axis_index("grp")])

    def buffer(count, columns, dtype):
        return pltpu.VMEM((count, columns), dtype)

    to_first, to_second, states = gather_rows(place, states, fine_send_lo, fine_send_hi)
    first, second = exchange(to_first, to_second)

    (
        counts, columns, columns_t, coarse_columns, coarse_columns_t, cotangent, matrices, sends,
        coarse_sends, owner,
    ) = call(
        functools.partial(prepare_kernel, halo_rows=halo_rows, coarse_halo=coarse_halo),
        [
            shape(2 * count_rows, features, bf16),
            shape(8, rows, f32),
            shape(rows, 8, f32),
            shape(8, coarse_rows, f32),
            shape(coarse_rows, 8, f32),
            shape(rows, features, bf16),
            shape(7 * features, features, bf16),
            shape(1, 2 * halo_rows, jnp.int32),
            shape(1, 2 * coarse_halo, jnp.int32),
            shape(rows // 128, 128, jnp.int32),
        ],
        [
            place, cotangent, owner, fine_nbr.T, fine_mask.T, coarse_nbr.T, coarse_mask.T,
            fine_send_lo[None], fine_send_hi[None], coarse_send_lo[None], coarse_send_hi[None],
            fine_self, fine_other, fine_node, coarse_self, coarse_other, coarse_node, prolong,
            to_first,
        ],
        [SMEM] + [HBM] * 17 + [ANY],
        [buffer(8, rows, jnp.int32)] * 2
        + [buffer(8, coarse_rows, jnp.int32)] * 2
        + [buffer(1, halo_rows, jnp.int32)] * 2
        + [buffer(1, coarse_halo, jnp.int32)] * 2
        + [pltpu.SemaphoreType.DMA((17,))],
    )

    summed, slope, totals = call(
        fine_forward_kernel,
        [
            shape(rows, features, bf16),
            pltpu.HBM((8 * rows, features), bf16),
            shape(coarse_rows + 2 * count_rows, features, bf16),
        ],
        [states, first, second, matrices, columns_t, owner, counts],
        scratch=[
            buffer(rows, features, f32),
            buffer(rows, features, bf16),
            buffer(2 * halo_rows, features, bf16),
            buffer(rows, features, bf16),
            buffer(8 * rows, features, bf16),
            pltpu.SemaphoreType.DMA,
        ],
        out_specs=[VMEM, HBM, VMEM],
        mib=32,
    )
    chip_totals = call(
        add_kernel, shape(*totals.shape, bf16), [totals, swapped(totals, "grp", 1)]
    )
    more_totals = swapped(chip_totals, "grp", 2)
    sums = call(
        sums_kernel,
        shape(coarse_rows, features, bf16),
        [owner, cotangent, totals],
        [VMEM, VMEM, ANY],
    )
    more_sums = swapped(sums, "grp", 1)
    owners_t = call(owners_kernel, shape(rows, 8, f32), [owner, chip_totals], [VMEM, ANY])

    coarse_in, to_first, to_second, chip_sums, counts = call(
        coarse_input_kernel,
        [
            shape(coarse_rows, features, bf16),
            shape(coarse_halo, features, bf16),
            shape(coarse_halo, features, bf16),
            shape(coarse_rows, features, bf16),
            shape(count_rows, features, f32),
        ],
        [chip_totals, more_totals, sums, more_sums, coarse_sends, owners_t],
        [VMEM] * 5 + [ANY],
    )
    coarse_first, coarse_second = exchange(to_first, to_second)
    more_sums = swapped(chip_sums, "grp", 2)

    coarse_part, first_grad, second_grad, sums, coarse_sum, coarse_ups, coarse_downs = call(
        coarse_kernel,
        [
            shape(coarse_rows, features, f32),
            shape(coarse_halo, features, bf16),
            shape(coarse_halo, features, bf16),
            shape(coarse_rows, features, bf16),
            shape(coarse_rows, features, bf16),
            shape(coarse_rows, features, bf16),
            shape(coarse_rows, 2 * features, bf16),
        ],
        [
            coarse_in, coarse_first, coarse_second, chip_sums, more_sums, matrices,
            coarse_columns, coarse_columns_t,
        ],
        scratch=[
            buffer(coarse_rows, features, f32),
            buffer(coarse_rows, features, bf16),
            buffer(2 * coarse_halo, features, bf16),
            buffer(coarse_rows, features, bf16),
            buffer(2 * coarse_halo, features, f32),
        ],
    )
    first_back, second_back = exchange(first_grad, second_grad)

    fine_term, coarse_weights = call(
        coarse_tail_kernel,
        [shape(coarse_rows, features, bf16), shape(features, features, bf16)],
        [
            place, coarse_in, coarse_first, coarse_second, sums, matrices,
            first_grad, second_grad, coarse_sum, coarse_ups, coarse_downs,
        ],
        [SMEM] + [VMEM] * 10,
    )
    result = call(
        result_kernel,
        pltpu.HBM((rows, features), bf16),
        [states, summed, matrices, owners_t, fine_term],
        scratch=[buffer(rows, features, bf16), pltpu.SemaphoreType.DMA],
        out_specs=HBM,
    )

    ups, downs, first_grad, second_grad, weights = call(
        fine_backward_kernel,
        [
            pltpu.HBM((rows, features), bf16),
            pltpu.HBM((rows, 2 * features), bf16),
            shape(halo_rows, features, bf16),
            shape(halo_rows, features, bf16),
            shape(4 * features, features, bf16),
        ],
        [
            states, first, second, cotangent, summed, slope, matrices, columns, owners_t,
            coarse_part, counts, coarse_downs, first_back, second_back, coarse_sends,
            coarse_weights,
        ],
        [VMEM] * 5 + [HBM] + [VMEM] * 10,
        [
            buffer(rows, features, bf16),
            buffer(rows, 2 * features, bf16),
            buffer(rows, features, bf16),
            buffer(2 * halo_rows, features, f32),
            buffer(coarse_rows, features, bf16),
            buffer(8 * rows, features, bf16),
            pltpu.SemaphoreType.DMA((rows // (STEP * BLOCK),)),
            pltpu.SemaphoreType.DMA((2,)),
        ],
        out_specs=[HBM, HBM, VMEM, VMEM, VMEM],
        mib=32,
    )
    first_back, second_back = exchange(first_grad, second_grad)

    grad_states = call(
        finish_kernel,
        pltpu.HBM((rows, features), bf16),
        [ups, downs, first_back, second_back, sends, matrices],
        [HBM, HBM] + [VMEM] * 4,
        [
            buffer(rows, features, bf16),
            buffer(rows, 2 * features, bf16),
            buffer(rows, features, bf16),
            pltpu.SemaphoreType.DMA((rows // CHUNK,)),
            pltpu.SemaphoreType.DMA((rows // CHUNK,)),
            pltpu.SemaphoreType.DMA,
        ],
        out_specs=HBM,
    )
    grad_weights = total_weights(weights, place, ((), (result,), (grad_states,)))
    return (result, grad_states, grad_weights.reshape(7, features, features))


def solution(mesh):
    fine = P(("grp", "sub"), None)
    fine_row = P(("grp", "sub"))
    in_specs = (
        (fine, fine)
        + (P(),) * 7
        + (fine, fine, fine_row, fine_row)
        + (P("sub", None), P("sub", None), P("sub"), P("sub"), fine_row)
    )
    return jax.shard_map(
        per_device, mesh=mesh, in_specs=in_specs, out_specs=(fine, fine, P()), check_vma=False
    )
```

```python
import functools

import jax
import jax.numpy as jnp
from jax import lax
from jax.experimental import pallas as pl
from jax.experimental.pallas import tpu as pltpu
from jax.sharding import PartitionSpec as P

f32 = jnp.float32
bf16 = jnp.bfloat16
BLOCK = 64
PAIR = 2 * BLOCK
STEP = 16
CHUNK = 1024
NEVER = -1e30
DIGIT = 64.0
VMEM = pl.BlockSpec(memory_space=pltpu.VMEM)
SMEM = pl.BlockSpec(memory_space=pltpu.SMEM)
ANY = pl.BlockSpec(memory_space=pl.ANY)
HBM = pl.BlockSpec(memory_space=pltpu.HBM)
MIB = 1024 * 1024


def dot(a, b):
    return jnp.dot(a, b, preferred_element_type=f32)


def dot_nt(a, b):
    return lax.dot_general(a, b, (((1,), (1,)), ((), ())), preferred_element_type=f32)


def dot_tn(a, b):
    return lax.dot_general(a, b, (((0,), (0,)), ((), ())), preferred_element_type=f32)


def pick(condition):
    return jnp.where(condition, 1.0, 0.0).astype(bf16)


def pick16(values, places):
    return jnp.where(values == places, jnp.ones((), bf16), jnp.zeros((), bf16))


def call(kernel, out_shape, args, in_specs=None, scratch=(), out_specs=None, mib=16):
    many = isinstance(out_shape, (list, tuple))
    in_specs = in_specs or [VMEM] * len(args)
    args = [
        pltpu.with_memory_space_constraint(arg, pltpu.HBM) if spec is HBM else arg
        for arg, spec in zip(args, in_specs)
    ]
    return pl.pallas_call(
        kernel,
        out_shape=out_shape,
        in_specs=in_specs,
        out_specs=out_specs or ([VMEM] * len(out_shape) if many else VMEM),
        scratch_shapes=list(scratch),
        compiler_params=pltpu.CompilerParams(vmem_limit_bytes=mib * MIB),
    )(*args)


def shape(rows, columns, dtype):
    return jax.ShapeDtypeStruct((rows, columns), dtype)


def slot_columns(nbr, mask, halo_rows, even):
    rows = nbr.shape[1]
    block = lax.broadcasted_iota(jnp.int32, nbr.shape, 1) // BLOCK
    halo = lax.rem(block, halo_rows // BLOCK) * BLOCK
    lower = jnp.where(even, 2 * BLOCK, BLOCK)
    column = jnp.where(
        nbr < rows,
        nbr - block * BLOCK,
        jnp.where(
            nbr < rows + halo_rows,
            lower + nbr - rows - halo,
            3 * BLOCK - lower + nbr - rows - halo_rows - halo,
        ),
    )
    return jnp.where(mask > 0, column, 3 * BLOCK).astype(f32)


def selector(columns_t):
    first = lax.broadcasted_iota(jnp.int32, (BLOCK, 128), 1).astype(bf16)
    second = (lax.broadcasted_iota(jnp.int32, (BLOCK, 128), 1) + 128).astype(bf16)
    parts = []
    for k in range(8):
        wide = jnp.broadcast_to(columns_t[:, k : k + 1], (BLOCK, 128)).astype(bf16)
        parts.append(jnp.concatenate([pick16(wide, first), pick16(wide, second)], 1))
    return jnp.concatenate(parts, 0)


def selector_t(columns, rolled, half):
    lane = lax.broadcasted_iota(jnp.int32, (1, 128), 1)
    place = lax.broadcasted_iota(jnp.int32, (3 * BLOCK, 128), 0).astype(bf16)
    parts = []
    for j in range(4):
        left, right = (columns, rolled) if half == 0 else (rolled, columns)
        row = jnp.where(lane < BLOCK, left[2 * j : 2 * j + 1], right[2 * j + 1 : 2 * j + 2])
        wide = jnp.broadcast_to(row, (3 * BLOCK, 128)).astype(bf16)
        parts.append(pick16(wide, place))
    return jnp.concatenate(parts, 1)


def window_of(far, halo, place):
    halo_rows = halo.shape[0] // 2
    start = place * BLOCK
    return jnp.concatenate(
        [
            far,
            halo[start : start + BLOCK, :],
            halo[halo_rows + start : halo_rows + start + BLOCK, :],
            jnp.full((BLOCK, far.shape[1]), NEVER, bf16),
        ],
        0,
    )


def chunk_of(index, count):
    return pl.ds(pl.multiple_of(index * count, count), count)


def matrix(weights_ref, n):
    return weights_ref[128 * n : 128 * (n + 1), :]


def level_terms(h_ref, halo_refs, self_weight, other_weight, own, far, halo):
    halo_rows = halo_refs[0].shape[0]
    other = other_weight * 0.5
    terms = dot(h_ref[...], jnp.concatenate([self_weight * 0.5, other], 1))
    own[...] = terms[:, :128]
    far[...] = terms[:, 128:].astype(bf16)
    halo[:halo_rows, :] = dot(halo_refs[0][...], other).astype(bf16)
    halo[halo_rows:, :] = dot(halo_refs[1][...], other).astype(bf16)


def edges(own_rows, far_rows, slots, halo):
    places = halo.shape[0] // (2 * BLOCK)
    assert STEP % places == 0
    tables = []
    for n in range(STEP):
        part = slice(n * BLOCK, (n + 1) * BLOCK)
        window = window_of(far_rows[part], halo, n % places)
        tables.append(dot(selector(slots[part]), window))
    sums, slopes = [], []
    for n, picked in enumerate(tables):
        own = own_rows[n * BLOCK : (n + 1) * BLOCK]
        values, pieces = [], []
        for k in range(8):
            y = (picked[k * BLOCK : (k + 1) * BLOCK] + own).astype(bf16)
            t = jnp.tanh(y)
            bent = y * t
            values.append(y + bent)
            pieces.append((1 + t) * (1 + (y - bent)))
        while len(values) > 1:
            values = [left + right for left, right in zip(values[::2], values[1::2])]
        sums.append(values[0])
        slopes.append(jnp.concatenate(pieces, 0))
    return jnp.concatenate(sums, 0), slopes


def edges_back(slopes, grad_sum, columns, halo_grad):
    places = halo_grad.shape[0] // (2 * BLOCK)
    halo_rows = halo_grad.shape[0] // 2
    windows, downs = [], []
    for n, slope in enumerate(slopes):
        part = grad_sum[n * BLOCK : (n + 1) * BLOCK]
        grads = [slope[k * BLOCK : (k + 1) * BLOCK] * part for k in range(8)]
        downs.append(sum(grad.astype(f32) for grad in grads))
        mine = columns[:, n // 2 * PAIR : (n // 2 + 1) * PAIR]
        selected = selector_t(mine, pltpu.roll(mine, BLOCK, 1), n % 2)
        windows.append(dot(selected, jnp.concatenate(grads, 0)))
    for place in range(places):
        for side in range(2):
            start = side * halo_rows + place * BLOCK
            total = halo_grad[start : start + BLOCK, :]
            for window in windows[place::places]:
                total = total + window[(side + 1) * BLOCK : (side + 2) * BLOCK]
            halo_grad[start : start + BLOCK, :] = total
    local = jnp.concatenate([window[:BLOCK] for window in windows], 0)
    down = jnp.concatenate(downs, 0)
    return jnp.concatenate([down, local], 1).astype(bf16)


def fetch(pairs, sems):
    copies = [pltpu.make_async_copy(src, dst, sems.at[n]) for n, (src, dst) in enumerate(pairs)]
    for copy in copies:
        copy.start()
    for copy in copies:
        copy.wait()


def gather_kernel(
    place_ref, lo_hbm, hi_hbm, x_hbm, first_ref, second_ref, x_ref, wide, up, down, lo, hi, sems
):
    fetch([(x_hbm, x_ref), (lo_hbm, lo), (hi_hbm, hi)], sems)
    wide[...] = x_ref[...].astype(f32)

    def step(r, carry):
        up[pl.ds(r, 1), :] = wide[pl.ds(hi[r], 1), :]
        down[pl.ds(r, 1), :] = wide[pl.ds(lo[r], 1), :]
        return carry

    lax.fori_loop(0, up.shape[0], step, None, unroll=16)
    even = place_ref[0] > 0
    first_ref[...] = jnp.where(even, up[...], down[...]).astype(bf16)
    second_ref[...] = jnp.where(even, down[...], up[...]).astype(bf16)


def gather_rows(place, x, send_lo, send_hi):
    rows, features = x.shape
    count = send_lo.shape[0]
    out = shape(count, features, bf16)
    return call(
        gather_kernel,
        [out, out, shape(rows, features, bf16)],
        [place, send_lo, send_hi, x],
        [SMEM, HBM, HBM, HBM],
        [
            pltpu.VMEM((rows, features), f32),
            pltpu.VMEM((count, features), f32),
            pltpu.VMEM((count, features), f32),
            pltpu.SMEM((count,), jnp.int32),
            pltpu.SMEM((count,), jnp.int32),
            pltpu.SemaphoreType.DMA((3,)),
        ],
    )


def owner_sums(owner_ref, tile, values):
    place = lax.broadcasted_iota(jnp.int32, (256, 128), 0).astype(bf16)
    owner = (owner_ref[...] - tile * 256).astype(f32)
    rows = jnp.concatenate(
        [
            pick16(jnp.broadcast_to(owner[q : q + 1], (256, 128)).astype(bf16), place)
            for q in range(owner.shape[0])
        ],
        1,
    )
    return dot(rows, values)


def prepare_kernel(
    place_ref,
    g_hbm,
    owner_hbm,
    nbr_hbm,
    mask_hbm,
    coarse_nbr_hbm,
    coarse_mask_hbm,
    lo_hbm,
    hi_hbm,
    coarse_lo_hbm,
    coarse_hi_hbm,
    *rest,
    halo_rows,
    coarse_halo,
):
    weight_hbms, rest = rest[:7], rest[7:]
    (
        after_ref,
        counts_ref,
        columns_ref,
        columns_t_ref,
        coarse_columns_ref,
        coarse_columns_t_ref,
        g_ref,
        weights_ref,
        sends_ref,
        coarse_sends_ref,
        owner_ref,
        nbr_ref,
        mask_ref,
        coarse_nbr_ref,
        coarse_mask_ref,
        lo_ref,
        hi_ref,
        coarse_lo_ref,
        coarse_hi_ref,
        sems,
    ) = rest
    fetch(
        [
            (g_hbm, g_ref),
            (owner_hbm, owner_ref),
            (nbr_hbm, nbr_ref),
            (mask_hbm, mask_ref),
            (coarse_nbr_hbm, coarse_nbr_ref),
            (coarse_mask_hbm, coarse_mask_ref),
            (lo_hbm, lo_ref),
            (hi_hbm, hi_ref),
            (coarse_lo_hbm, coarse_lo_ref),
            (coarse_hi_hbm, coarse_hi_ref),
        ]
        + [(w, weights_ref.at[pl.ds(128 * n, 128), :]) for n, w in enumerate(weight_hbms)],
        sems,
    )
    even = place_ref[0] > 0
    for low, high, out in (
        (lo_ref, hi_ref, sends_ref),
        (coarse_lo_ref, coarse_hi_ref, coarse_sends_ref),
    ):
        first = jnp.where(even, high[...], low[...])
        second = jnp.where(even, low[...], high[...])
        out[...] = jnp.concatenate([first, second], 1)
    columns_ref[...] = slot_columns(nbr_ref[...], mask_ref[...], halo_rows, even)
    columns_t_ref[...] = columns_ref[...].T
    coarse_columns_ref[...] = slot_columns(
        coarse_nbr_ref[...], coarse_mask_ref[...], coarse_halo, even
    )
    coarse_columns_t_ref[...] = coarse_columns_ref[...].T
    tiles = counts_ref.shape[0] // 2
    owner = owner_ref[...]
    high, low = owner // 128, lax.rem(owner, 128)
    groups = owner.shape[0]
    place = lax.broadcasted_iota(jnp.int32, (128, 128), 0)
    high_rows = jnp.concatenate(
        [pick(high[q : q + 1, :] == place[:tiles]) for q in range(groups)], 1
    )
    low_rows = jnp.concatenate(
        [pick(low[q : q + 1, :] == place) for q in range(groups)], 1
    )
    counts = dot_nt(high_rows, low_rows)
    most = jnp.floor(counts * (1 / DIGIT))
    counts_ref[...] = jnp.concatenate([most, counts - DIGIT * most], 0).astype(bf16)


def sums_kernel(owner_ref, g_ref, after_ref, sums_ref):
    def step(tile, carry):
        sums_ref[chunk_of(tile, 256), :] = owner_sums(owner_ref, tile, g_ref[...]).astype(bf16)
        return carry

    lax.fori_loop(0, sums_ref.shape[0] // 256, step, None)


def owners_kernel(owner_ref, after_ref, owners_ref):
    owners_ref[...] = owner_columns(owner_ref)


def fine_forward_kernel(
    h_ref,
    first_ref,
    second_ref,
    weights_ref,
    columns_t_ref,
    owner_ref,
    counts_ref,
    summed_ref,
    slope_hbm,
    totals_ref,
    own,
    far,
    halo,
    new,
    slope_ref,
    sem,
):
    self_weight, other_weight = matrix(weights_ref, 0), matrix(weights_ref, 1)
    level_terms(h_ref, (first_ref, second_ref), self_weight, other_weight, own, far, halo)

    def step(index, carry):
        here = chunk_of(index, STEP * BLOCK)
        total, slopes = edges(own[here, :], far[here, :], columns_t_ref[here, :], halo)
        summed_ref[here, :] = total
        edge = chunk_of(index, 8 * STEP * BLOCK)
        slope_ref[edge, :] = jnp.concatenate(slopes, 0)
        pltpu.make_async_copy(slope_ref.at[edge, :], slope_hbm.at[edge, :], sem).start()
        return carry

    lax.fori_loop(0, h_ref.shape[0] // (STEP * BLOCK), step, None)
    new[...] = jnp.concatenate([h_ref[...], summed_ref[...]], 1)
    coarse_rows = totals_ref.shape[0] - counts_ref.shape[0]

    def tile_step(tile, carry):
        sums = owner_sums(owner_ref, tile, new[...])
        totals = sums[:, :128] + dot(sums[:, 128:].astype(bf16), matrix(weights_ref, 2))
        totals_ref[chunk_of(tile, 256), :] = totals.astype(bf16)
        return carry

    lax.fori_loop(0, coarse_rows // 256, tile_step, None)
    totals_ref[coarse_rows:, :] = counts_ref[...]
    pltpu.make_async_copy(slope_ref, slope_hbm, sem).wait()


def coarse_input_kernel(
    totals_ref,
    more_totals_ref,
    sums_ref,
    more_sums_ref,
    sends_ref,
    after_ref,
    cin_ref,
    first_ref,
    second_ref,
    chip_sums_ref,
    counts_ref,
):
    coarse_rows = cin_ref.shape[0]
    tiles = coarse_rows // 128
    chip_sums_ref[...] = (sums_ref[...].astype(f32) + more_sums_ref[...].astype(f32)).astype(bf16)
    totals = totals_ref[...].astype(f32) + more_totals_ref[...].astype(f32)
    digits = totals[coarse_rows:]
    counts_ref[...] = DIGIT * digits[:tiles] + digits[tiles:]
    per_row = counts_ref[...].T
    for tile in range(tiles):
        here = slice(tile * 128, (tile + 1) * 128)
        cin_ref[here, :] = (totals[here] / per_row[:, tile : tile + 1]).astype(bf16)
    cin = cin_ref[...]
    place = lax.broadcasted_iota(jnp.int32, (coarse_rows, sends_ref.shape[1]), 0)
    sent = dot_tn(pick(sends_ref[...] == place), cin).astype(bf16)
    halo_rows = first_ref.shape[0]
    first_ref[...] = sent[:halo_rows]
    second_ref[...] = sent[halo_rows:]


def coarse_kernel(
    cin_ref,
    first_ref,
    second_ref,
    chip_sums_ref,
    more_sums_ref,
    weights_ref,
    columns_ref,
    columns_t_ref,
    part_ref,
    first_grad_ref,
    second_grad_ref,
    sums_ref,
    summed_ref,
    ups_ref,
    downs_ref,
    own,
    far,
    halo,
    grad_sum,
    halo_grad,
):
    halo_rows = first_ref.shape[0]
    self_weight, other_weight = matrix(weights_ref, 3), matrix(weights_ref, 4)
    level_terms(cin_ref, (first_ref, second_ref), self_weight, other_weight, own, far, halo)
    halo_grad[...] = jnp.zeros_like(halo_grad)
    sums_ref[...] = (chip_sums_ref[...].astype(f32) + more_sums_ref[...].astype(f32)).astype(bf16)
    part_ref[...] = dot_nt(sums_ref[...], matrix(weights_ref, 6))
    ups_ref[...] = part_ref[...].astype(bf16)
    grad_sum[...] = (dot_nt(ups_ref[...], matrix(weights_ref, 5)) * 0.5).astype(bf16)

    def step(index, carry):
        here = chunk_of(index, STEP * BLOCK)
        total, slopes = edges(own[here, :], far[here, :], columns_t_ref[here, :], halo)
        summed_ref[here, :] = total
        downs_ref[here, :] = edges_back(
            slopes, grad_sum[here, :], columns_ref[:, here], halo_grad
        )
        return carry

    lax.fori_loop(0, cin_ref.shape[0] // (STEP * BLOCK), step, None)
    first_grad_ref[...] = halo_grad[:halo_rows, :].astype(bf16)
    second_grad_ref[...] = halo_grad[halo_rows:, :].astype(bf16)


def coarse_tail_kernel(
    place_ref,
    cin_ref,
    first_ref,
    second_ref,
    sums_ref,
    matrices_ref,
    first_grad_ref,
    second_grad_ref,
    summed_ref,
    ups_ref,
    downs_ref,
    fine_ref,
    weights_ref,
):
    cin = cin_ref[...]
    out = (cin.astype(f32) + dot(summed_ref[...], matrix(matrices_ref, 5))).astype(bf16)
    fine_ref[...] = dot(out, matrix(matrices_ref, 6)).astype(bf16)
    pair_grad = dot_tn(cin, downs_ref[...])
    other_grad = (
        pair_grad[:, 128:]
        + dot_tn(first_ref[...], first_grad_ref[...])
        + dot_tn(second_ref[...], second_grad_ref[...])
    )
    grads = [
        pair_grad[:, :128],
        other_grad,
        dot_tn(summed_ref[...], ups_ref[...]),
        dot_tn(out, sums_ref[...]),
    ]
    weights_ref[...] = choose(place_ref[1], grads).astype(bf16)


def choose(place, values):
    picked = values[-1]
    for n, value in enumerate(values[:-1]):
        picked = jnp.where(place == n, value, picked)
    return picked


def owner_columns(owner_ref):
    owner = owner_ref[...].astype(f32)
    row = jnp.concatenate([owner[q : q + 1, :] for q in range(owner.shape[0])], 1)
    return jnp.broadcast_to(row, (8, row.shape[1])).T


def owner_rows(owners, values):
    count = owners.shape[0]
    wide = jnp.broadcast_to(owners[:, 0:1], (count, 128))
    lane = lax.broadcasted_iota(jnp.int32, (count, 128), 1)
    first, second = lane.astype(bf16), (lane + 128).astype(bf16)
    rows = []
    for tile in range(values.shape[0] // 256):
        here = (wide - 256.0 * tile).astype(bf16)
        rows += [pick16(here, first), pick16(here, second)]
    return dot(jnp.concatenate(rows, 1), values)


def result_kernel(h_ref, summed_ref, weights_ref, owners_ref, fine_ref, out_hbm, out_ref, sem):
    def step(index, carry):
        here = chunk_of(index, CHUNK)
        updated = h_ref[here, :].astype(f32) + dot(summed_ref[here, :], matrix(weights_ref, 2))
        out_ref[here, :] = (updated + owner_rows(owners_ref[here, :], fine_ref[...])).astype(bf16)
        pltpu.make_async_copy(out_ref.at[here, :], out_hbm.at[here, :], sem).start()
        return carry

    lax.fori_loop(0, h_ref.shape[0] // CHUNK, step, None)
    pltpu.make_async_copy(out_ref, out_hbm, sem).wait()


def fine_backward_kernel(
    h_ref,
    first_ref,
    second_ref,
    g_ref,
    summed_ref,
    slope_hbm,
    matrices_ref,
    columns_ref,
    owners_ref,
    part_ref,
    counts_ref,
    coarse_downs_ref,
    first_back_ref,
    second_back_ref,
    sends_ref,
    coarse_weights_ref,
    ups_ref,
    downs_ref,
    first_grad_ref,
    second_grad_ref,
    weights_ref,
    grad_sum,
    halo_grad,
    mean,
    slope_ref,
    slope_sems,
):
    count = STEP * BLOCK
    steps = h_ref.shape[0] // count

    def slope_copy(index):
        edge = chunk_of(index, 8 * count)
        return pltpu.make_async_copy(
            slope_hbm.at[edge, :], slope_ref.at[edge, :], slope_sems.at[index]
        )

    for index in range(steps):
        slope_copy(index).start()
    halo_rows = first_ref.shape[0]
    coarse_rows = part_ref.shape[0]
    halo_grad[...] = jnp.zeros_like(halo_grad)

    place = lax.broadcasted_iota(jnp.int32, (coarse_rows, sends_ref.shape[1]), 0)
    sends = pick(sends_ref[...] == place)
    back = jnp.concatenate([first_back_ref[...], second_back_ref[...]], 0)
    back = dot_nt(back, matrix(matrices_ref, 4)).astype(bf16)
    plain = jnp.concatenate([matrix(matrices_ref, 3), matrix(matrices_ref, 4)], 1)
    grad_in = part_ref[...] + dot_nt(coarse_downs_ref[...], plain) + dot(sends, back)
    per_row = counts_ref[...].T
    for tile in range(coarse_rows // 128):
        here = slice(tile * 128, (tile + 1) * 128)
        mean[here, :] = (grad_in[here, :] / per_row[:, tile : tile + 1]).astype(bf16)

    def owner_step(index):
        here = chunk_of(index, count)
        grad_up = g_ref[here, :].astype(f32) + owner_rows(owners_ref[here, :], mean[...])
        ups = grad_up.astype(bf16)
        ups_ref[here, :] = ups
        grad_sum[here, :] = (dot_nt(ups, matrix(matrices_ref, 2)) * 0.5).astype(bf16)

    def edge_step(index):
        here = chunk_of(index, count)
        slope_copy(index).wait()
        slope = slope_ref[chunk_of(index, 8 * count), :]
        slopes = [slope[n * 8 * BLOCK : (n + 1) * 8 * BLOCK] for n in range(STEP)]
        downs_ref[here, :] = edges_back(
            slopes, grad_sum[here, :], columns_ref[:, here], halo_grad
        )

    owner_step(0)

    def step(index, carry):
        edge_step(index)
        owner_step(index + 1)
        return carry

    lax.fori_loop(0, steps - 1, step, None)
    edge_step(steps - 1)
    first_grad = halo_grad[:halo_rows, :].astype(bf16)
    second_grad = halo_grad[halo_rows:, :].astype(bf16)
    first_grad_ref[...] = first_grad
    second_grad_ref[...] = second_grad
    pair_grad = dot_tn(h_ref[...], downs_ref[...])
    weights_ref[0:128, :] = pair_grad[:, :128].astype(bf16)
    weights_ref[128:256, :] = (
        pair_grad[:, 128:]
        + dot_tn(first_ref[...], first_grad)
        + dot_tn(second_ref[...], second_grad)
    ).astype(bf16)
    weights_ref[256:384, :] = dot_tn(summed_ref[...], ups_ref[...]).astype(bf16)
    weights_ref[384:512, :] = coarse_weights_ref[...]


def finish_kernel(
    ups_ref,
    downs_ref,
    first_back_ref,
    second_back_ref,
    sends_ref,
    matrices_ref,
    out_hbm,
    out_ref,
    sem,
):
    other = matrix(matrices_ref, 1)
    plain = jnp.concatenate([matrix(matrices_ref, 0), other], 1)
    back = jnp.concatenate([first_back_ref[...], second_back_ref[...]], 0)
    back = dot_nt(back, other).astype(bf16)
    sends = sends_ref[...]
    place = lax.broadcasted_iota(jnp.int32, (256, sends.shape[1]), 0).astype(bf16)

    def step(index, carry):
        here = chunk_of(index, CHUNK)
        rows = []
        for part in range(CHUNK // 256):
            local = (sends - (index * CHUNK + 256 * part)).astype(f32)
            rows.append(pick16(jnp.broadcast_to(local, place.shape).astype(bf16), place))
        grad = ups_ref[here, :].astype(f32) + dot_nt(downs_ref[here, :], plain)
        out_ref[here, :] = (grad + dot(jnp.concatenate(rows, 0), back)).astype(bf16)
        pltpu.make_async_copy(out_ref.at[here, :], out_hbm.at[here, :], sem).start()
        return carry

    lax.fori_loop(0, ups_ref.shape[0] // CHUNK, step, None)
    pltpu.make_async_copy(out_ref, out_hbm, sem).wait()


def add_kernel(mine_ref, theirs_ref, *rest):
    out_ref = rest[-1]
    out_ref[...] = (mine_ref[...].astype(f32) + theirs_ref[...].astype(f32)).astype(bf16)


def add_gather_kernel(mine_ref, theirs_ref, after_ref, out_ref):
    mine, theirs = mine_ref[...].astype(f32), theirs_ref[...].astype(f32)
    out_ref[:384, :] = mine[:384] + theirs[:384]
    out_ref[384:512, :] = mine[384:]
    out_ref[512:, :] = theirs[384:]


def weights_kernel(place_ref, mine_ref, theirs_ref, out_ref):
    out_ref[:384, :] = mine_ref[:384, :] + theirs_ref[:384, :]
    group = place_ref[1]
    low, high = lax.rem(group, 2), group // 2
    for n in range(4):
        row = jnp.where(high == n // 2, 384, 512)
        here = pl.ds(pl.multiple_of(row, 128), 128)
        value = jnp.where(low == n % 2, mine_ref[here, :], theirs_ref[here, :])
        out_ref[384 + 128 * n : 512 + 128 * n, :] = value


def exchange(first, second):
    count = lax.axis_size("sub")
    routes = []
    for start in range(2):
        pairs = [(i, i + 1) for i in range(start, count - 1, 2)]
        routes.append(pairs + [(j, i) for i, j in pairs])
    return lax.ppermute(first, "sub", routes[0]), lax.ppermute(second, "sub", routes[1])


def swapped(block, axis, distance):
    return lax.ppermute(block, axis, [(i, i ^ distance) for i in range(lax.axis_size(axis))])


def total_weights(weights, place, after, last):
    distance, number = 1, 0
    while distance < lax.axis_size("sub"):
        theirs = swapped(weights, "sub", distance)
        waits = after[number] if number < len(after) else ()
        weights = call(
            add_kernel,
            shape(*weights.shape, bf16),
            [weights, theirs, *waits],
            [VMEM, VMEM] + [HBM] * len(waits),
        )
        distance, number = 2 * distance, number + 1
    weights = call(
        add_gather_kernel,
        shape(640, 128, f32),
        [weights, swapped(weights, "grp", 2), last],
        [VMEM, VMEM, HBM],
    )
    return call(
        weights_kernel,
        shape(896, 128, f32),
        [place, weights, swapped(weights, "grp", 1)],
        [SMEM, VMEM, VMEM],
    )


def per_device(
    states,
    cotangent,
    fine_self,
    fine_other,
    fine_node,
    coarse_self,
    coarse_other,
    coarse_node,
    prolong,
    fine_nbr,
    fine_mask,
    fine_send_lo,
    fine_send_hi,
    coarse_nbr,
    coarse_mask,
    coarse_send_lo,
    coarse_send_hi,
    coarse_owner,
):
    rows, features = states.shape
    coarse_rows = coarse_nbr.shape[0]
    halo_rows = fine_send_lo.shape[0]
    coarse_halo = coarse_send_lo.shape[0]
    count_rows = coarse_rows // 128
    owner = coarse_owner.reshape(rows // 128, 128)
    place = jnp.stack([1 - lax.rem(lax.axis_index("sub"), 2), lax.axis_index("grp")])

    def buffer(count, columns, dtype):
        return pltpu.VMEM((count, columns), dtype)

    to_first, to_second, states = gather_rows(place, states, fine_send_lo, fine_send_hi)
    first, second = exchange(to_first, to_second)

    (
        counts, columns, columns_t, coarse_columns, coarse_columns_t, cotangent, matrices, sends,
        coarse_sends, owner,
    ) = call(
        functools.partial(prepare_kernel, halo_rows=halo_rows, coarse_halo=coarse_halo),
        [
            shape(2 * count_rows, features, bf16),
            shape(8, rows, f32),
            shape(rows, 8, f32),
            shape(8, coarse_rows, f32),
            shape(coarse_rows, 8, f32),
            shape(rows, features, bf16),
            shape(7 * features, features, bf16),
            shape(1, 2 * halo_rows, jnp.int32),
            shape(1, 2 * coarse_halo, jnp.int32),
            shape(rows // 128, 128, jnp.int32),
        ],
        [
            place, cotangent, owner, fine_nbr.T, fine_mask.T, coarse_nbr.T, coarse_mask.T,
            fine_send_lo[None], fine_send_hi[None], coarse_send_lo[None], coarse_send_hi[None],
            fine_self, fine_other, fine_node, coarse_self, coarse_other, coarse_node, prolong,
            to_first,
        ],
        [SMEM] + [HBM] * 17 + [ANY],
        [buffer(8, rows, jnp.int32)] * 2
        + [buffer(8, coarse_rows, jnp.int32)] * 2
        + [buffer(1, halo_rows, jnp.int32)] * 2
        + [buffer(1, coarse_halo, jnp.int32)] * 2
        + [pltpu.SemaphoreType.DMA((17,))],
    )

    summed, slope, totals = call(
        fine_forward_kernel,
        [
            shape(rows, features, bf16),
            pltpu.HBM((8 * rows, features), bf16),
            shape(coarse_rows + 2 * count_rows, features, bf16),
        ],
        [states, first, second, matrices, columns_t, owner, counts],
        scratch=[
            buffer(rows, features, f32),
            buffer(rows, features, bf16),
            buffer(2 * halo_rows, features, bf16),
            buffer(rows, 2 * features, bf16),
            buffer(8 * rows, features, bf16),
            pltpu.SemaphoreType.DMA,
        ],
        out_specs=[VMEM, HBM, VMEM],
        mib=32,
    )
    chip_totals = call(
        add_kernel, shape(*totals.shape, bf16), [totals, swapped(totals, "grp", 1)]
    )
    more_totals = swapped(chip_totals, "grp", 2)
    sums = call(
        sums_kernel,
        shape(coarse_rows, features, bf16),
        [owner, cotangent, totals],
        [VMEM, VMEM, ANY],
    )
    more_sums = swapped(sums, "grp", 1)
    owners_t = call(owners_kernel, shape(rows, 8, f32), [owner, chip_totals], [VMEM, ANY])

    coarse_in, to_first, to_second, chip_sums, counts = call(
        coarse_input_kernel,
        [
            shape(coarse_rows, features, bf16),
            shape(coarse_halo, features, bf16),
            shape(coarse_halo, features, bf16),
            shape(coarse_rows, features, bf16),
            shape(count_rows, features, f32),
        ],
        [chip_totals, more_totals, sums, more_sums, coarse_sends, owners_t],
        [VMEM] * 5 + [ANY],
    )
    coarse_first, coarse_second = exchange(to_first, to_second)
    more_sums = swapped(chip_sums, "grp", 2)

    coarse_part, first_grad, second_grad, sums, coarse_sum, coarse_ups, coarse_downs = call(
        coarse_kernel,
        [
            shape(coarse_rows, features, f32),
            shape(coarse_halo, features, bf16),
            shape(coarse_halo, features, bf16),
            shape(coarse_rows, features, bf16),
            shape(coarse_rows, features, bf16),
            shape(coarse_rows, features, bf16),
            shape(coarse_rows, 2 * features, bf16),
        ],
        [
            coarse_in, coarse_first, coarse_second, chip_sums, more_sums, matrices,
            coarse_columns, coarse_columns_t,
        ],
        scratch=[
            buffer(coarse_rows, features, f32),
            buffer(coarse_rows, features, bf16),
            buffer(2 * coarse_halo, features, bf16),
            buffer(coarse_rows, features, bf16),
            buffer(2 * coarse_halo, features, f32),
        ],
    )
    first_back, second_back = exchange(first_grad, second_grad)

    fine_term, coarse_weights = call(
        coarse_tail_kernel,
        [shape(coarse_rows, features, bf16), shape(features, features, bf16)],
        [
            place, coarse_in, coarse_first, coarse_second, sums, matrices,
            first_grad, second_grad, coarse_sum, coarse_ups, coarse_downs,
        ],
        [SMEM] + [VMEM] * 10,
    )
    result = call(
        result_kernel,
        pltpu.HBM((rows, features), bf16),
        [states, summed, matrices, owners_t, fine_term],
        scratch=[buffer(rows, features, bf16), pltpu.SemaphoreType.DMA],
        out_specs=HBM,
    )

    ups, downs, first_grad, second_grad, weights = call(
        fine_backward_kernel,
        [
            shape(rows, features, bf16),
            shape(rows, 2 * features, bf16),
            shape(halo_rows, features, bf16),
            shape(halo_rows, features, bf16),
            shape(4 * features, features, bf16),
        ],
        [
            states, first, second, cotangent, summed, slope, matrices, columns, owners_t,
            coarse_part, counts, coarse_downs, first_back, second_back, coarse_sends,
            coarse_weights,
        ],
        [VMEM] * 5 + [HBM] + [VMEM] * 10,
        [
            buffer(rows, features, bf16),
            buffer(2 * halo_rows, features, f32),
            buffer(coarse_rows, features, bf16),
            buffer(8 * rows, features, bf16),
            pltpu.SemaphoreType.DMA((rows // (STEP * BLOCK),)),
        ],
        mib=32,
    )
    first_back, second_back = exchange(first_grad, second_grad)

    grad_states = call(
        finish_kernel,
        pltpu.HBM((rows, features), bf16),
        [ups, downs, first_back, second_back, sends, matrices],
        scratch=[buffer(rows, features, bf16), pltpu.SemaphoreType.DMA],
        out_specs=HBM,
    )
    grad_weights = total_weights(weights, place, ((), (), (grad_states,)), result)
    return (result, grad_states, grad_weights.reshape(7, features, features))


def solution(mesh):
    fine = P(("grp", "sub"), None)
    fine_row = P(("grp", "sub"))
    in_specs = (
        (fine, fine)
        + (P(),) * 7
        + (fine, fine, fine_row, fine_row)
        + (P("sub", None), P("sub", None), P("sub"), P("sub"), fine_row)
    )
    return jax.shard_map(
        per_device, mesh=mesh, in_specs=in_specs, out_specs=(fine, fine, P()), check_vma=False
    )
```

```python
import functools

import jax
import jax.numpy as jnp
from jax import lax
from jax.experimental import pallas as pl
from jax.experimental.pallas import tpu as pltpu
from jax.sharding import PartitionSpec as P

f32 = jnp.float32
bf16 = jnp.bfloat16
BLOCK = 64
PAIR = 2 * BLOCK
STEP = 16
CHUNK = 1024
NEVER = -1e30
DIGIT = 64.0
VMEM = pl.BlockSpec(memory_space=pltpu.VMEM)
SMEM = pl.BlockSpec(memory_space=pltpu.SMEM)
ANY = pl.BlockSpec(memory_space=pl.ANY)
HBM = pl.BlockSpec(memory_space=pltpu.HBM)
MIB = 1024 * 1024


def dot(a, b):
    return jnp.dot(a, b, preferred_element_type=f32)


def dot_nt(a, b):
    return lax.dot_general(a, b, (((1,), (1,)), ((), ())), preferred_element_type=f32)


def dot_tn(a, b):
    return lax.dot_general(a, b, (((0,), (0,)), ((), ())), preferred_element_type=f32)


def pick(condition):
    return jnp.where(condition, 1.0, 0.0).astype(bf16)


def pick16(values, places):
    return jnp.where(values == places, jnp.ones((), bf16), jnp.zeros((), bf16))


def call(kernel, out_shape, args, in_specs=None, scratch=(), out_specs=None, mib=16):
    many = isinstance(out_shape, (list, tuple))
    in_specs = in_specs or [VMEM] * len(args)
    args = [
        pltpu.with_memory_space_constraint(arg, pltpu.HBM) if spec is HBM else arg
        for arg, spec in zip(args, in_specs)
    ]
    return pl.pallas_call(
        kernel,
        out_shape=out_shape,
        in_specs=in_specs,
        out_specs=out_specs or ([VMEM] * len(out_shape) if many else VMEM),
        scratch_shapes=list(scratch),
        compiler_params=pltpu.CompilerParams(vmem_limit_bytes=mib * MIB),
    )(*args)


def shape(rows, columns, dtype):
    return jax.ShapeDtypeStruct((rows, columns), dtype)


def slot_columns(nbr, mask, halo_rows, even):
    rows = nbr.shape[1]
    block = lax.broadcasted_iota(jnp.int32, nbr.shape, 1) // BLOCK
    halo = lax.rem(block, halo_rows // BLOCK) * BLOCK
    lower = jnp.where(even, 2 * BLOCK, BLOCK)
    column = jnp.where(
        nbr < rows,
        nbr - block * BLOCK,
        jnp.where(
            nbr < rows + halo_rows,
            lower + nbr - rows - halo,
            3 * BLOCK - lower + nbr - rows - halo_rows - halo,
        ),
    )
    return jnp.where(mask > 0, column, 3 * BLOCK).astype(f32)


def selector(columns_t):
    first = lax.broadcasted_iota(jnp.int32, (BLOCK, 128), 1).astype(bf16)
    second = (lax.broadcasted_iota(jnp.int32, (BLOCK, 128), 1) + 128).astype(bf16)
    parts = []
    for k in range(8):
        wide = jnp.broadcast_to(columns_t[:, k : k + 1], (BLOCK, 128)).astype(bf16)
        parts.append(jnp.concatenate([pick16(wide, first), pick16(wide, second)], 1))
    return jnp.concatenate(parts, 0)


def selector_t(columns, rolled, half):
    lane = lax.broadcasted_iota(jnp.int32, (1, 128), 1)
    place = lax.broadcasted_iota(jnp.int32, (3 * BLOCK, 128), 0).astype(bf16)
    parts = []
    for j in range(4):
        left, right = (columns, rolled) if half == 0 else (rolled, columns)
        row = jnp.where(lane < BLOCK, left[2 * j : 2 * j + 1], right[2 * j + 1 : 2 * j + 2])
        wide = jnp.broadcast_to(row, (3 * BLOCK, 128)).astype(bf16)
        parts.append(pick16(wide, place))
    return jnp.concatenate(parts, 1)


def window_of(far, halo, place):
    halo_rows = halo.shape[0] // 2
    start = place * BLOCK
    return jnp.concatenate(
        [
            far,
            halo[start : start + BLOCK, :],
            halo[halo_rows + start : halo_rows + start + BLOCK, :],
            jnp.full((BLOCK, far.shape[1]), NEVER, bf16),
        ],
        0,
    )


def chunk_of(index, count):
    return pl.ds(pl.multiple_of(index * count, count), count)


def matrix(weights_ref, n):
    return weights_ref[128 * n : 128 * (n + 1), :]


def level_terms(h_ref, halo_refs, self_weight, other_weight, own, far, halo):
    halo_rows = halo_refs[0].shape[0]
    other = other_weight * 0.5
    terms = dot(h_ref[...], jnp.concatenate([self_weight * 0.5, other], 1))
    own[...] = terms[:, :128]
    far[...] = terms[:, 128:].astype(bf16)
    halo[:halo_rows, :] = dot(halo_refs[0][...], other).astype(bf16)
    halo[halo_rows:, :] = dot(halo_refs[1][...], other).astype(bf16)


def edges(own_rows, far_rows, slots, halo):
    places = halo.shape[0] // (2 * BLOCK)
    assert STEP % places == 0
    tables = []
    for n in range(STEP):
        part = slice(n * BLOCK, (n + 1) * BLOCK)
        window = window_of(far_rows[part], halo, n % places)
        tables.append(dot(selector(slots[part]), window))
    sums, slopes = [], []
    for n, picked in enumerate(tables):
        own = own_rows[n * BLOCK : (n + 1) * BLOCK]
        values, pieces = [], []
        for k in range(8):
            y = (picked[k * BLOCK : (k + 1) * BLOCK] + own).astype(bf16)
            t = jnp.tanh(y)
            bent = y * t
            values.append(y + bent)
            pieces.append((1 + t) * (1 + (y - bent)))
        while len(values) > 1:
            values = [left + right for left, right in zip(values[::2], values[1::2])]
        sums.append(values[0])
        slopes.append(jnp.concatenate(pieces, 0))
    return jnp.concatenate(sums, 0), slopes


def edges_back(slopes, grad_sum, columns, halo_grad):
    places = halo_grad.shape[0] // (2 * BLOCK)
    halo_rows = halo_grad.shape[0] // 2
    windows, downs = [], []
    for n, slope in enumerate(slopes):
        part = grad_sum[n * BLOCK : (n + 1) * BLOCK]
        grads = [slope[k * BLOCK : (k + 1) * BLOCK] * part for k in range(8)]
        downs.append(sum(grad.astype(f32) for grad in grads))
        mine = columns[:, n // 2 * PAIR : (n // 2 + 1) * PAIR]
        selected = selector_t(mine, pltpu.roll(mine, BLOCK, 1), n % 2)
        windows.append(dot(selected, jnp.concatenate(grads, 0)))
    for place in range(places):
        for side in range(2):
            start = side * halo_rows + place * BLOCK
            total = halo_grad[start : start + BLOCK, :]
            for window in windows[place::places]:
                total = total + window[(side + 1) * BLOCK : (side + 2) * BLOCK]
            halo_grad[start : start + BLOCK, :] = total
    local = jnp.concatenate([window[:BLOCK] for window in windows], 0)
    down = jnp.concatenate(downs, 0)
    return jnp.concatenate([down, local], 1).astype(bf16)


def fetch(pairs, sems):
    copies = [pltpu.make_async_copy(src, dst, sems.at[n]) for n, (src, dst) in enumerate(pairs)]
    for copy in copies:
        copy.start()
    for copy in copies:
        copy.wait()


def gather_kernel(
    place_ref, lo_hbm, hi_hbm, x_hbm, first_ref, second_ref, x_ref, wide, up, down, lo, hi, sems
):
    fetch([(x_hbm, x_ref), (lo_hbm, lo), (hi_hbm, hi)], sems)
    wide[...] = x_ref[...].astype(f32)

    def step(r, carry):
        up[pl.ds(r, 1), :] = wide[pl.ds(hi[r], 1), :]
        down[pl.ds(r, 1), :] = wide[pl.ds(lo[r], 1), :]
        return carry

    lax.fori_loop(0, up.shape[0], step, None, unroll=16)
    even = place_ref[0] > 0
    first_ref[...] = jnp.where(even, up[...], down[...]).astype(bf16)
    second_ref[...] = jnp.where(even, down[...], up[...]).astype(bf16)


def gather_rows(place, x, send_lo, send_hi):
    rows, features = x.shape
    count = send_lo.shape[0]
    out = shape(count, features, bf16)
    return call(
        gather_kernel,
        [out, out, shape(rows, features, bf16)],
        [place, send_lo, send_hi, x],
        [SMEM, HBM, HBM, HBM],
        [
            pltpu.VMEM((rows, features), f32),
            pltpu.VMEM((count, features), f32),
            pltpu.VMEM((count, features), f32),
            pltpu.SMEM((count,), jnp.int32),
            pltpu.SMEM((count,), jnp.int32),
            pltpu.SemaphoreType.DMA((3,)),
        ],
    )


def owner_sums(owner_ref, tile, values):
    place = lax.broadcasted_iota(jnp.int32, (256, 128), 0).astype(bf16)
    owner = (owner_ref[...] - tile * 256).astype(f32)
    rows = jnp.concatenate(
        [
            pick16(jnp.broadcast_to(owner[q : q + 1], (256, 128)).astype(bf16), place)
            for q in range(owner.shape[0])
        ],
        1,
    )
    return dot(rows, values)


def prepare_kernel(
    place_ref,
    g_hbm,
    owner_hbm,
    nbr_hbm,
    mask_hbm,
    coarse_nbr_hbm,
    coarse_mask_hbm,
    lo_hbm,
    hi_hbm,
    coarse_lo_hbm,
    coarse_hi_hbm,
    *rest,
    halo_rows,
    coarse_halo,
):
    weight_hbms, rest = rest[:7], rest[7:]
    (
        after_ref,
        counts_ref,
        columns_ref,
        columns_t_ref,
        coarse_columns_ref,
        coarse_columns_t_ref,
        g_ref,
        weights_ref,
        sends_ref,
        coarse_sends_ref,
        owner_ref,
        nbr_ref,
        mask_ref,
        coarse_nbr_ref,
        coarse_mask_ref,
        lo_ref,
        hi_ref,
        coarse_lo_ref,
        coarse_hi_ref,
        sems,
    ) = rest
    fetch(
        [
            (g_hbm, g_ref),
            (owner_hbm, owner_ref),
            (nbr_hbm, nbr_ref),
            (mask_hbm, mask_ref),
            (coarse_nbr_hbm, coarse_nbr_ref),
            (coarse_mask_hbm, coarse_mask_ref),
            (lo_hbm, lo_ref),
            (hi_hbm, hi_ref),
            (coarse_lo_hbm, coarse_lo_ref),
            (coarse_hi_hbm, coarse_hi_ref),
        ]
        + [(w, weights_ref.at[pl.ds(128 * n, 128), :]) for n, w in enumerate(weight_hbms)],
        sems,
    )
    even = place_ref[0] > 0
    for low, high, out in (
        (lo_ref, hi_ref, sends_ref),
        (coarse_lo_ref, coarse_hi_ref, coarse_sends_ref),
    ):
        first = jnp.where(even, high[...], low[...])
        second = jnp.where(even, low[...], high[...])
        out[...] = jnp.concatenate([first, second], 1)
    columns_ref[...] = slot_columns(nbr_ref[...], mask_ref[...], halo_rows, even)
    columns_t_ref[...] = columns_ref[...].T
    coarse_columns_ref[...] = slot_columns(
        coarse_nbr_ref[...], coarse_mask_ref[...], coarse_halo, even
    )
    coarse_columns_t_ref[...] = coarse_columns_ref[...].T
    tiles = counts_ref.shape[0] // 2
    owner = owner_ref[...]
    high, low = owner // 128, lax.rem(owner, 128)
    groups = owner.shape[0]
    place = lax.broadcasted_iota(jnp.int32, (128, 128), 0)
    high_rows = jnp.concatenate(
        [pick(high[q : q + 1, :] == place[:tiles]) for q in range(groups)], 1
    )
    low_rows = jnp.concatenate(
        [pick(low[q : q + 1, :] == place) for q in range(groups)], 1
    )
    counts = dot_nt(high_rows, low_rows)
    most = jnp.floor(counts * (1 / DIGIT))
    counts_ref[...] = jnp.concatenate([most, counts - DIGIT * most], 0).astype(bf16)


def sums_kernel(owner_ref, g_ref, after_ref, sums_ref):
    def step(tile, carry):
        sums_ref[chunk_of(tile, 256), :] = owner_sums(owner_ref, tile, g_ref[...]).astype(bf16)
        return carry

    lax.fori_loop(0, sums_ref.shape[0] // 256, step, None)


def owners_kernel(owner_ref, after_ref, owners_ref):
    owners_ref[...] = owner_columns(owner_ref)


def half_totals(owner_ref, new_ref, counts_ref, half, out_ref):
    tiles = (out_ref.shape[0] - counts_ref.shape[0]) // 256
    for tile in range(tiles):
        totals = owner_sums(owner_ref, half * tiles + tile, new_ref[...])
        out_ref[256 * tile : 256 * (tile + 1), :] = totals.astype(bf16)
    out_ref[256 * tiles :, :] = counts_ref[...]


def keep_kernel(place_ref, owner_ref, new_ref, counts_ref, out_ref):
    half_totals(owner_ref, new_ref, counts_ref, lax.rem(place_ref[1], 2), out_ref)


def fine_forward_kernel(
    place_ref,
    h_ref,
    first_ref,
    second_ref,
    weights_ref,
    columns_t_ref,
    owner_ref,
    counts_ref,
    summed_ref,
    slope_hbm,
    new_ref,
    give_ref,
    own,
    far,
    halo,
    slope_ref,
    sem,
):
    self_weight, other_weight = matrix(weights_ref, 0), matrix(weights_ref, 1)
    level_terms(h_ref, (first_ref, second_ref), self_weight, other_weight, own, far, halo)

    def step(index, carry):
        here = chunk_of(index, STEP * BLOCK)
        total, slopes = edges(own[here, :], far[here, :], columns_t_ref[here, :], halo)
        summed_ref[here, :] = total
        edge = chunk_of(index, 8 * STEP * BLOCK)
        slope_ref[edge, :] = jnp.concatenate(slopes, 0)
        pltpu.make_async_copy(slope_ref.at[edge, :], slope_hbm.at[edge, :], sem).start()
        return carry

    lax.fori_loop(0, h_ref.shape[0] // (STEP * BLOCK), step, None)
    new_ref[...] = (
        h_ref[...].astype(f32) + dot(summed_ref[...], matrix(weights_ref, 2))
    ).astype(bf16)
    half_totals(owner_ref, new_ref, counts_ref, 1 - lax.rem(place_ref[1], 2), give_ref)
    pltpu.make_async_copy(slope_ref, slope_hbm, sem).wait()


def half_kernel(place_ref, totals_ref, more_totals_ref, after_ref, half_ref, counts_ref):
    half_rows = half_ref.shape[0]
    totals = totals_ref[...].astype(f32) + more_totals_ref[...].astype(f32)
    digits = totals[half_rows:]
    tiles = counts_ref.shape[0]
    counts_ref[...] = DIGIT * digits[:tiles] + digits[tiles:]
    per_row = counts_ref[...].T
    first = lax.rem(place_ref[1], 2) == 0
    for tile in range(tiles // 2):
        here = slice(tile * 128, (tile + 1) * 128)
        later = tile + tiles // 2
        count = jnp.where(first, per_row[:, tile : tile + 1], per_row[:, later : later + 1])
        half_ref[here, :] = (totals[here] / count).astype(bf16)


def coarse_input_kernel(
    place_ref,
    half_ref,
    their_half_ref,
    sums_ref,
    more_sums_ref,
    sends_ref,
    cin_ref,
    first_ref,
    second_ref,
    chip_sums_ref,
):
    mine, theirs = half_ref[...], their_half_ref[...]
    first = lax.rem(place_ref[1], 2) == 0
    cin = jnp.concatenate([jnp.where(first, mine, theirs), jnp.where(first, theirs, mine)], 0)
    cin_ref[...] = cin
    place = lax.broadcasted_iota(jnp.int32, (cin.shape[0], sends_ref.shape[1]), 0)
    sent = dot_tn(pick(sends_ref[...] == place), cin).astype(bf16)
    halo_rows = first_ref.shape[0]
    first_ref[...] = sent[:halo_rows]
    second_ref[...] = sent[halo_rows:]
    chip_sums_ref[...] = (sums_ref[...].astype(f32) + more_sums_ref[...].astype(f32)).astype(bf16)


def coarse_forward_kernel(
    cin_ref,
    first_ref,
    second_ref,
    weights_ref,
    columns_t_ref,
    summed_ref,
    slope_ref,
    own,
    far,
    halo,
):
    self_weight, other_weight = matrix(weights_ref, 3), matrix(weights_ref, 4)
    level_terms(cin_ref, (first_ref, second_ref), self_weight, other_weight, own, far, halo)

    def step(index, carry):
        here = chunk_of(index, STEP * BLOCK)
        total, slopes = edges(own[here, :], far[here, :], columns_t_ref[here, :], halo)
        summed_ref[here, :] = total
        slope_ref[chunk_of(index, 8 * STEP * BLOCK), :] = jnp.concatenate(slopes, 0)
        return carry

    lax.fori_loop(0, cin_ref.shape[0] // (STEP * BLOCK), step, None)


def coarse_backward_kernel(
    slope_ref,
    chip_sums_ref,
    more_sums_ref,
    weights_ref,
    columns_ref,
    part_ref,
    first_grad_ref,
    second_grad_ref,
    sums_ref,
    ups_ref,
    downs_ref,
    grad_sum,
    halo_grad,
):
    halo_rows = first_grad_ref.shape[0]
    halo_grad[...] = jnp.zeros_like(halo_grad)
    sums_ref[...] = (chip_sums_ref[...].astype(f32) + more_sums_ref[...].astype(f32)).astype(bf16)
    part_ref[...] = dot_nt(sums_ref[...], matrix(weights_ref, 6))
    ups_ref[...] = part_ref[...].astype(bf16)
    grad_sum[...] = (dot_nt(ups_ref[...], matrix(weights_ref, 5)) * 0.5).astype(bf16)
    count = STEP * BLOCK

    def step(index, carry):
        here = chunk_of(index, count)
        slope = slope_ref[chunk_of(index, 8 * count), :]
        slopes = [slope[n * 8 * BLOCK : (n + 1) * 8 * BLOCK] for n in range(STEP)]
        downs_ref[here, :] = edges_back(
            slopes, grad_sum[here, :], columns_ref[:, here], halo_grad
        )
        return carry

    lax.fori_loop(0, part_ref.shape[0] // count, step, None)
    first_grad_ref[...] = halo_grad[:halo_rows, :].astype(bf16)
    second_grad_ref[...] = halo_grad[halo_rows:, :].astype(bf16)


def coarse_tail_kernel(
    place_ref,
    cin_ref,
    first_ref,
    second_ref,
    sums_ref,
    matrices_ref,
    first_grad_ref,
    second_grad_ref,
    summed_ref,
    ups_ref,
    downs_ref,
    fine_ref,
    weights_ref,
):
    cin = cin_ref[...]
    out = (cin.astype(f32) + dot(summed_ref[...], matrix(matrices_ref, 5))).astype(bf16)
    fine_ref[...] = dot(out, matrix(matrices_ref, 6)).astype(bf16)
    pair_grad = dot_tn(cin, downs_ref[...])
    other_grad = (
        pair_grad[:, 128:]
        + dot_tn(first_ref[...], first_grad_ref[...])
        + dot_tn(second_ref[...], second_grad_ref[...])
    )
    grads = [
        pair_grad[:, :128],
        other_grad,
        dot_tn(summed_ref[...], ups_ref[...]),
        dot_tn(out, sums_ref[...]),
    ]
    weights_ref[...] = choose(place_ref[1], grads).astype(bf16)


def choose(place, values):
    picked = values[-1]
    for n, value in enumerate(values[:-1]):
        picked = jnp.where(place == n, value, picked)
    return picked


def owner_columns(owner_ref):
    owner = owner_ref[...].astype(f32)
    row = jnp.concatenate([owner[q : q + 1, :] for q in range(owner.shape[0])], 1)
    return jnp.broadcast_to(row, (8, row.shape[1])).T


def owner_rows(owners, values):
    count = owners.shape[0]
    wide = jnp.broadcast_to(owners[:, 0:1], (count, 128))
    lane = lax.broadcasted_iota(jnp.int32, (count, 128), 1)
    first, second = lane.astype(bf16), (lane + 128).astype(bf16)
    rows = []
    for tile in range(values.shape[0] // 256):
        here = (wide - 256.0 * tile).astype(bf16)
        rows += [pick16(here, first), pick16(here, second)]
    return dot(jnp.concatenate(rows, 1), values)


def result_kernel(h_ref, summed_ref, weights_ref, owners_ref, fine_ref, out_hbm, out_ref, sem):
    def step(index, carry):
        here = chunk_of(index, CHUNK)
        updated = h_ref[here, :].astype(f32) + dot(summed_ref[here, :], matrix(weights_ref, 2))
        out_ref[here, :] = (updated + owner_rows(owners_ref[here, :], fine_ref[...])).astype(bf16)
        pltpu.make_async_copy(out_ref.at[here, :], out_hbm.at[here, :], sem).start()
        return carry

    lax.fori_loop(0, h_ref.shape[0] // CHUNK, step, None)
    pltpu.make_async_copy(out_ref, out_hbm, sem).wait()


def fine_backward_kernel(
    h_ref,
    first_ref,
    second_ref,
    g_ref,
    summed_ref,
    slope_hbm,
    matrices_ref,
    columns_ref,
    owners_ref,
    part_ref,
    counts_ref,
    coarse_downs_ref,
    first_back_ref,
    second_back_ref,
    sends_ref,
    coarse_weights_ref,
    ups_ref,
    downs_ref,
    first_grad_ref,
    second_grad_ref,
    weights_ref,
    grad_sum,
    halo_grad,
    mean,
    slope_ref,
    slope_sems,
):
    count = STEP * BLOCK
    steps = h_ref.shape[0] // count

    def slope_copy(index):
        edge = chunk_of(index, 8 * count)
        return pltpu.make_async_copy(
            slope_hbm.at[edge, :], slope_ref.at[edge, :], slope_sems.at[index]
        )

    for index in range(steps):
        slope_copy(index).start()
    halo_rows = first_ref.shape[0]
    coarse_rows = part_ref.shape[0]
    halo_grad[...] = jnp.zeros_like(halo_grad)

    place = lax.broadcasted_iota(jnp.int32, (coarse_rows, sends_ref.shape[1]), 0)
    sends = pick(sends_ref[...] == place)
    back = jnp.concatenate([first_back_ref[...], second_back_ref[...]], 0)
    back = dot_nt(back, matrix(matrices_ref, 4)).astype(bf16)
    plain = jnp.concatenate([matrix(matrices_ref, 3), matrix(matrices_ref, 4)], 1)
    grad_in = part_ref[...] + dot_nt(coarse_downs_ref[...], plain) + dot(sends, back)
    per_row = counts_ref[...].T
    for tile in range(coarse_rows // 128):
        here = slice(tile * 128, (tile + 1) * 128)
        mean[here, :] = (grad_in[here, :] / per_row[:, tile : tile + 1]).astype(bf16)

    def owner_step(index):
        here = chunk_of(index, count)
        grad_up = g_ref[here, :].astype(f32) + owner_rows(owners_ref[here, :], mean[...])
        ups = grad_up.astype(bf16)
        ups_ref[here, :] = ups
        grad_sum[here, :] = (dot_nt(ups, matrix(matrices_ref, 2)) * 0.5).astype(bf16)

    def edge_step(index):
        here = chunk_of(index, count)
        slope_copy(index).wait()
        slope = slope_ref[chunk_of(index, 8 * count), :]
        slopes = [slope[n * 8 * BLOCK : (n + 1) * 8 * BLOCK] for n in range(STEP)]
        downs_ref[here, :] = edges_back(
            slopes, grad_sum[here, :], columns_ref[:, here], halo_grad
        )

    owner_step(0)

    def step(index, carry):
        edge_step(index)
        owner_step(index + 1)
        return carry

    lax.fori_loop(0, steps - 1, step, None)
    edge_step(steps - 1)
    first_grad = halo_grad[:halo_rows, :].astype(bf16)
    second_grad = halo_grad[halo_rows:, :].astype(bf16)
    first_grad_ref[...] = first_grad
    second_grad_ref[...] = second_grad
    pair_grad = dot_tn(h_ref[...], downs_ref[...])
    weights_ref[0:128, :] = pair_grad[:, :128].astype(bf16)
    weights_ref[128:256, :] = (
        pair_grad[:, 128:]
        + dot_tn(first_ref[...], first_grad)
        + dot_tn(second_ref[...], second_grad)
    ).astype(bf16)
    weights_ref[256:384, :] = dot_tn(summed_ref[...], ups_ref[...]).astype(bf16)
    weights_ref[384:512, :] = coarse_weights_ref[...]


def finish_kernel(
    ups_ref,
    downs_ref,
    first_back_ref,
    second_back_ref,
    sends_ref,
    matrices_ref,
    out_hbm,
    out_ref,
    sem,
):
    other = matrix(matrices_ref, 1)
    plain = jnp.concatenate([matrix(matrices_ref, 0), other], 1)
    back = jnp.concatenate([first_back_ref[...], second_back_ref[...]], 0)
    back = dot_nt(back, other).astype(bf16)
    sends = sends_ref[...]
    place = lax.broadcasted_iota(jnp.int32, (256, sends.shape[1]), 0).astype(bf16)

    def step(index, carry):
        here = chunk_of(index, CHUNK)
        rows = []
        for part in range(CHUNK // 256):
            local = (sends - (index * CHUNK + 256 * part)).astype(f32)
            rows.append(pick16(jnp.broadcast_to(local, place.shape).astype(bf16), place))
        grad = ups_ref[here, :].astype(f32) + dot_nt(downs_ref[here, :], plain)
        out_ref[here, :] = (grad + dot(jnp.concatenate(rows, 0), back)).astype(bf16)
        pltpu.make_async_copy(out_ref.at[here, :], out_hbm.at[here, :], sem).start()
        return carry

    lax.fori_loop(0, ups_ref.shape[0] // CHUNK, step, None)
    pltpu.make_async_copy(out_ref, out_hbm, sem).wait()


def add_kernel(mine_ref, theirs_ref, *rest):
    out_ref = rest[-1]
    out_ref[...] = (mine_ref[...].astype(f32) + theirs_ref[...].astype(f32)).astype(bf16)


def add_gather_kernel(mine_ref, theirs_ref, after_ref, out_ref):
    mine, theirs = mine_ref[...].astype(f32), theirs_ref[...].astype(f32)
    out_ref[:384, :] = mine[:384] + theirs[:384]
    out_ref[384:512, :] = mine[384:]
    out_ref[512:, :] = theirs[384:]


def weights_kernel(place_ref, mine_ref, theirs_ref, out_ref):
    out_ref[:384, :] = mine_ref[:384, :] + theirs_ref[:384, :]
    group = place_ref[1]
    low, high = lax.rem(group, 2), group // 2
    for n in range(4):
        row = jnp.where(high == n // 2, 384, 512)
        here = pl.ds(pl.multiple_of(row, 128), 128)
        value = jnp.where(low == n % 2, mine_ref[here, :], theirs_ref[here, :])
        out_ref[384 + 128 * n : 512 + 128 * n, :] = value


def exchange(first, second):
    count = lax.axis_size("sub")
    routes = []
    for start in range(2):
        pairs = [(i, i + 1) for i in range(start, count - 1, 2)]
        routes.append(pairs + [(j, i) for i, j in pairs])
    return lax.ppermute(first, "sub", routes[0]), lax.ppermute(second, "sub", routes[1])


def swapped(block, axis, distance):
    return lax.ppermute(block, axis, [(i, i ^ distance) for i in range(lax.axis_size(axis))])


def total_weights(weights, place, after, last):
    distance, number = 1, 0
    while distance < lax.axis_size("sub"):
        theirs = swapped(weights, "sub", distance)
        waits = after[number] if number < len(after) else ()
        weights = call(
            add_kernel,
            shape(*weights.shape, bf16),
            [weights, theirs, *waits],
            [VMEM, VMEM] + [HBM] * len(waits),
        )
        distance, number = 2 * distance, number + 1
    weights = call(
        add_gather_kernel,
        shape(640, 128, f32),
        [weights, swapped(weights, "grp", 2), last],
        [VMEM, VMEM, HBM],
    )
    return call(
        weights_kernel,
        shape(896, 128, f32),
        [place, weights, swapped(weights, "grp", 1)],
        [SMEM, VMEM, VMEM],
    )


def per_device(
    states,
    cotangent,
    fine_self,
    fine_other,
    fine_node,
    coarse_self,
    coarse_other,
    coarse_node,
    prolong,
    fine_nbr,
    fine_mask,
    fine_send_lo,
    fine_send_hi,
    coarse_nbr,
    coarse_mask,
    coarse_send_lo,
    coarse_send_hi,
    coarse_owner,
):
    rows, features = states.shape
    coarse_rows = coarse_nbr.shape[0]
    halo_rows = fine_send_lo.shape[0]
    coarse_halo = coarse_send_lo.shape[0]
    count_rows = coarse_rows // 128
    owner = coarse_owner.reshape(rows // 128, 128)
    place = jnp.stack([1 - lax.rem(lax.axis_index("sub"), 2), lax.axis_index("grp")])

    def buffer(count, columns, dtype):
        return pltpu.VMEM((count, columns), dtype)

    to_first, to_second, states = gather_rows(place, states, fine_send_lo, fine_send_hi)
    first, second = exchange(to_first, to_second)

    (
        counts, columns, columns_t, coarse_columns, coarse_columns_t, cotangent, matrices, sends,
        coarse_sends, owner,
    ) = call(
        functools.partial(prepare_kernel, halo_rows=halo_rows, coarse_halo=coarse_halo),
        [
            shape(2 * count_rows, features, bf16),
            shape(8, rows, f32),
            shape(rows, 8, f32),
            shape(8, coarse_rows, f32),
            shape(coarse_rows, 8, f32),
            shape(rows, features, bf16),
            shape(7 * features, features, bf16),
            shape(1, 2 * halo_rows, jnp.int32),
            shape(1, 2 * coarse_halo, jnp.int32),
            shape(rows // 128, 128, jnp.int32),
        ],
        [
            place, cotangent, owner, fine_nbr.T, fine_mask.T, coarse_nbr.T, coarse_mask.T,
            fine_send_lo[None], fine_send_hi[None], coarse_send_lo[None], coarse_send_hi[None],
            fine_self, fine_other, fine_node, coarse_self, coarse_other, coarse_node, prolong,
            to_first,
        ],
        [SMEM] + [HBM] * 17 + [ANY],
        [buffer(8, rows, jnp.int32)] * 2
        + [buffer(8, coarse_rows, jnp.int32)] * 2
        + [buffer(1, halo_rows, jnp.int32)] * 2
        + [buffer(1, coarse_halo, jnp.int32)] * 2
        + [pltpu.SemaphoreType.DMA((17,))],
    )

    half_rows = coarse_rows // 2 + 2 * count_rows
    summed, slope, new, give = call(
        fine_forward_kernel,
        [
            shape(rows, features, bf16),
            pltpu.HBM((8 * rows, features), bf16),
            shape(rows, features, bf16),
            shape(half_rows, features, bf16),
        ],
        [place, states, first, second, matrices, columns_t, owner, counts],
        [SMEM] + [VMEM] * 7,
        [
            buffer(rows, features, f32),
            buffer(rows, features, bf16),
            buffer(2 * halo_rows, features, bf16),
            buffer(8 * rows, features, bf16),
            pltpu.SemaphoreType.DMA,
        ],
        [VMEM, HBM, VMEM, VMEM],
        mib=32,
    )
    theirs = swapped(give, "grp", 1)
    keep = call(
        keep_kernel,
        shape(half_rows, features, bf16),
        [place, owner, new, counts],
        [SMEM] + [VMEM] * 3,
    )
    chip_totals = call(add_kernel, shape(half_rows, features, bf16), [keep, theirs])
    more_totals = swapped(chip_totals, "grp", 2)
    sums = call(
        sums_kernel,
        shape(coarse_rows, features, bf16),
        [owner, cotangent, chip_totals],
        [VMEM, VMEM, ANY],
    )
    more_sums = swapped(sums, "grp", 1)
    owners_t = call(owners_kernel, shape(rows, 8, f32), [owner, sums], [VMEM, ANY])

    half, counts = call(
        half_kernel,
        [shape(coarse_rows // 2, features, bf16), shape(count_rows, features, f32)],
        [place, chip_totals, more_totals, sums],
        [SMEM, VMEM, VMEM, ANY],
    )
    their_half = swapped(half, "grp", 1)
    coarse_in, to_first, to_second, chip_sums = call(
        coarse_input_kernel,
        [
            shape(coarse_rows, features, bf16),
            shape(coarse_halo, features, bf16),
            shape(coarse_halo, features, bf16),
            shape(coarse_rows, features, bf16),
        ],
        [place, half, their_half, sums, more_sums, coarse_sends],
        [SMEM] + [VMEM] * 5,
    )
    coarse_first, coarse_second = exchange(to_first, to_second)
    more_sums = swapped(chip_sums, "grp", 2)

    coarse_sum, coarse_slope = call(
        coarse_forward_kernel,
        [shape(coarse_rows, features, bf16), shape(8 * coarse_rows, features, bf16)],
        [coarse_in, coarse_first, coarse_second, matrices, coarse_columns_t],
        scratch=[
            buffer(coarse_rows, features, f32),
            buffer(coarse_rows, features, bf16),
            buffer(2 * coarse_halo, features, bf16),
        ],
    )
    coarse_part, first_grad, second_grad, sums, coarse_ups, coarse_downs = call(
        coarse_backward_kernel,
        [
            shape(coarse_rows, features, f32),
            shape(coarse_halo, features, bf16),
            shape(coarse_halo, features, bf16),
            shape(coarse_rows, features, bf16),
            shape(coarse_rows, features, bf16),
            shape(coarse_rows, 2 * features, bf16),
        ],
        [coarse_slope, chip_sums, more_sums, matrices, coarse_columns],
        scratch=[
            buffer(coarse_rows, features, bf16),
            buffer(2 * coarse_halo, features, f32),
        ],
    )
    first_back, second_back = exchange(first_grad, second_grad)

    fine_term, coarse_weights = call(
        coarse_tail_kernel,
        [shape(coarse_rows, features, bf16), shape(features, features, bf16)],
        [
            place, coarse_in, coarse_first, coarse_second, sums, matrices,
            first_grad, second_grad, coarse_sum, coarse_ups, coarse_downs,
        ],
        [SMEM] + [VMEM] * 10,
    )
    result = call(
        result_kernel,
        pltpu.HBM((rows, features), bf16),
        [states, summed, matrices, owners_t, fine_term],
        scratch=[buffer(rows, features, bf16), pltpu.SemaphoreType.DMA],
        out_specs=HBM,
    )

    ups, downs, first_grad, second_grad, weights = call(
        fine_backward_kernel,
        [
            shape(rows, features, bf16),
            shape(rows, 2 * features, bf16),
            shape(halo_rows, features, bf16),
            shape(halo_rows, features, bf16),
            shape(4 * features, features, bf16),
        ],
        [
            states, first, second, cotangent, summed, slope, matrices, columns, owners_t,
            coarse_part, counts, coarse_downs, first_back, second_back, coarse_sends,
            coarse_weights,
        ],
        [VMEM] * 5 + [HBM] + [VMEM] * 10,
        [
            buffer(rows, features, bf16),
            buffer(2 * halo_rows, features, f32),
            buffer(coarse_rows, features, bf16),
            buffer(8 * rows, features, bf16),
            pltpu.SemaphoreType.DMA((rows // (STEP * BLOCK),)),
        ],
        mib=32,
    )
    first_back, second_back = exchange(first_grad, second_grad)

    grad_states = call(
        finish_kernel,
        pltpu.HBM((rows, features), bf16),
        [ups, downs, first_back, second_back, sends, matrices],
        scratch=[buffer(rows, features, bf16), pltpu.SemaphoreType.DMA],
        out_specs=HBM,
    )
    grad_weights = total_weights(weights, place, ((), (), (grad_states,)), result)
    return (result, grad_states, grad_weights.reshape(7, features, features))


def solution(mesh):
    fine = P(("grp", "sub"), None)
    fine_row = P(("grp", "sub"))
    in_specs = (
        (fine, fine)
        + (P(),) * 7
        + (fine, fine, fine_row, fine_row)
        + (P("sub", None), P("sub", None), P("sub"), P("sub"), fine_row)
    )
    return jax.shard_map(
        per_device, mesh=mesh, in_specs=in_specs, out_specs=(fine, fine, P()), check_vma=False
    )
```

```python
import functools

import jax
import jax.numpy as jnp
from jax import lax
from jax.experimental import pallas as pl
from jax.experimental.pallas import tpu as pltpu
from jax.sharding import PartitionSpec as P

f32 = jnp.float32
bf16 = jnp.bfloat16
BLOCK = 64
PAIR = 2 * BLOCK
STEP = 16
CHUNK = 1024
NEVER = -1e30
DIGIT = 64.0
VMEM = pl.BlockSpec(memory_space=pltpu.VMEM)
SMEM = pl.BlockSpec(memory_space=pltpu.SMEM)
ANY = pl.BlockSpec(memory_space=pl.ANY)
HBM = pl.BlockSpec(memory_space=pltpu.HBM)
MIB = 1024 * 1024


def dot(a, b):
    return jnp.dot(a, b, preferred_element_type=f32)


def dot_nt(a, b):
    return lax.dot_general(a, b, (((1,), (1,)), ((), ())), preferred_element_type=f32)


def dot_tn(a, b):
    return lax.dot_general(a, b, (((0,), (0,)), ((), ())), preferred_element_type=f32)


def pick(condition):
    return jnp.where(condition, 1.0, 0.0).astype(bf16)


def pick16(values, places):
    return jnp.where(values == places, jnp.ones((), bf16), jnp.zeros((), bf16))


def call(kernel, out_shape, args, in_specs=None, scratch=(), out_specs=None, mib=16):
    many = isinstance(out_shape, (list, tuple))
    in_specs = in_specs or [VMEM] * len(args)
    args = [
        pltpu.with_memory_space_constraint(arg, pltpu.HBM) if spec is HBM else arg
        for arg, spec in zip(args, in_specs)
    ]
    return pl.pallas_call(
        kernel,
        out_shape=out_shape,
        in_specs=in_specs,
        out_specs=out_specs or ([VMEM] * len(out_shape) if many else VMEM),
        scratch_shapes=list(scratch),
        compiler_params=pltpu.CompilerParams(vmem_limit_bytes=mib * MIB),
    )(*args)


def shape(rows, columns, dtype):
    return jax.ShapeDtypeStruct((rows, columns), dtype)


def slot_columns(nbr, mask, halo_rows, even):
    rows = nbr.shape[1]
    block = lax.broadcasted_iota(jnp.int32, nbr.shape, 1) // BLOCK
    halo = lax.rem(block, halo_rows // BLOCK) * BLOCK
    lower = jnp.where(even, 2 * BLOCK, BLOCK)
    column = jnp.where(
        nbr < rows,
        nbr - block * BLOCK,
        jnp.where(
            nbr < rows + halo_rows,
            lower + nbr - rows - halo,
            3 * BLOCK - lower + nbr - rows - halo_rows - halo,
        ),
    )
    return jnp.where(mask > 0, column, 3 * BLOCK).astype(f32)


def selector(columns_t):
    first = lax.broadcasted_iota(jnp.int32, (BLOCK, 128), 1).astype(bf16)
    second = (lax.broadcasted_iota(jnp.int32, (BLOCK, 128), 1) + 128).astype(bf16)
    parts = []
    for k in range(8):
        wide = jnp.broadcast_to(columns_t[:, k : k + 1], (BLOCK, 128)).astype(bf16)
        parts.append(jnp.concatenate([pick16(wide, first), pick16(wide, second)], 1))
    return jnp.concatenate(parts, 0)


def selector_t(columns, rolled, half):
    lane = lax.broadcasted_iota(jnp.int32, (1, 128), 1)
    place = lax.broadcasted_iota(jnp.int32, (3 * BLOCK, 128), 0).astype(bf16)
    parts = []
    for j in range(4):
        left, right = (columns, rolled) if half == 0 else (rolled, columns)
        row = jnp.where(lane < BLOCK, left[2 * j : 2 * j + 1], right[2 * j + 1 : 2 * j + 2])
        wide = jnp.broadcast_to(row, (3 * BLOCK, 128)).astype(bf16)
        parts.append(pick16(wide, place))
    return jnp.concatenate(parts, 1)


def window_of(far, halo, place):
    halo_rows = halo.shape[0] // 2
    start = place * BLOCK
    return jnp.concatenate(
        [
            far,
            halo[start : start + BLOCK, :],
            halo[halo_rows + start : halo_rows + start + BLOCK, :],
            jnp.full((BLOCK, far.shape[1]), NEVER, bf16),
        ],
        0,
    )


def chunk_of(index, count):
    return pl.ds(pl.multiple_of(index * count, count), count)


def matrix(weights_ref, n):
    return weights_ref[128 * n : 128 * (n + 1), :]


def level_terms(h_ref, halo_refs, self_weight, other_weight, own, far, halo):
    halo_rows = halo_refs[0].shape[0]
    other = other_weight * 0.5
    terms = dot(h_ref[...], jnp.concatenate([self_weight * 0.5, other], 1))
    own[...] = terms[:, :128]
    far[...] = terms[:, 128:].astype(bf16)
    halo[:halo_rows, :] = dot(halo_refs[0][...], other).astype(bf16)
    halo[halo_rows:, :] = dot(halo_refs[1][...], other).astype(bf16)


def edges(own_rows, far_rows, slots, halo):
    places = halo.shape[0] // (2 * BLOCK)
    assert STEP % places == 0
    tables = []
    for n in range(STEP):
        part = slice(n * BLOCK, (n + 1) * BLOCK)
        window = window_of(far_rows[part], halo, n % places)
        tables.append(dot(selector(slots[part]), window))
    sums, slopes = [], []
    for n, picked in enumerate(tables):
        own = own_rows[n * BLOCK : (n + 1) * BLOCK]
        values, pieces = [], []
        for k in range(8):
            y = (picked[k * BLOCK : (k + 1) * BLOCK] + own).astype(bf16)
            t = jnp.tanh(y)
            bent = y * t
            values.append(y + bent)
            pieces.append((1 + t) * (1 + (y - bent)))
        while len(values) > 1:
            values = [left + right for left, right in zip(values[::2], values[1::2])]
        sums.append(values[0])
        slopes.append(jnp.concatenate(pieces, 0))
    return jnp.concatenate(sums, 0), slopes


def edges_back(slopes, grad_sum, columns, halo_grad):
    places = halo_grad.shape[0] // (2 * BLOCK)
    halo_rows = halo_grad.shape[0] // 2
    windows, downs = [], []
    for n, slope in enumerate(slopes):
        part = grad_sum[n * BLOCK : (n + 1) * BLOCK]
        grads = [slope[k * BLOCK : (k + 1) * BLOCK] * part for k in range(8)]
        downs.append(sum(grad.astype(f32) for grad in grads))
        mine = columns[:, n // 2 * PAIR : (n // 2 + 1) * PAIR]
        selected = selector_t(mine, pltpu.roll(mine, BLOCK, 1), n % 2)
        windows.append(dot(selected, jnp.concatenate(grads, 0)))
    for place in range(places):
        for side in range(2):
            start = side * halo_rows + place * BLOCK
            total = halo_grad[start : start + BLOCK, :]
            for window in windows[place::places]:
                total = total + window[(side + 1) * BLOCK : (side + 2) * BLOCK]
            halo_grad[start : start + BLOCK, :] = total
    local = jnp.concatenate([window[:BLOCK] for window in windows], 0)
    down = jnp.concatenate(downs, 0)
    return jnp.concatenate([down, local], 1).astype(bf16)


def fetch(pairs, sems):
    copies = [pltpu.make_async_copy(src, dst, sems.at[n]) for n, (src, dst) in enumerate(pairs)]
    for copy in copies:
        copy.start()
    for copy in copies:
        copy.wait()


def gather_kernel(
    place_ref, lo_hbm, hi_hbm, x_hbm, first_ref, second_ref, x_ref, wide, up, down, lo, hi, sems
):
    fetch([(x_hbm, x_ref), (lo_hbm, lo), (hi_hbm, hi)], sems)
    wide[...] = x_ref[...].astype(f32)

    def step(r, carry):
        up[pl.ds(r, 1), :] = wide[pl.ds(hi[r], 1), :]
        down[pl.ds(r, 1), :] = wide[pl.ds(lo[r], 1), :]
        return carry

    lax.fori_loop(0, up.shape[0], step, None, unroll=16)
    even = place_ref[0] > 0
    first_ref[...] = jnp.where(even, up[...], down[...]).astype(bf16)
    second_ref[...] = jnp.where(even, down[...], up[...]).astype(bf16)


def gather_rows(place, x, send_lo, send_hi):
    rows, features = x.shape
    count = send_lo.shape[0]
    out = shape(count, features, bf16)
    return call(
        gather_kernel,
        [out, out, shape(rows, features, bf16)],
        [place, send_lo, send_hi, x],
        [SMEM, HBM, HBM, HBM],
        [
            pltpu.VMEM((rows, features), f32),
            pltpu.VMEM((count, features), f32),
            pltpu.VMEM((count, features), f32),
            pltpu.SMEM((count,), jnp.int32),
            pltpu.SMEM((count,), jnp.int32),
            pltpu.SemaphoreType.DMA((3,)),
        ],
    )


def owner_sums(owner_ref, tile, values):
    place = lax.broadcasted_iota(jnp.int32, (256, 128), 0).astype(bf16)
    owner = (owner_ref[...] - tile * 256).astype(f32)
    rows = jnp.concatenate(
        [
            pick16(jnp.broadcast_to(owner[q : q + 1], (256, 128)).astype(bf16), place)
            for q in range(owner.shape[0])
        ],
        1,
    )
    return dot(rows, values)


def prepare_kernel(
    place_ref,
    g_hbm,
    owner_hbm,
    nbr_hbm,
    mask_hbm,
    coarse_nbr_hbm,
    coarse_mask_hbm,
    lo_hbm,
    hi_hbm,
    coarse_lo_hbm,
    coarse_hi_hbm,
    *rest,
    halo_rows,
    coarse_halo,
):
    weight_hbms, rest = rest[:7], rest[7:]
    (
        after_ref,
        counts_ref,
        columns_ref,
        columns_t_ref,
        coarse_columns_ref,
        coarse_columns_t_ref,
        g_ref,
        weights_ref,
        sends_ref,
        coarse_sends_ref,
        owner_ref,
        nbr_ref,
        mask_ref,
        coarse_nbr_ref,
        coarse_mask_ref,
        lo_ref,
        hi_ref,
        coarse_lo_ref,
        coarse_hi_ref,
        sems,
    ) = rest
    fetch(
        [
            (g_hbm, g_ref),
            (owner_hbm, owner_ref),
            (nbr_hbm, nbr_ref),
            (mask_hbm, mask_ref),
            (coarse_nbr_hbm, coarse_nbr_ref),
            (coarse_mask_hbm, coarse_mask_ref),
            (lo_hbm, lo_ref),
            (hi_hbm, hi_ref),
            (coarse_lo_hbm, coarse_lo_ref),
            (coarse_hi_hbm, coarse_hi_ref),
        ]
        + [(w, weights_ref.at[pl.ds(128 * n, 128), :]) for n, w in enumerate(weight_hbms)],
        sems,
    )
    even = place_ref[0] > 0
    for low, high, out in (
        (lo_ref, hi_ref, sends_ref),
        (coarse_lo_ref, coarse_hi_ref, coarse_sends_ref),
    ):
        first = jnp.where(even, high[...], low[...])
        second = jnp.where(even, low[...], high[...])
        out[...] = jnp.concatenate([first, second], 1)
    columns_ref[...] = slot_columns(nbr_ref[...], mask_ref[...], halo_rows, even)
    columns_t_ref[...] = columns_ref[...].T
    coarse_columns_ref[...] = slot_columns(
        coarse_nbr_ref[...], coarse_mask_ref[...], coarse_halo, even
    )
    coarse_columns_t_ref[...] = coarse_columns_ref[...].T
    tiles = counts_ref.shape[0] // 2
    owner = owner_ref[...]
    high, low = owner // 128, lax.rem(owner, 128)
    groups = owner.shape[0]
    place = lax.broadcasted_iota(jnp.int32, (128, 128), 0)
    high_rows = jnp.concatenate(
        [pick(high[q : q + 1, :] == place[:tiles]) for q in range(groups)], 1
    )
    low_rows = jnp.concatenate(
        [pick(low[q : q + 1, :] == place) for q in range(groups)], 1
    )
    counts = dot_nt(high_rows, low_rows)
    most = jnp.floor(counts * (1 / DIGIT))
    counts_ref[...] = jnp.concatenate([most, counts - DIGIT * most], 0).astype(bf16)


def sums_kernel(owner_ref, g_ref, after_ref, sums_ref):
    def step(tile, carry):
        sums_ref[chunk_of(tile, 256), :] = owner_sums(owner_ref, tile, g_ref[...]).astype(bf16)
        return carry

    lax.fori_loop(0, sums_ref.shape[0] // 256, step, None)


def relay_kernel(x_ref, after_ref, also_after_ref, out_ref):
    out_ref[...] = x_ref[...]


def owners_kernel(owner_ref, after_ref, owners_ref):
    owners_ref[...] = owner_columns(owner_ref)


def half_totals(owner_ref, new_ref, counts_ref, half, out_ref):
    tiles = (out_ref.shape[0] - counts_ref.shape[0]) // 256
    for tile in range(tiles):
        totals = owner_sums(owner_ref, half * tiles + tile, new_ref[...])
        out_ref[256 * tile : 256 * (tile + 1), :] = totals.astype(bf16)
    out_ref[256 * tiles :, :] = counts_ref[...]


def keep_kernel(place_ref, owner_ref, new_ref, counts_ref, out_ref):
    half_totals(owner_ref, new_ref, counts_ref, lax.rem(place_ref[1], 2), out_ref)


def forward_steps(own, far, halo, columns_t_ref, first_row, summed_ref, slope_ref, slope_hbm, sem):
    def step(index, carry):
        here = chunk_of(index, STEP * BLOCK)
        there = pl.ds(pl.multiple_of(first_row + index * STEP * BLOCK, BLOCK), STEP * BLOCK)
        total, slopes = edges(own[here, :], far[here, :], columns_t_ref[there, :], halo)
        summed_ref[there, :] = total
        edge = chunk_of(index, 8 * STEP * BLOCK)
        slope_ref[edge, :] = jnp.concatenate(slopes, 0)
        pltpu.make_async_copy(slope_ref.at[edge, :], slope_hbm.at[edge, :], sem).start()
        return carry

    lax.fori_loop(0, own.shape[0] // (STEP * BLOCK), step, None)


def early_forward_kernel(
    h_ref,
    first_ref,
    second_ref,
    weights_ref,
    columns_t_ref,
    after_ref,
    summed_ref,
    slope_hbm,
    own,
    far,
    halo,
    slope_ref,
    sem,
):
    self_weight, other_weight = matrix(weights_ref, 0), matrix(weights_ref, 1)
    h = h_ref.at[: own.shape[0], :]
    level_terms(h, (first_ref, second_ref), self_weight, other_weight, own, far, halo)
    forward_steps(own, far, halo, columns_t_ref, 0, summed_ref, slope_ref, slope_hbm, sem)
    pltpu.make_async_copy(slope_ref, slope_hbm, sem).wait()


def late_forward_kernel(
    place_ref,
    h_ref,
    first_ref,
    second_ref,
    weights_ref,
    columns_t_ref,
    owner_ref,
    counts_ref,
    early_ref,
    after_ref,
    summed_ref,
    slope_hbm,
    new_ref,
    give_ref,
    own,
    far,
    halo,
    slope_ref,
    sem,
):
    half = own.shape[0]
    self_weight, other_weight = matrix(weights_ref, 0), matrix(weights_ref, 1)
    h = h_ref.at[half:, :]
    level_terms(h, (first_ref, second_ref), self_weight, other_weight, own, far, halo)
    summed_ref[:half, :] = early_ref[...]
    forward_steps(own, far, halo, columns_t_ref, half, summed_ref, slope_ref, slope_hbm, sem)
    new_ref[...] = (
        h_ref[...].astype(f32) + dot(summed_ref[...], matrix(weights_ref, 2))
    ).astype(bf16)
    half_totals(owner_ref, new_ref, counts_ref, 1 - lax.rem(place_ref[1], 2), give_ref)
    pltpu.make_async_copy(slope_ref, slope_hbm, sem).wait()


def half_kernel(place_ref, totals_ref, more_totals_ref, after_ref, half_ref, counts_ref):
    half_rows = half_ref.shape[0]
    totals = totals_ref[...].astype(f32) + more_totals_ref[...].astype(f32)
    digits = totals[half_rows:]
    tiles = counts_ref.shape[0]
    counts_ref[...] = DIGIT * digits[:tiles] + digits[tiles:]
    per_row = counts_ref[...].T
    first = lax.rem(place_ref[1], 2) == 0
    for tile in range(tiles // 2):
        here = slice(tile * 128, (tile + 1) * 128)
        later = tile + tiles // 2
        count = jnp.where(first, per_row[:, tile : tile + 1], per_row[:, later : later + 1])
        half_ref[here, :] = (totals[here] / count).astype(bf16)


def coarse_input_kernel(
    place_ref,
    half_ref,
    their_half_ref,
    sends_ref,
    cin_ref,
    first_ref,
    second_ref,
):
    mine, theirs = half_ref[...], their_half_ref[...]
    first = lax.rem(place_ref[1], 2) == 0
    cin = jnp.concatenate([jnp.where(first, mine, theirs), jnp.where(first, theirs, mine)], 0)
    cin_ref[...] = cin
    place = lax.broadcasted_iota(jnp.int32, (cin.shape[0], sends_ref.shape[1]), 0)
    sent = dot_tn(pick(sends_ref[...] == place), cin).astype(bf16)
    halo_rows = first_ref.shape[0]
    first_ref[...] = sent[:halo_rows]
    second_ref[...] = sent[halo_rows:]


def coarse_forward_kernel(
    cin_ref,
    first_ref,
    second_ref,
    weights_ref,
    columns_t_ref,
    summed_ref,
    slope_ref,
    own,
    far,
    halo,
):
    self_weight, other_weight = matrix(weights_ref, 3), matrix(weights_ref, 4)
    level_terms(cin_ref, (first_ref, second_ref), self_weight, other_weight, own, far, halo)

    def step(index, carry):
        here = chunk_of(index, STEP * BLOCK)
        total, slopes = edges(own[here, :], far[here, :], columns_t_ref[here, :], halo)
        summed_ref[here, :] = total
        slope_ref[chunk_of(index, 8 * STEP * BLOCK), :] = jnp.concatenate(slopes, 0)
        return carry

    lax.fori_loop(0, cin_ref.shape[0] // (STEP * BLOCK), step, None)


def coarse_backward_kernel(
    slope_ref,
    chip_sums_ref,
    more_sums_ref,
    weights_ref,
    columns_ref,
    part_ref,
    first_grad_ref,
    second_grad_ref,
    sums_ref,
    ups_ref,
    downs_ref,
    grad_sum,
    halo_grad,
):
    halo_rows = first_grad_ref.shape[0]
    halo_grad[...] = jnp.zeros_like(halo_grad)
    sums_ref[...] = (chip_sums_ref[...].astype(f32) + more_sums_ref[...].astype(f32)).astype(bf16)
    part_ref[...] = dot_nt(sums_ref[...], matrix(weights_ref, 6))
    ups_ref[...] = part_ref[...].astype(bf16)
    grad_sum[...] = (dot_nt(ups_ref[...], matrix(weights_ref, 5)) * 0.5).astype(bf16)
    count = STEP * BLOCK

    def step(index, carry):
        here = chunk_of(index, count)
        slope = slope_ref[chunk_of(index, 8 * count), :]
        slopes = [slope[n * 8 * BLOCK : (n + 1) * 8 * BLOCK] for n in range(STEP)]
        downs_ref[here, :] = edges_back(
            slopes, grad_sum[here, :], columns_ref[:, here], halo_grad
        )
        return carry

    lax.fori_loop(0, part_ref.shape[0] // count, step, None)
    first_grad_ref[...] = halo_grad[:halo_rows, :].astype(bf16)
    second_grad_ref[...] = halo_grad[halo_rows:, :].astype(bf16)


def coarse_tail_kernel(
    place_ref,
    cin_ref,
    first_ref,
    second_ref,
    sums_ref,
    matrices_ref,
    first_grad_ref,
    second_grad_ref,
    summed_ref,
    ups_ref,
    downs_ref,
    fine_ref,
    weights_ref,
):
    cin = cin_ref[...]
    out = (cin.astype(f32) + dot(summed_ref[...], matrix(matrices_ref, 5))).astype(bf16)
    fine_ref[...] = dot(out, matrix(matrices_ref, 6)).astype(bf16)
    pair_grad = dot_tn(cin, downs_ref[...])
    other_grad = (
        pair_grad[:, 128:]
        + dot_tn(first_ref[...], first_grad_ref[...])
        + dot_tn(second_ref[...], second_grad_ref[...])
    )
    grads = [
        pair_grad[:, :128],
        other_grad,
        dot_tn(summed_ref[...], ups_ref[...]),
        dot_tn(out, sums_ref[...]),
    ]
    weights_ref[...] = choose(place_ref[1], grads).astype(bf16)


def choose(place, values):
    picked = values[-1]
    for n, value in enumerate(values[:-1]):
        picked = jnp.where(place == n, value, picked)
    return picked


def owner_columns(owner_ref):
    owner = owner_ref[...].astype(f32)
    row = jnp.concatenate([owner[q : q + 1, :] for q in range(owner.shape[0])], 1)
    return jnp.broadcast_to(row, (8, row.shape[1])).T


def owner_rows(owners, values):
    count = owners.shape[0]
    wide = jnp.broadcast_to(owners[:, 0:1], (count, 128))
    lane = lax.broadcasted_iota(jnp.int32, (count, 128), 1)
    first, second = lane.astype(bf16), (lane + 128).astype(bf16)
    rows = []
    for tile in range(values.shape[0] // 256):
        here = (wide - 256.0 * tile).astype(bf16)
        rows += [pick16(here, first), pick16(here, second)]
    return dot(jnp.concatenate(rows, 1), values)


def result_kernel(h_ref, summed_ref, weights_ref, owners_ref, fine_ref, out_hbm, out_ref, sem):
    def step(index, carry):
        here = chunk_of(index, CHUNK)
        updated = h_ref[here, :].astype(f32) + dot(summed_ref[here, :], matrix(weights_ref, 2))
        out_ref[here, :] = (updated + owner_rows(owners_ref[here, :], fine_ref[...])).astype(bf16)
        pltpu.make_async_copy(out_ref.at[here, :], out_hbm.at[here, :], sem).start()
        return carry

    lax.fori_loop(0, h_ref.shape[0] // CHUNK, step, None)
    pltpu.make_async_copy(out_ref, out_hbm, sem).wait()


def fine_backward_kernel(
    h_ref,
    first_ref,
    second_ref,
    g_ref,
    summed_ref,
    early_slope_hbm,
    late_slope_hbm,
    matrices_ref,
    columns_ref,
    owners_ref,
    part_ref,
    counts_ref,
    coarse_downs_ref,
    first_back_ref,
    second_back_ref,
    sends_ref,
    coarse_weights_ref,
    ups_ref,
    downs_ref,
    first_grad_ref,
    second_grad_ref,
    weights_ref,
    grad_sum,
    halo_grad,
    mean,
    slope_ref,
    slope_sems,
):
    count = STEP * BLOCK
    steps = h_ref.shape[0] // count

    edge_rows = 8 * count
    for index in range(steps):
        late = index >= steps // 2
        source = (late_slope_hbm if late else early_slope_hbm).at[
            pl.ds((index - late * (steps // 2)) * edge_rows, edge_rows), :
        ]
        target = slope_ref.at[pl.ds(index * edge_rows, edge_rows), :]
        pltpu.make_async_copy(source, target, slope_sems.at[index]).start()

    def slope_wait(index):
        edge = chunk_of(index, edge_rows)
        pltpu.make_async_copy(
            slope_ref.at[edge, :], slope_ref.at[edge, :], slope_sems.at[index]
        ).wait()

    halo_rows = first_ref.shape[0]
    coarse_rows = part_ref.shape[0]
    halo_grad[...] = jnp.zeros_like(halo_grad)

    place = lax.broadcasted_iota(jnp.int32, (coarse_rows, sends_ref.shape[1]), 0)
    sends = pick(sends_ref[...] == place)
    back = jnp.concatenate([first_back_ref[...], second_back_ref[...]], 0)
    back = dot_nt(back, matrix(matrices_ref, 4)).astype(bf16)
    plain = jnp.concatenate([matrix(matrices_ref, 3), matrix(matrices_ref, 4)], 1)
    grad_in = part_ref[...] + dot_nt(coarse_downs_ref[...], plain) + dot(sends, back)
    per_row = counts_ref[...].T
    for tile in range(coarse_rows // 128):
        here = slice(tile * 128, (tile + 1) * 128)
        mean[here, :] = (grad_in[here, :] / per_row[:, tile : tile + 1]).astype(bf16)

    def owner_step(index):
        here = chunk_of(index, count)
        grad_up = g_ref[here, :].astype(f32) + owner_rows(owners_ref[here, :], mean[...])
        ups = grad_up.astype(bf16)
        ups_ref[here, :] = ups
        grad_sum[here, :] = (dot_nt(ups, matrix(matrices_ref, 2)) * 0.5).astype(bf16)

    def edge_step(index):
        here = chunk_of(index, count)
        slope_wait(index)
        slope = slope_ref[chunk_of(index, 8 * count), :]
        slopes = [slope[n * 8 * BLOCK : (n + 1) * 8 * BLOCK] for n in range(STEP)]
        downs_ref[here, :] = edges_back(
            slopes, grad_sum[here, :], columns_ref[:, here], halo_grad
        )

    owner_step(0)

    def step(index, carry):
        edge_step(index)
        owner_step(index + 1)
        return carry

    lax.fori_loop(0, steps - 1, step, None)
    edge_step(steps - 1)
    first_grad = halo_grad[:halo_rows, :].astype(bf16)
    second_grad = halo_grad[halo_rows:, :].astype(bf16)
    first_grad_ref[...] = first_grad
    second_grad_ref[...] = second_grad
    pair_grad = dot_tn(h_ref[...], downs_ref[...])
    weights_ref[0:128, :] = pair_grad[:, :128].astype(bf16)
    weights_ref[128:256, :] = (
        pair_grad[:, 128:]
        + dot_tn(first_ref[...], first_grad)
        + dot_tn(second_ref[...], second_grad)
    ).astype(bf16)
    weights_ref[256:384, :] = dot_tn(summed_ref[...], ups_ref[...]).astype(bf16)
    weights_ref[384:512, :] = coarse_weights_ref[...]


def finish_kernel(
    ups_ref,
    downs_ref,
    first_back_ref,
    second_back_ref,
    sends_ref,
    matrices_ref,
    out_hbm,
    out_ref,
    sem,
):
    other = matrix(matrices_ref, 1)
    plain = jnp.concatenate([matrix(matrices_ref, 0), other], 1)
    back = jnp.concatenate([first_back_ref[...], second_back_ref[...]], 0)
    back = dot_nt(back, other).astype(bf16)
    sends = sends_ref[...]
    place = lax.broadcasted_iota(jnp.int32, (256, sends.shape[1]), 0).astype(bf16)

    def step(index, carry):
        here = chunk_of(index, CHUNK)
        rows = []
        for part in range(CHUNK // 256):
            local = (sends - (index * CHUNK + 256 * part)).astype(f32)
            rows.append(pick16(jnp.broadcast_to(local, place.shape).astype(bf16), place))
        grad = ups_ref[here, :].astype(f32) + dot_nt(downs_ref[here, :], plain)
        out_ref[here, :] = (grad + dot(jnp.concatenate(rows, 0), back)).astype(bf16)
        pltpu.make_async_copy(out_ref.at[here, :], out_hbm.at[here, :], sem).start()
        return carry

    lax.fori_loop(0, ups_ref.shape[0] // CHUNK, step, None)
    pltpu.make_async_copy(out_ref, out_hbm, sem).wait()


def add_kernel(mine_ref, theirs_ref, *rest):
    out_ref = rest[-1]
    out_ref[...] = (mine_ref[...].astype(f32) + theirs_ref[...].astype(f32)).astype(bf16)


def add_gather_kernel(mine_ref, theirs_ref, after_ref, out_ref):
    mine, theirs = mine_ref[...].astype(f32), theirs_ref[...].astype(f32)
    out_ref[:384, :] = mine[:384] + theirs[:384]
    out_ref[384:512, :] = mine[384:]
    out_ref[512:, :] = theirs[384:]


def weights_kernel(place_ref, mine_ref, theirs_ref, out_ref):
    out_ref[:384, :] = mine_ref[:384, :] + theirs_ref[:384, :]
    group = place_ref[1]
    low, high = lax.rem(group, 2), group // 2
    for n in range(4):
        row = jnp.where(high == n // 2, 384, 512)
        here = pl.ds(pl.multiple_of(row, 128), 128)
        value = jnp.where(low == n % 2, mine_ref[here, :], theirs_ref[here, :])
        out_ref[384 + 128 * n : 512 + 128 * n, :] = value


def exchange(first, second):
    count = lax.axis_size("sub")
    routes = []
    for start in range(2):
        pairs = [(i, i + 1) for i in range(start, count - 1, 2)]
        routes.append(pairs + [(j, i) for i, j in pairs])
    return lax.ppermute(first, "sub", routes[0]), lax.ppermute(second, "sub", routes[1])


def swapped(block, axis, distance):
    return lax.ppermute(block, axis, [(i, i ^ distance) for i in range(lax.axis_size(axis))])


def total_weights(weights, place, after, last):
    distance, number = 1, 0
    while distance < lax.axis_size("sub"):
        theirs = swapped(weights, "sub", distance)
        waits = after[number] if number < len(after) else ()
        weights = call(
            add_kernel,
            shape(*weights.shape, bf16),
            [weights, theirs, *waits],
            [VMEM, VMEM] + [HBM] * len(waits),
        )
        distance, number = 2 * distance, number + 1
    weights = call(
        add_gather_kernel,
        shape(640, 128, f32),
        [weights, swapped(weights, "grp", 2), last],
        [VMEM, VMEM, HBM],
    )
    return call(
        weights_kernel,
        shape(896, 128, f32),
        [place, weights, swapped(weights, "grp", 1)],
        [SMEM, VMEM, VMEM],
    )


def per_device(
    states,
    cotangent,
    fine_self,
    fine_other,
    fine_node,
    coarse_self,
    coarse_other,
    coarse_node,
    prolong,
    fine_nbr,
    fine_mask,
    fine_send_lo,
    fine_send_hi,
    coarse_nbr,
    coarse_mask,
    coarse_send_lo,
    coarse_send_hi,
    coarse_owner,
):
    rows, features = states.shape
    coarse_rows = coarse_nbr.shape[0]
    halo_rows = fine_send_lo.shape[0]
    coarse_halo = coarse_send_lo.shape[0]
    count_rows = coarse_rows // 128
    owner = coarse_owner.reshape(rows // 128, 128)
    place = jnp.stack([1 - lax.rem(lax.axis_index("sub"), 2), lax.axis_index("grp")])

    def buffer(count, columns, dtype):
        return pltpu.VMEM((count, columns), dtype)

    to_first, to_second, states = gather_rows(place, states, fine_send_lo, fine_send_hi)
    first, second = exchange(to_first, to_second)

    (
        counts, columns, columns_t, coarse_columns, coarse_columns_t, cotangent, matrices, sends,
        coarse_sends, owner,
    ) = call(
        functools.partial(prepare_kernel, halo_rows=halo_rows, coarse_halo=coarse_halo),
        [
            shape(2 * count_rows, features, bf16),
            shape(8, rows, f32),
            shape(rows, 8, f32),
            shape(8, coarse_rows, f32),
            shape(coarse_rows, 8, f32),
            shape(rows, features, bf16),
            shape(7 * features, features, bf16),
            shape(1, 2 * halo_rows, jnp.int32),
            shape(1, 2 * coarse_halo, jnp.int32),
            shape(rows // 128, 128, jnp.int32),
        ],
        [
            place, cotangent, owner, fine_nbr.T, fine_mask.T, coarse_nbr.T, coarse_mask.T,
            fine_send_lo[None], fine_send_hi[None], coarse_send_lo[None], coarse_send_hi[None],
            fine_self, fine_other, fine_node, coarse_self, coarse_other, coarse_node, prolong,
            to_first,
        ],
        [SMEM] + [HBM] * 17 + [ANY],
        [buffer(8, rows, jnp.int32)] * 2
        + [buffer(8, coarse_rows, jnp.int32)] * 2
        + [buffer(1, halo_rows, jnp.int32)] * 2
        + [buffer(1, coarse_halo, jnp.int32)] * 2
        + [pltpu.SemaphoreType.DMA((17,))],
    )

    sums = call(
        sums_kernel,
        shape(coarse_rows, features, bf16),
        [owner, cotangent, sends],
        [VMEM, VMEM, ANY],
    )
    sent_sums = call(
        relay_kernel,
        shape(coarse_rows, features, bf16),
        [sums, first, second],
        [VMEM, ANY, ANY],
    )
    more_sums = swapped(sent_sums, "grp", 1)

    half_rows = coarse_rows // 2 + 2 * count_rows
    forward_scratch = [
        buffer(rows // 2, features, f32),
        buffer(rows // 2, features, bf16),
        buffer(2 * halo_rows, features, bf16),
        buffer(4 * rows, features, bf16),
        pltpu.SemaphoreType.DMA,
    ]
    summed, early_slope = call(
        early_forward_kernel,
        [shape(rows // 2, features, bf16), pltpu.HBM((4 * rows, features), bf16)],
        [states, first, second, matrices, columns_t, sums],
        [VMEM] * 5 + [ANY],
        forward_scratch,
        [VMEM, HBM],
        mib=24,
    )
    chip_sums = call(
        add_kernel,
        shape(coarse_rows, features, bf16),
        [sums, more_sums, summed],
        [VMEM, VMEM, ANY],
    )
    more_sums = swapped(chip_sums, "grp", 2)
    summed, late_slope, new, give = call(
        late_forward_kernel,
        [
            shape(rows, features, bf16),
            pltpu.HBM((4 * rows, features), bf16),
            shape(rows, features, bf16),
            shape(half_rows, features, bf16),
        ],
        [
            place, states, first, second, matrices, columns_t, owner, counts, summed, chip_sums,
        ],
        [SMEM] + [VMEM] * 8 + [ANY],
        forward_scratch,
        [VMEM, HBM, VMEM, VMEM],
        mib=24,
    )
    theirs = swapped(give, "grp", 1)
    keep = call(
        keep_kernel,
        shape(half_rows, features, bf16),
        [place, owner, new, counts],
        [SMEM] + [VMEM] * 3,
    )
    chip_totals = call(
        add_kernel,
        shape(half_rows, features, bf16),
        [keep, theirs, more_sums],
        [VMEM, VMEM, ANY],
    )
    more_totals = swapped(chip_totals, "grp", 2)
    owners_t = call(owners_kernel, shape(rows, 8, f32), [owner, chip_totals], [VMEM, ANY])

    half, counts = call(
        half_kernel,
        [shape(coarse_rows // 2, features, bf16), shape(count_rows, features, f32)],
        [place, chip_totals, more_totals, owners_t],
        [SMEM, VMEM, VMEM, ANY],
    )
    their_half = swapped(half, "grp", 1)
    coarse_in, to_first, to_second = call(
        coarse_input_kernel,
        [
            shape(coarse_rows, features, bf16),
            shape(coarse_halo, features, bf16),
            shape(coarse_halo, features, bf16),
        ],
        [place, half, their_half, coarse_sends],
        [SMEM] + [VMEM] * 3,
    )
    coarse_first, coarse_second = exchange(to_first, to_second)

    coarse_sum, coarse_slope = call(
        coarse_forward_kernel,
        [shape(coarse_rows, features, bf16), shape(8 * coarse_rows, features, bf16)],
        [coarse_in, coarse_first, coarse_second, matrices, coarse_columns_t],
        scratch=[
            buffer(coarse_rows, features, f32),
            buffer(coarse_rows, features, bf16),
            buffer(2 * coarse_halo, features, bf16),
        ],
    )
    coarse_part, first_grad, second_grad, sums, coarse_ups, coarse_downs = call(
        coarse_backward_kernel,
        [
            shape(coarse_rows, features, f32),
            shape(coarse_halo, features, bf16),
            shape(coarse_halo, features, bf16),
            shape(coarse_rows, features, bf16),
            shape(coarse_rows, features, bf16),
            shape(coarse_rows, 2 * features, bf16),
        ],
        [coarse_slope, chip_sums, more_sums, matrices, coarse_columns],
        scratch=[
            buffer(coarse_rows, features, bf16),
            buffer(2 * coarse_halo, features, f32),
        ],
    )
    first_back, second_back = exchange(first_grad, second_grad)

    fine_term, coarse_weights = call(
        coarse_tail_kernel,
        [shape(coarse_rows, features, bf16), shape(features, features, bf16)],
        [
            place, coarse_in, coarse_first, coarse_second, sums, matrices,
            first_grad, second_grad, coarse_sum, coarse_ups, coarse_downs,
        ],
        [SMEM] + [VMEM] * 10,
    )
    result = call(
        result_kernel,
        pltpu.HBM((rows, features), bf16),
        [states, summed, matrices, owners_t, fine_term],
        scratch=[buffer(rows, features, bf16), pltpu.SemaphoreType.DMA],
        out_specs=HBM,
    )

    ups, downs, first_grad, second_grad, weights = call(
        fine_backward_kernel,
        [
            shape(rows, features, bf16),
            shape(rows, 2 * features, bf16),
            shape(halo_rows, features, bf16),
            shape(halo_rows, features, bf16),
            shape(4 * features, features, bf16),
        ],
        [
            states, first, second, cotangent, summed, early_slope, late_slope, matrices, columns,
            owners_t, coarse_part, counts, coarse_downs, first_back, second_back, coarse_sends,
            coarse_weights,
        ],
        [VMEM] * 5 + [HBM] * 2 + [VMEM] * 10,
        [
            buffer(rows, features, bf16),
            buffer(2 * halo_rows, features, f32),
            buffer(coarse_rows, features, bf16),
            buffer(8 * rows, features, bf16),
            pltpu.SemaphoreType.DMA((rows // (STEP * BLOCK),)),
        ],
        mib=32,
    )
    first_back, second_back = exchange(first_grad, second_grad)

    grad_states = call(
        finish_kernel,
        pltpu.HBM((rows, features), bf16),
        [ups, downs, first_back, second_back, sends, matrices],
        scratch=[buffer(rows, features, bf16), pltpu.SemaphoreType.DMA],
        out_specs=HBM,
    )
    grad_weights = total_weights(weights, place, ((), (), (result,)), grad_states)
    return (result, grad_states, grad_weights.reshape(7, features, features))


def solution(mesh):
    fine = P(("grp", "sub"), None)
    fine_row = P(("grp", "sub"))
    in_specs = (
        (fine, fine)
        + (P(),) * 7
        + (fine, fine, fine_row, fine_row)
        + (P("sub", None), P("sub", None), P("sub"), P("sub"), fine_row)
    )
    return jax.shard_map(
        per_device, mesh=mesh, in_specs=in_specs, out_specs=(fine, fine, P()), check_vma=False
    )
```

```python
import functools

import jax
import jax.numpy as jnp
from jax import lax
from jax.experimental import pallas as pl
from jax.experimental.pallas import tpu as pltpu
from jax.sharding import PartitionSpec as P

f32 = jnp.float32
bf16 = jnp.bfloat16
BLOCK = 64
PAIR = 2 * BLOCK
STEP = 16
CHUNK = 1024
NEVER = -1e30
DIGIT = 64.0
VMEM = pl.BlockSpec(memory_space=pltpu.VMEM)
SMEM = pl.BlockSpec(memory_space=pltpu.SMEM)
ANY = pl.BlockSpec(memory_space=pl.ANY)
HBM = pl.BlockSpec(memory_space=pltpu.HBM)
MIB = 1024 * 1024


def dot(a, b):
    return jnp.dot(a, b, preferred_element_type=f32)


def dot_nt(a, b):
    return lax.dot_general(a, b, (((1,), (1,)), ((), ())), preferred_element_type=f32)


def dot_tn(a, b):
    return lax.dot_general(a, b, (((0,), (0,)), ((), ())), preferred_element_type=f32)


def pick(condition):
    return jnp.where(condition, 1.0, 0.0).astype(bf16)


def pick16(values, places):
    return jnp.where(values == places, jnp.ones((), bf16), jnp.zeros((), bf16))


def call(kernel, out_shape, args, in_specs=None, scratch=(), out_specs=None, mib=16):
    many = isinstance(out_shape, (list, tuple))
    in_specs = in_specs or [VMEM] * len(args)
    args = [
        pltpu.with_memory_space_constraint(arg, pltpu.HBM) if spec is HBM else arg
        for arg, spec in zip(args, in_specs)
    ]
    return pl.pallas_call(
        kernel,
        out_shape=out_shape,
        in_specs=in_specs,
        out_specs=out_specs or ([VMEM] * len(out_shape) if many else VMEM),
        scratch_shapes=list(scratch),
        compiler_params=pltpu.CompilerParams(vmem_limit_bytes=mib * MIB),
    )(*args)


def shape(rows, columns, dtype):
    return jax.ShapeDtypeStruct((rows, columns), dtype)


def slot_columns(nbr, mask, halo_rows, even):
    rows = nbr.shape[1]
    block = lax.broadcasted_iota(jnp.int32, nbr.shape, 1) // BLOCK
    halo = lax.rem(block, halo_rows // BLOCK) * BLOCK
    lower = jnp.where(even, 2 * BLOCK, BLOCK)
    column = jnp.where(
        nbr < rows,
        nbr - block * BLOCK,
        jnp.where(
            nbr < rows + halo_rows,
            lower + nbr - rows - halo,
            3 * BLOCK - lower + nbr - rows - halo_rows - halo,
        ),
    )
    return jnp.where(mask > 0, column, 3 * BLOCK).astype(f32)


def selector(columns_t):
    first = lax.broadcasted_iota(jnp.int32, (BLOCK, 128), 1).astype(bf16)
    second = (lax.broadcasted_iota(jnp.int32, (BLOCK, 128), 1) + 128).astype(bf16)
    parts = []
    for k in range(8):
        wide = jnp.broadcast_to(columns_t[:, k : k + 1], (BLOCK, 128)).astype(bf16)
        parts.append(jnp.concatenate([pick16(wide, first), pick16(wide, second)], 1))
    return jnp.concatenate(parts, 0)


def selector_t(columns, rolled, half):
    lane = lax.broadcasted_iota(jnp.int32, (1, 128), 1)
    place = lax.broadcasted_iota(jnp.int32, (3 * BLOCK, 128), 0).astype(bf16)
    parts = []
    for j in range(4):
        left, right = (columns, rolled) if half == 0 else (rolled, columns)
        row = jnp.where(lane < BLOCK, left[2 * j : 2 * j + 1], right[2 * j + 1 : 2 * j + 2])
        wide = jnp.broadcast_to(row, (3 * BLOCK, 128)).astype(bf16)
        parts.append(pick16(wide, place))
    return jnp.concatenate(parts, 1)


def window_of(far, halo, place):
    halo_rows = halo.shape[0] // 2
    start = place * BLOCK
    return jnp.concatenate(
        [
            far,
            halo[start : start + BLOCK, :],
            halo[halo_rows + start : halo_rows + start + BLOCK, :],
            jnp.full((BLOCK, far.shape[1]), NEVER, bf16),
        ],
        0,
    )


def chunk_of(index, count):
    return pl.ds(pl.multiple_of(index * count, count), count)


def matrix(weights_ref, n):
    return weights_ref[128 * n : 128 * (n + 1), :]


def level_terms(h_ref, halo_refs, self_weight, other_weight, own, far, halo):
    halo_rows = halo_refs[0].shape[0]
    other = other_weight * 0.5
    terms = dot(h_ref[...], jnp.concatenate([self_weight * 0.5, other], 1))
    own[...] = terms[:, :128]
    far[...] = terms[:, 128:].astype(bf16)
    halo[:halo_rows, :] = dot(halo_refs[0][...], other).astype(bf16)
    halo[halo_rows:, :] = dot(halo_refs[1][...], other).astype(bf16)


def edges(own_rows, far_rows, slots, halo):
    places = halo.shape[0] // (2 * BLOCK)
    assert STEP % places == 0
    tables = []
    for n in range(STEP):
        part = slice(n * BLOCK, (n + 1) * BLOCK)
        window = window_of(far_rows[part], halo, n % places)
        tables.append(dot(selector(slots[part]), window))
    sums, slopes = [], []
    for n, picked in enumerate(tables):
        own = own_rows[n * BLOCK : (n + 1) * BLOCK]
        values, pieces = [], []
        for k in range(8):
            y = (picked[k * BLOCK : (k + 1) * BLOCK] + own).astype(bf16)
            t = jnp.tanh(y)
            bent = y * t
            values.append(y + bent)
            pieces.append((1 + t) * (1 + (y - bent)))
        while len(values) > 1:
            values = [left + right for left, right in zip(values[::2], values[1::2])]
        sums.append(values[0])
        slopes.append(jnp.concatenate(pieces, 0))
    return jnp.concatenate(sums, 0), slopes


def edges_back(slopes, grad_sum, columns, halo_grad):
    places = halo_grad.shape[0] // (2 * BLOCK)
    halo_rows = halo_grad.shape[0] // 2
    windows, downs = [], []
    for n, slope in enumerate(slopes):
        part = grad_sum[n * BLOCK : (n + 1) * BLOCK]
        grads = [slope[k * BLOCK : (k + 1) * BLOCK] * part for k in range(8)]
        downs.append(sum(grad.astype(f32) for grad in grads))
        mine = columns[:, n // 2 * PAIR : (n // 2 + 1) * PAIR]
        selected = selector_t(mine, pltpu.roll(mine, BLOCK, 1), n % 2)
        windows.append(dot(selected, jnp.concatenate(grads, 0)))
    for place in range(places):
        for side in range(2):
            start = side * halo_rows + place * BLOCK
            total = halo_grad[start : start + BLOCK, :]
            for window in windows[place::places]:
                total = total + window[(side + 1) * BLOCK : (side + 2) * BLOCK]
            halo_grad[start : start + BLOCK, :] = total
    local = jnp.concatenate([window[:BLOCK] for window in windows], 0)
    down = jnp.concatenate(downs, 0)
    return jnp.concatenate([down, local], 1).astype(bf16)


def fetch(pairs, sems):
    copies = [pltpu.make_async_copy(src, dst, sems.at[n]) for n, (src, dst) in enumerate(pairs)]
    for copy in copies:
        copy.start()
    for copy in copies:
        copy.wait()


def gather_kernel(
    place_ref, lo_hbm, hi_hbm, x_hbm, first_ref, second_ref, x_ref, wide, up, down, lo, hi, sems
):
    fetch([(x_hbm, x_ref), (lo_hbm, lo), (hi_hbm, hi)], sems)
    wide[...] = x_ref[...].astype(f32)

    def step(r, carry):
        up[pl.ds(r, 1), :] = wide[pl.ds(hi[r], 1), :]
        down[pl.ds(r, 1), :] = wide[pl.ds(lo[r], 1), :]
        return carry

    lax.fori_loop(0, up.shape[0], step, None, unroll=16)
    even = place_ref[0] > 0
    first_ref[...] = jnp.where(even, up[...], down[...]).astype(bf16)
    second_ref[...] = jnp.where(even, down[...], up[...]).astype(bf16)


def gather_rows(place, x, send_lo, send_hi):
    rows, features = x.shape
    count = send_lo.shape[0]
    out = shape(count, features, bf16)
    return call(
        gather_kernel,
        [out, out, shape(rows, features, bf16)],
        [place, send_lo, send_hi, x],
        [SMEM, HBM, HBM, HBM],
        [
            pltpu.VMEM((rows, features), f32),
            pltpu.VMEM((count, features), f32),
            pltpu.VMEM((count, features), f32),
            pltpu.SMEM((count,), jnp.int32),
            pltpu.SMEM((count,), jnp.int32),
            pltpu.SemaphoreType.DMA((3,)),
        ],
    )


def owner_sums(owner_ref, tile, values):
    place = lax.broadcasted_iota(jnp.int32, (256, 128), 0).astype(bf16)
    owner = (owner_ref[...] - tile * 256).astype(f32)
    rows = jnp.concatenate(
        [
            pick16(jnp.broadcast_to(owner[q : q + 1], (256, 128)).astype(bf16), place)
            for q in range(owner.shape[0])
        ],
        1,
    )
    return dot(rows, values)


def prepare_kernel(
    place_ref,
    g_hbm,
    owner_hbm,
    nbr_hbm,
    mask_hbm,
    coarse_nbr_hbm,
    coarse_mask_hbm,
    lo_hbm,
    hi_hbm,
    coarse_lo_hbm,
    coarse_hi_hbm,
    *rest,
    halo_rows,
    coarse_halo,
):
    weight_hbms, rest = rest[:7], rest[7:]
    (
        after_ref,
        counts_ref,
        columns_ref,
        columns_t_ref,
        coarse_columns_ref,
        coarse_columns_t_ref,
        g_ref,
        weights_ref,
        sends_ref,
        coarse_sends_ref,
        owner_ref,
        nbr_ref,
        mask_ref,
        coarse_nbr_ref,
        coarse_mask_ref,
        lo_ref,
        hi_ref,
        coarse_lo_ref,
        coarse_hi_ref,
        sems,
    ) = rest
    fetch(
        [
            (g_hbm, g_ref),
            (owner_hbm, owner_ref),
            (nbr_hbm, nbr_ref),
            (mask_hbm, mask_ref),
            (coarse_nbr_hbm, coarse_nbr_ref),
            (coarse_mask_hbm, coarse_mask_ref),
            (lo_hbm, lo_ref),
            (hi_hbm, hi_ref),
            (coarse_lo_hbm, coarse_lo_ref),
            (coarse_hi_hbm, coarse_hi_ref),
        ]
        + [(w, weights_ref.at[pl.ds(128 * n, 128), :]) for n, w in enumerate(weight_hbms)],
        sems,
    )
    even = place_ref[0] > 0
    for low, high, out in (
        (lo_ref, hi_ref, sends_ref),
        (coarse_lo_ref, coarse_hi_ref, coarse_sends_ref),
    ):
        first = jnp.where(even, high[...], low[...])
        second = jnp.where(even, low[...], high[...])
        out[...] = jnp.concatenate([first, second], 1)
    columns_ref[...] = slot_columns(nbr_ref[...], mask_ref[...], halo_rows, even)
    columns_t_ref[...] = columns_ref[...].T
    coarse_columns_ref[...] = slot_columns(
        coarse_nbr_ref[...], coarse_mask_ref[...], coarse_halo, even
    )
    coarse_columns_t_ref[...] = coarse_columns_ref[...].T
    tiles = counts_ref.shape[0] // 2
    owner = owner_ref[...]
    high, low = owner // 128, lax.rem(owner, 128)
    groups = owner.shape[0]
    place = lax.broadcasted_iota(jnp.int32, (128, 128), 0)
    high_rows = jnp.concatenate(
        [pick(high[q : q + 1, :] == place[:tiles]) for q in range(groups)], 1
    )
    low_rows = jnp.concatenate(
        [pick(low[q : q + 1, :] == place) for q in range(groups)], 1
    )
    counts = dot_nt(high_rows, low_rows)
    most = jnp.floor(counts * (1 / DIGIT))
    counts_ref[...] = jnp.concatenate([most, counts - DIGIT * most], 0).astype(bf16)


def sums_kernel(owner_ref, g_ref, after_ref, sums_ref):
    def step(tile, carry):
        sums_ref[chunk_of(tile, 256), :] = owner_sums(owner_ref, tile, g_ref[...]).astype(bf16)
        return carry

    lax.fori_loop(0, sums_ref.shape[0] // 256, step, None)


def owners_kernel(owner_ref, after_ref, owners_ref):
    owners_ref[...] = owner_columns(owner_ref)


def half_totals(owner_ref, new_ref, counts_ref, half, out_ref):
    tiles = (out_ref.shape[0] - counts_ref.shape[0]) // 256
    for tile in range(tiles):
        totals = owner_sums(owner_ref, half * tiles + tile, new_ref[...])
        out_ref[256 * tile : 256 * (tile + 1), :] = totals.astype(bf16)
    out_ref[256 * tiles :, :] = counts_ref[...]


def keep_kernel(place_ref, owner_ref, new_ref, counts_ref, out_ref):
    half_totals(owner_ref, new_ref, counts_ref, lax.rem(place_ref[1], 2), out_ref)


def fine_forward_kernel(
    place_ref,
    h_ref,
    first_ref,
    second_ref,
    weights_ref,
    columns_t_ref,
    owner_ref,
    counts_ref,
    summed_ref,
    slope_hbm,
    new_ref,
    give_ref,
    own,
    far,
    halo,
    slope_ref,
    sem,
):
    self_weight, other_weight = matrix(weights_ref, 0), matrix(weights_ref, 1)
    level_terms(h_ref, (first_ref, second_ref), self_weight, other_weight, own, far, halo)

    def step(index, carry):
        here = chunk_of(index, STEP * BLOCK)
        total, slopes = edges(own[here, :], far[here, :], columns_t_ref[here, :], halo)
        summed_ref[here, :] = total
        edge = chunk_of(index, 8 * STEP * BLOCK)
        slope_ref[edge, :] = jnp.concatenate(slopes, 0)
        pltpu.make_async_copy(slope_ref.at[edge, :], slope_hbm.at[edge, :], sem).start()
        return carry

    lax.fori_loop(0, h_ref.shape[0] // (STEP * BLOCK), step, None)
    new_ref[...] = (
        h_ref[...].astype(f32) + dot(summed_ref[...], matrix(weights_ref, 2))
    ).astype(bf16)
    half_totals(owner_ref, new_ref, counts_ref, 1 - lax.rem(place_ref[1], 2), give_ref)
    pltpu.make_async_copy(slope_ref, slope_hbm, sem).wait()


def half_kernel(place_ref, totals_ref, more_totals_ref, after_ref, half_ref, counts_ref):
    half_rows = half_ref.shape[0]
    totals = totals_ref[...].astype(f32) + more_totals_ref[...].astype(f32)
    digits = totals[half_rows:]
    tiles = counts_ref.shape[0]
    counts_ref[...] = DIGIT * digits[:tiles] + digits[tiles:]
    per_row = counts_ref[...].T
    first = lax.rem(place_ref[1], 2) == 0
    for tile in range(tiles // 2):
        here = slice(tile * 128, (tile + 1) * 128)
        later = tile + tiles // 2
        count = jnp.where(first, per_row[:, tile : tile + 1], per_row[:, later : later + 1])
        half_ref[here, :] = (totals[here] / count).astype(bf16)


def coarse_input_kernel(
    place_ref,
    half_ref,
    their_half_ref,
    sends_ref,
    cin_ref,
    first_ref,
    second_ref,
):
    mine, theirs = half_ref[...], their_half_ref[...]
    first = lax.rem(place_ref[1], 2) == 0
    cin = jnp.concatenate([jnp.where(first, mine, theirs), jnp.where(first, theirs, mine)], 0)
    cin_ref[...] = cin
    place = lax.broadcasted_iota(jnp.int32, (cin.shape[0], sends_ref.shape[1]), 0)
    sent = dot_tn(pick(sends_ref[...] == place), cin).astype(bf16)
    halo_rows = first_ref.shape[0]
    first_ref[...] = sent[:halo_rows]
    second_ref[...] = sent[halo_rows:]


def coarse_forward_kernel(
    cin_ref,
    first_ref,
    second_ref,
    weights_ref,
    columns_t_ref,
    summed_ref,
    slope_ref,
    own,
    far,
    halo,
):
    self_weight, other_weight = matrix(weights_ref, 3), matrix(weights_ref, 4)
    level_terms(cin_ref, (first_ref, second_ref), self_weight, other_weight, own, far, halo)

    def step(index, carry):
        here = chunk_of(index, STEP * BLOCK)
        total, slopes = edges(own[here, :], far[here, :], columns_t_ref[here, :], halo)
        summed_ref[here, :] = total
        slope_ref[chunk_of(index, 8 * STEP * BLOCK), :] = jnp.concatenate(slopes, 0)
        return carry

    lax.fori_loop(0, cin_ref.shape[0] // (STEP * BLOCK), step, None)


def coarse_backward_kernel(
    slope_ref,
    chip_sums_ref,
    more_sums_ref,
    weights_ref,
    columns_ref,
    part_ref,
    first_grad_ref,
    second_grad_ref,
    sums_ref,
    ups_ref,
    downs_ref,
    grad_sum,
    halo_grad,
):
    halo_rows = first_grad_ref.shape[0]
    halo_grad[...] = jnp.zeros_like(halo_grad)
    sums_ref[...] = (chip_sums_ref[...].astype(f32) + more_sums_ref[...].astype(f32)).astype(bf16)
    part_ref[...] = dot_nt(sums_ref[...], matrix(weights_ref, 6))
    ups_ref[...] = part_ref[...].astype(bf16)
    grad_sum[...] = (dot_nt(ups_ref[...], matrix(weights_ref, 5)) * 0.5).astype(bf16)
    count = STEP * BLOCK

    def step(index, carry):
        here = chunk_of(index, count)
        slope = slope_ref[chunk_of(index, 8 * count), :]
        slopes = [slope[n * 8 * BLOCK : (n + 1) * 8 * BLOCK] for n in range(STEP)]
        downs_ref[here, :] = edges_back(
            slopes, grad_sum[here, :], columns_ref[:, here], halo_grad
        )
        return carry

    lax.fori_loop(0, part_ref.shape[0] // count, step, None)
    first_grad_ref[...] = halo_grad[:halo_rows, :].astype(bf16)
    second_grad_ref[...] = halo_grad[halo_rows:, :].astype(bf16)


def coarse_tail_kernel(
    place_ref,
    cin_ref,
    first_ref,
    second_ref,
    sums_ref,
    matrices_ref,
    first_grad_ref,
    second_grad_ref,
    summed_ref,
    ups_ref,
    downs_ref,
    fine_ref,
    weights_ref,
):
    cin = cin_ref[...]
    out = (cin.astype(f32) + dot(summed_ref[...], matrix(matrices_ref, 5))).astype(bf16)
    fine_ref[...] = dot(out, matrix(matrices_ref, 6)).astype(bf16)
    pair_grad = dot_tn(cin, downs_ref[...])
    other_grad = (
        pair_grad[:, 128:]
        + dot_tn(first_ref[...], first_grad_ref[...])
        + dot_tn(second_ref[...], second_grad_ref[...])
    )
    grads = [
        pair_grad[:, :128],
        other_grad,
        dot_tn(summed_ref[...], ups_ref[...]),
        dot_tn(out, sums_ref[...]),
    ]
    weights_ref[...] = choose(place_ref[1], grads).astype(bf16)


def choose(place, values):
    picked = values[-1]
    for n, value in enumerate(values[:-1]):
        picked = jnp.where(place == n, value, picked)
    return picked


def owner_columns(owner_ref):
    owner = owner_ref[...].astype(f32)
    row = jnp.concatenate([owner[q : q + 1, :] for q in range(owner.shape[0])], 1)
    return jnp.broadcast_to(row, (8, row.shape[1])).T


def owner_rows(owners, values):
    count = owners.shape[0]
    wide = jnp.broadcast_to(owners[:, 0:1], (count, 128))
    lane = lax.broadcasted_iota(jnp.int32, (count, 128), 1)
    first, second = lane.astype(bf16), (lane + 128).astype(bf16)
    rows = []
    for tile in range(values.shape[0] // 256):
        here = (wide - 256.0 * tile).astype(bf16)
        rows += [pick16(here, first), pick16(here, second)]
    return dot(jnp.concatenate(rows, 1), values)


def result_kernel(h_ref, summed_ref, weights_ref, owners_ref, fine_ref, out_hbm, out_ref, sem):
    def step(index, carry):
        here = chunk_of(index, CHUNK)
        updated = h_ref[here, :].astype(f32) + dot(summed_ref[here, :], matrix(weights_ref, 2))
        out_ref[here, :] = (updated + owner_rows(owners_ref[here, :], fine_ref[...])).astype(bf16)
        pltpu.make_async_copy(out_ref.at[here, :], out_hbm.at[here, :], sem).start()
        return carry

    lax.fori_loop(0, h_ref.shape[0] // CHUNK, step, None)
    pltpu.make_async_copy(out_ref, out_hbm, sem).wait()


def fine_backward_kernel(
    place_ref,
    h_ref,
    first_ref,
    second_ref,
    g_ref,
    summed_ref,
    slope_hbm,
    matrices_ref,
    columns_ref,
    owners_ref,
    part_ref,
    counts_ref,
    coarse_downs_ref,
    first_back_ref,
    second_back_ref,
    sends_ref,
    coarse_weights_ref,
    ups_ref,
    downs_ref,
    first_grad_ref,
    second_grad_ref,
    give_ref,
    keep_ref,
    grad_sum,
    halo_grad,
    mean,
    slope_ref,
    weights,
    slope_sems,
):
    count = STEP * BLOCK
    steps = h_ref.shape[0] // count

    def slope_copy(index):
        edge = chunk_of(index, 8 * count)
        return pltpu.make_async_copy(
            slope_hbm.at[edge, :], slope_ref.at[edge, :], slope_sems.at[index]
        )

    for index in range(steps):
        slope_copy(index).start()
    halo_rows = first_ref.shape[0]
    coarse_rows = part_ref.shape[0]
    halo_grad[...] = jnp.zeros_like(halo_grad)

    place = lax.broadcasted_iota(jnp.int32, (coarse_rows, sends_ref.shape[1]), 0)
    sends = pick(sends_ref[...] == place)
    back = jnp.concatenate([first_back_ref[...], second_back_ref[...]], 0)
    back = dot_nt(back, matrix(matrices_ref, 4)).astype(bf16)
    plain = jnp.concatenate([matrix(matrices_ref, 3), matrix(matrices_ref, 4)], 1)
    grad_in = part_ref[...] + dot_nt(coarse_downs_ref[...], plain) + dot(sends, back)
    per_row = counts_ref[...].T
    for tile in range(coarse_rows // 128):
        here = slice(tile * 128, (tile + 1) * 128)
        mean[here, :] = (grad_in[here, :] / per_row[:, tile : tile + 1]).astype(bf16)

    def owner_step(index):
        here = chunk_of(index, count)
        grad_up = g_ref[here, :].astype(f32) + owner_rows(owners_ref[here, :], mean[...])
        ups = grad_up.astype(bf16)
        ups_ref[here, :] = ups
        grad_sum[here, :] = (dot_nt(ups, matrix(matrices_ref, 2)) * 0.5).astype(bf16)

    def edge_step(index):
        here = chunk_of(index, count)
        slope_copy(index).wait()
        slope = slope_ref[chunk_of(index, 8 * count), :]
        slopes = [slope[n * 8 * BLOCK : (n + 1) * 8 * BLOCK] for n in range(STEP)]
        downs_ref[here, :] = edges_back(
            slopes, grad_sum[here, :], columns_ref[:, here], halo_grad
        )

    owner_step(0)

    def step(index, carry):
        edge_step(index)
        owner_step(index + 1)
        return carry

    lax.fori_loop(0, steps - 1, step, None)
    edge_step(steps - 1)
    first_grad = halo_grad[:halo_rows, :].astype(bf16)
    second_grad = halo_grad[halo_rows:, :].astype(bf16)
    first_grad_ref[...] = first_grad
    second_grad_ref[...] = second_grad
    pair_grad = dot_tn(h_ref[...], downs_ref[...])
    weights[0:128, :] = pair_grad[:, :128]
    weights[128:256, :] = (
        pair_grad[:, 128:]
        + dot_tn(first_ref[...], first_grad)
        + dot_tn(second_ref[...], second_grad)
    )
    weights[256:384, :] = dot_tn(summed_ref[...], ups_ref[...])
    core = lax.rem(place_ref[1], 2)
    give_ref[...] = weights[pl.ds(pl.multiple_of((1 - core) * 192, 64), 192), :]
    keep_ref[:192, :] = weights[pl.ds(pl.multiple_of(core * 192, 64), 192), :]
    keep_ref[192:, :] = coarse_weights_ref[...].astype(f32)


def finish_kernel(
    ups_ref,
    downs_ref,
    first_back_ref,
    second_back_ref,
    sends_ref,
    matrices_ref,
    out_hbm,
    out_ref,
    sem,
):
    other = matrix(matrices_ref, 1)
    plain = jnp.concatenate([matrix(matrices_ref, 0), other], 1)
    back = jnp.concatenate([first_back_ref[...], second_back_ref[...]], 0)
    back = dot_nt(back, other).astype(bf16)
    sends = sends_ref[...]
    place = lax.broadcasted_iota(jnp.int32, (256, sends.shape[1]), 0).astype(bf16)

    def step(index, carry):
        here = chunk_of(index, CHUNK)
        rows = []
        for part in range(CHUNK // 256):
            local = (sends - (index * CHUNK + 256 * part)).astype(f32)
            rows.append(pick16(jnp.broadcast_to(local, place.shape).astype(bf16), place))
        grad = ups_ref[here, :].astype(f32) + dot_nt(downs_ref[here, :], plain)
        out_ref[here, :] = (grad + dot(jnp.concatenate(rows, 0), back)).astype(bf16)
        pltpu.make_async_copy(out_ref.at[here, :], out_hbm.at[here, :], sem).start()
        return carry

    lax.fori_loop(0, ups_ref.shape[0] // CHUNK, step, None)
    pltpu.make_async_copy(out_ref, out_hbm, sem).wait()


def add_kernel(mine_ref, theirs_ref, *rest):
    out_ref = rest[-1]
    out_ref[...] = (mine_ref[...].astype(f32) + theirs_ref[...].astype(f32)).astype(bf16)


def add_first_kernel(keep_ref, theirs_ref, out_ref):
    out_ref[:192, :] = (keep_ref[:192, :] + theirs_ref[...]).astype(bf16)
    out_ref[192:, :] = keep_ref[192:, :].astype(bf16)


def add_gather_kernel(mine_ref, y_ref, x_ref, both_ref, after_ref, out_ref):
    mine = mine_ref[...].astype(f32) + y_ref[...].astype(f32)
    theirs = x_ref[...].astype(f32) + both_ref[...].astype(f32)
    out_ref[:192, :] = mine[:192] + theirs[:192]
    out_ref[192:320, :] = mine[192:]
    out_ref[320:, :] = theirs[192:]


def weights_kernel(place_ref, mine_ref, theirs_ref, out_ref):
    group = place_ref[1]
    low, high = lax.rem(group, 2), group // 2
    mine, theirs = mine_ref[:192, :], theirs_ref[:192, :]
    out_ref[:192, :] = jnp.where(low == 0, mine, theirs)
    out_ref[192:384, :] = jnp.where(low == 0, theirs, mine)
    for n in range(4):
        row = jnp.where(high == n // 2, 192, 320)
        here = pl.ds(pl.multiple_of(row, 64), 128)
        value = jnp.where(low == n % 2, mine_ref[here, :], theirs_ref[here, :])
        out_ref[384 + 128 * n : 512 + 128 * n, :] = value


def exchange(first, second):
    count = lax.axis_size("sub")
    routes = []
    for start in range(2):
        pairs = [(i, i + 1) for i in range(start, count - 1, 2)]
        routes.append(pairs + [(j, i) for i, j in pairs])
    return lax.ppermute(first, "sub", routes[0]), lax.ppermute(second, "sub", routes[1])


def swapped(block, axis, distance):
    return lax.ppermute(block, axis, [(i, i ^ distance) for i in range(lax.axis_size(axis))])


def total_weights(give, keep, place, after, last):
    weights = call(
        add_first_kernel, shape(320, 128, bf16), [keep, swapped(give, "grp", 1)]
    )
    distance, number = 2, 0
    while distance < lax.axis_size("sub"):
        theirs = swapped(weights, "sub", distance)
        waits = after[number] if number < len(after) else ()
        weights = call(
            add_kernel,
            shape(320, 128, bf16),
            [weights, theirs, *waits],
            [VMEM, VMEM] + [HBM] * len(waits),
        )
        distance, number = 2 * distance, number + 1
    count = lax.axis_size("sub")
    corners = [
        (g * count + s, (g ^ 2) * count + (s ^ 1))
        for g in range(lax.axis_size("grp"))
        for s in range(count)
    ]
    weights = call(
        add_gather_kernel,
        shape(448, 128, f32),
        [
            weights,
            swapped(weights, "sub", 1),
            swapped(weights, "grp", 2),
            lax.ppermute(weights, ("grp", "sub"), corners),
            last,
        ],
        [VMEM] * 4 + [HBM],
    )
    return call(
        weights_kernel,
        shape(896, 128, f32),
        [place, weights, swapped(weights, "grp", 1)],
        [SMEM, VMEM, VMEM],
    )


def per_device(
    states,
    cotangent,
    fine_self,
    fine_other,
    fine_node,
    coarse_self,
    coarse_other,
    coarse_node,
    prolong,
    fine_nbr,
    fine_mask,
    fine_send_lo,
    fine_send_hi,
    coarse_nbr,
    coarse_mask,
    coarse_send_lo,
    coarse_send_hi,
    coarse_owner,
):
    rows, features = states.shape
    coarse_rows = coarse_nbr.shape[0]
    halo_rows = fine_send_lo.shape[0]
    coarse_halo = coarse_send_lo.shape[0]
    count_rows = coarse_rows // 128
    owner = coarse_owner.reshape(rows // 128, 128)
    place = jnp.stack([1 - lax.rem(lax.axis_index("sub"), 2), lax.axis_index("grp")])

    def buffer(count, columns, dtype):
        return pltpu.VMEM((count, columns), dtype)

    to_first, to_second, states = gather_rows(place, states, fine_send_lo, fine_send_hi)
    first, second = exchange(to_first, to_second)

    (
        counts, columns, columns_t, coarse_columns, coarse_columns_t, cotangent, matrices, sends,
        coarse_sends, owner,
    ) = call(
        functools.partial(prepare_kernel, halo_rows=halo_rows, coarse_halo=coarse_halo),
        [
            shape(2 * count_rows, features, bf16),
            shape(8, rows, f32),
            shape(rows, 8, f32),
            shape(8, coarse_rows, f32),
            shape(coarse_rows, 8, f32),
            shape(rows, features, bf16),
            shape(7 * features, features, bf16),
            shape(1, 2 * halo_rows, jnp.int32),
            shape(1, 2 * coarse_halo, jnp.int32),
            shape(rows // 128, 128, jnp.int32),
        ],
        [
            place, cotangent, owner, fine_nbr.T, fine_mask.T, coarse_nbr.T, coarse_mask.T,
            fine_send_lo[None], fine_send_hi[None], coarse_send_lo[None], coarse_send_hi[None],
            fine_self, fine_other, fine_node, coarse_self, coarse_other, coarse_node, prolong,
            to_first,
        ],
        [SMEM] + [HBM] * 17 + [ANY],
        [buffer(8, rows, jnp.int32)] * 2
        + [buffer(8, coarse_rows, jnp.int32)] * 2
        + [buffer(1, halo_rows, jnp.int32)] * 2
        + [buffer(1, coarse_halo, jnp.int32)] * 2
        + [pltpu.SemaphoreType.DMA((17,))],
    )

    half_rows = coarse_rows // 2 + 2 * count_rows
    summed, slope, new, give = call(
        fine_forward_kernel,
        [
            shape(rows, features, bf16),
            pltpu.HBM((8 * rows, features), bf16),
            shape(rows, features, bf16),
            shape(half_rows, features, bf16),
        ],
        [place, states, first, second, matrices, columns_t, owner, counts],
        [SMEM] + [VMEM] * 7,
        [
            buffer(rows, features, f32),
            buffer(rows, features, bf16),
            buffer(2 * halo_rows, features, bf16),
            buffer(8 * rows, features, bf16),
            pltpu.SemaphoreType.DMA,
        ],
        [VMEM, HBM, VMEM, VMEM],
        mib=32,
    )
    theirs = swapped(give, "grp", 1)
    keep = call(
        keep_kernel,
        shape(half_rows, features, bf16),
        [place, owner, new, counts],
        [SMEM] + [VMEM] * 3,
    )
    chip_totals = call(add_kernel, shape(half_rows, features, bf16), [keep, theirs])
    more_totals = swapped(chip_totals, "grp", 2)
    sums = call(
        sums_kernel,
        shape(coarse_rows, features, bf16),
        [owner, cotangent, chip_totals],
        [VMEM, VMEM, ANY],
    )
    more_sums = swapped(sums, "grp", 1)
    owners_t = call(owners_kernel, shape(rows, 8, f32), [owner, sums], [VMEM, ANY])

    half, counts = call(
        half_kernel,
        [shape(coarse_rows // 2, features, bf16), shape(count_rows, features, f32)],
        [place, chip_totals, more_totals, sums],
        [SMEM, VMEM, VMEM, ANY],
    )
    their_half = swapped(half, "grp", 1)
    chip_sums = call(add_kernel, shape(coarse_rows, features, bf16), [sums, more_sums])
    coarse_in, to_first, to_second = call(
        coarse_input_kernel,
        [
            shape(coarse_rows, features, bf16),
            shape(coarse_halo, features, bf16),
            shape(coarse_halo, features, bf16),
        ],
        [place, half, their_half, coarse_sends],
        [SMEM] + [VMEM] * 3,
    )
    coarse_first, coarse_second = exchange(to_first, to_second)
    more_sums = swapped(chip_sums, "grp", 2)

    coarse_sum, coarse_slope = call(
        coarse_forward_kernel,
        [shape(coarse_rows, features, bf16), shape(8 * coarse_rows, features, bf16)],
        [coarse_in, coarse_first, coarse_second, matrices, coarse_columns_t],
        scratch=[
            buffer(coarse_rows, features, f32),
            buffer(coarse_rows, features, bf16),
            buffer(2 * coarse_halo, features, bf16),
        ],
    )
    coarse_part, first_grad, second_grad, sums, coarse_ups, coarse_downs = call(
        coarse_backward_kernel,
        [
            shape(coarse_rows, features, f32),
            shape(coarse_halo, features, bf16),
            shape(coarse_halo, features, bf16),
            shape(coarse_rows, features, bf16),
            shape(coarse_rows, features, bf16),
            shape(coarse_rows, 2 * features, bf16),
        ],
        [coarse_slope, chip_sums, more_sums, matrices, coarse_columns],
        scratch=[
            buffer(coarse_rows, features, bf16),
            buffer(2 * coarse_halo, features, f32),
        ],
    )
    first_back, second_back = exchange(first_grad, second_grad)

    fine_term, coarse_weights = call(
        coarse_tail_kernel,
        [shape(coarse_rows, features, bf16), shape(features, features, bf16)],
        [
            place, coarse_in, coarse_first, coarse_second, sums, matrices,
            first_grad, second_grad, coarse_sum, coarse_ups, coarse_downs,
        ],
        [SMEM] + [VMEM] * 10,
    )
    result = call(
        result_kernel,
        pltpu.HBM((rows, features), bf16),
        [states, summed, matrices, owners_t, fine_term],
        scratch=[buffer(rows, features, bf16), pltpu.SemaphoreType.DMA],
        out_specs=HBM,
    )

    ups, downs, first_grad, second_grad, give, keep = call(
        fine_backward_kernel,
        [
            shape(rows, features, bf16),
            shape(rows, 2 * features, bf16),
            shape(halo_rows, features, bf16),
            shape(halo_rows, features, bf16),
            shape(192, features, f32),
            shape(320, features, f32),
        ],
        [
            place, states, first, second, cotangent, summed, slope, matrices, columns, owners_t,
            coarse_part, counts, coarse_downs, first_back, second_back, coarse_sends,
            coarse_weights,
        ],
        [SMEM] + [VMEM] * 5 + [HBM] + [VMEM] * 10,
        [
            buffer(rows, features, bf16),
            buffer(2 * halo_rows, features, f32),
            buffer(coarse_rows, features, bf16),
            buffer(8 * rows, features, bf16),
            buffer(384, features, f32),
            pltpu.SemaphoreType.DMA((rows // (STEP * BLOCK),)),
        ],
        mib=32,
    )
    first_back, second_back = exchange(first_grad, second_grad)

    grad_states = call(
        finish_kernel,
        pltpu.HBM((rows, features), bf16),
        [ups, downs, first_back, second_back, sends, matrices],
        scratch=[buffer(rows, features, bf16), pltpu.SemaphoreType.DMA],
        out_specs=HBM,
    )
    grad_weights = total_weights(give, keep, place, ((), (grad_states,)), result)
    return (result, grad_states, grad_weights.reshape(7, features, features))


def solution(mesh):
    fine = P(("grp", "sub"), None)
    fine_row = P(("grp", "sub"))
    in_specs = (
        (fine, fine)
        + (P(),) * 7
        + (fine, fine, fine_row, fine_row)
        + (P("sub", None), P("sub", None), P("sub"), P("sub"), fine_row)
    )
    return jax.shard_map(
        per_device, mesh=mesh, in_specs=in_specs, out_specs=(fine, fine, P()), check_vma=False
    )
```

```python
import functools

import jax
import jax.numpy as jnp
from jax import lax
from jax.experimental import pallas as pl
from jax.experimental.pallas import tpu as pltpu
from jax.sharding import PartitionSpec as P

f32 = jnp.float32
bf16 = jnp.bfloat16
BLOCK = 64
PAIR = 2 * BLOCK
STEP = 16
CHUNK = 1024
NEVER = -1e30
DIGIT = 64.0
VMEM = pl.BlockSpec(memory_space=pltpu.VMEM)
SMEM = pl.BlockSpec(memory_space=pltpu.SMEM)
ANY = pl.BlockSpec(memory_space=pl.ANY)
HBM = pl.BlockSpec(memory_space=pltpu.HBM)
MIB = 1024 * 1024


def dot(a, b):
    return jnp.dot(a, b, preferred_element_type=f32)


def dot_nt(a, b):
    return lax.dot_general(a, b, (((1,), (1,)), ((), ())), preferred_element_type=f32)


def dot_tn(a, b):
    return lax.dot_general(a, b, (((0,), (0,)), ((), ())), preferred_element_type=f32)


def pick(condition):
    return jnp.where(condition, 1.0, 0.0).astype(bf16)


def pick16(values, places):
    return jnp.where(values == places, jnp.ones((), bf16), jnp.zeros((), bf16))


def call(kernel, out_shape, args, in_specs=None, scratch=(), out_specs=None, mib=16):
    many = isinstance(out_shape, (list, tuple))
    in_specs = in_specs or [VMEM] * len(args)
    args = [
        pltpu.with_memory_space_constraint(arg, pltpu.HBM) if spec is HBM else arg
        for arg, spec in zip(args, in_specs)
    ]
    return pl.pallas_call(
        kernel,
        out_shape=out_shape,
        in_specs=in_specs,
        out_specs=out_specs or ([VMEM] * len(out_shape) if many else VMEM),
        scratch_shapes=list(scratch),
        compiler_params=pltpu.CompilerParams(vmem_limit_bytes=mib * MIB),
    )(*args)


def shape(rows, columns, dtype):
    return jax.ShapeDtypeStruct((rows, columns), dtype)


def lanes(row, count):
    return row[:, :count] if count < 128 else jnp.concatenate([row] * (count // 128), 1)


def is_even(place_ref):
    return place_ref[0:1, :]


def group_of(place_ref):
    return place_ref[8:9, :]


def core_of(place_ref):
    return lax.rem(place_ref[8:9, :], 2)


def slot_columns(nbr, mask, halo_rows, even):
    rows = nbr.shape[1]
    block = lax.broadcasted_iota(jnp.int32, nbr.shape, 1) // BLOCK
    halo = lax.rem(block, halo_rows // BLOCK) * BLOCK
    lower = BLOCK + BLOCK * lanes(even, rows)
    column = jnp.where(
        nbr < rows,
        nbr - block * BLOCK,
        jnp.where(
            nbr < rows + halo_rows,
            lower + nbr - rows - halo,
            3 * BLOCK - lower + nbr - rows - halo_rows - halo,
        ),
    )
    return jnp.where(mask > 0, column, 3 * BLOCK).astype(f32)


def selector(columns_t):
    first = lax.broadcasted_iota(jnp.int32, (BLOCK, 128), 1).astype(bf16)
    second = (lax.broadcasted_iota(jnp.int32, (BLOCK, 128), 1) + 128).astype(bf16)
    parts = []
    for k in range(8):
        wide = jnp.broadcast_to(columns_t[:, k : k + 1], (BLOCK, 128)).astype(bf16)
        parts.append(jnp.concatenate([pick16(wide, first), pick16(wide, second)], 1))
    return jnp.concatenate(parts, 0)


def selector_t(columns, rolled, half):
    lane = lax.broadcasted_iota(jnp.int32, (1, 128), 1)
    place = lax.broadcasted_iota(jnp.int32, (3 * BLOCK, 128), 0).astype(bf16)
    parts = []
    for j in range(4):
        left, right = (columns, rolled) if half == 0 else (rolled, columns)
        row = jnp.where(lane < BLOCK, left[2 * j : 2 * j + 1], right[2 * j + 1 : 2 * j + 2])
        wide = jnp.broadcast_to(row, (3 * BLOCK, 128)).astype(bf16)
        parts.append(pick16(wide, place))
    return jnp.concatenate(parts, 1)


def window_of(far, halo, place):
    halo_rows = halo.shape[0] // 2
    start = place * BLOCK
    return jnp.concatenate(
        [
            far,
            halo[start : start + BLOCK, :],
            halo[halo_rows + start : halo_rows + start + BLOCK, :],
            jnp.full((BLOCK, far.shape[1]), NEVER, bf16),
        ],
        0,
    )


def chunk_of(index, count):
    return pl.ds(pl.multiple_of(index * count, count), count)


def matrix(weights_ref, n):
    return weights_ref[128 * n : 128 * (n + 1), :]


def level_terms(h_ref, halo_refs, self_weight, other_weight, own, far, halo):
    halo_rows = halo_refs[0].shape[0]
    other = other_weight * 0.5
    terms = dot(h_ref[...], jnp.concatenate([self_weight * 0.5, other], 1))
    own[...] = terms[:, :128]
    far[...] = terms[:, 128:].astype(bf16)
    halo[:halo_rows, :] = dot(halo_refs[0][...], other).astype(bf16)
    halo[halo_rows:, :] = dot(halo_refs[1][...], other).astype(bf16)


def edges(own_rows, far_rows, slots, halo):
    places = halo.shape[0] // (2 * BLOCK)
    assert STEP % places == 0
    tables = []
    for n in range(STEP):
        part = slice(n * BLOCK, (n + 1) * BLOCK)
        window = window_of(far_rows[part], halo, n % places)
        tables.append(dot(selector(slots[part]), window))
    sums, slopes = [], []
    for n, picked in enumerate(tables):
        own = own_rows[n * BLOCK : (n + 1) * BLOCK]
        values, pieces = [], []
        for k in range(8):
            y = (picked[k * BLOCK : (k + 1) * BLOCK] + own).astype(bf16)
            t = jnp.tanh(y)
            bent = y * t
            values.append(y + bent)
            pieces.append((1 + t) * (1 + (y - bent)))
        while len(values) > 1:
            values = [left + right for left, right in zip(values[::2], values[1::2])]
        sums.append(values[0])
        slopes.append(jnp.concatenate(pieces, 0))
    return jnp.concatenate(sums, 0), slopes


def edges_back(slopes, grad_sum, columns, halo_grad):
    places = halo_grad.shape[0] // (2 * BLOCK)
    halo_rows = halo_grad.shape[0] // 2
    windows, downs = [], []
    for n, slope in enumerate(slopes):
        part = grad_sum[n * BLOCK : (n + 1) * BLOCK]
        grads = [slope[k * BLOCK : (k + 1) * BLOCK] * part for k in range(8)]
        downs.append(sum(grad.astype(f32) for grad in grads))
        mine = columns[:, n // 2 * PAIR : (n // 2 + 1) * PAIR]
        selected = selector_t(mine, pltpu.roll(mine, BLOCK, 1), n % 2)
        windows.append(dot(selected, jnp.concatenate(grads, 0)))
    for place in range(places):
        for side in range(2):
            start = side * halo_rows + place * BLOCK
            total = halo_grad[start : start + BLOCK, :]
            for window in windows[place::places]:
                total = total + window[(side + 1) * BLOCK : (side + 2) * BLOCK]
            halo_grad[start : start + BLOCK, :] = total
    local = jnp.concatenate([window[:BLOCK] for window in windows], 0)
    down = jnp.concatenate(downs, 0)
    return jnp.concatenate([down, local], 1).astype(bf16)


def fetch(pairs, sems):
    copies = [pltpu.make_async_copy(src, dst, sems.at[n]) for n, (src, dst) in enumerate(pairs)]
    for copy in copies:
        copy.start()
    for copy in copies:
        copy.wait()


def gather_kernel(
    place_ref,
    lo_hbm,
    hi_hbm,
    x_hbm,
    first_ref,
    second_ref,
    x_ref,
    vector_ref,
    wide,
    up,
    down,
    lo,
    hi,
    sems,
):
    fetch([(x_hbm, x_ref), (lo_hbm, lo), (hi_hbm, hi)], sems)
    wide[...] = x_ref[...].astype(f32)

    def step(r, carry):
        up[pl.ds(r, 1), :] = wide[pl.ds(hi[r], 1), :]
        down[pl.ds(r, 1), :] = wide[pl.ds(lo[r], 1), :]
        return carry

    lax.fori_loop(0, up.shape[0], step, None, unroll=16)
    even = place_ref[0] > 0
    vector_ref[:8, :] = jnp.full((8, 128), place_ref[0], jnp.int32)
    vector_ref[8:, :] = jnp.full((8, 128), place_ref[1], jnp.int32)
    first_ref[...] = jnp.where(even, up[...], down[...]).astype(bf16)
    second_ref[...] = jnp.where(even, down[...], up[...]).astype(bf16)


def gather_rows(place, x, send_lo, send_hi):
    rows, features = x.shape
    count = send_lo.shape[0]
    out = shape(count, features, bf16)
    return call(
        gather_kernel,
        [out, out, shape(rows, features, bf16), shape(16, 128, jnp.int32)],
        [place, send_lo, send_hi, x],
        [SMEM, HBM, HBM, HBM],
        [
            pltpu.VMEM((rows, features), f32),
            pltpu.VMEM((count, features), f32),
            pltpu.VMEM((count, features), f32),
            pltpu.SMEM((count,), jnp.int32),
            pltpu.SMEM((count,), jnp.int32),
            pltpu.SemaphoreType.DMA((3,)),
        ],
    )


def owner_sums(owner_ref, tile, values):
    place = lax.broadcasted_iota(jnp.int32, (256, 128), 0).astype(bf16)
    owner = (owner_ref[...] - tile * 256).astype(f32)
    rows = jnp.concatenate(
        [
            pick16(jnp.broadcast_to(owner[q : q + 1], (256, 128)).astype(bf16), place)
            for q in range(owner.shape[0])
        ],
        1,
    )
    return dot(rows, values)


def prepare_kernel(
    place_ref,
    g_hbm,
    owner_hbm,
    nbr_hbm,
    mask_hbm,
    coarse_nbr_hbm,
    coarse_mask_hbm,
    lo_hbm,
    hi_hbm,
    coarse_lo_hbm,
    coarse_hi_hbm,
    *rest,
    halo_rows,
    coarse_halo,
):
    weight_hbms, rest = rest[:7], rest[7:]
    (
        after_ref,
        counts_ref,
        columns_ref,
        columns_t_ref,
        coarse_columns_ref,
        coarse_columns_t_ref,
        g_ref,
        weights_ref,
        sends_ref,
        coarse_sends_ref,
        owner_ref,
        nbr_ref,
        mask_ref,
        coarse_nbr_ref,
        coarse_mask_ref,
        lo_ref,
        hi_ref,
        coarse_lo_ref,
        coarse_hi_ref,
        sems,
    ) = rest
    fetch(
        [
            (g_hbm, g_ref),
            (owner_hbm, owner_ref),
            (nbr_hbm, nbr_ref),
            (mask_hbm, mask_ref),
            (coarse_nbr_hbm, coarse_nbr_ref),
            (coarse_mask_hbm, coarse_mask_ref),
            (lo_hbm, lo_ref),
            (hi_hbm, hi_ref),
            (coarse_lo_hbm, coarse_lo_ref),
            (coarse_hi_hbm, coarse_hi_ref),
        ]
        + [(w, weights_ref.at[pl.ds(128 * n, 128), :]) for n, w in enumerate(weight_hbms)],
        sems,
    )
    even = is_even(place_ref)
    for low, high, out in (
        (lo_ref, hi_ref, sends_ref),
        (coarse_lo_ref, coarse_hi_ref, coarse_sends_ref),
    ):
        up = lanes(even, low.shape[1]) > 0
        first = jnp.where(up, high[...], low[...])
        second = jnp.where(up, low[...], high[...])
        out[...] = jnp.concatenate([first, second], 1)
    columns_ref[...] = slot_columns(nbr_ref[...], mask_ref[...], halo_rows, even)
    columns_t_ref[...] = columns_ref[...].T
    coarse_columns_ref[...] = slot_columns(
        coarse_nbr_ref[...], coarse_mask_ref[...], coarse_halo, even
    )
    coarse_columns_t_ref[...] = coarse_columns_ref[...].T
    tiles = counts_ref.shape[0] // 2
    owner = owner_ref[...]
    high, low = owner // 128, lax.rem(owner, 128)
    groups = owner.shape[0]
    place = lax.broadcasted_iota(jnp.int32, (128, 128), 0)
    high_rows = jnp.concatenate(
        [pick(high[q : q + 1, :] == place[:tiles]) for q in range(groups)], 1
    )
    low_rows = jnp.concatenate(
        [pick(low[q : q + 1, :] == place) for q in range(groups)], 1
    )
    counts = dot_nt(high_rows, low_rows)
    most = jnp.floor(counts * (1 / DIGIT))
    counts_ref[...] = jnp.concatenate([most, counts - DIGIT * most], 0).astype(bf16)


def sums_kernel(owner_ref, g_ref, after_ref, sums_ref):
    def step(tile, carry):
        sums_ref[chunk_of(tile, 256), :] = owner_sums(owner_ref, tile, g_ref[...]).astype(bf16)
        return carry

    lax.fori_loop(0, sums_ref.shape[0] // 256, step, None)


def owners_kernel(owner_ref, after_ref, owners_ref):
    owners_ref[...] = owner_columns(owner_ref)


def half_totals(owner_ref, new_ref, counts_ref, half, out_ref):
    tiles = (out_ref.shape[0] - counts_ref.shape[0]) // 256
    for tile in range(tiles):
        totals = owner_sums(owner_ref, half * tiles + tile, new_ref[...])
        out_ref[256 * tile : 256 * (tile + 1), :] = totals.astype(bf16)
    out_ref[256 * tiles :, :] = counts_ref[...]


def keep_kernel(place_ref, owner_ref, new_ref, counts_ref, out_ref):
    half_totals(owner_ref, new_ref, counts_ref, core_of(place_ref), out_ref)


def fine_forward_kernel(
    place_ref,
    h_ref,
    first_ref,
    second_ref,
    weights_ref,
    columns_t_ref,
    owner_ref,
    counts_ref,
    summed_ref,
    slope_hbm,
    new_ref,
    give_ref,
    own,
    far,
    halo,
    slope_ref,
    sem,
):
    self_weight, other_weight = matrix(weights_ref, 0), matrix(weights_ref, 1)
    level_terms(h_ref, (first_ref, second_ref), self_weight, other_weight, own, far, halo)

    def step(index, carry):
        here = chunk_of(index, STEP * BLOCK)
        total, slopes = edges(own[here, :], far[here, :], columns_t_ref[here, :], halo)
        summed_ref[here, :] = total
        edge = chunk_of(index, 8 * STEP * BLOCK)
        slope_ref[edge, :] = jnp.concatenate(slopes, 0)
        pltpu.make_async_copy(slope_ref.at[edge, :], slope_hbm.at[edge, :], sem).start()
        return carry

    lax.fori_loop(0, h_ref.shape[0] // (STEP * BLOCK), step, None)
    new_ref[...] = (
        h_ref[...].astype(f32) + dot(summed_ref[...], matrix(weights_ref, 2))
    ).astype(bf16)
    half_totals(owner_ref, new_ref, counts_ref, 1 - core_of(place_ref), give_ref)
    pltpu.make_async_copy(slope_ref, slope_hbm, sem).wait()


def half_kernel(place_ref, totals_ref, more_totals_ref, after_ref, half_ref, counts_ref):
    half_rows = half_ref.shape[0]
    totals = totals_ref[...].astype(f32) + more_totals_ref[...].astype(f32)
    digits = totals[half_rows:]
    tiles = counts_ref.shape[0]
    counts_ref[...] = DIGIT * digits[:tiles] + digits[tiles:]
    per_row = counts_ref[...].T
    first = core_of(place_ref) == 0
    for tile in range(tiles // 2):
        here = slice(tile * 128, (tile + 1) * 128)
        later = tile + tiles // 2
        low = jnp.broadcast_to(per_row[:, tile : tile + 1], (128, 128))
        high = jnp.broadcast_to(per_row[:, later : later + 1], (128, 128))
        half_ref[here, :] = (totals[here] / jnp.where(first, low, high)).astype(bf16)


def coarse_input_kernel(
    place_ref,
    half_ref,
    their_half_ref,
    sums_ref,
    more_sums_ref,
    sends_ref,
    cin_ref,
    first_ref,
    second_ref,
    chip_sums_ref,
):
    mine, theirs = half_ref[...].astype(f32), their_half_ref[...].astype(f32)
    first = core_of(place_ref) == 0
    cin = jnp.concatenate([jnp.where(first, mine, theirs), jnp.where(first, theirs, mine)], 0)
    cin = cin.astype(bf16)
    cin_ref[...] = cin
    place = lax.broadcasted_iota(jnp.int32, (cin.shape[0], sends_ref.shape[1]), 0)
    sent = dot_tn(pick(sends_ref[...] == place), cin).astype(bf16)
    halo_rows = first_ref.shape[0]
    first_ref[...] = sent[:halo_rows]
    second_ref[...] = sent[halo_rows:]
    chip_sums_ref[...] = (sums_ref[...].astype(f32) + more_sums_ref[...].astype(f32)).astype(bf16)


def coarse_forward_kernel(
    cin_ref,
    first_ref,
    second_ref,
    weights_ref,
    columns_t_ref,
    summed_ref,
    slope_ref,
    own,
    far,
    halo,
):
    self_weight, other_weight = matrix(weights_ref, 3), matrix(weights_ref, 4)
    level_terms(cin_ref, (first_ref, second_ref), self_weight, other_weight, own, far, halo)

    def step(index, carry):
        here = chunk_of(index, STEP * BLOCK)
        total, slopes = edges(own[here, :], far[here, :], columns_t_ref[here, :], halo)
        summed_ref[here, :] = total
        slope_ref[chunk_of(index, 8 * STEP * BLOCK), :] = jnp.concatenate(slopes, 0)
        return carry

    lax.fori_loop(0, cin_ref.shape[0] // (STEP * BLOCK), step, None)


def coarse_backward_kernel(
    slope_ref,
    chip_sums_ref,
    more_sums_ref,
    weights_ref,
    columns_ref,
    part_ref,
    first_grad_ref,
    second_grad_ref,
    sums_ref,
    ups_ref,
    downs_ref,
    grad_sum,
    halo_grad,
):
    halo_rows = first_grad_ref.shape[0]
    halo_grad[...] = jnp.zeros_like(halo_grad)
    sums_ref[...] = (chip_sums_ref[...].astype(f32) + more_sums_ref[...].astype(f32)).astype(bf16)
    part_ref[...] = dot_nt(sums_ref[...], matrix(weights_ref, 6))
    ups_ref[...] = part_ref[...].astype(bf16)
    grad_sum[...] = (dot_nt(ups_ref[...], matrix(weights_ref, 5)) * 0.5).astype(bf16)
    count = STEP * BLOCK

    def step(index, carry):
        here = chunk_of(index, count)
        slope = slope_ref[chunk_of(index, 8 * count), :]
        slopes = [slope[n * 8 * BLOCK : (n + 1) * 8 * BLOCK] for n in range(STEP)]
        downs_ref[here, :] = edges_back(
            slopes, grad_sum[here, :], columns_ref[:, here], halo_grad
        )
        return carry

    lax.fori_loop(0, part_ref.shape[0] // count, step, None)
    first_grad_ref[...] = halo_grad[:halo_rows, :].astype(bf16)
    second_grad_ref[...] = halo_grad[halo_rows:, :].astype(bf16)


def coarse_tail_kernel(
    place_ref,
    cin_ref,
    first_ref,
    second_ref,
    sums_ref,
    matrices_ref,
    first_grad_ref,
    second_grad_ref,
    summed_ref,
    ups_ref,
    downs_ref,
    fine_ref,
    weights_ref,
):
    cin = cin_ref[...]
    out = (cin.astype(f32) + dot(summed_ref[...], matrix(matrices_ref, 5))).astype(bf16)
    fine_ref[...] = dot(out, matrix(matrices_ref, 6)).astype(bf16)
    pair_grad = dot_tn(cin, downs_ref[...])
    other_grad = (
        pair_grad[:, 128:]
        + dot_tn(first_ref[...], first_grad_ref[...])
        + dot_tn(second_ref[...], second_grad_ref[...])
    )
    grads = [
        pair_grad[:, :128],
        other_grad,
        dot_tn(summed_ref[...], ups_ref[...]),
        dot_tn(out, sums_ref[...]),
    ]
    weights_ref[...] = choose(group_of(place_ref), grads).astype(bf16)


def choose(place, values):
    picked = values[-1]
    for n, value in enumerate(values[:-1]):
        picked = jnp.where(place == n, value, picked)
    return picked


def owner_columns(owner_ref):
    owner = owner_ref[...].astype(f32)
    row = jnp.concatenate([owner[q : q + 1, :] for q in range(owner.shape[0])], 1)
    return jnp.broadcast_to(row, (8, row.shape[1])).T


def owner_rows(owners, values):
    count = owners.shape[0]
    wide = jnp.broadcast_to(owners[:, 0:1], (count, 128))
    lane = lax.broadcasted_iota(jnp.int32, (count, 128), 1)
    first, second = lane.astype(bf16), (lane + 128).astype(bf16)
    rows = []
    for tile in range(values.shape[0] // 256):
        here = (wide - 256.0 * tile).astype(bf16)
        rows += [pick16(here, first), pick16(here, second)]
    return dot(jnp.concatenate(rows, 1), values)


def result_kernel(h_ref, summed_ref, weights_ref, owners_ref, fine_ref, out_hbm, out_ref, sem):
    def step(index, carry):
        here = chunk_of(index, CHUNK)
        updated = h_ref[here, :].astype(f32) + dot(summed_ref[here, :], matrix(weights_ref, 2))
        out_ref[here, :] = (updated + owner_rows(owners_ref[here, :], fine_ref[...])).astype(bf16)
        pltpu.make_async_copy(out_ref.at[here, :], out_hbm.at[here, :], sem).start()
        return carry

    lax.fori_loop(0, h_ref.shape[0] // CHUNK, step, None)
    pltpu.make_async_copy(out_ref, out_hbm, sem).wait()


def fine_backward_kernel(
    place_ref,
    h_ref,
    first_ref,
    second_ref,
    g_ref,
    summed_ref,
    slope_hbm,
    matrices_ref,
    columns_ref,
    owners_ref,
    part_ref,
    counts_ref,
    coarse_downs_ref,
    first_back_ref,
    second_back_ref,
    sends_ref,
    coarse_weights_ref,
    ups_ref,
    downs_ref,
    first_grad_ref,
    second_grad_ref,
    give_ref,
    keep_ref,
    grad_sum,
    halo_grad,
    mean,
    slope_ref,
    weights,
    slope_sems,
):
    count = STEP * BLOCK
    steps = h_ref.shape[0] // count

    def slope_copy(index):
        edge = chunk_of(index, 8 * count)
        return pltpu.make_async_copy(
            slope_hbm.at[edge, :], slope_ref.at[edge, :], slope_sems.at[index]
        )

    for index in range(steps):
        slope_copy(index).start()
    halo_rows = first_ref.shape[0]
    coarse_rows = part_ref.shape[0]
    halo_grad[...] = jnp.zeros_like(halo_grad)

    place = lax.broadcasted_iota(jnp.int32, (coarse_rows, sends_ref.shape[1]), 0)
    sends = pick(sends_ref[...] == place)
    back = jnp.concatenate([first_back_ref[...], second_back_ref[...]], 0)
    back = dot_nt(back, matrix(matrices_ref, 4)).astype(bf16)
    plain = jnp.concatenate([matrix(matrices_ref, 3), matrix(matrices_ref, 4)], 1)
    grad_in = part_ref[...] + dot_nt(coarse_downs_ref[...], plain) + dot(sends, back)
    per_row = counts_ref[...].T
    for tile in range(coarse_rows // 128):
        here = slice(tile * 128, (tile + 1) * 128)
        mean[here, :] = (grad_in[here, :] / per_row[:, tile : tile + 1]).astype(bf16)

    def owner_step(index):
        here = chunk_of(index, count)
        grad_up = g_ref[here, :].astype(f32) + owner_rows(owners_ref[here, :], mean[...])
        ups = grad_up.astype(bf16)
        ups_ref[here, :] = ups
        grad_sum[here, :] = (dot_nt(ups, matrix(matrices_ref, 2)) * 0.5).astype(bf16)

    def edge_step(index):
        here = chunk_of(index, count)
        slope_copy(index).wait()
        slope = slope_ref[chunk_of(index, 8 * count), :]
        slopes = [slope[n * 8 * BLOCK : (n + 1) * 8 * BLOCK] for n in range(STEP)]
        downs_ref[here, :] = edges_back(
            slopes, grad_sum[here, :], columns_ref[:, here], halo_grad
        )

    owner_step(0)

    def step(index, carry):
        edge_step(index)
        owner_step(index + 1)
        return carry

    lax.fori_loop(0, steps - 1, step, None)
    edge_step(steps - 1)
    first_grad = halo_grad[:halo_rows, :].astype(bf16)
    second_grad = halo_grad[halo_rows:, :].astype(bf16)
    first_grad_ref[...] = first_grad
    second_grad_ref[...] = second_grad
    pair_grad = dot_tn(h_ref[...], downs_ref[...])
    weights[0:128, :] = pair_grad[:, :128]
    weights[128:256, :] = (
        pair_grad[:, 128:]
        + dot_tn(first_ref[...], first_grad)
        + dot_tn(second_ref[...], second_grad)
    )
    weights[256:384, :] = dot_tn(summed_ref[...], ups_ref[...])
    first = core_of(place_ref) == 0
    low, high = weights[:192, :], weights[192:, :]
    give_ref[...] = jnp.where(first, high, low)
    keep_ref[:192, :] = jnp.where(first, low, high)
    keep_ref[192:, :] = coarse_weights_ref[...].astype(f32)


def finish_kernel(
    ups_ref,
    downs_ref,
    first_back_ref,
    second_back_ref,
    sends_ref,
    matrices_ref,
    out_hbm,
    out_ref,
    sem,
):
    other = matrix(matrices_ref, 1)
    plain = jnp.concatenate([matrix(matrices_ref, 0), other], 1)
    back = jnp.concatenate([first_back_ref[...], second_back_ref[...]], 0)
    back = dot_nt(back, other).astype(bf16)
    sends = sends_ref[...]
    place = lax.broadcasted_iota(jnp.int32, (256, sends.shape[1]), 0).astype(bf16)

    def step(index, carry):
        here = chunk_of(index, CHUNK)
        rows = []
        for part in range(CHUNK // 256):
            local = (sends - (index * CHUNK + 256 * part)).astype(f32)
            rows.append(pick16(jnp.broadcast_to(local, place.shape).astype(bf16), place))
        grad = ups_ref[here, :].astype(f32) + dot_nt(downs_ref[here, :], plain)
        out_ref[here, :] = (grad + dot(jnp.concatenate(rows, 0), back)).astype(bf16)
        pltpu.make_async_copy(out_ref.at[here, :], out_hbm.at[here, :], sem).start()
        return carry

    lax.fori_loop(0, ups_ref.shape[0] // CHUNK, step, None)
    pltpu.make_async_copy(out_ref, out_hbm, sem).wait()


def add_kernel(mine_ref, theirs_ref, *rest):
    out_ref = rest[-1]
    out_ref[...] = (mine_ref[...].astype(f32) + theirs_ref[...].astype(f32)).astype(bf16)


def add_first_kernel(keep_ref, theirs_ref, out_ref):
    out_ref[:192, :] = (keep_ref[:192, :] + theirs_ref[...]).astype(bf16)
    out_ref[192:, :] = keep_ref[192:, :].astype(bf16)


def add_gather_kernel(mine_ref, y_ref, x_ref, both_ref, after_ref, out_ref):
    mine = mine_ref[...].astype(f32) + y_ref[...].astype(f32)
    theirs = x_ref[...].astype(f32) + both_ref[...].astype(f32)
    out_ref[:192, :] = mine[:192] + theirs[:192]
    out_ref[192:320, :] = mine[192:]
    out_ref[320:, :] = theirs[192:]


def weights_kernel(place_ref, mine_ref, theirs_ref, out_ref):
    group = group_of(place_ref)
    low, high = lax.rem(group, 2), group // 2
    mine, theirs = mine_ref[:192, :], theirs_ref[:192, :]
    out_ref[:192, :] = jnp.where(low == 0, mine, theirs)
    out_ref[192:384, :] = jnp.where(low == 0, theirs, mine)
    for n in range(4):
        near = jnp.where(low == n % 2, mine_ref[192:320, :], theirs_ref[192:320, :])
        far = jnp.where(low == n % 2, mine_ref[320:448, :], theirs_ref[320:448, :])
        value = jnp.where(high == n // 2, near, far)
        out_ref[384 + 128 * n : 512 + 128 * n, :] = value


def exchange(first, second):
    count = lax.axis_size("sub")
    routes = []
    for start in range(2):
        pairs = [(i, i + 1) for i in range(start, count - 1, 2)]
        routes.append(pairs + [(j, i) for i, j in pairs])
    return lax.ppermute(first, "sub", routes[0]), lax.ppermute(second, "sub", routes[1])


def swapped(block, axis, distance):
    return lax.ppermute(block, axis, [(i, i ^ distance) for i in range(lax.axis_size(axis))])


def total_weights(give, keep, place, after, last):
    weights = call(
        add_first_kernel, shape(320, 128, bf16), [keep, swapped(give, "grp", 1)]
    )
    distance, number = 2, 0
    while distance < lax.axis_size("sub"):
        theirs = swapped(weights, "sub", distance)
        waits = after[number] if number < len(after) else ()
        weights = call(
            add_kernel,
            shape(320, 128, bf16),
            [weights, theirs, *waits],
            [VMEM, VMEM] + [HBM] * len(waits),
        )
        distance, number = 2 * distance, number + 1
    count = lax.axis_size("sub")
    corners = [
        (g * count + s, (g ^ 2) * count + (s ^ 1))
        for g in range(lax.axis_size("grp"))
        for s in range(count)
    ]
    weights = call(
        add_gather_kernel,
        shape(448, 128, f32),
        [
            weights,
            swapped(weights, "sub", 1),
            swapped(weights, "grp", 2),
            lax.ppermute(weights, ("grp", "sub"), corners),
            last,
        ],
        [VMEM] * 4 + [HBM],
    )
    return call(
        weights_kernel,
        shape(896, 128, f32),
        [place, weights, swapped(weights, "grp", 1)],
        [VMEM] * 3,
    )


def per_device(
    states,
    cotangent,
    fine_self,
    fine_other,
    fine_node,
    coarse_self,
    coarse_other,
    coarse_node,
    prolong,
    fine_nbr,
    fine_mask,
    fine_send_lo,
    fine_send_hi,
    coarse_nbr,
    coarse_mask,
    coarse_send_lo,
    coarse_send_hi,
    coarse_owner,
):
    rows, features = states.shape
    coarse_rows = coarse_nbr.shape[0]
    halo_rows = fine_send_lo.shape[0]
    coarse_halo = coarse_send_lo.shape[0]
    count_rows = coarse_rows // 128
    owner = coarse_owner.reshape(rows // 128, 128)
    place = jnp.stack([1 - lax.rem(lax.axis_index("sub"), 2), lax.axis_index("grp")])

    def buffer(count, columns, dtype):
        return pltpu.VMEM((count, columns), dtype)

    to_first, to_second, states, place = gather_rows(place, states, fine_send_lo, fine_send_hi)
    first, second = exchange(to_first, to_second)

    (
        counts, columns, columns_t, coarse_columns, coarse_columns_t, cotangent, matrices, sends,
        coarse_sends, owner,
    ) = call(
        functools.partial(prepare_kernel, halo_rows=halo_rows, coarse_halo=coarse_halo),
        [
            shape(2 * count_rows, features, bf16),
            shape(8, rows, f32),
            shape(rows, 8, f32),
            shape(8, coarse_rows, f32),
            shape(coarse_rows, 8, f32),
            shape(rows, features, bf16),
            shape(7 * features, features, bf16),
            shape(1, 2 * halo_rows, jnp.int32),
            shape(1, 2 * coarse_halo, jnp.int32),
            shape(rows // 128, 128, jnp.int32),
        ],
        [
            place, cotangent, owner, fine_nbr.T, fine_mask.T, coarse_nbr.T, coarse_mask.T,
            fine_send_lo[None], fine_send_hi[None], coarse_send_lo[None], coarse_send_hi[None],
            fine_self, fine_other, fine_node, coarse_self, coarse_other, coarse_node, prolong,
            to_first,
        ],
        [VMEM] + [HBM] * 17 + [ANY],
        [buffer(8, rows, jnp.int32)] * 2
        + [buffer(8, coarse_rows, jnp.int32)] * 2
        + [buffer(1, halo_rows, jnp.int32)] * 2
        + [buffer(1, coarse_halo, jnp.int32)] * 2
        + [pltpu.SemaphoreType.DMA((17,))],
    )

    half_rows = coarse_rows // 2 + 2 * count_rows
    summed, slope, new, give = call(
        fine_forward_kernel,
        [
            shape(rows, features, bf16),
            pltpu.HBM((8 * rows, features), bf16),
            shape(rows, features, bf16),
            shape(half_rows, features, bf16),
        ],
        [place, states, first, second, matrices, columns_t, owner, counts],
        [VMEM] + [VMEM] * 7,
        [
            buffer(rows, features, f32),
            buffer(rows, features, bf16),
            buffer(2 * halo_rows, features, bf16),
            buffer(8 * rows, features, bf16),
            pltpu.SemaphoreType.DMA,
        ],
        [VMEM, HBM, VMEM, VMEM],
        mib=32,
    )
    theirs = swapped(give, "grp", 1)
    keep = call(
        keep_kernel,
        shape(half_rows, features, bf16),
        [place, owner, new, counts],
        [VMEM] + [VMEM] * 3,
    )
    chip_totals = call(add_kernel, shape(half_rows, features, bf16), [keep, theirs])
    more_totals = swapped(chip_totals, "grp", 2)
    sums = call(
        sums_kernel,
        shape(coarse_rows, features, bf16),
        [owner, cotangent, chip_totals],
        [VMEM, VMEM, ANY],
    )
    more_sums = swapped(sums, "grp", 1)
    owners_t = call(owners_kernel, shape(rows, 8, f32), [owner, sums], [VMEM, ANY])

    half, counts = call(
        half_kernel,
        [shape(coarse_rows // 2, features, bf16), shape(count_rows, features, f32)],
        [place, chip_totals, more_totals, sums],
        [VMEM, VMEM, VMEM, ANY],
    )
    their_half = swapped(half, "grp", 1)
    coarse_in, to_first, to_second, chip_sums = call(
        coarse_input_kernel,
        [
            shape(coarse_rows, features, bf16),
            shape(coarse_halo, features, bf16),
            shape(coarse_halo, features, bf16),
            shape(coarse_rows, features, bf16),
        ],
        [place, half, their_half, sums, more_sums, coarse_sends],
    )
    coarse_first, coarse_second = exchange(to_first, to_second)
    more_sums = swapped(chip_sums, "grp", 2)

    coarse_sum, coarse_slope = call(
        coarse_forward_kernel,
        [shape(coarse_rows, features, bf16), shape(8 * coarse_rows, features, bf16)],
        [coarse_in, coarse_first, coarse_second, matrices, coarse_columns_t],
        scratch=[
            buffer(coarse_rows, features, f32),
            buffer(coarse_rows, features, bf16),
            buffer(2 * coarse_halo, features, bf16),
        ],
    )
    coarse_part, first_grad, second_grad, sums, coarse_ups, coarse_downs = call(
        coarse_backward_kernel,
        [
            shape(coarse_rows, features, f32),
            shape(coarse_halo, features, bf16),
            shape(coarse_halo, features, bf16),
            shape(coarse_rows, features, bf16),
            shape(coarse_rows, features, bf16),
            shape(coarse_rows, 2 * features, bf16),
        ],
        [coarse_slope, chip_sums, more_sums, matrices, coarse_columns],
        scratch=[
            buffer(coarse_rows, features, bf16),
            buffer(2 * coarse_halo, features, f32),
        ],
    )
    first_back, second_back = exchange(first_grad, second_grad)

    fine_term, coarse_weights = call(
        coarse_tail_kernel,
        [shape(coarse_rows, features, bf16), shape(features, features, bf16)],
        [
            place, coarse_in, coarse_first, coarse_second, sums, matrices,
            first_grad, second_grad, coarse_sum, coarse_ups, coarse_downs,
        ],
        [VMEM] + [VMEM] * 10,
    )
    result = call(
        result_kernel,
        pltpu.HBM((rows, features), bf16),
        [states, summed, matrices, owners_t, fine_term],
        scratch=[buffer(rows, features, bf16), pltpu.SemaphoreType.DMA],
        out_specs=HBM,
    )

    ups, downs, first_grad, second_grad, give, keep = call(
        fine_backward_kernel,
        [
            shape(rows, features, bf16),
            shape(rows, 2 * features, bf16),
            shape(halo_rows, features, bf16),
            shape(halo_rows, features, bf16),
            shape(192, features, f32),
            shape(320, features, f32),
        ],
        [
            place, states, first, second, cotangent, summed, slope, matrices, columns, owners_t,
            coarse_part, counts, coarse_downs, first_back, second_back, coarse_sends,
            coarse_weights,
        ],
        [VMEM] + [VMEM] * 5 + [HBM] + [VMEM] * 10,
        [
            buffer(rows, features, bf16),
            buffer(2 * halo_rows, features, f32),
            buffer(coarse_rows, features, bf16),
            buffer(8 * rows, features, bf16),
            buffer(384, features, f32),
            pltpu.SemaphoreType.DMA((rows // (STEP * BLOCK),)),
        ],
        mib=32,
    )
    first_back, second_back = exchange(first_grad, second_grad)

    grad_states = call(
        finish_kernel,
        pltpu.HBM((rows, features), bf16),
        [ups, downs, first_back, second_back, sends, matrices],
        scratch=[buffer(rows, features, bf16), pltpu.SemaphoreType.DMA],
        out_specs=HBM,
    )
    grad_weights = total_weights(give, keep, place, ((), (grad_states,)), result)
    return (result, grad_states, grad_weights.reshape(7, features, features))


def solution(mesh):
    fine = P(("grp", "sub"), None)
    fine_row = P(("grp", "sub"))
    in_specs = (
        (fine, fine)
        + (P(),) * 7
        + (fine, fine, fine_row, fine_row)
        + (P("sub", None), P("sub", None), P("sub"), P("sub"), fine_row)
    )
    return jax.shard_map(
        per_device, mesh=mesh, in_specs=in_specs, out_specs=(fine, fine, P()), check_vma=False
    )
```

```python
import functools

import jax
import jax.numpy as jnp
from jax import lax
from jax.experimental import pallas as pl
from jax.experimental.pallas import tpu as pltpu
from jax.sharding import PartitionSpec as P

f32 = jnp.float32
bf16 = jnp.bfloat16
BLOCK = 64
PAIR = 2 * BLOCK
STEP = 16
CHUNK = 1024
NEVER = -1e30
DIGIT = 64.0
VMEM = pl.BlockSpec(memory_space=pltpu.VMEM)
SMEM = pl.BlockSpec(memory_space=pltpu.SMEM)
ANY = pl.BlockSpec(memory_space=pl.ANY)
HBM = pl.BlockSpec(memory_space=pltpu.HBM)
MIB = 1024 * 1024


def dot(a, b):
    return jnp.dot(a, b, preferred_element_type=f32)


def dot_nt(a, b):
    return lax.dot_general(a, b, (((1,), (1,)), ((), ())), preferred_element_type=f32)


def dot_tn(a, b):
    return lax.dot_general(a, b, (((0,), (0,)), ((), ())), preferred_element_type=f32)


def pick(condition):
    return jnp.where(condition, 1.0, 0.0).astype(bf16)


def pick16(values, places):
    return jnp.where(values == places, jnp.ones((), bf16), jnp.zeros((), bf16))


def call(kernel, out_shape, args, in_specs=None, scratch=(), out_specs=None, mib=16):
    many = isinstance(out_shape, (list, tuple))
    in_specs = in_specs or [VMEM] * len(args)
    args = [
        pltpu.with_memory_space_constraint(arg, pltpu.HBM) if spec is HBM else arg
        for arg, spec in zip(args, in_specs)
    ]
    return pl.pallas_call(
        kernel,
        out_shape=out_shape,
        in_specs=in_specs,
        out_specs=out_specs or ([VMEM] * len(out_shape) if many else VMEM),
        scratch_shapes=list(scratch),
        compiler_params=pltpu.CompilerParams(vmem_limit_bytes=mib * MIB),
    )(*args)


def shape(rows, columns, dtype):
    return jax.ShapeDtypeStruct((rows, columns), dtype)


def lanes(row, count):
    return row[:, :count] if count < 128 else jnp.concatenate([row] * (count // 128), 1)


def is_even(place_ref):
    return place_ref[0:1, :]


def group_of(place_ref):
    return place_ref[8:9, :]


def core_of(place_ref):
    return lax.rem(place_ref[8:9, :], 2)


def slot_columns(nbr, mask, halo_rows, even):
    rows = nbr.shape[1]
    block = lax.broadcasted_iota(jnp.int32, nbr.shape, 1) // BLOCK
    halo = lax.rem(block, halo_rows // BLOCK) * BLOCK
    lower = BLOCK + BLOCK * lanes(even, rows)
    column = jnp.where(
        nbr < rows,
        nbr - block * BLOCK,
        jnp.where(
            nbr < rows + halo_rows,
            lower + nbr - rows - halo,
            3 * BLOCK - lower + nbr - rows - halo_rows - halo,
        ),
    )
    return jnp.where(mask > 0, column, 3 * BLOCK).astype(f32)


def selector(columns_t):
    first = lax.broadcasted_iota(jnp.int32, (BLOCK, 128), 1).astype(bf16)
    second = (lax.broadcasted_iota(jnp.int32, (BLOCK, 128), 1) + 128).astype(bf16)
    parts = []
    for k in range(8):
        wide = jnp.broadcast_to(columns_t[:, k : k + 1], (BLOCK, 128)).astype(bf16)
        parts.append(jnp.concatenate([pick16(wide, first), pick16(wide, second)], 1))
    return jnp.concatenate(parts, 0)


def selector_t(columns, rolled, half):
    lane = lax.broadcasted_iota(jnp.int32, (1, 128), 1)
    place = lax.broadcasted_iota(jnp.int32, (3 * BLOCK, 128), 0).astype(bf16)
    parts = []
    for j in range(4):
        left, right = (columns, rolled) if half == 0 else (rolled, columns)
        row = jnp.where(lane < BLOCK, left[2 * j : 2 * j + 1], right[2 * j + 1 : 2 * j + 2])
        wide = jnp.broadcast_to(row, (3 * BLOCK, 128)).astype(bf16)
        parts.append(pick16(wide, place))
    return jnp.concatenate(parts, 1)


def window_of(far, halo, place):
    halo_rows = halo.shape[0] // 2
    start = place * BLOCK
    return jnp.concatenate(
        [
            far,
            halo[start : start + BLOCK, :],
            halo[halo_rows + start : halo_rows + start + BLOCK, :],
            jnp.full((BLOCK, far.shape[1]), NEVER, bf16),
        ],
        0,
    )


def chunk_of(index, count):
    return pl.ds(pl.multiple_of(index * count, count), count)


def matrix(weights_ref, n):
    return weights_ref[128 * n : 128 * (n + 1), :]


def level_terms(h_ref, halo_refs, self_weight, other_weight, own, far, halo):
    halo_rows = halo_refs[0].shape[0]
    other = other_weight * 0.5
    terms = dot(h_ref[...], jnp.concatenate([self_weight * 0.5, other], 1))
    own[...] = terms[:, :128]
    far[...] = terms[:, 128:].astype(bf16)
    halo[:halo_rows, :] = dot(halo_refs[0][...], other).astype(bf16)
    halo[halo_rows:, :] = dot(halo_refs[1][...], other).astype(bf16)


def edges(own_rows, far_rows, slots, halo):
    places = halo.shape[0] // (2 * BLOCK)
    assert STEP % places == 0
    tables = []
    for n in range(STEP):
        part = slice(n * BLOCK, (n + 1) * BLOCK)
        window = window_of(far_rows[part], halo, n % places)
        tables.append(dot(selector(slots[part]), window))
    sums, slopes = [], []
    for n, picked in enumerate(tables):
        own = own_rows[n * BLOCK : (n + 1) * BLOCK]
        values, pieces = [], []
        for k in range(8):
            y = (picked[k * BLOCK : (k + 1) * BLOCK] + own).astype(bf16)
            t = jnp.tanh(y)
            bent = y * t
            values.append(y + bent)
            pieces.append((1 + t) * (1 + (y - bent)))
        while len(values) > 1:
            values = [left + right for left, right in zip(values[::2], values[1::2])]
        sums.append(values[0])
        slopes.append(jnp.concatenate(pieces, 0))
    return jnp.concatenate(sums, 0), slopes


def edges_back(slopes, grad_sum, columns, halo_grad):
    places = halo_grad.shape[0] // (2 * BLOCK)
    halo_rows = halo_grad.shape[0] // 2
    windows, downs = [], []
    for n, slope in enumerate(slopes):
        part = grad_sum[n * BLOCK : (n + 1) * BLOCK]
        grads = [slope[k * BLOCK : (k + 1) * BLOCK] * part for k in range(8)]
        downs.append(sum(grad.astype(f32) for grad in grads))
        mine = columns[:, n // 2 * PAIR : (n // 2 + 1) * PAIR]
        selected = selector_t(mine, pltpu.roll(mine, BLOCK, 1), n % 2)
        windows.append(dot(selected, jnp.concatenate(grads, 0)))
    for place in range(places):
        for side in range(2):
            start = side * halo_rows + place * BLOCK
            total = halo_grad[start : start + BLOCK, :]
            for window in windows[place::places]:
                total = total + window[(side + 1) * BLOCK : (side + 2) * BLOCK]
            halo_grad[start : start + BLOCK, :] = total
    local = jnp.concatenate([window[:BLOCK] for window in windows], 0)
    down = jnp.concatenate(downs, 0)
    return jnp.concatenate([down, local], 1).astype(bf16)


def fetch(pairs, sems):
    copies = [pltpu.make_async_copy(src, dst, sems.at[n]) for n, (src, dst) in enumerate(pairs)]
    for copy in copies:
        copy.start()
    for copy in copies:
        copy.wait()


def gather_kernel(
    lo_hbm,
    hi_hbm,
    x_hbm,
    first_ref,
    second_ref,
    x_ref,
    vector_ref,
    wide,
    up,
    down,
    lo,
    hi,
    sems,
):
    fetch([(x_hbm, x_ref), (lo_hbm, lo), (hi_hbm, hi)], sems)
    wide[...] = x_ref[...].astype(f32)

    def step(r, carry):
        up[pl.ds(r, 1), :] = wide[pl.ds(hi[r], 1), :]
        down[pl.ds(r, 1), :] = wide[pl.ds(lo[r], 1), :]
        return carry

    lax.fori_loop(0, up.shape[0], step, None, unroll=16)
    parity = 1 - lax.rem(lax.axis_index("sub"), 2)
    even = parity > 0
    vector_ref[:8, :] = jnp.full((8, 128), parity, jnp.int32)
    vector_ref[8:, :] = jnp.full((8, 128), lax.axis_index("grp"), jnp.int32)
    first_ref[...] = jnp.where(even, up[...], down[...]).astype(bf16)
    second_ref[...] = jnp.where(even, down[...], up[...]).astype(bf16)


def gather_rows(x, send_lo, send_hi):
    rows, features = x.shape
    count = send_lo.shape[0]
    out = shape(count, features, bf16)
    return call(
        gather_kernel,
        [out, out, shape(rows, features, bf16), shape(16, 128, jnp.int32)],
        [send_lo, send_hi, x],
        [HBM, HBM, HBM],
        [
            pltpu.VMEM((rows, features), f32),
            pltpu.VMEM((count, features), f32),
            pltpu.VMEM((count, features), f32),
            pltpu.SMEM((count,), jnp.int32),
            pltpu.SMEM((count,), jnp.int32),
            pltpu.SemaphoreType.DMA((3,)),
        ],
    )


def owner_sums(owner_ref, tile, values):
    place = lax.broadcasted_iota(jnp.int32, (256, 128), 0).astype(bf16)
    owner = (owner_ref[...] - tile * 256).astype(f32)
    rows = jnp.concatenate(
        [
            pick16(jnp.broadcast_to(owner[q : q + 1], (256, 128)).astype(bf16), place)
            for q in range(owner.shape[0])
        ],
        1,
    )
    return dot(rows, values)


def prepare_kernel(
    place_ref,
    g_hbm,
    owner_hbm,
    nbr_hbm,
    mask_hbm,
    coarse_nbr_hbm,
    coarse_mask_hbm,
    lo_hbm,
    hi_hbm,
    coarse_lo_hbm,
    coarse_hi_hbm,
    *rest,
    halo_rows,
    coarse_halo,
):
    weight_hbms, rest = rest[:7], rest[7:]
    (
        after_ref,
        counts_ref,
        columns_ref,
        columns_t_ref,
        coarse_columns_ref,
        coarse_columns_t_ref,
        g_ref,
        weights_ref,
        sends_ref,
        coarse_sends_ref,
        owner_ref,
        nbr_ref,
        mask_ref,
        coarse_nbr_ref,
        coarse_mask_ref,
        lo_ref,
        hi_ref,
        coarse_lo_ref,
        coarse_hi_ref,
        sems,
    ) = rest
    fetch(
        [
            (g_hbm, g_ref),
            (owner_hbm, owner_ref),
            (nbr_hbm, nbr_ref),
            (mask_hbm, mask_ref),
            (coarse_nbr_hbm, coarse_nbr_ref),
            (coarse_mask_hbm, coarse_mask_ref),
            (lo_hbm, lo_ref),
            (hi_hbm, hi_ref),
            (coarse_lo_hbm, coarse_lo_ref),
            (coarse_hi_hbm, coarse_hi_ref),
        ]
        + [(w, weights_ref.at[pl.ds(128 * n, 128), :]) for n, w in enumerate(weight_hbms)],
        sems,
    )
    even = is_even(place_ref)
    for low, high, out in (
        (lo_ref, hi_ref, sends_ref),
        (coarse_lo_ref, coarse_hi_ref, coarse_sends_ref),
    ):
        up = lanes(even, low.shape[1]) > 0
        first = jnp.where(up, high[...], low[...])
        second = jnp.where(up, low[...], high[...])
        out[...] = jnp.concatenate([first, second], 1)
    columns_ref[...] = slot_columns(nbr_ref[...], mask_ref[...], halo_rows, even)
    columns_t_ref[...] = columns_ref[...].T
    coarse_columns_ref[...] = slot_columns(
        coarse_nbr_ref[...], coarse_mask_ref[...], coarse_halo, even
    )
    coarse_columns_t_ref[...] = coarse_columns_ref[...].T
    tiles = counts_ref.shape[0] // 2
    owner = owner_ref[...]
    high, low = owner // 128, lax.rem(owner, 128)
    groups = owner.shape[0]
    place = lax.broadcasted_iota(jnp.int32, (128, 128), 0)
    high_rows = jnp.concatenate(
        [pick(high[q : q + 1, :] == place[:tiles]) for q in range(groups)], 1
    )
    low_rows = jnp.concatenate(
        [pick(low[q : q + 1, :] == place) for q in range(groups)], 1
    )
    counts = dot_nt(high_rows, low_rows)
    most = jnp.floor(counts * (1 / DIGIT))
    counts_ref[...] = jnp.concatenate([most, counts - DIGIT * most], 0).astype(bf16)


def sums_kernel(owner_ref, g_ref, after_ref, sums_ref):
    def step(tile, carry):
        sums_ref[chunk_of(tile, 256), :] = owner_sums(owner_ref, tile, g_ref[...]).astype(bf16)
        return carry

    lax.fori_loop(0, sums_ref.shape[0] // 256, step, None)


def relay_kernel(x_ref, after_ref, also_after_ref, out_ref):
    out_ref[...] = x_ref[...]


def owners_kernel(owner_ref, after_ref, owners_ref):
    owners_ref[...] = owner_columns(owner_ref)


def half_totals(owner_ref, new_ref, counts_ref, half, out_ref):
    tiles = (out_ref.shape[0] - counts_ref.shape[0]) // 256
    for tile in range(tiles):
        totals = owner_sums(owner_ref, half * tiles + tile, new_ref[...])
        out_ref[256 * tile : 256 * (tile + 1), :] = totals.astype(bf16)
    out_ref[256 * tiles :, :] = counts_ref[...]


def keep_kernel(place_ref, owner_ref, new_ref, counts_ref, out_ref):
    half_totals(owner_ref, new_ref, counts_ref, core_of(place_ref), out_ref)


def fine_forward_kernel(
    place_ref,
    h_ref,
    first_ref,
    second_ref,
    weights_ref,
    columns_t_ref,
    owner_ref,
    counts_ref,
    after_ref,
    summed_ref,
    slope_hbm,
    new_ref,
    give_ref,
    own,
    far,
    halo,
    slope_ref,
    sem,
):
    self_weight, other_weight = matrix(weights_ref, 0), matrix(weights_ref, 1)
    level_terms(h_ref, (first_ref, second_ref), self_weight, other_weight, own, far, halo)

    def step(index, carry):
        here = chunk_of(index, STEP * BLOCK)
        total, slopes = edges(own[here, :], far[here, :], columns_t_ref[here, :], halo)
        summed_ref[here, :] = total
        edge = chunk_of(index, 8 * STEP * BLOCK)
        slope_ref[edge, :] = jnp.concatenate(slopes, 0)
        pltpu.make_async_copy(slope_ref.at[edge, :], slope_hbm.at[edge, :], sem).start()
        return carry

    lax.fori_loop(0, h_ref.shape[0] // (STEP * BLOCK), step, None)
    new_ref[...] = (
        h_ref[...].astype(f32) + dot(summed_ref[...], matrix(weights_ref, 2))
    ).astype(bf16)
    half_totals(owner_ref, new_ref, counts_ref, 1 - core_of(place_ref), give_ref)
    pltpu.make_async_copy(slope_ref, slope_hbm, sem).wait()


def half_kernel(place_ref, totals_ref, more_totals_ref, after_ref, half_ref, counts_ref):
    half_rows = half_ref.shape[0]
    totals = totals_ref[...].astype(f32) + more_totals_ref[...].astype(f32)
    digits = totals[half_rows:]
    tiles = counts_ref.shape[0]
    counts_ref[...] = DIGIT * digits[:tiles] + digits[tiles:]
    per_row = counts_ref[...].T
    first = core_of(place_ref) == 0
    for tile in range(tiles // 2):
        here = slice(tile * 128, (tile + 1) * 128)
        later = tile + tiles // 2
        low = jnp.broadcast_to(per_row[:, tile : tile + 1], (128, 128))
        high = jnp.broadcast_to(per_row[:, later : later + 1], (128, 128))
        half_ref[here, :] = (totals[here] / jnp.where(first, low, high)).astype(bf16)


def coarse_input_kernel(
    place_ref,
    half_ref,
    their_half_ref,
    sends_ref,
    cin_ref,
    first_ref,
    second_ref,
):
    mine, theirs = half_ref[...].astype(f32), their_half_ref[...].astype(f32)
    first = core_of(place_ref) == 0
    cin = jnp.concatenate([jnp.where(first, mine, theirs), jnp.where(first, theirs, mine)], 0)
    cin = cin.astype(bf16)
    cin_ref[...] = cin
    place = lax.broadcasted_iota(jnp.int32, (cin.shape[0], sends_ref.shape[1]), 0)
    sent = dot_tn(pick(sends_ref[...] == place), cin).astype(bf16)
    halo_rows = first_ref.shape[0]
    first_ref[...] = sent[:halo_rows]
    second_ref[...] = sent[halo_rows:]


def coarse_forward_kernel(
    cin_ref,
    first_ref,
    second_ref,
    weights_ref,
    columns_t_ref,
    summed_ref,
    slope_ref,
    own,
    far,
    halo,
):
    self_weight, other_weight = matrix(weights_ref, 3), matrix(weights_ref, 4)
    level_terms(cin_ref, (first_ref, second_ref), self_weight, other_weight, own, far, halo)

    def step(index, carry):
        here = chunk_of(index, STEP * BLOCK)
        total, slopes = edges(own[here, :], far[here, :], columns_t_ref[here, :], halo)
        summed_ref[here, :] = total
        slope_ref[chunk_of(index, 8 * STEP * BLOCK), :] = jnp.concatenate(slopes, 0)
        return carry

    lax.fori_loop(0, cin_ref.shape[0] // (STEP * BLOCK), step, None)


def coarse_backward_kernel(
    slope_ref,
    chip_sums_ref,
    more_sums_ref,
    weights_ref,
    columns_ref,
    part_ref,
    first_grad_ref,
    second_grad_ref,
    sums_ref,
    ups_ref,
    downs_ref,
    grad_sum,
    halo_grad,
):
    halo_rows = first_grad_ref.shape[0]
    halo_grad[...] = jnp.zeros_like(halo_grad)
    sums_ref[...] = (chip_sums_ref[...].astype(f32) + more_sums_ref[...].astype(f32)).astype(bf16)
    part_ref[...] = dot_nt(sums_ref[...], matrix(weights_ref, 6))
    ups_ref[...] = part_ref[...].astype(bf16)
    grad_sum[...] = (dot_nt(ups_ref[...], matrix(weights_ref, 5)) * 0.5).astype(bf16)
    count = STEP * BLOCK

    def step(index, carry):
        here = chunk_of(index, count)
        slope = slope_ref[chunk_of(index, 8 * count), :]
        slopes = [slope[n * 8 * BLOCK : (n + 1) * 8 * BLOCK] for n in range(STEP)]
        downs_ref[here, :] = edges_back(
            slopes, grad_sum[here, :], columns_ref[:, here], halo_grad
        )
        return carry

    lax.fori_loop(0, part_ref.shape[0] // count, step, None)
    first_grad_ref[...] = halo_grad[:halo_rows, :].astype(bf16)
    second_grad_ref[...] = halo_grad[halo_rows:, :].astype(bf16)


def coarse_tail_kernel(
    place_ref,
    cin_ref,
    first_ref,
    second_ref,
    sums_ref,
    matrices_ref,
    first_grad_ref,
    second_grad_ref,
    summed_ref,
    ups_ref,
    downs_ref,
    fine_ref,
    weights_ref,
):
    cin = cin_ref[...]
    out = (cin.astype(f32) + dot(summed_ref[...], matrix(matrices_ref, 5))).astype(bf16)
    fine_ref[...] = dot(out, matrix(matrices_ref, 6)).astype(bf16)
    pair_grad = dot_tn(cin, downs_ref[...])
    other_grad = (
        pair_grad[:, 128:]
        + dot_tn(first_ref[...], first_grad_ref[...])
        + dot_tn(second_ref[...], second_grad_ref[...])
    )
    grads = [
        pair_grad[:, :128],
        other_grad,
        dot_tn(summed_ref[...], ups_ref[...]),
        dot_tn(out, sums_ref[...]),
    ]
    weights_ref[...] = choose(group_of(place_ref), grads).astype(bf16)


def choose(place, values):
    picked = values[-1]
    for n, value in enumerate(values[:-1]):
        picked = jnp.where(place == n, value, picked)
    return picked


def owner_columns(owner_ref):
    owner = owner_ref[...].astype(f32)
    row = jnp.concatenate([owner[q : q + 1, :] for q in range(owner.shape[0])], 1)
    return jnp.broadcast_to(row, (8, row.shape[1])).T


def owner_rows(owners, values):
    count = owners.shape[0]
    wide = jnp.broadcast_to(owners[:, 0:1], (count, 128))
    lane = lax.broadcasted_iota(jnp.int32, (count, 128), 1)
    first, second = lane.astype(bf16), (lane + 128).astype(bf16)
    rows = []
    for tile in range(values.shape[0] // 256):
        here = (wide - 256.0 * tile).astype(bf16)
        rows += [pick16(here, first), pick16(here, second)]
    return dot(jnp.concatenate(rows, 1), values)


def result_kernel(h_ref, summed_ref, weights_ref, owners_ref, fine_ref, out_hbm, out_ref, sem):
    def step(index, carry):
        here = chunk_of(index, CHUNK)
        updated = h_ref[here, :].astype(f32) + dot(summed_ref[here, :], matrix(weights_ref, 2))
        out_ref[here, :] = (updated + owner_rows(owners_ref[here, :], fine_ref[...])).astype(bf16)
        pltpu.make_async_copy(out_ref.at[here, :], out_hbm.at[here, :], sem).start()
        return carry

    lax.fori_loop(0, h_ref.shape[0] // CHUNK, step, None)
    pltpu.make_async_copy(out_ref, out_hbm, sem).wait()


def fine_backward_kernel(
    place_ref,
    h_ref,
    first_ref,
    second_ref,
    g_ref,
    summed_ref,
    slope_hbm,
    matrices_ref,
    columns_ref,
    owners_ref,
    part_ref,
    counts_ref,
    coarse_downs_ref,
    first_back_ref,
    second_back_ref,
    sends_ref,
    coarse_weights_ref,
    ups_ref,
    downs_ref,
    first_grad_ref,
    second_grad_ref,
    give_ref,
    keep_ref,
    grad_sum,
    halo_grad,
    mean,
    slope_ref,
    weights,
    slope_sems,
):
    count = STEP * BLOCK
    steps = h_ref.shape[0] // count

    def slope_copy(index):
        edge = chunk_of(index, 8 * count)
        return pltpu.make_async_copy(
            slope_hbm.at[edge, :], slope_ref.at[edge, :], slope_sems.at[index]
        )

    for index in range(steps):
        slope_copy(index).start()
    halo_rows = first_ref.shape[0]
    coarse_rows = part_ref.shape[0]
    halo_grad[...] = jnp.zeros_like(halo_grad)

    place = lax.broadcasted_iota(jnp.int32, (coarse_rows, sends_ref.shape[1]), 0)
    sends = pick(sends_ref[...] == place)
    back = jnp.concatenate([first_back_ref[...], second_back_ref[...]], 0)
    back = dot_nt(back, matrix(matrices_ref, 4)).astype(bf16)
    plain = jnp.concatenate([matrix(matrices_ref, 3), matrix(matrices_ref, 4)], 1)
    grad_in = part_ref[...] + dot_nt(coarse_downs_ref[...], plain) + dot(sends, back)
    per_row = counts_ref[...].T
    for tile in range(coarse_rows // 128):
        here = slice(tile * 128, (tile + 1) * 128)
        mean[here, :] = (grad_in[here, :] / per_row[:, tile : tile + 1]).astype(bf16)

    def owner_step(index):
        here = chunk_of(index, count)
        grad_up = g_ref[here, :].astype(f32) + owner_rows(owners_ref[here, :], mean[...])
        ups = grad_up.astype(bf16)
        ups_ref[here, :] = ups
        grad_sum[here, :] = (dot_nt(ups, matrix(matrices_ref, 2)) * 0.5).astype(bf16)

    def edge_step(index):
        here = chunk_of(index, count)
        slope_copy(index).wait()
        slope = slope_ref[chunk_of(index, 8 * count), :]
        slopes = [slope[n * 8 * BLOCK : (n + 1) * 8 * BLOCK] for n in range(STEP)]
        downs_ref[here, :] = edges_back(
            slopes, grad_sum[here, :], columns_ref[:, here], halo_grad
        )

    owner_step(0)

    def step(index, carry):
        edge_step(index)
        owner_step(index + 1)
        return carry

    lax.fori_loop(0, steps - 1, step, None)
    edge_step(steps - 1)
    first_grad = halo_grad[:halo_rows, :].astype(bf16)
    second_grad = halo_grad[halo_rows:, :].astype(bf16)
    first_grad_ref[...] = first_grad
    second_grad_ref[...] = second_grad
    pair_grad = dot_tn(h_ref[...], downs_ref[...])
    weights[0:128, :] = pair_grad[:, :128]
    weights[128:256, :] = (
        pair_grad[:, 128:]
        + dot_tn(first_ref[...], first_grad)
        + dot_tn(second_ref[...], second_grad)
    )
    weights[256:384, :] = dot_tn(summed_ref[...], ups_ref[...])
    first = core_of(place_ref) == 0
    low, high = weights[:192, :], weights[192:, :]
    give_ref[...] = jnp.where(first, high, low)
    keep_ref[:192, :] = jnp.where(first, low, high)
    keep_ref[192:, :] = coarse_weights_ref[...].astype(f32)


def finish_kernel(
    ups_ref,
    downs_ref,
    first_back_ref,
    second_back_ref,
    sends_ref,
    matrices_ref,
    out_hbm,
    out_ref,
    sem,
):
    other = matrix(matrices_ref, 1)
    plain = jnp.concatenate([matrix(matrices_ref, 0), other], 1)
    back = jnp.concatenate([first_back_ref[...], second_back_ref[...]], 0)
    back = dot_nt(back, other).astype(bf16)
    sends = sends_ref[...]
    place = lax.broadcasted_iota(jnp.int32, (256, sends.shape[1]), 0).astype(bf16)

    def step(index, carry):
        here = chunk_of(index, CHUNK)
        rows = []
        for part in range(CHUNK // 256):
            local = (sends - (index * CHUNK + 256 * part)).astype(f32)
            rows.append(pick16(jnp.broadcast_to(local, place.shape).astype(bf16), place))
        grad = ups_ref[here, :].astype(f32) + dot_nt(downs_ref[here, :], plain)
        out_ref[here, :] = (grad + dot(jnp.concatenate(rows, 0), back)).astype(bf16)
        pltpu.make_async_copy(out_ref.at[here, :], out_hbm.at[here, :], sem).start()
        return carry

    lax.fori_loop(0, ups_ref.shape[0] // CHUNK, step, None)
    pltpu.make_async_copy(out_ref, out_hbm, sem).wait()


def add_kernel(mine_ref, theirs_ref, *rest):
    out_ref = rest[-1]
    out_ref[...] = (mine_ref[...].astype(f32) + theirs_ref[...].astype(f32)).astype(bf16)


def add_first_kernel(keep_ref, theirs_ref, out_ref):
    out_ref[:192, :] = (keep_ref[:192, :] + theirs_ref[...]).astype(bf16)
    out_ref[192:, :] = keep_ref[192:, :].astype(bf16)


def add_gather_kernel(mine_ref, y_ref, x_ref, both_ref, after_ref, out_ref):
    mine = mine_ref[...].astype(f32) + y_ref[...].astype(f32)
    theirs = x_ref[...].astype(f32) + both_ref[...].astype(f32)
    out_ref[:192, :] = mine[:192] + theirs[:192]
    out_ref[192:320, :] = mine[192:]
    out_ref[320:, :] = theirs[192:]


def weights_kernel(place_ref, mine_ref, theirs_ref, out_ref):
    group = group_of(place_ref)
    low, high = lax.rem(group, 2), group // 2
    mine, theirs = mine_ref[:192, :], theirs_ref[:192, :]
    out_ref[:192, :] = jnp.where(low == 0, mine, theirs)
    out_ref[192:384, :] = jnp.where(low == 0, theirs, mine)
    for n in range(4):
        near = jnp.where(low == n % 2, mine_ref[192:320, :], theirs_ref[192:320, :])
        far = jnp.where(low == n % 2, mine_ref[320:448, :], theirs_ref[320:448, :])
        value = jnp.where(high == n // 2, near, far)
        out_ref[384 + 128 * n : 512 + 128 * n, :] = value


def exchange(first, second):
    count = lax.axis_size("sub")
    routes = []
    for start in range(2):
        pairs = [(i, i + 1) for i in range(start, count - 1, 2)]
        routes.append(pairs + [(j, i) for i, j in pairs])
    return lax.ppermute(first, "sub", routes[0]), lax.ppermute(second, "sub", routes[1])


def swapped(block, axis, distance):
    return lax.ppermute(block, axis, [(i, i ^ distance) for i in range(lax.axis_size(axis))])


def total_weights(give, keep, place, after, last):
    weights = call(
        add_first_kernel, shape(320, 128, bf16), [keep, swapped(give, "grp", 1)]
    )
    distance, number = 2, 0
    while distance < lax.axis_size("sub"):
        theirs = swapped(weights, "sub", distance)
        waits = after[number] if number < len(after) else ()
        weights = call(
            add_kernel,
            shape(320, 128, bf16),
            [weights, theirs, *waits],
            [VMEM, VMEM] + [HBM] * len(waits),
        )
        distance, number = 2 * distance, number + 1
    count = lax.axis_size("sub")
    corners = [
        (g * count + s, (g ^ 2) * count + (s ^ 1))
        for g in range(lax.axis_size("grp"))
        for s in range(count)
    ]
    weights = call(
        add_gather_kernel,
        shape(448, 128, f32),
        [
            weights,
            swapped(weights, "sub", 1),
            swapped(weights, "grp", 2),
            lax.ppermute(weights, ("grp", "sub"), corners),
            last,
        ],
        [VMEM] * 4 + [HBM],
    )
    return call(
        weights_kernel,
        shape(896, 128, f32),
        [place, weights, swapped(weights, "grp", 1)],
        [VMEM] * 3,
    )


def per_device(
    states,
    cotangent,
    fine_self,
    fine_other,
    fine_node,
    coarse_self,
    coarse_other,
    coarse_node,
    prolong,
    fine_nbr,
    fine_mask,
    fine_send_lo,
    fine_send_hi,
    coarse_nbr,
    coarse_mask,
    coarse_send_lo,
    coarse_send_hi,
    coarse_owner,
):
    rows, features = states.shape
    coarse_rows = coarse_nbr.shape[0]
    halo_rows = fine_send_lo.shape[0]
    coarse_halo = coarse_send_lo.shape[0]
    count_rows = coarse_rows // 128
    owner = coarse_owner.reshape(rows // 128, 128)

    def buffer(count, columns, dtype):
        return pltpu.VMEM((count, columns), dtype)

    to_first, to_second, states, place = gather_rows(states, fine_send_lo, fine_send_hi)
    first, second = exchange(to_first, to_second)

    (
        counts, columns, columns_t, coarse_columns, coarse_columns_t, cotangent, matrices, sends,
        coarse_sends, owner,
    ) = call(
        functools.partial(prepare_kernel, halo_rows=halo_rows, coarse_halo=coarse_halo),
        [
            shape(2 * count_rows, features, bf16),
            shape(8, rows, f32),
            shape(rows, 8, f32),
            shape(8, coarse_rows, f32),
            shape(coarse_rows, 8, f32),
            shape(rows, features, bf16),
            shape(7 * features, features, bf16),
            shape(1, 2 * halo_rows, jnp.int32),
            shape(1, 2 * coarse_halo, jnp.int32),
            shape(rows // 128, 128, jnp.int32),
        ],
        [
            place, cotangent, owner, fine_nbr.T, fine_mask.T, coarse_nbr.T, coarse_mask.T,
            fine_send_lo[None], fine_send_hi[None], coarse_send_lo[None], coarse_send_hi[None],
            fine_self, fine_other, fine_node, coarse_self, coarse_other, coarse_node, prolong,
            to_first,
        ],
        [VMEM] + [HBM] * 17 + [ANY],
        [buffer(8, rows, jnp.int32)] * 2
        + [buffer(8, coarse_rows, jnp.int32)] * 2
        + [buffer(1, halo_rows, jnp.int32)] * 2
        + [buffer(1, coarse_halo, jnp.int32)] * 2
        + [pltpu.SemaphoreType.DMA((17,))],
    )

    sums = call(
        sums_kernel,
        shape(coarse_rows, features, bf16),
        [owner, cotangent, sends],
        [VMEM, VMEM, ANY],
    )
    sums = call(
        relay_kernel,
        shape(coarse_rows, features, bf16),
        [sums, first, second],
        [VMEM, ANY, ANY],
    )
    more_sums = swapped(sums, "grp", 1)

    half_rows = coarse_rows // 2 + 2 * count_rows
    summed, slope, new, give = call(
        fine_forward_kernel,
        [
            shape(rows, features, bf16),
            pltpu.HBM((8 * rows, features), bf16),
            shape(rows, features, bf16),
            shape(half_rows, features, bf16),
        ],
        [place, states, first, second, matrices, columns_t, owner, counts, sums],
        [VMEM] * 8 + [ANY],
        [
            buffer(rows, features, f32),
            buffer(rows, features, bf16),
            buffer(2 * halo_rows, features, bf16),
            buffer(8 * rows, features, bf16),
            pltpu.SemaphoreType.DMA,
        ],
        [VMEM, HBM, VMEM, VMEM],
        mib=32,
    )
    theirs = swapped(give, "grp", 1)
    keep = call(
        keep_kernel,
        shape(half_rows, features, bf16),
        [place, owner, new, counts],
        [VMEM] + [VMEM] * 3,
    )
    chip_totals = call(add_kernel, shape(half_rows, features, bf16), [keep, theirs])
    more_totals = swapped(chip_totals, "grp", 2)
    chip_sums = call(
        add_kernel,
        shape(coarse_rows, features, bf16),
        [sums, more_sums, chip_totals],
        [VMEM, VMEM, ANY],
    )
    more_sums = swapped(chip_sums, "grp", 2)
    owners_t = call(owners_kernel, shape(rows, 8, f32), [owner, chip_totals], [VMEM, ANY])

    half, counts = call(
        half_kernel,
        [shape(coarse_rows // 2, features, bf16), shape(count_rows, features, f32)],
        [place, chip_totals, more_totals, owners_t],
        [VMEM, VMEM, VMEM, ANY],
    )
    their_half = swapped(half, "grp", 1)
    coarse_in, to_first, to_second = call(
        coarse_input_kernel,
        [
            shape(coarse_rows, features, bf16),
            shape(coarse_halo, features, bf16),
            shape(coarse_halo, features, bf16),
        ],
        [place, half, their_half, coarse_sends],
    )
    coarse_first, coarse_second = exchange(to_first, to_second)

    coarse_sum, coarse_slope = call(
        coarse_forward_kernel,
        [shape(coarse_rows, features, bf16), shape(8 * coarse_rows, features, bf16)],
        [coarse_in, coarse_first, coarse_second, matrices, coarse_columns_t],
        scratch=[
            buffer(coarse_rows, features, f32),
            buffer(coarse_rows, features, bf16),
            buffer(2 * coarse_halo, features, bf16),
        ],
    )
    coarse_part, first_grad, second_grad, sums, coarse_ups, coarse_downs = call(
        coarse_backward_kernel,
        [
            shape(coarse_rows, features, f32),
            shape(coarse_halo, features, bf16),
            shape(coarse_halo, features, bf16),
            shape(coarse_rows, features, bf16),
            shape(coarse_rows, features, bf16),
            shape(coarse_rows, 2 * features, bf16),
        ],
        [coarse_slope, chip_sums, more_sums, matrices, coarse_columns],
        scratch=[
            buffer(coarse_rows, features, bf16),
            buffer(2 * coarse_halo, features, f32),
        ],
    )
    first_back, second_back = exchange(first_grad, second_grad)

    fine_term, coarse_weights = call(
        coarse_tail_kernel,
        [shape(coarse_rows, features, bf16), shape(features, features, bf16)],
        [
            place, coarse_in, coarse_first, coarse_second, sums, matrices,
            first_grad, second_grad, coarse_sum, coarse_ups, coarse_downs,
        ],
        [VMEM] + [VMEM] * 10,
    )
    result = call(
        result_kernel,
        pltpu.HBM((rows, features), bf16),
        [states, summed, matrices, owners_t, fine_term],
        scratch=[buffer(rows, features, bf16), pltpu.SemaphoreType.DMA],
        out_specs=HBM,
    )

    ups, downs, first_grad, second_grad, give, keep = call(
        fine_backward_kernel,
        [
            shape(rows, features, bf16),
            shape(rows, 2 * features, bf16),
            shape(halo_rows, features, bf16),
            shape(halo_rows, features, bf16),
            shape(192, features, f32),
            shape(320, features, f32),
        ],
        [
            place, states, first, second, cotangent, summed, slope, matrices, columns, owners_t,
            coarse_part, counts, coarse_downs, first_back, second_back, coarse_sends,
            coarse_weights,
        ],
        [VMEM] + [VMEM] * 5 + [HBM] + [VMEM] * 10,
        [
            buffer(rows, features, bf16),
            buffer(2 * halo_rows, features, f32),
            buffer(coarse_rows, features, bf16),
            buffer(8 * rows, features, bf16),
            buffer(384, features, f32),
            pltpu.SemaphoreType.DMA((rows // (STEP * BLOCK),)),
        ],
        mib=32,
    )
    first_back, second_back = exchange(first_grad, second_grad)

    grad_states = call(
        finish_kernel,
        pltpu.HBM((rows, features), bf16),
        [ups, downs, first_back, second_back, sends, matrices],
        scratch=[buffer(rows, features, bf16), pltpu.SemaphoreType.DMA],
        out_specs=HBM,
    )
    grad_weights = total_weights(give, keep, place, ((), (grad_states,)), result)
    return (result, grad_states, grad_weights.reshape(7, features, features))


def solution(mesh):
    fine = P(("grp", "sub"), None)
    fine_row = P(("grp", "sub"))
    in_specs = (
        (fine, fine)
        + (P(),) * 7
        + (fine, fine, fine_row, fine_row)
        + (P("sub", None), P("sub", None), P("sub"), P("sub"), fine_row)
    )
    return jax.shard_map(
        per_device, mesh=mesh, in_specs=in_specs, out_specs=(fine, fine, P()), check_vma=False
    )
```

```python
import functools

import jax
import jax.numpy as jnp
from jax import lax
from jax.experimental import pallas as pl
from jax.experimental.pallas import tpu as pltpu
from jax.sharding import PartitionSpec as P

f32 = jnp.float32
bf16 = jnp.bfloat16
BLOCK = 64
PAIR = 2 * BLOCK
STEP = 16
CHUNK = 1024
NEVER = -1e30
DIGIT = 64.0
VMEM = pl.BlockSpec(memory_space=pltpu.VMEM)
SMEM = pl.BlockSpec(memory_space=pltpu.SMEM)
ANY = pl.BlockSpec(memory_space=pl.ANY)
HBM = pl.BlockSpec(memory_space=pltpu.HBM)
MIB = 1024 * 1024


def dot(a, b):
    return jnp.dot(a, b, preferred_element_type=f32)


def dot_nt(a, b):
    return lax.dot_general(a, b, (((1,), (1,)), ((), ())), preferred_element_type=f32)


def dot_tn(a, b):
    return lax.dot_general(a, b, (((0,), (0,)), ((), ())), preferred_element_type=f32)


def pick(condition):
    return jnp.where(condition, 1.0, 0.0).astype(bf16)


def pick16(values, places):
    return jnp.where(values == places, jnp.ones((), bf16), jnp.zeros((), bf16))


def call(kernel, out_shape, args, in_specs=None, scratch=(), out_specs=None, mib=16):
    many = isinstance(out_shape, (list, tuple))
    in_specs = in_specs or [VMEM] * len(args)
    args = [
        pltpu.with_memory_space_constraint(arg, pltpu.HBM) if spec is HBM else arg
        for arg, spec in zip(args, in_specs)
    ]
    return pl.pallas_call(
        kernel,
        out_shape=out_shape,
        in_specs=in_specs,
        out_specs=out_specs or ([VMEM] * len(out_shape) if many else VMEM),
        scratch_shapes=list(scratch),
        compiler_params=pltpu.CompilerParams(vmem_limit_bytes=mib * MIB),
    )(*args)


def shape(rows, columns, dtype):
    return jax.ShapeDtypeStruct((rows, columns), dtype)


def lanes(row, count):
    return row[:, :count] if count < 128 else jnp.concatenate([row] * (count // 128), 1)


def is_even(place_ref):
    return place_ref[0:1, :]


def group_of(place_ref):
    return place_ref[8:9, :]


def core_of(place_ref):
    return lax.rem(place_ref[8:9, :], 2)


def slot_columns(nbr, mask, halo_rows, even):
    rows = nbr.shape[1]
    block = lax.broadcasted_iota(jnp.int32, nbr.shape, 1) // BLOCK
    halo = lax.rem(block, halo_rows // BLOCK) * BLOCK
    lower = BLOCK + BLOCK * lanes(even, rows)
    column = jnp.where(
        nbr < rows,
        nbr - block * BLOCK,
        jnp.where(
            nbr < rows + halo_rows,
            lower + nbr - rows - halo,
            3 * BLOCK - lower + nbr - rows - halo_rows - halo,
        ),
    )
    return jnp.where(mask > 0, column, 3 * BLOCK).astype(f32)


def selector(columns_t):
    first = lax.broadcasted_iota(jnp.int32, (BLOCK, 128), 1).astype(bf16)
    second = (lax.broadcasted_iota(jnp.int32, (BLOCK, 128), 1) + 128).astype(bf16)
    parts = []
    for k in range(8):
        wide = jnp.broadcast_to(columns_t[:, k : k + 1], (BLOCK, 128)).astype(bf16)
        parts.append(jnp.concatenate([pick16(wide, first), pick16(wide, second)], 1))
    return jnp.concatenate(parts, 0)


def selector_t(columns, rolled, half):
    lane = lax.broadcasted_iota(jnp.int32, (1, 128), 1)
    place = lax.broadcasted_iota(jnp.int32, (3 * BLOCK, 128), 0).astype(bf16)
    parts = []
    for j in range(4):
        left, right = (columns, rolled) if half == 0 else (rolled, columns)
        row = jnp.where(lane < BLOCK, left[2 * j : 2 * j + 1], right[2 * j + 1 : 2 * j + 2])
        wide = jnp.broadcast_to(row, (3 * BLOCK, 128)).astype(bf16)
        parts.append(pick16(wide, place))
    return jnp.concatenate(parts, 1)


def window_of(far, halo, place):
    halo_rows = halo.shape[0] // 2
    start = place * BLOCK
    return jnp.concatenate(
        [
            far,
            halo[start : start + BLOCK, :],
            halo[halo_rows + start : halo_rows + start + BLOCK, :],
            jnp.full((BLOCK, far.shape[1]), NEVER, bf16),
        ],
        0,
    )


def chunk_of(index, count):
    return pl.ds(pl.multiple_of(index * count, count), count)


def matrix(weights_ref, n):
    return weights_ref[128 * n : 128 * (n + 1), :]


def level_terms(h_ref, halo_refs, self_weight, other_weight, own, far, halo):
    halo_rows = halo_refs[0].shape[0]
    other = other_weight * 0.5
    terms = dot(h_ref[...], jnp.concatenate([self_weight * 0.5, other], 1))
    own[...] = terms[:, :128]
    far[...] = terms[:, 128:].astype(bf16)
    halo[:halo_rows, :] = dot(halo_refs[0][...], other).astype(bf16)
    halo[halo_rows:, :] = dot(halo_refs[1][...], other).astype(bf16)


def edges(own_rows, far_rows, slots, halo):
    places = halo.shape[0] // (2 * BLOCK)
    assert STEP % places == 0
    tables = []
    for n in range(STEP):
        part = slice(n * BLOCK, (n + 1) * BLOCK)
        window = window_of(far_rows[part], halo, n % places)
        tables.append(dot(selector(slots[part]), window))
    sums, slopes = [], []
    for n, picked in enumerate(tables):
        own = own_rows[n * BLOCK : (n + 1) * BLOCK]
        values, pieces = [], []
        for k in range(8):
            y = (picked[k * BLOCK : (k + 1) * BLOCK] + own).astype(bf16)
            t = jnp.tanh(y)
            bent = y * t
            values.append(y + bent)
            pieces.append((1 + t) * (1 + (y - bent)))
        while len(values) > 1:
            values = [left + right for left, right in zip(values[::2], values[1::2])]
        sums.append(values[0])
        slopes.append(jnp.concatenate(pieces, 0))
    return jnp.concatenate(sums, 0), slopes


def edges_back(slopes, grad_sum, columns, halo_grad):
    places = halo_grad.shape[0] // (2 * BLOCK)
    halo_rows = halo_grad.shape[0] // 2
    windows, downs = [], []
    for n, slope in enumerate(slopes):
        part = grad_sum[n * BLOCK : (n + 1) * BLOCK]
        grads = [slope[k * BLOCK : (k + 1) * BLOCK] * part for k in range(8)]
        downs.append(sum(grad.astype(f32) for grad in grads))
        mine = columns[:, n // 2 * PAIR : (n // 2 + 1) * PAIR]
        selected = selector_t(mine, pltpu.roll(mine, BLOCK, 1), n % 2)
        windows.append(dot(selected, jnp.concatenate(grads, 0)))
    for place in range(places):
        for side in range(2):
            start = side * halo_rows + place * BLOCK
            total = halo_grad[start : start + BLOCK, :]
            for window in windows[place::places]:
                total = total + window[(side + 1) * BLOCK : (side + 2) * BLOCK]
            halo_grad[start : start + BLOCK, :] = total
    local = jnp.concatenate([window[:BLOCK] for window in windows], 0)
    down = jnp.concatenate(downs, 0)
    return jnp.concatenate([down, local], 1).astype(bf16)


def fetch(pairs, sems):
    copies = [pltpu.make_async_copy(src, dst, sems.at[n]) for n, (src, dst) in enumerate(pairs)]
    for copy in copies:
        copy.start()
    for copy in copies:
        copy.wait()


def gather_kernel(
    lo_hbm,
    hi_hbm,
    x_hbm,
    first_ref,
    second_ref,
    x_ref,
    vector_ref,
    wide,
    up,
    down,
    lo,
    hi,
    sems,
):
    fetch([(x_hbm, x_ref), (lo_hbm, lo), (hi_hbm, hi)], sems)
    wide[...] = x_ref[...].astype(f32)

    def step(r, carry):
        up[pl.ds(r, 1), :] = wide[pl.ds(hi[r], 1), :]
        down[pl.ds(r, 1), :] = wide[pl.ds(lo[r], 1), :]
        return carry

    lax.fori_loop(0, up.shape[0], step, None, unroll=16)
    parity = 1 - lax.rem(lax.axis_index("sub"), 2)
    even = parity > 0
    vector_ref[:8, :] = jnp.full((8, 128), parity, jnp.int32)
    vector_ref[8:, :] = jnp.full((8, 128), lax.axis_index("grp"), jnp.int32)
    first_ref[...] = jnp.where(even, up[...], down[...]).astype(bf16)
    second_ref[...] = jnp.where(even, down[...], up[...]).astype(bf16)


def gather_rows(x, send_lo, send_hi):
    rows, features = x.shape
    count = send_lo.shape[0]
    out = shape(count, features, bf16)
    return call(
        gather_kernel,
        [out, out, shape(rows, features, bf16), shape(16, 128, jnp.int32)],
        [send_lo, send_hi, x],
        [HBM, HBM, HBM],
        [
            pltpu.VMEM((rows, features), f32),
            pltpu.VMEM((count, features), f32),
            pltpu.VMEM((count, features), f32),
            pltpu.SMEM((count,), jnp.int32),
            pltpu.SMEM((count,), jnp.int32),
            pltpu.SemaphoreType.DMA((3,)),
        ],
    )


def owner_sums(owner_ref, tile, values):
    place = lax.broadcasted_iota(jnp.int32, (256, 128), 0).astype(bf16)
    owner = (owner_ref[...] - tile * 256).astype(f32)
    rows = jnp.concatenate(
        [
            pick16(jnp.broadcast_to(owner[q : q + 1], (256, 128)).astype(bf16), place)
            for q in range(owner.shape[0])
        ],
        1,
    )
    return dot(rows, values)


def prepare_kernel(
    place_ref,
    g_hbm,
    owner_hbm,
    nbr_hbm,
    mask_hbm,
    coarse_nbr_hbm,
    coarse_mask_hbm,
    lo_hbm,
    hi_hbm,
    coarse_lo_hbm,
    coarse_hi_hbm,
    *rest,
    halo_rows,
    coarse_halo,
):
    weight_hbms, rest = rest[:7], rest[7:]
    (
        after_ref,
        counts_ref,
        columns_ref,
        columns_t_ref,
        coarse_columns_ref,
        coarse_columns_t_ref,
        g_ref,
        weights_ref,
        sends_ref,
        coarse_sends_ref,
        owner_ref,
        nbr_ref,
        mask_ref,
        coarse_nbr_ref,
        coarse_mask_ref,
        lo_ref,
        hi_ref,
        coarse_lo_ref,
        coarse_hi_ref,
        sems,
    ) = rest
    fetch(
        [
            (g_hbm, g_ref),
            (owner_hbm, owner_ref),
            (nbr_hbm, nbr_ref),
            (mask_hbm, mask_ref),
            (coarse_nbr_hbm, coarse_nbr_ref),
            (coarse_mask_hbm, coarse_mask_ref),
            (lo_hbm, lo_ref),
            (hi_hbm, hi_ref),
            (coarse_lo_hbm, coarse_lo_ref),
            (coarse_hi_hbm, coarse_hi_ref),
        ]
        + [(w, weights_ref.at[pl.ds(128 * n, 128), :]) for n, w in enumerate(weight_hbms)],
        sems,
    )
    even = is_even(place_ref)
    for low, high, out in (
        (lo_ref, hi_ref, sends_ref),
        (coarse_lo_ref, coarse_hi_ref, coarse_sends_ref),
    ):
        up = lanes(even, low.shape[1]) > 0
        first = jnp.where(up, high[...], low[...])
        second = jnp.where(up, low[...], high[...])
        out[...] = jnp.concatenate([first, second], 1)
    columns_ref[...] = slot_columns(nbr_ref[...], mask_ref[...], halo_rows, even)
    columns_t_ref[...] = columns_ref[...].T
    coarse_columns_ref[...] = slot_columns(
        coarse_nbr_ref[...], coarse_mask_ref[...], coarse_halo, even
    )
    coarse_columns_t_ref[...] = coarse_columns_ref[...].T
    tiles = counts_ref.shape[0] // 2
    owner = owner_ref[...]
    high, low = owner // 128, lax.rem(owner, 128)
    groups = owner.shape[0]
    place = lax.broadcasted_iota(jnp.int32, (128, 128), 0)
    high_rows = jnp.concatenate(
        [pick(high[q : q + 1, :] == place[:tiles]) for q in range(groups)], 1
    )
    low_rows = jnp.concatenate(
        [pick(low[q : q + 1, :] == place) for q in range(groups)], 1
    )
    counts = dot_nt(high_rows, low_rows)
    most = jnp.floor(counts * (1 / DIGIT))
    counts_ref[...] = jnp.concatenate([most, counts - DIGIT * most], 0).astype(bf16)


def sums_kernel(owner_ref, g_ref, after_ref, sums_ref):
    def step(tile, carry):
        sums_ref[chunk_of(tile, 256), :] = owner_sums(owner_ref, tile, g_ref[...]).astype(bf16)
        return carry

    lax.fori_loop(0, sums_ref.shape[0] // 256, step, None)


def relay_kernel(x_ref, after_ref, also_after_ref, out_ref):
    out_ref[...] = x_ref[...]


def owners_kernel(owner_ref, after_ref, owners_ref):
    owners_ref[...] = owner_columns(owner_ref)


def half_totals(owner_ref, new_ref, counts_ref, half, out_ref):
    tiles = (out_ref.shape[0] - counts_ref.shape[0]) // 256
    for tile in range(tiles):
        totals = owner_sums(owner_ref, half * tiles + tile, new_ref[...])
        out_ref[256 * tile : 256 * (tile + 1), :] = totals.astype(bf16)
    out_ref[256 * tiles :, :] = counts_ref[...]


def keep_kernel(place_ref, owner_ref, new_ref, counts_ref, out_ref):
    half_totals(owner_ref, new_ref, counts_ref, core_of(place_ref), out_ref)


def fine_forward_kernel(
    place_ref,
    h_ref,
    first_ref,
    second_ref,
    weights_ref,
    columns_t_ref,
    owner_ref,
    counts_ref,
    after_ref,
    summed_ref,
    slope_hbm,
    new_ref,
    give_ref,
    own,
    far,
    halo,
    slope_ref,
    sem,
):
    self_weight, other_weight = matrix(weights_ref, 0), matrix(weights_ref, 1)
    level_terms(h_ref, (first_ref, second_ref), self_weight, other_weight, own, far, halo)

    def step(index, carry):
        here = chunk_of(index, STEP * BLOCK)
        total, slopes = edges(own[here, :], far[here, :], columns_t_ref[here, :], halo)
        summed_ref[here, :] = total
        edge = chunk_of(index, 8 * STEP * BLOCK)
        slope_ref[edge, :] = jnp.concatenate(slopes, 0)
        pltpu.make_async_copy(slope_ref.at[edge, :], slope_hbm.at[edge, :], sem).start()
        return carry

    lax.fori_loop(0, h_ref.shape[0] // (STEP * BLOCK), step, None)
    new_ref[...] = (
        h_ref[...].astype(f32) + dot(summed_ref[...], matrix(weights_ref, 2))
    ).astype(bf16)
    half_totals(owner_ref, new_ref, counts_ref, 1 - core_of(place_ref), give_ref)
    pltpu.make_async_copy(slope_ref, slope_hbm, sem).wait()


def half_kernel(place_ref, totals_ref, more_totals_ref, after_ref, half_ref, counts_ref):
    half_rows = half_ref.shape[0]
    totals = totals_ref[...].astype(f32) + more_totals_ref[...].astype(f32)
    digits = totals[half_rows:]
    tiles = counts_ref.shape[0]
    counts_ref[...] = DIGIT * digits[:tiles] + digits[tiles:]
    per_row = counts_ref[...].T
    first = core_of(place_ref) == 0
    for tile in range(tiles // 2):
        here = slice(tile * 128, (tile + 1) * 128)
        later = tile + tiles // 2
        low = jnp.broadcast_to(per_row[:, tile : tile + 1], (128, 128))
        high = jnp.broadcast_to(per_row[:, later : later + 1], (128, 128))
        half_ref[here, :] = (totals[here] / jnp.where(first, low, high)).astype(bf16)


def coarse_input_kernel(
    place_ref,
    half_ref,
    their_half_ref,
    sends_ref,
    cin_ref,
    first_ref,
    second_ref,
):
    mine, theirs = half_ref[...].astype(f32), their_half_ref[...].astype(f32)
    first = core_of(place_ref) == 0
    cin = jnp.concatenate([jnp.where(first, mine, theirs), jnp.where(first, theirs, mine)], 0)
    cin = cin.astype(bf16)
    cin_ref[...] = cin
    place = lax.broadcasted_iota(jnp.int32, (cin.shape[0], sends_ref.shape[1]), 0)
    sent = dot_tn(pick(sends_ref[...] == place), cin).astype(bf16)
    halo_rows = first_ref.shape[0]
    first_ref[...] = sent[:halo_rows]
    second_ref[...] = sent[halo_rows:]


def coarse_forward_kernel(
    cin_ref,
    first_ref,
    second_ref,
    weights_ref,
    columns_t_ref,
    summed_ref,
    slope_ref,
    own,
    far,
    halo,
):
    self_weight, other_weight = matrix(weights_ref, 3), matrix(weights_ref, 4)
    level_terms(cin_ref, (first_ref, second_ref), self_weight, other_weight, own, far, halo)

    def step(index, carry):
        here = chunk_of(index, STEP * BLOCK)
        total, slopes = edges(own[here, :], far[here, :], columns_t_ref[here, :], halo)
        summed_ref[here, :] = total
        slope_ref[chunk_of(index, 8 * STEP * BLOCK), :] = jnp.concatenate(slopes, 0)
        return carry

    lax.fori_loop(0, cin_ref.shape[0] // (STEP * BLOCK), step, None)


def coarse_backward_kernel(
    slope_ref,
    chip_sums_ref,
    more_sums_ref,
    weights_ref,
    columns_ref,
    part_ref,
    first_grad_ref,
    second_grad_ref,
    sums_ref,
    ups_ref,
    downs_ref,
    grad_sum,
    halo_grad,
):
    halo_rows = first_grad_ref.shape[0]
    halo_grad[...] = jnp.zeros_like(halo_grad)
    sums_ref[...] = (chip_sums_ref[...].astype(f32) + more_sums_ref[...].astype(f32)).astype(bf16)
    part_ref[...] = dot_nt(sums_ref[...], matrix(weights_ref, 6))
    ups_ref[...] = part_ref[...].astype(bf16)
    grad_sum[...] = (dot_nt(ups_ref[...], matrix(weights_ref, 5)) * 0.5).astype(bf16)
    count = STEP * BLOCK

    def step(index, carry):
        here = chunk_of(index, count)
        slope = slope_ref[chunk_of(index, 8 * count), :]
        slopes = [slope[n * 8 * BLOCK : (n + 1) * 8 * BLOCK] for n in range(STEP)]
        downs_ref[here, :] = edges_back(
            slopes, grad_sum[here, :], columns_ref[:, here], halo_grad
        )
        return carry

    lax.fori_loop(0, part_ref.shape[0] // count, step, None)
    first_grad_ref[...] = halo_grad[:halo_rows, :].astype(bf16)
    second_grad_ref[...] = halo_grad[halo_rows:, :].astype(bf16)


def coarse_tail_kernel(
    place_ref,
    cin_ref,
    first_ref,
    second_ref,
    sums_ref,
    matrices_ref,
    first_grad_ref,
    second_grad_ref,
    summed_ref,
    ups_ref,
    downs_ref,
    fine_ref,
    weights_ref,
):
    cin = cin_ref[...]
    out = (cin.astype(f32) + dot(summed_ref[...], matrix(matrices_ref, 5))).astype(bf16)
    fine_ref[...] = dot(out, matrix(matrices_ref, 6)).astype(bf16)
    pair_grad = dot_tn(cin, downs_ref[...])
    other_grad = (
        pair_grad[:, 128:]
        + dot_tn(first_ref[...], first_grad_ref[...])
        + dot_tn(second_ref[...], second_grad_ref[...])
    )
    grads = [
        pair_grad[:, :128],
        other_grad,
        dot_tn(summed_ref[...], ups_ref[...]),
        dot_tn(out, sums_ref[...]),
    ]
    weights_ref[...] = choose(group_of(place_ref), grads).astype(bf16)


def choose(place, values):
    picked = values[-1]
    for n, value in enumerate(values[:-1]):
        picked = jnp.where(place == n, value, picked)
    return picked


def owner_columns(owner_ref):
    owner = owner_ref[...].astype(f32)
    row = jnp.concatenate([owner[q : q + 1, :] for q in range(owner.shape[0])], 1)
    return jnp.broadcast_to(row, (8, row.shape[1])).T


def owner_rows(owners, values):
    count = owners.shape[0]
    wide = jnp.broadcast_to(owners[:, 0:1], (count, 128))
    lane = lax.broadcasted_iota(jnp.int32, (count, 128), 1)
    first, second = lane.astype(bf16), (lane + 128).astype(bf16)
    rows = []
    for tile in range(values.shape[0] // 256):
        here = (wide - 256.0 * tile).astype(bf16)
        rows += [pick16(here, first), pick16(here, second)]
    return dot(jnp.concatenate(rows, 1), values)


def result_kernel(h_ref, summed_ref, weights_ref, owners_ref, fine_ref, out_hbm, out_ref, sem):
    def step(index, carry):
        here = chunk_of(index, CHUNK)
        updated = h_ref[here, :].astype(f32) + dot(summed_ref[here, :], matrix(weights_ref, 2))
        out_ref[here, :] = (updated + owner_rows(owners_ref[here, :], fine_ref[...])).astype(bf16)
        pltpu.make_async_copy(out_ref.at[here, :], out_hbm.at[here, :], sem).start()
        return carry

    lax.fori_loop(0, h_ref.shape[0] // CHUNK, step, None)
    pltpu.make_async_copy(out_ref, out_hbm, sem).wait()


def fine_backward_kernel(
    place_ref,
    h_ref,
    first_ref,
    second_ref,
    g_ref,
    summed_ref,
    slope_hbm,
    matrices_ref,
    columns_ref,
    owners_ref,
    part_ref,
    counts_ref,
    coarse_downs_ref,
    first_back_ref,
    second_back_ref,
    sends_ref,
    coarse_weights_ref,
    ups_ref,
    downs_ref,
    first_grad_ref,
    second_grad_ref,
    give_ref,
    keep_ref,
    grad_sum,
    halo_grad,
    mean,
    slope_ref,
    weights,
    slope_sems,
):
    count = STEP * BLOCK
    steps = h_ref.shape[0] // count

    def slope_copy(index):
        edge = chunk_of(index, 8 * count)
        return pltpu.make_async_copy(
            slope_hbm.at[edge, :], slope_ref.at[edge, :], slope_sems.at[index]
        )

    for index in range(steps):
        slope_copy(index).start()
    halo_rows = first_ref.shape[0]
    coarse_rows = part_ref.shape[0]
    halo_grad[...] = jnp.zeros_like(halo_grad)

    place = lax.broadcasted_iota(jnp.int32, (coarse_rows, sends_ref.shape[1]), 0)
    sends = pick(sends_ref[...] == place)
    back = jnp.concatenate([first_back_ref[...], second_back_ref[...]], 0)
    back = dot_nt(back, matrix(matrices_ref, 4)).astype(bf16)
    plain = jnp.concatenate([matrix(matrices_ref, 3), matrix(matrices_ref, 4)], 1)
    grad_in = part_ref[...] + dot_nt(coarse_downs_ref[...], plain) + dot(sends, back)
    per_row = counts_ref[...].T
    for tile in range(coarse_rows // 128):
        here = slice(tile * 128, (tile + 1) * 128)
        mean[here, :] = (grad_in[here, :] / per_row[:, tile : tile + 1]).astype(bf16)

    def owner_step(index):
        here = chunk_of(index, count)
        grad_up = g_ref[here, :].astype(f32) + owner_rows(owners_ref[here, :], mean[...])
        ups = grad_up.astype(bf16)
        ups_ref[here, :] = ups
        grad_sum[here, :] = (dot_nt(ups, matrix(matrices_ref, 2)) * 0.5).astype(bf16)

    def edge_step(index):
        here = chunk_of(index, count)
        slope_copy(index).wait()
        slope = slope_ref[chunk_of(index, 8 * count), :]
        slopes = [slope[n * 8 * BLOCK : (n + 1) * 8 * BLOCK] for n in range(STEP)]
        downs_ref[here, :] = edges_back(
            slopes, grad_sum[here, :], columns_ref[:, here], halo_grad
        )

    owner_step(0)

    def step(index, carry):
        edge_step(index)
        owner_step(index + 1)
        return carry

    lax.fori_loop(0, steps - 1, step, None)
    edge_step(steps - 1)
    first_grad = halo_grad[:halo_rows, :].astype(bf16)
    second_grad = halo_grad[halo_rows:, :].astype(bf16)
    first_grad_ref[...] = first_grad
    second_grad_ref[...] = second_grad
    pair_grad = dot_tn(h_ref[...], downs_ref[...])
    weights[0:128, :] = pair_grad[:, :128]
    weights[128:256, :] = (
        pair_grad[:, 128:]
        + dot_tn(first_ref[...], first_grad)
        + dot_tn(second_ref[...], second_grad)
    )
    weights[256:384, :] = dot_tn(summed_ref[...], ups_ref[...])
    first = core_of(place_ref) == 0
    low, high = weights[:192, :], weights[192:, :]
    give_ref[...] = jnp.where(first, high, low)
    keep_ref[:192, :] = jnp.where(first, low, high)
    keep_ref[192:, :] = coarse_weights_ref[...].astype(f32)


def finish_kernel(
    ups_ref,
    downs_ref,
    first_back_ref,
    second_back_ref,
    sends_ref,
    matrices_ref,
    out_hbm,
    out_ref,
    sem,
):
    other = matrix(matrices_ref, 1)
    plain = jnp.concatenate([matrix(matrices_ref, 0), other], 1)
    back = jnp.concatenate([first_back_ref[...], second_back_ref[...]], 0)
    back = dot_nt(back, other).astype(bf16)
    sends = sends_ref[...]
    place = lax.broadcasted_iota(jnp.int32, (256, sends.shape[1]), 0).astype(bf16)

    def step(index, carry):
        here = chunk_of(index, CHUNK)
        rows = []
        for part in range(CHUNK // 256):
            local = (sends - (index * CHUNK + 256 * part)).astype(f32)
            rows.append(pick16(jnp.broadcast_to(local, place.shape).astype(bf16), place))
        grad = ups_ref[here, :].astype(f32) + dot_nt(downs_ref[here, :], plain)
        out_ref[here, :] = (grad + dot(jnp.concatenate(rows, 0), back)).astype(bf16)
        pltpu.make_async_copy(out_ref.at[here, :], out_hbm.at[here, :], sem).start()
        return carry

    lax.fori_loop(0, ups_ref.shape[0] // CHUNK, step, None)
    pltpu.make_async_copy(out_ref, out_hbm, sem).wait()


def add_kernel(mine_ref, theirs_ref, *rest):
    out_ref = rest[-1]
    out_ref[...] = (mine_ref[...].astype(f32) + theirs_ref[...].astype(f32)).astype(bf16)


def add_first_kernel(keep_ref, theirs_ref, out_ref):
    out_ref[:192, :] = (keep_ref[:192, :] + theirs_ref[...]).astype(bf16)
    out_ref[192:, :] = keep_ref[192:, :].astype(bf16)


def add_gather_kernel(mine_ref, y_ref, x_ref, both_ref, after_ref, out_ref):
    mine = mine_ref[...].astype(f32) + y_ref[...].astype(f32)
    theirs = x_ref[...].astype(f32) + both_ref[...].astype(f32)
    out_ref[:192, :] = mine[:192] + theirs[:192]
    out_ref[192:320, :] = mine[192:]
    out_ref[320:, :] = theirs[192:]


def weights_kernel(place_ref, mine_ref, theirs_ref, out_ref):
    group = group_of(place_ref)
    low, high = lax.rem(group, 2), group // 2
    mine, theirs = mine_ref[:192, :], theirs_ref[:192, :]
    out_ref[:192, :] = jnp.where(low == 0, mine, theirs)
    out_ref[192:384, :] = jnp.where(low == 0, theirs, mine)
    for n in range(4):
        near = jnp.where(low == n % 2, mine_ref[192:320, :], theirs_ref[192:320, :])
        far = jnp.where(low == n % 2, mine_ref[320:448, :], theirs_ref[320:448, :])
        value = jnp.where(high == n // 2, near, far)
        out_ref[384 + 128 * n : 512 + 128 * n, :] = value


def exchange(first, second):
    count = lax.axis_size("sub")
    routes = []
    for start in range(2):
        pairs = [(i, i + 1) for i in range(start, count - 1, 2)]
        routes.append(pairs + [(j, i) for i, j in pairs])
    return lax.ppermute(first, "sub", routes[0]), lax.ppermute(second, "sub", routes[1])


def swapped(block, axis, distance):
    return lax.ppermute(block, axis, [(i, i ^ distance) for i in range(lax.axis_size(axis))])


def total_weights(give, keep, place, after, last):
    weights = call(
        add_first_kernel, shape(320, 128, bf16), [keep, swapped(give, "grp", 1)]
    )
    distance, number = 2, 0
    while distance < lax.axis_size("sub"):
        theirs = swapped(weights, "sub", distance)
        waits = after[number] if number < len(after) else ()
        weights = call(
            add_kernel,
            shape(320, 128, bf16),
            [weights, theirs, *waits],
            [VMEM, VMEM] + [HBM, ANY, ANY][: len(waits)],
        )
        distance, number = 2 * distance, number + 1
    count = lax.axis_size("sub")
    corners = [
        (g * count + s, (g ^ 2) * count + (s ^ 1))
        for g in range(lax.axis_size("grp"))
        for s in range(count)
    ]
    weights = call(
        add_gather_kernel,
        shape(448, 128, f32),
        [
            weights,
            swapped(weights, "sub", 1),
            swapped(weights, "grp", 2),
            lax.ppermute(weights, ("grp", "sub"), corners),
            last,
        ],
        [VMEM] * 4 + [HBM],
    )
    return call(
        weights_kernel,
        shape(896, 128, f32),
        [place, weights, swapped(weights, "grp", 1)],
        [VMEM] * 3,
    )


def per_device(
    states,
    cotangent,
    fine_self,
    fine_other,
    fine_node,
    coarse_self,
    coarse_other,
    coarse_node,
    prolong,
    fine_nbr,
    fine_mask,
    fine_send_lo,
    fine_send_hi,
    coarse_nbr,
    coarse_mask,
    coarse_send_lo,
    coarse_send_hi,
    coarse_owner,
):
    rows, features = states.shape
    coarse_rows = coarse_nbr.shape[0]
    halo_rows = fine_send_lo.shape[0]
    coarse_halo = coarse_send_lo.shape[0]
    count_rows = coarse_rows // 128
    owner = coarse_owner.reshape(rows // 128, 128)

    def buffer(count, columns, dtype):
        return pltpu.VMEM((count, columns), dtype)

    to_first, to_second, states, place = gather_rows(states, fine_send_lo, fine_send_hi)
    first, second = exchange(to_first, to_second)

    (
        counts, columns, columns_t, coarse_columns, coarse_columns_t, cotangent, matrices, sends,
        coarse_sends, owner,
    ) = call(
        functools.partial(prepare_kernel, halo_rows=halo_rows, coarse_halo=coarse_halo),
        [
            shape(2 * count_rows, features, bf16),
            shape(8, rows, f32),
            shape(rows, 8, f32),
            shape(8, coarse_rows, f32),
            shape(coarse_rows, 8, f32),
            shape(rows, features, bf16),
            shape(7 * features, features, bf16),
            shape(1, 2 * halo_rows, jnp.int32),
            shape(1, 2 * coarse_halo, jnp.int32),
            shape(rows // 128, 128, jnp.int32),
        ],
        [
            place, cotangent, owner, fine_nbr.T, fine_mask.T, coarse_nbr.T, coarse_mask.T,
            fine_send_lo[None], fine_send_hi[None], coarse_send_lo[None], coarse_send_hi[None],
            fine_self, fine_other, fine_node, coarse_self, coarse_other, coarse_node, prolong,
            to_first,
        ],
        [VMEM] + [HBM] * 17 + [ANY],
        [buffer(8, rows, jnp.int32)] * 2
        + [buffer(8, coarse_rows, jnp.int32)] * 2
        + [buffer(1, halo_rows, jnp.int32)] * 2
        + [buffer(1, coarse_halo, jnp.int32)] * 2
        + [pltpu.SemaphoreType.DMA((17,))],
    )

    sums = call(
        sums_kernel,
        shape(coarse_rows, features, bf16),
        [owner, cotangent, sends],
        [VMEM, VMEM, ANY],
    )
    sums = call(
        relay_kernel,
        shape(coarse_rows, features, bf16),
        [sums, first, second],
        [VMEM, ANY, ANY],
    )
    more_sums = swapped(sums, "grp", 1)

    half_rows = coarse_rows // 2 + 2 * count_rows
    summed, slope, new, give = call(
        fine_forward_kernel,
        [
            shape(rows, features, bf16),
            pltpu.HBM((8 * rows, features), bf16),
            shape(rows, features, bf16),
            shape(half_rows, features, bf16),
        ],
        [place, states, first, second, matrices, columns_t, owner, counts, sums],
        [VMEM] * 8 + [ANY],
        [
            buffer(rows, features, f32),
            buffer(rows, features, bf16),
            buffer(2 * halo_rows, features, bf16),
            buffer(8 * rows, features, bf16),
            pltpu.SemaphoreType.DMA,
        ],
        [VMEM, HBM, VMEM, VMEM],
        mib=32,
    )
    theirs = swapped(give, "grp", 1)
    keep = call(
        keep_kernel,
        shape(half_rows, features, bf16),
        [place, owner, new, counts],
        [VMEM] + [VMEM] * 3,
    )
    chip_totals = call(add_kernel, shape(half_rows, features, bf16), [keep, theirs])
    more_totals = swapped(chip_totals, "grp", 2)
    chip_sums = call(
        add_kernel,
        shape(coarse_rows, features, bf16),
        [sums, more_sums, chip_totals],
        [VMEM, VMEM, ANY],
    )
    more_sums = swapped(chip_sums, "grp", 2)
    owners_t = call(owners_kernel, shape(rows, 8, f32), [owner, chip_totals], [VMEM, ANY])

    half, counts = call(
        half_kernel,
        [shape(coarse_rows // 2, features, bf16), shape(count_rows, features, f32)],
        [place, chip_totals, more_totals, owners_t],
        [VMEM, VMEM, VMEM, ANY],
    )
    their_half = swapped(half, "grp", 1)
    coarse_in, to_first, to_second = call(
        coarse_input_kernel,
        [
            shape(coarse_rows, features, bf16),
            shape(coarse_halo, features, bf16),
            shape(coarse_halo, features, bf16),
        ],
        [place, half, their_half, coarse_sends],
    )
    coarse_first, coarse_second = exchange(to_first, to_second)

    coarse_sum, coarse_slope = call(
        coarse_forward_kernel,
        [shape(coarse_rows, features, bf16), shape(8 * coarse_rows, features, bf16)],
        [coarse_in, coarse_first, coarse_second, matrices, coarse_columns_t],
        scratch=[
            buffer(coarse_rows, features, f32),
            buffer(coarse_rows, features, bf16),
            buffer(2 * coarse_halo, features, bf16),
        ],
    )
    coarse_part, first_grad, second_grad, sums, coarse_ups, coarse_downs = call(
        coarse_backward_kernel,
        [
            shape(coarse_rows, features, f32),
            shape(coarse_halo, features, bf16),
            shape(coarse_halo, features, bf16),
            shape(coarse_rows, features, bf16),
            shape(coarse_rows, features, bf16),
            shape(coarse_rows, 2 * features, bf16),
        ],
        [coarse_slope, chip_sums, more_sums, matrices, coarse_columns],
        scratch=[
            buffer(coarse_rows, features, bf16),
            buffer(2 * coarse_halo, features, f32),
        ],
    )
    first_back, second_back = exchange(first_grad, second_grad)

    fine_term, coarse_weights = call(
        coarse_tail_kernel,
        [shape(coarse_rows, features, bf16), shape(features, features, bf16)],
        [
            place, coarse_in, coarse_first, coarse_second, sums, matrices,
            first_grad, second_grad, coarse_sum, coarse_ups, coarse_downs,
        ],
        [VMEM] + [VMEM] * 10,
    )
    result = call(
        result_kernel,
        pltpu.HBM((rows, features), bf16),
        [states, summed, matrices, owners_t, fine_term],
        scratch=[buffer(rows, features, bf16), pltpu.SemaphoreType.DMA],
        out_specs=HBM,
    )

    ups, downs, first_grad, second_grad, give, keep = call(
        fine_backward_kernel,
        [
            shape(rows, features, bf16),
            shape(rows, 2 * features, bf16),
            shape(halo_rows, features, bf16),
            shape(halo_rows, features, bf16),
            shape(192, features, f32),
            shape(320, features, f32),
        ],
        [
            place, states, first, second, cotangent, summed, slope, matrices, columns, owners_t,
            coarse_part, counts, coarse_downs, first_back, second_back, coarse_sends,
            coarse_weights,
        ],
        [VMEM] + [VMEM] * 5 + [HBM] + [VMEM] * 10,
        [
            buffer(rows, features, bf16),
            buffer(2 * halo_rows, features, f32),
            buffer(coarse_rows, features, bf16),
            buffer(8 * rows, features, bf16),
            buffer(384, features, f32),
            pltpu.SemaphoreType.DMA((rows // (STEP * BLOCK),)),
        ],
        mib=32,
    )
    first_back, second_back = exchange(first_grad, second_grad)

    grad_states = call(
        finish_kernel,
        pltpu.HBM((rows, features), bf16),
        [ups, downs, first_back, second_back, sends, matrices],
        scratch=[buffer(rows, features, bf16), pltpu.SemaphoreType.DMA],
        out_specs=HBM,
    )
    grad_weights = total_weights(
        give, keep, place, ((), (result, first_back, second_back)), grad_states
    )
    return (result, grad_states, grad_weights.reshape(7, features, features))


def solution(mesh):
    fine = P(("grp", "sub"), None)
    fine_row = P(("grp", "sub"))
    in_specs = (
        (fine, fine)
        + (P(),) * 7
        + (fine, fine, fine_row, fine_row)
        + (P("sub", None), P("sub", None), P("sub"), P("sub"), fine_row)
    )
    return jax.shard_map(
        per_device, mesh=mesh, in_specs=in_specs, out_specs=(fine, fine, P()), check_vma=False
    )
```

```python
import functools

import jax
import jax.numpy as jnp
from jax import lax
from jax.experimental import pallas as pl
from jax.experimental.pallas import tpu as pltpu
from jax.sharding import PartitionSpec as P

f32 = jnp.float32
bf16 = jnp.bfloat16
BLOCK = 64
PAIR = 2 * BLOCK
STEP = 16
CHUNK = 1024
NEVER = -1e30
DIGIT = 64.0
VMEM = pl.BlockSpec(memory_space=pltpu.VMEM)
SMEM = pl.BlockSpec(memory_space=pltpu.SMEM)
ANY = pl.BlockSpec(memory_space=pl.ANY)
HBM = pl.BlockSpec(memory_space=pltpu.HBM)
MIB = 1024 * 1024


def dot(a, b):
    return jnp.dot(a, b, preferred_element_type=f32)


def dot_nt(a, b):
    return lax.dot_general(a, b, (((1,), (1,)), ((), ())), preferred_element_type=f32)


def dot_tn(a, b):
    return lax.dot_general(a, b, (((0,), (0,)), ((), ())), preferred_element_type=f32)


def pick(condition):
    return jnp.where(condition, 1.0, 0.0).astype(bf16)


def pick16(values, places):
    return jnp.where(values == places, jnp.ones((), bf16), jnp.zeros((), bf16))


def call(kernel, out_shape, args, in_specs=None, scratch=(), out_specs=None, mib=16):
    many = isinstance(out_shape, (list, tuple))
    in_specs = in_specs or [VMEM] * len(args)
    args = [
        pltpu.with_memory_space_constraint(arg, pltpu.HBM) if spec is HBM else arg
        for arg, spec in zip(args, in_specs)
    ]
    return pl.pallas_call(
        kernel,
        out_shape=out_shape,
        in_specs=in_specs,
        out_specs=out_specs or ([VMEM] * len(out_shape) if many else VMEM),
        scratch_shapes=list(scratch),
        compiler_params=pltpu.CompilerParams(vmem_limit_bytes=mib * MIB),
    )(*args)


def shape(rows, columns, dtype):
    return jax.ShapeDtypeStruct((rows, columns), dtype)


def lanes(row, count):
    return row[:, :count] if count < 128 else jnp.concatenate([row] * (count // 128), 1)


def is_even(place_ref):
    return place_ref[0:1, :]


def group_of(place_ref):
    return place_ref[8:9, :]


def core_of(place_ref):
    return lax.rem(place_ref[8:9, :], 2)


def slot_columns(nbr, mask, halo_rows, even):
    rows = nbr.shape[1]
    block = lax.broadcasted_iota(jnp.int32, nbr.shape, 1) // BLOCK
    halo = lax.rem(block, halo_rows // BLOCK) * BLOCK
    lower = BLOCK + BLOCK * lanes(even, rows)
    column = jnp.where(
        nbr < rows,
        nbr - block * BLOCK,
        jnp.where(
            nbr < rows + halo_rows,
            lower + nbr - rows - halo,
            3 * BLOCK - lower + nbr - rows - halo_rows - halo,
        ),
    )
    return jnp.where(mask > 0, column, 3 * BLOCK).astype(f32)


def selector(columns_t):
    first = lax.broadcasted_iota(jnp.int32, (BLOCK, 128), 1).astype(bf16)
    second = (lax.broadcasted_iota(jnp.int32, (BLOCK, 128), 1) + 128).astype(bf16)
    parts = []
    for k in range(8):
        wide = jnp.broadcast_to(columns_t[:, k : k + 1], (BLOCK, 128)).astype(bf16)
        parts.append(jnp.concatenate([pick16(wide, first), pick16(wide, second)], 1))
    return jnp.concatenate(parts, 0)


def selector_t(columns, rolled, half):
    lane = lax.broadcasted_iota(jnp.int32, (1, 128), 1)
    place = lax.broadcasted_iota(jnp.int32, (3 * BLOCK, 128), 0).astype(bf16)
    parts = []
    for j in range(4):
        left, right = (columns, rolled) if half == 0 else (rolled, columns)
        row = jnp.where(lane < BLOCK, left[2 * j : 2 * j + 1], right[2 * j + 1 : 2 * j + 2])
        wide = jnp.broadcast_to(row, (3 * BLOCK, 128)).astype(bf16)
        parts.append(pick16(wide, place))
    return jnp.concatenate(parts, 1)


def window_of(far, halo, place):
    halo_rows = halo.shape[0] // 2
    start = place * BLOCK
    return jnp.concatenate(
        [
            far,
            halo[start : start + BLOCK, :],
            halo[halo_rows + start : halo_rows + start + BLOCK, :],
            jnp.full((BLOCK, far.shape[1]), NEVER, bf16),
        ],
        0,
    )


def chunk_of(index, count):
    return pl.ds(pl.multiple_of(index * count, count), count)


def matrix(weights_ref, n):
    return weights_ref[128 * n : 128 * (n + 1), :]


def level_terms(h_ref, halo_refs, self_weight, other_weight, own, far, halo):
    halo_rows = halo_refs[0].shape[0]
    other = other_weight * 0.5
    terms = dot(h_ref[...], jnp.concatenate([self_weight * 0.5, other], 1))
    own[...] = terms[:, :128]
    far[...] = terms[:, 128:].astype(bf16)
    halo[:halo_rows, :] = dot(halo_refs[0][...], other).astype(bf16)
    halo[halo_rows:, :] = dot(halo_refs[1][...], other).astype(bf16)


def edges(own_rows, far_rows, slots, halo):
    places = halo.shape[0] // (2 * BLOCK)
    assert STEP % places == 0
    tables = []
    for n in range(STEP):
        part = slice(n * BLOCK, (n + 1) * BLOCK)
        window = window_of(far_rows[part], halo, n % places)
        tables.append(dot(selector(slots[part]), window))
    sums, slopes = [], []
    for n, picked in enumerate(tables):
        own = own_rows[n * BLOCK : (n + 1) * BLOCK]
        values, pieces = [], []
        for k in range(8):
            y = (picked[k * BLOCK : (k + 1) * BLOCK] + own).astype(bf16)
            t = jnp.tanh(y)
            bent = y * t
            values.append(y + bent)
            pieces.append((1 + t) * (1 + (y - bent)))
        while len(values) > 1:
            values = [left + right for left, right in zip(values[::2], values[1::2])]
        sums.append(values[0])
        slopes.append(jnp.concatenate(pieces, 0))
    return jnp.concatenate(sums, 0), slopes


def edges_back(slopes, grad_sum, columns, halo_grad):
    places = halo_grad.shape[0] // (2 * BLOCK)
    halo_rows = halo_grad.shape[0] // 2
    windows, downs = [], []
    for n, slope in enumerate(slopes):
        part = grad_sum[n * BLOCK : (n + 1) * BLOCK]
        grads = [slope[k * BLOCK : (k + 1) * BLOCK] * part for k in range(8)]
        downs.append(sum(grad.astype(f32) for grad in grads))
        mine = columns[:, n // 2 * PAIR : (n // 2 + 1) * PAIR]
        selected = selector_t(mine, pltpu.roll(mine, BLOCK, 1), n % 2)
        windows.append(dot(selected, jnp.concatenate(grads, 0)))
    for place in range(places):
        for side in range(2):
            start = side * halo_rows + place * BLOCK
            total = halo_grad[start : start + BLOCK, :]
            for window in windows[place::places]:
                total = total + window[(side + 1) * BLOCK : (side + 2) * BLOCK]
            halo_grad[start : start + BLOCK, :] = total
    local = jnp.concatenate([window[:BLOCK] for window in windows], 0)
    down = jnp.concatenate(downs, 0)
    return jnp.concatenate([down, local], 1).astype(bf16)


def fetch(pairs, sems):
    copies = [pltpu.make_async_copy(src, dst, sems.at[n]) for n, (src, dst) in enumerate(pairs)]
    for copy in copies:
        copy.start()
    for copy in copies:
        copy.wait()


def gather_kernel(
    lo_hbm,
    hi_hbm,
    x_hbm,
    first_ref,
    second_ref,
    x_ref,
    vector_ref,
    wide,
    up,
    down,
    lo,
    hi,
    sems,
):
    fetch([(x_hbm, x_ref), (lo_hbm, lo), (hi_hbm, hi)], sems)
    wide[...] = x_ref[...].astype(f32)

    def step(r, carry):
        up[pl.ds(r, 1), :] = wide[pl.ds(hi[r], 1), :]
        down[pl.ds(r, 1), :] = wide[pl.ds(lo[r], 1), :]
        return carry

    lax.fori_loop(0, up.shape[0], step, None, unroll=16)
    parity = 1 - lax.rem(lax.axis_index("sub"), 2)
    even = parity > 0
    vector_ref[:8, :] = jnp.full((8, 128), parity, jnp.int32)
    vector_ref[8:, :] = jnp.full((8, 128), lax.axis_index("grp"), jnp.int32)
    first_ref[...] = jnp.where(even, up[...], down[...]).astype(bf16)
    second_ref[...] = jnp.where(even, down[...], up[...]).astype(bf16)


def gather_rows(x, send_lo, send_hi):
    rows, features = x.shape
    count = send_lo.shape[0]
    out = shape(count, features, bf16)
    return call(
        gather_kernel,
        [out, out, shape(rows, features, bf16), shape(16, 128, jnp.int32)],
        [send_lo, send_hi, x],
        [HBM, HBM, HBM],
        [
            pltpu.VMEM((rows, features), f32),
            pltpu.VMEM((count, features), f32),
            pltpu.VMEM((count, features), f32),
            pltpu.SMEM((count,), jnp.int32),
            pltpu.SMEM((count,), jnp.int32),
            pltpu.SemaphoreType.DMA((3,)),
        ],
    )


def owner_sums(owner_ref, tile, values):
    place = lax.broadcasted_iota(jnp.int32, (256, 128), 0).astype(bf16)
    owner = (owner_ref[...] - tile * 256).astype(f32)
    rows = jnp.concatenate(
        [
            pick16(jnp.broadcast_to(owner[q : q + 1], (256, 128)).astype(bf16), place)
            for q in range(owner.shape[0])
        ],
        1,
    )
    return dot(rows, values)


def prepare_kernel(
    place_ref,
    g_hbm,
    owner_hbm,
    nbr_hbm,
    mask_hbm,
    coarse_nbr_hbm,
    coarse_mask_hbm,
    lo_hbm,
    hi_hbm,
    coarse_lo_hbm,
    coarse_hi_hbm,
    *rest,
    halo_rows,
    coarse_halo,
):
    weight_hbms, rest = rest[:7], rest[7:]
    (
        after_ref,
        counts_ref,
        columns_ref,
        columns_t_ref,
        coarse_columns_ref,
        coarse_columns_t_ref,
        g_ref,
        weights_ref,
        sends_ref,
        coarse_sends_ref,
        owner_ref,
        nbr_ref,
        mask_ref,
        coarse_nbr_ref,
        coarse_mask_ref,
        lo_ref,
        hi_ref,
        coarse_lo_ref,
        coarse_hi_ref,
        sems,
    ) = rest
    fetch(
        [
            (g_hbm, g_ref),
            (owner_hbm, owner_ref),
            (nbr_hbm, nbr_ref),
            (mask_hbm, mask_ref),
            (coarse_nbr_hbm, coarse_nbr_ref),
            (coarse_mask_hbm, coarse_mask_ref),
            (lo_hbm, lo_ref),
            (hi_hbm, hi_ref),
            (coarse_lo_hbm, coarse_lo_ref),
            (coarse_hi_hbm, coarse_hi_ref),
        ]
        + [(w, weights_ref.at[pl.ds(128 * n, 128), :]) for n, w in enumerate(weight_hbms)],
        sems,
    )
    even = is_even(place_ref)
    for low, high, out in (
        (lo_ref, hi_ref, sends_ref),
        (coarse_lo_ref, coarse_hi_ref, coarse_sends_ref),
    ):
        up = lanes(even, low.shape[1]) > 0
        first = jnp.where(up, high[...], low[...])
        second = jnp.where(up, low[...], high[...])
        out[...] = jnp.concatenate([first, second], 1)
    columns_ref[...] = slot_columns(nbr_ref[...], mask_ref[...], halo_rows, even)
    columns_t_ref[...] = columns_ref[...].T
    coarse_columns_ref[...] = slot_columns(
        coarse_nbr_ref[...], coarse_mask_ref[...], coarse_halo, even
    )
    coarse_columns_t_ref[...] = coarse_columns_ref[...].T
    tiles = counts_ref.shape[0] // 2
    owner = owner_ref[...]
    high, low = owner // 128, lax.rem(owner, 128)
    groups = owner.shape[0]
    place = lax.broadcasted_iota(jnp.int32, (128, 128), 0)
    high_rows = jnp.concatenate(
        [pick(high[q : q + 1, :] == place[:tiles]) for q in range(groups)], 1
    )
    low_rows = jnp.concatenate(
        [pick(low[q : q + 1, :] == place) for q in range(groups)], 1
    )
    counts = dot_nt(high_rows, low_rows)
    most = jnp.floor(counts * (1 / DIGIT))
    counts_ref[...] = jnp.concatenate([most, counts - DIGIT * most], 0).astype(bf16)


def sums_kernel(owner_ref, g_ref, after_ref, sums_ref):
    def step(tile, carry):
        sums_ref[chunk_of(tile, 256), :] = owner_sums(owner_ref, tile, g_ref[...]).astype(bf16)
        return carry

    lax.fori_loop(0, sums_ref.shape[0] // 256, step, None)


def relay_kernel(x_ref, after_ref, also_after_ref, out_ref):
    out_ref[...] = x_ref[...]


def owners_kernel(owner_ref, after_ref, owners_ref):
    owners_ref[...] = owner_columns(owner_ref)


def half_totals(owner_ref, new_ref, counts_ref, half, out_ref):
    tiles = (out_ref.shape[0] - counts_ref.shape[0]) // 256
    for tile in range(tiles):
        totals = owner_sums(owner_ref, half * tiles + tile, new_ref[...])
        out_ref[256 * tile : 256 * (tile + 1), :] = totals.astype(bf16)
    out_ref[256 * tiles :, :] = counts_ref[...]


def keep_kernel(place_ref, owner_ref, new_ref, counts_ref, out_ref):
    half_totals(owner_ref, new_ref, counts_ref, core_of(place_ref), out_ref)


def fine_forward_kernel(
    place_ref,
    h_ref,
    first_ref,
    second_ref,
    weights_ref,
    columns_t_ref,
    owner_ref,
    counts_ref,
    after_ref,
    summed_ref,
    slope_hbm,
    new_ref,
    give_ref,
    own,
    far,
    halo,
    slope_ref,
    sem,
):
    self_weight, other_weight = matrix(weights_ref, 0), matrix(weights_ref, 1)
    level_terms(h_ref, (first_ref, second_ref), self_weight, other_weight, own, far, halo)

    def step(index, carry):
        here = chunk_of(index, STEP * BLOCK)
        total, slopes = edges(own[here, :], far[here, :], columns_t_ref[here, :], halo)
        summed_ref[here, :] = total
        edge = chunk_of(index, 8 * STEP * BLOCK)
        slope_ref[edge, :] = jnp.concatenate(slopes, 0)
        pltpu.make_async_copy(slope_ref.at[edge, :], slope_hbm.at[edge, :], sem).start()
        return carry

    lax.fori_loop(0, h_ref.shape[0] // (STEP * BLOCK), step, None)
    new_ref[...] = (
        h_ref[...].astype(f32) + dot(summed_ref[...], matrix(weights_ref, 2))
    ).astype(bf16)
    half_totals(owner_ref, new_ref, counts_ref, 1 - core_of(place_ref), give_ref)
    pltpu.make_async_copy(slope_ref, slope_hbm, sem).wait()


def half_kernel(place_ref, totals_ref, more_totals_ref, after_ref, half_ref, counts_ref):
    half_rows = half_ref.shape[0]
    totals = totals_ref[...].astype(f32) + more_totals_ref[...].astype(f32)
    digits = totals[half_rows:]
    tiles = counts_ref.shape[0]
    counts_ref[...] = DIGIT * digits[:tiles] + digits[tiles:]
    per_row = counts_ref[...].T
    first = core_of(place_ref) == 0
    for tile in range(tiles // 2):
        here = slice(tile * 128, (tile + 1) * 128)
        later = tile + tiles // 2
        low = jnp.broadcast_to(per_row[:, tile : tile + 1], (128, 128))
        high = jnp.broadcast_to(per_row[:, later : later + 1], (128, 128))
        half_ref[here, :] = (totals[here] / jnp.where(first, low, high)).astype(bf16)


def coarse_input_kernel(
    place_ref,
    half_ref,
    their_half_ref,
    sends_ref,
    cin_ref,
    first_ref,
    second_ref,
):
    mine, theirs = half_ref[...].astype(f32), their_half_ref[...].astype(f32)
    first = core_of(place_ref) == 0
    cin = jnp.concatenate([jnp.where(first, mine, theirs), jnp.where(first, theirs, mine)], 0)
    cin = cin.astype(bf16)
    cin_ref[...] = cin
    place = lax.broadcasted_iota(jnp.int32, (cin.shape[0], sends_ref.shape[1]), 0)
    sent = dot_tn(pick(sends_ref[...] == place), cin).astype(bf16)
    halo_rows = first_ref.shape[0]
    first_ref[...] = sent[:halo_rows]
    second_ref[...] = sent[halo_rows:]


def coarse_forward_kernel(
    cin_ref,
    first_ref,
    second_ref,
    weights_ref,
    columns_t_ref,
    summed_ref,
    slope_ref,
    own,
    far,
    halo,
):
    self_weight, other_weight = matrix(weights_ref, 3), matrix(weights_ref, 4)
    level_terms(cin_ref, (first_ref, second_ref), self_weight, other_weight, own, far, halo)

    def step(index, carry):
        here = chunk_of(index, STEP * BLOCK)
        total, slopes = edges(own[here, :], far[here, :], columns_t_ref[here, :], halo)
        summed_ref[here, :] = total
        slope_ref[chunk_of(index, 8 * STEP * BLOCK), :] = jnp.concatenate(slopes, 0)
        return carry

    lax.fori_loop(0, cin_ref.shape[0] // (STEP * BLOCK), step, None)


def coarse_backward_kernel(
    slope_ref,
    chip_sums_ref,
    more_sums_ref,
    weights_ref,
    columns_ref,
    part_ref,
    first_grad_ref,
    second_grad_ref,
    sums_ref,
    ups_ref,
    downs_ref,
    grad_sum,
    halo_grad,
):
    halo_rows = first_grad_ref.shape[0]
    halo_grad[...] = jnp.zeros_like(halo_grad)
    sums_ref[...] = (chip_sums_ref[...].astype(f32) + more_sums_ref[...].astype(f32)).astype(bf16)
    part_ref[...] = dot_nt(sums_ref[...], matrix(weights_ref, 6))
    ups_ref[...] = part_ref[...].astype(bf16)
    grad_sum[...] = (dot_nt(ups_ref[...], matrix(weights_ref, 5)) * 0.5).astype(bf16)
    count = STEP * BLOCK

    def step(index, carry):
        here = chunk_of(index, count)
        slope = slope_ref[chunk_of(index, 8 * count), :]
        slopes = [slope[n * 8 * BLOCK : (n + 1) * 8 * BLOCK] for n in range(STEP)]
        downs_ref[here, :] = edges_back(
            slopes, grad_sum[here, :], columns_ref[:, here], halo_grad
        )
        return carry

    lax.fori_loop(0, part_ref.shape[0] // count, step, None)
    first_grad_ref[...] = halo_grad[:halo_rows, :].astype(bf16)
    second_grad_ref[...] = halo_grad[halo_rows:, :].astype(bf16)


def coarse_tail_kernel(
    place_ref,
    cin_ref,
    first_ref,
    second_ref,
    sums_ref,
    matrices_ref,
    first_grad_ref,
    second_grad_ref,
    summed_ref,
    ups_ref,
    downs_ref,
    fine_ref,
    weights_ref,
):
    cin = cin_ref[...]
    out = (cin.astype(f32) + dot(summed_ref[...], matrix(matrices_ref, 5))).astype(bf16)
    fine_ref[...] = dot(out, matrix(matrices_ref, 6)).astype(bf16)
    pair_grad = dot_tn(cin, downs_ref[...])
    other_grad = (
        pair_grad[:, 128:]
        + dot_tn(first_ref[...], first_grad_ref[...])
        + dot_tn(second_ref[...], second_grad_ref[...])
    )
    grads = [
        pair_grad[:, :128],
        other_grad,
        dot_tn(summed_ref[...], ups_ref[...]),
        dot_tn(out, sums_ref[...]),
    ]
    weights_ref[...] = choose(group_of(place_ref), grads).astype(bf16)


def choose(place, values):
    picked = values[-1]
    for n, value in enumerate(values[:-1]):
        picked = jnp.where(place == n, value, picked)
    return picked


def owner_columns(owner_ref):
    owner = owner_ref[...].astype(f32)
    row = jnp.concatenate([owner[q : q + 1, :] for q in range(owner.shape[0])], 1)
    return jnp.broadcast_to(row, (8, row.shape[1])).T


def owner_rows(owners, values):
    count = owners.shape[0]
    wide = jnp.broadcast_to(owners[:, 0:1], (count, 128))
    lane = lax.broadcasted_iota(jnp.int32, (count, 128), 1)
    first, second = lane.astype(bf16), (lane + 128).astype(bf16)
    rows = []
    for tile in range(values.shape[0] // 256):
        here = (wide - 256.0 * tile).astype(bf16)
        rows += [pick16(here, first), pick16(here, second)]
    return dot(jnp.concatenate(rows, 1), values)


def result_kernel(h_ref, summed_ref, weights_ref, owners_ref, fine_ref, out_hbm, out_ref, sem):
    def step(index, carry):
        here = chunk_of(index, CHUNK)
        updated = h_ref[here, :].astype(f32) + dot(summed_ref[here, :], matrix(weights_ref, 2))
        out_ref[here, :] = (updated + owner_rows(owners_ref[here, :], fine_ref[...])).astype(bf16)
        pltpu.make_async_copy(out_ref.at[here, :], out_hbm.at[here, :], sem).start()
        return carry

    lax.fori_loop(0, h_ref.shape[0] // CHUNK, step, None)
    pltpu.make_async_copy(out_ref, out_hbm, sem).wait()


def fine_backward_kernel(
    place_ref,
    h_ref,
    first_ref,
    second_ref,
    g_ref,
    summed_ref,
    slope_hbm,
    matrices_ref,
    columns_ref,
    owners_ref,
    part_ref,
    counts_ref,
    coarse_downs_ref,
    first_back_ref,
    second_back_ref,
    sends_ref,
    coarse_weights_ref,
    ups_ref,
    downs_ref,
    first_grad_ref,
    second_grad_ref,
    give_ref,
    keep_ref,
    grad_sum,
    halo_grad,
    mean,
    slope_ref,
    weights,
    pair,
    slope_sems,
):
    count = STEP * BLOCK
    steps = h_ref.shape[0] // count

    def slope_copy(index):
        edge = chunk_of(index, 8 * count)
        return pltpu.make_async_copy(
            slope_hbm.at[edge, :], slope_ref.at[edge, :], slope_sems.at[index]
        )

    for index in range(steps):
        slope_copy(index).start()
    halo_rows = first_ref.shape[0]
    coarse_rows = part_ref.shape[0]
    halo_grad[...] = jnp.zeros_like(halo_grad)

    place = lax.broadcasted_iota(jnp.int32, (coarse_rows, sends_ref.shape[1]), 0)
    sends = pick(sends_ref[...] == place)
    back = jnp.concatenate([first_back_ref[...], second_back_ref[...]], 0)
    back = dot_nt(back, matrix(matrices_ref, 4)).astype(bf16)
    plain = jnp.concatenate([matrix(matrices_ref, 3), matrix(matrices_ref, 4)], 1)
    grad_in = part_ref[...] + dot_nt(coarse_downs_ref[...], plain) + dot(sends, back)
    per_row = counts_ref[...].T
    for tile in range(coarse_rows // 128):
        here = slice(tile * 128, (tile + 1) * 128)
        mean[here, :] = (grad_in[here, :] / per_row[:, tile : tile + 1]).astype(bf16)

    def owner_step(index):
        here = chunk_of(index, count)
        grad_up = g_ref[here, :].astype(f32) + owner_rows(owners_ref[here, :], mean[...])
        ups = grad_up.astype(bf16)
        ups_ref[here, :] = ups
        weights[256:384, :] += dot_tn(summed_ref[here, :], ups)
        grad_sum[here, :] = (dot_nt(ups, matrix(matrices_ref, 2)) * 0.5).astype(bf16)

    def edge_step(index):
        here = chunk_of(index, count)
        slope_copy(index).wait()
        slope = slope_ref[chunk_of(index, 8 * count), :]
        slopes = [slope[n * 8 * BLOCK : (n + 1) * 8 * BLOCK] for n in range(STEP)]
        both = edges_back(slopes, grad_sum[here, :], columns_ref[:, here], halo_grad)
        downs_ref[here, :] = both
        pair[...] += dot_tn(h_ref[here, :], both)

    pair[...] = jnp.zeros_like(pair)
    weights[256:384, :] = jnp.zeros((128, 128), f32)
    owner_step(0)

    def step(index, carry):
        edge_step(index)
        owner_step(index + 1)
        return carry

    lax.fori_loop(0, steps - 1, step, None)
    edge_step(steps - 1)
    first_grad = halo_grad[:halo_rows, :].astype(bf16)
    second_grad = halo_grad[halo_rows:, :].astype(bf16)
    first_grad_ref[...] = first_grad
    second_grad_ref[...] = second_grad
    weights[0:128, :] = pair[:, :128]
    weights[128:256, :] = (
        pair[:, 128:]
        + dot_tn(first_ref[...], first_grad)
        + dot_tn(second_ref[...], second_grad)
    )
    first = core_of(place_ref) == 0
    low, high = weights[:192, :], weights[192:, :]
    give_ref[...] = jnp.where(first, high, low)
    keep_ref[:192, :] = jnp.where(first, low, high)
    keep_ref[192:, :] = coarse_weights_ref[...].astype(f32)


def finish_kernel(
    ups_ref,
    downs_ref,
    first_back_ref,
    second_back_ref,
    sends_ref,
    matrices_ref,
    out_hbm,
    out_ref,
    sem,
):
    other = matrix(matrices_ref, 1)
    plain = jnp.concatenate([matrix(matrices_ref, 0), other], 1)
    back = jnp.concatenate([first_back_ref[...], second_back_ref[...]], 0)
    back = dot_nt(back, other).astype(bf16)
    sends = sends_ref[...]
    place = lax.broadcasted_iota(jnp.int32, (256, sends.shape[1]), 0).astype(bf16)

    def step(index, carry):
        here = chunk_of(index, CHUNK)
        rows = []
        for part in range(CHUNK // 256):
            local = (sends - (index * CHUNK + 256 * part)).astype(f32)
            rows.append(pick16(jnp.broadcast_to(local, place.shape).astype(bf16), place))
        grad = ups_ref[here, :].astype(f32) + dot_nt(downs_ref[here, :], plain)
        out_ref[here, :] = (grad + dot(jnp.concatenate(rows, 0), back)).astype(bf16)
        pltpu.make_async_copy(out_ref.at[here, :], out_hbm.at[here, :], sem).start()
        return carry

    lax.fori_loop(0, ups_ref.shape[0] // CHUNK, step, None)
    pltpu.make_async_copy(out_ref, out_hbm, sem).wait()


def add_kernel(mine_ref, theirs_ref, *rest):
    out_ref = rest[-1]
    out_ref[...] = (mine_ref[...].astype(f32) + theirs_ref[...].astype(f32)).astype(bf16)


def add_first_kernel(keep_ref, theirs_ref, out_ref):
    out_ref[:192, :] = (keep_ref[:192, :] + theirs_ref[...]).astype(bf16)
    out_ref[192:, :] = keep_ref[192:, :].astype(bf16)


def add_gather_kernel(mine_ref, y_ref, x_ref, both_ref, after_ref, out_ref):
    mine = mine_ref[...].astype(f32) + y_ref[...].astype(f32)
    theirs = x_ref[...].astype(f32) + both_ref[...].astype(f32)
    out_ref[:192, :] = mine[:192] + theirs[:192]
    out_ref[192:320, :] = mine[192:]
    out_ref[320:, :] = theirs[192:]


def weights_kernel(place_ref, mine_ref, theirs_ref, out_ref):
    group = group_of(place_ref)
    low, high = lax.rem(group, 2), group // 2
    mine, theirs = mine_ref[:192, :], theirs_ref[:192, :]
    out_ref[:192, :] = jnp.where(low == 0, mine, theirs)
    out_ref[192:384, :] = jnp.where(low == 0, theirs, mine)
    for n in range(4):
        near = jnp.where(low == n % 2, mine_ref[192:320, :], theirs_ref[192:320, :])
        far = jnp.where(low == n % 2, mine_ref[320:448, :], theirs_ref[320:448, :])
        value = jnp.where(high == n // 2, near, far)
        out_ref[384 + 128 * n : 512 + 128 * n, :] = value


def exchange(first, second):
    count = lax.axis_size("sub")
    routes = []
    for start in range(2):
        pairs = [(i, i + 1) for i in range(start, count - 1, 2)]
        routes.append(pairs + [(j, i) for i, j in pairs])
    return lax.ppermute(first, "sub", routes[0]), lax.ppermute(second, "sub", routes[1])


def swapped(block, axis, distance):
    return lax.ppermute(block, axis, [(i, i ^ distance) for i in range(lax.axis_size(axis))])


def total_weights(give, keep, place, after, last):
    weights = call(
        add_first_kernel, shape(320, 128, bf16), [keep, swapped(give, "grp", 1)]
    )
    distance, number = 2, 0
    while distance < lax.axis_size("sub"):
        theirs = swapped(weights, "sub", distance)
        waits = after[number] if number < len(after) else ()
        weights = call(
            add_kernel,
            shape(320, 128, bf16),
            [weights, theirs, *waits],
            [VMEM, VMEM] + [HBM, ANY, ANY][: len(waits)],
        )
        distance, number = 2 * distance, number + 1
    count = lax.axis_size("sub")
    corners = [
        (g * count + s, (g ^ 2) * count + (s ^ 1))
        for g in range(lax.axis_size("grp"))
        for s in range(count)
    ]
    weights = call(
        add_gather_kernel,
        shape(448, 128, f32),
        [
            weights,
            swapped(weights, "sub", 1),
            swapped(weights, "grp", 2),
            lax.ppermute(weights, ("grp", "sub"), corners),
            last,
        ],
        [VMEM] * 4 + [HBM],
    )
    return call(
        weights_kernel,
        shape(896, 128, f32),
        [place, weights, swapped(weights, "grp", 1)],
        [VMEM] * 3,
    )


def per_device(
    states,
    cotangent,
    fine_self,
    fine_other,
    fine_node,
    coarse_self,
    coarse_other,
    coarse_node,
    prolong,
    fine_nbr,
    fine_mask,
    fine_send_lo,
    fine_send_hi,
    coarse_nbr,
    coarse_mask,
    coarse_send_lo,
    coarse_send_hi,
    coarse_owner,
):
    rows, features = states.shape
    coarse_rows = coarse_nbr.shape[0]
    halo_rows = fine_send_lo.shape[0]
    coarse_halo = coarse_send_lo.shape[0]
    count_rows = coarse_rows // 128
    owner = coarse_owner.reshape(rows // 128, 128)

    def buffer(count, columns, dtype):
        return pltpu.VMEM((count, columns), dtype)

    to_first, to_second, states, place = gather_rows(states, fine_send_lo, fine_send_hi)
    first, second = exchange(to_first, to_second)

    (
        counts, columns, columns_t, coarse_columns, coarse_columns_t, cotangent, matrices, sends,
        coarse_sends, owner,
    ) = call(
        functools.partial(prepare_kernel, halo_rows=halo_rows, coarse_halo=coarse_halo),
        [
            shape(2 * count_rows, features, bf16),
            shape(8, rows, f32),
            shape(rows, 8, f32),
            shape(8, coarse_rows, f32),
            shape(coarse_rows, 8, f32),
            shape(rows, features, bf16),
            shape(7 * features, features, bf16),
            shape(1, 2 * halo_rows, jnp.int32),
            shape(1, 2 * coarse_halo, jnp.int32),
            shape(rows // 128, 128, jnp.int32),
        ],
        [
            place, cotangent, owner, fine_nbr.T, fine_mask.T, coarse_nbr.T, coarse_mask.T,
            fine_send_lo[None], fine_send_hi[None], coarse_send_lo[None], coarse_send_hi[None],
            fine_self, fine_other, fine_node, coarse_self, coarse_other, coarse_node, prolong,
            to_first,
        ],
        [VMEM] + [HBM] * 17 + [ANY],
        [buffer(8, rows, jnp.int32)] * 2
        + [buffer(8, coarse_rows, jnp.int32)] * 2
        + [buffer(1, halo_rows, jnp.int32)] * 2
        + [buffer(1, coarse_halo, jnp.int32)] * 2
        + [pltpu.SemaphoreType.DMA((17,))],
    )

    sums = call(
        sums_kernel,
        shape(coarse_rows, features, bf16),
        [owner, cotangent, sends],
        [VMEM, VMEM, ANY],
    )
    sums = call(
        relay_kernel,
        shape(coarse_rows, features, bf16),
        [sums, first, second],
        [VMEM, ANY, ANY],
    )
    more_sums = swapped(sums, "grp", 1)

    half_rows = coarse_rows // 2 + 2 * count_rows
    summed, slope, new, give = call(
        fine_forward_kernel,
        [
            shape(rows, features, bf16),
            pltpu.HBM((8 * rows, features), bf16),
            shape(rows, features, bf16),
            shape(half_rows, features, bf16),
        ],
        [place, states, first, second, matrices, columns_t, owner, counts, sums],
        [VMEM] * 8 + [ANY],
        [
            buffer(rows, features, f32),
            buffer(rows, features, bf16),
            buffer(2 * halo_rows, features, bf16),
            buffer(8 * rows, features, bf16),
            pltpu.SemaphoreType.DMA,
        ],
        [VMEM, HBM, VMEM, VMEM],
        mib=32,
    )
    theirs = swapped(give, "grp", 1)
    keep = call(
        keep_kernel,
        shape(half_rows, features, bf16),
        [place, owner, new, counts],
        [VMEM] + [VMEM] * 3,
    )
    chip_totals = call(add_kernel, shape(half_rows, features, bf16), [keep, theirs])
    more_totals = swapped(chip_totals, "grp", 2)
    chip_sums = call(
        add_kernel,
        shape(coarse_rows, features, bf16),
        [sums, more_sums, chip_totals],
        [VMEM, VMEM, ANY],
    )
    more_sums = swapped(chip_sums, "grp", 2)
    owners_t = call(owners_kernel, shape(rows, 8, f32), [owner, chip_totals], [VMEM, ANY])

    half, counts = call(
        half_kernel,
        [shape(coarse_rows // 2, features, bf16), shape(count_rows, features, f32)],
        [place, chip_totals, more_totals, owners_t],
        [VMEM, VMEM, VMEM, ANY],
    )
    their_half = swapped(half, "grp", 1)
    coarse_in, to_first, to_second = call(
        coarse_input_kernel,
        [
            shape(coarse_rows, features, bf16),
            shape(coarse_halo, features, bf16),
            shape(coarse_halo, features, bf16),
        ],
        [place, half, their_half, coarse_sends],
    )
    coarse_first, coarse_second = exchange(to_first, to_second)

    coarse_sum, coarse_slope = call(
        coarse_forward_kernel,
        [shape(coarse_rows, features, bf16), shape(8 * coarse_rows, features, bf16)],
        [coarse_in, coarse_first, coarse_second, matrices, coarse_columns_t],
        scratch=[
            buffer(coarse_rows, features, f32),
            buffer(coarse_rows, features, bf16),
            buffer(2 * coarse_halo, features, bf16),
        ],
    )
    coarse_part, first_grad, second_grad, sums, coarse_ups, coarse_downs = call(
        coarse_backward_kernel,
        [
            shape(coarse_rows, features, f32),
            shape(coarse_halo, features, bf16),
            shape(coarse_halo, features, bf16),
            shape(coarse_rows, features, bf16),
            shape(coarse_rows, features, bf16),
            shape(coarse_rows, 2 * features, bf16),
        ],
        [coarse_slope, chip_sums, more_sums, matrices, coarse_columns],
        scratch=[
            buffer(coarse_rows, features, bf16),
            buffer(2 * coarse_halo, features, f32),
        ],
    )
    first_back, second_back = exchange(first_grad, second_grad)

    fine_term, coarse_weights = call(
        coarse_tail_kernel,
        [shape(coarse_rows, features, bf16), shape(features, features, bf16)],
        [
            place, coarse_in, coarse_first, coarse_second, sums, matrices,
            first_grad, second_grad, coarse_sum, coarse_ups, coarse_downs,
        ],
        [VMEM] + [VMEM] * 10,
    )
    result = call(
        result_kernel,
        pltpu.HBM((rows, features), bf16),
        [states, summed, matrices, owners_t, fine_term],
        scratch=[buffer(rows, features, bf16), pltpu.SemaphoreType.DMA],
        out_specs=HBM,
    )

    ups, downs, first_grad, second_grad, give, keep = call(
        fine_backward_kernel,
        [
            shape(rows, features, bf16),
            shape(rows, 2 * features, bf16),
            shape(halo_rows, features, bf16),
            shape(halo_rows, features, bf16),
            shape(192, features, f32),
            shape(320, features, f32),
        ],
        [
            place, states, first, second, cotangent, summed, slope, matrices, columns, owners_t,
            coarse_part, counts, coarse_downs, first_back, second_back, coarse_sends,
            coarse_weights,
        ],
        [VMEM] + [VMEM] * 5 + [HBM] + [VMEM] * 10,
        [
            buffer(rows, features, bf16),
            buffer(2 * halo_rows, features, f32),
            buffer(coarse_rows, features, bf16),
            buffer(8 * rows, features, bf16),
            buffer(384, features, f32),
            buffer(features, 2 * features, f32),
            pltpu.SemaphoreType.DMA((rows // (STEP * BLOCK),)),
        ],
        mib=32,
    )
    first_back, second_back = exchange(first_grad, second_grad)

    grad_states = call(
        finish_kernel,
        pltpu.HBM((rows, features), bf16),
        [ups, downs, first_back, second_back, sends, matrices],
        scratch=[buffer(rows, features, bf16), pltpu.SemaphoreType.DMA],
        out_specs=HBM,
    )
    grad_weights = total_weights(
        give, keep, place, ((), (result, first_back, second_back)), grad_states
    )
    return (result, grad_states, grad_weights.reshape(7, features, features))


def solution(mesh):
    fine = P(("grp", "sub"), None)
    fine_row = P(("grp", "sub"))
    in_specs = (
        (fine, fine)
        + (P(),) * 7
        + (fine, fine, fine_row, fine_row)
        + (P("sub", None), P("sub", None), P("sub"), P("sub"), fine_row)
    )
    return jax.shard_map(
        per_device, mesh=mesh, in_specs=in_specs, out_specs=(fine, fine, P()), check_vma=False
    )
```
